32 devices in a mesh: frames: 8 (over z, y), heads: 4 (over x, core).
Axes of the slice: x: 2, y: 2, z: 4, core: 2. Of those that a mesh axis runs over, the one named last changes fastest.
Arguments:
- queries: bfloat16 [768, 2560], P('frames', 'heads'), may hold values from -40 to 40
- keys_values: bfloat16 [2, 768, 2560], P(None, 'frames', 'heads'), may hold values from -40 to 40
- out_weight: bfloat16 [2560, 5120], P('heads', 'frames'), may hold values from -0.5 to 0.5
Outputs:
- projected: bfloat16 [768, 5120], P('frames', 'heads')
The draws below stay inside these ranges and needn't reach their ends.
All inputs are finite; a program needn't handle non-finite values.
Results may differ from the reference program's by a relative error of at most 0.015.
Values may be sent and summed in bfloat16 or wider, within the bound.
No kernel may reach another device: no remote copies, remote signals or barrier semaphores. Data moves between devices by JAX's collectives and lax.ppermute only.
A program may use at most 64 MiB of HBM per device.

```python
import math
import jax
import jax.numpy as jnp
from jax import lax

D = 5120
HD = 128
HEADS = 20
TPF = 32
FRAMES = 24
BAND = 11
TOKENS = 768


def shared_fields(key):
    base = jax.random.fold_in(key, 11)
    first, second, third = jax.random.split(base, 3)
    shape = (TOKENS, HEADS * HD)
    scale = jnp.exp(jax.random.uniform(third, (TOKENS, 1), jnp.float32, math.log(0.25), math.log(2.5)))
    keys = jnp.clip(jax.random.normal(first, shape, jnp.float32), -6.0, 6.0) * scale
    queries = jnp.clip(jax.random.normal(second, shape, jnp.float32), -6.0, 6.0)
    return (queries, keys)


def draw_queries(key, part):
    queries, keys = shared_fields(key)
    return queries.astype(jnp.bfloat16)


def draw_keys_values(key, part):
    queries, keys = shared_fields(key)
    value_key = jax.random.fold_in(key, 23)
    values = jnp.clip(jax.random.normal(value_key, (TOKENS, HEADS * HD), jnp.float32), -6.0, 6.0)
    return jnp.stack([keys, values]).astype(jnp.bfloat16)


def block_levels(rng, shape, shards, smallest, largest):
    def one(position, blocks):
        draws = jax.random.uniform(jax.random.fold_in(jax.random.fold_in(rng, 6), position), (blocks,), jnp.float32, smallest / len(shards), largest / len(shards))
        return jnp.repeat(jnp.exp(draws), shape[position] // blocks).reshape((-1,) + (1,) * (len(shape) - position - 1))

    factor_of = one(*shards[0])
    for cut in shards[1:]:
        factor_of = factor_of * one(*cut)
    return factor_of


def scatter_about(rng, shape, spread, limit, pieces=(), held_as=jnp.bfloat16):
    result = jax.random.normal(rng, shape, jnp.float32) * spread
    if len(pieces) > 0:
        result = block_levels(rng, shape, pieces, -0.22, 0.18) * result
    return jnp.clip(result, min=-limit, max=limit).astype(held_as)


def setup_inputs(seed: int = 0) -> dict:
    seeds = jax.random.split(jax.random.key(seed), 4)
    return {
        "queries": draw_queries(jax.random.fold_in(seeds[3], 71), 0),
        "keys_values": draw_keys_values(jax.random.fold_in(seeds[3], 71), 0),
        "out_weight": scatter_about(seeds[2], (HEADS * HD, D), HD ** -0.5, 0.5, ((0, 4), (1, 8))),
    }


def reference(queries, keys_values, out_weight):
    query_frames = queries.reshape(FRAMES, TPF, HEADS, HD)
    key_frames = keys_values[0].reshape(FRAMES, TPF, HEADS, HD)
    value_frames = keys_values[1].reshape(FRAMES, TPF, HEADS, HD)
    offsets = jnp.arange(2 * BAND + 1, dtype=jnp.int32) - BAND

    def one_frame(frame):
        picks = ((frame + offsets) % FRAMES).astype(jnp.int32)
        keys = key_frames[picks].reshape((2 * BAND + 1) * TPF, HEADS, HD).astype(jnp.float32)
        values = value_frames[picks].reshape((2 * BAND + 1) * TPF, HEADS, HD).astype(jnp.float32)
        query = query_frames[frame].astype(jnp.float32)
        scores = jnp.einsum("qhd,khd->hqk", query, keys, precision=lax.Precision.HIGHEST)
        scores = scores * (HD ** -0.5)
        top = jnp.max(scores, axis=2, keepdims=True)
        weights = jnp.exp(scores - top)
        probs = (weights / jnp.sum(weights, axis=2, keepdims=True)).astype(jnp.bfloat16)
        attended = jnp.einsum("hqk,khd->qhd", probs.astype(jnp.float32), values, precision=lax.Precision.HIGHEST)
        return attended.astype(jnp.bfloat16).reshape(TPF, HEADS * HD)

    attended = lax.map(one_frame, jnp.arange(FRAMES, dtype=jnp.int32)).reshape(TOKENS, HEADS * HD)
    return jnp.dot(attended, out_weight, preferred_element_type=jnp.float32).astype(jnp.bfloat16)
```

```python
import functools
import math

import jax
import jax.numpy as jnp
from jax import lax
from jax.experimental import pallas as pl
from jax.experimental.pallas import tpu as pltpu
from jax.sharding import PartitionSpec as P

HD = 128
TPF = 32
FR_DEV = 3
ROWS = FR_DEV * TPF


reach_cap = 32


def from_behind(x, axis, by):
    devices = lax.axis_size(axis)
    return lax.ppermute(x, axis, [(i, (i + by) % devices) for i in range(devices)])


def on_device_band(queries, keys_values, out_weight):
    total_frames = lax.axis_size("frames") * FR_DEV
    reach = min(reach_cap, (total_frames - 1) // 2)
    steps = (reach + FR_DEV - 1) // FR_DEV
    width = keys_values.shape[2]
    span = FR_DEV + 2 * reach
    stacked = keys_values.reshape(2, FR_DEV, TPF, width)
    pieces = []
    for offset in range(-steps, steps + 1):
        if offset == 0:
            pieces.append(stacked)
        else:
            pieces.append(from_behind(stacked, "frames", -offset))
    window = jnp.concatenate(pieces, axis=1)
    lower_frame = steps * FR_DEV - reach
    extended = window[:, lower_frame : lower_frame + span]
    keys_ext = extended[0].reshape(span * TPF, width)
    values_ext = extended[1].reshape(span * TPF, width)
    row_frame = jnp.arange(FR_DEV * TPF, dtype=jnp.int32) // TPF
    col_frame = jnp.arange(span * TPF, dtype=jnp.int32) // TPF
    allowed = (col_frame[None, :] >= row_frame[:, None]) & (
        col_frame[None, :] <= row_frame[:, None] + 2 * reach
    )
    results = []
    for head in range(width // HD):
        lower = head * HD
        query_cols = queries[:, lower : lower + HD]
        key_cols = keys_ext[:, lower : lower + HD]
        scores = lax.dot_general(
            query_cols, key_cols, (((1,), (1,)), ((), ())), preferred_element_type=jnp.float32
        )
        scores = scores * HD ** (-0.5)
        top = jnp.max(jnp.where(allowed, scores, -1e30), axis=1, keepdims=True)
        weights = jnp.where(allowed, jnp.exp(scores - top), 0.0)
        probs = (weights / jnp.sum(weights, axis=1, keepdims=True)).astype(jnp.bfloat16)
        results.append(
            jnp.dot(
                probs, values_ext[:, lower : lower + HD], preferred_element_type=jnp.float32
            ).astype(jnp.bfloat16)
        )
    attended = jnp.concatenate(results, axis=1)
    partial_rows = jnp.dot(
        attended,
        lax.all_gather(out_weight, "frames", axis=1, tiled=True),
        preferred_element_type=jnp.float32,
    )
    return lax.psum_scatter(
        partial_rows.astype(jnp.bfloat16), "heads", scatter_dimension=1, tiled=True
    )


def ring_order(n):
    return list(range(0, n, 2)) + list(range(n - 1, 0, -2))


def hop(x, n, by):
    order = ring_order(n)
    return lax.ppermute(x, "frames", [(order[i], order[(i + by) % n]) for i in range(n)])


def gather_ring(parts, n):
    order = jnp.array(ring_order(n), jnp.int32)
    me = lax.axis_index("frames")
    place = jnp.argmax(order == me).astype(jnp.int32)
    stacks = [
        lax.dynamic_update_slice_in_dim(jnp.zeros((n,) + p.shape, p.dtype), p[None], me, 0) for p in parts
    ]
    ups, downs = list(parts), list(parts)
    for step in range(1, n // 2 + 1):
        last = step == n // 2
        for j in range(len(parts)):
            for by, held in ((1, ups), (-1, downs)):
                if last and (j % 2 == 0) == (by > 0):
                    continue
                held[j] = hop(held[j], n, by)
                owner = order[(place - by * step) % n]
                stacks[j] = lax.dynamic_update_slice_in_dim(stacks[j], held[j][None], owner, 0)
    return stacks


def attend_kernel(heads, total_frames, reach, count, first_ref, q_ref, kv_ref, w_ref, out_ref):
    first = first_ref[0]
    tokens = kv_ref.shape[0] * ROWS
    scale = HD ** (-0.5) * math.log2(math.e)

    def block(i, carry):
        owner = 2 * i + first
        row_frame = owner * FR_DEV + lax.broadcasted_iota(jnp.int32, (ROWS, tokens), 0) // TPF
        col_frame = lax.broadcasted_iota(jnp.int32, (ROWS, tokens), 1) // TPF
        apart = jnp.abs(row_frame - col_frame)
        bias = jnp.where(jnp.minimum(apart, total_frames - apart) <= reach, 0.0, -1e30)
        attended = []
        for head in range(heads):
            cols = slice(head * HD, (head + 1) * HD)
            keys = kv_ref[:, 0, :, cols].reshape(tokens, HD)
            values = kv_ref[:, 1, :, cols].reshape(tokens, HD)
            scores = lax.dot_general(
                q_ref[owner, :, cols], keys, (((1,), (1,)), ((), ())), preferred_element_type=jnp.float32
            )
            scores = scores * scale + bias
            weights = jnp.exp2(scores - jnp.max(scores, axis=1, keepdims=True))
            total = jnp.sum(weights, axis=1, keepdims=True)
            mixed = jnp.dot(weights.astype(jnp.bfloat16), values, preferred_element_type=jnp.float32)
            attended.append((mixed / total).astype(jnp.bfloat16))
        rows = jnp.concatenate(attended, axis=1)
        out_ref[i] = jnp.dot(rows, w_ref[...], preferred_element_type=jnp.float32).astype(out_ref.dtype)
        return carry

    lax.fori_loop(0, count, block, 0)


def attend(first, q_all, kv_all, out_weight, out_dtype):
    n, rows, width = q_all.shape
    count = n // 2
    total_frames = n * FR_DEV
    reach = min(reach_cap, (total_frames - 1) // 2)
    cols = out_weight.shape[1]
    vmem = pl.BlockSpec(memory_space=pltpu.VMEM)
    return pl.pallas_call(
        functools.partial(attend_kernel, width // HD, total_frames, reach, count),
        out_shape=jax.ShapeDtypeStruct((count, rows, cols), out_dtype),
        in_specs=[pl.BlockSpec(memory_space=pltpu.SMEM), vmem, vmem, vmem],
        out_specs=vmem,
        compiler_params=pltpu.CompilerParams(vmem_limit_bytes=32 * 1024 * 1024),
        cost_estimate=pl.CostEstimate(
            flops=count * rows * width * (4 * n * rows + 2 * cols),
            bytes_accessed=2 * (3 * q_all.size + out_weight.size),
            transcendentals=count * rows * n * rows * (width // HD),
        ),
    )(first.reshape(1), q_all, kv_all, out_weight)


def on_device_ring(queries, keys_values, out_weight):
    n = lax.axis_size("frames")
    cores = 2
    frame, head = lax.axis_index("frames"), lax.axis_index("heads")
    wide = lax.axis_size("heads") // cores
    x, core = head // cores, head % cores
    kv_all, q_all = gather_ring([keys_values, queries], n)
    given = attend(1 - core, q_all, kv_all, out_weight, jnp.bfloat16)
    taken = lax.ppermute(
        given, "heads", [(h, h // cores * cores + (h + 1) % cores) for h in range(wide * cores)]
    )
    kept = attend(core, q_all, kv_all, out_weight, jnp.float32)
    sources = 2 * wide
    source = frame % 2 * wide + x
    arrived = []
    for slot in range(sources):
        pairs = []
        for f in range(n):
            for h in range(wide * cores):
                block = slot ^ (f % 2 * wide + h // cores)
                pairs.append((f * wide * cores + h, (2 * block + h % cores) * wide * cores + f // 2))
        which = slot ^ source
        total = kept[which] + taken[which].astype(jnp.float32)
        arrived.append(lax.ppermute(total.astype(jnp.bfloat16), ("frames", "heads"), pairs))
    stack = jnp.stack(arrived)
    mine = frame // 2
    halves = []
    for y in range(2):
        total = sum(stack[mine ^ (y * wide + other)].astype(jnp.float32) for other in range(wide))
        halves.append(total.astype(jnp.bfloat16))
    return jnp.concatenate(halves, axis=1)


def solution(mesh):
    in_specs = (P("frames", "heads"), P(None, "frames", "heads"), P("heads", "frames"))
    out_specs = P("frames", "heads")
    n, heads = mesh.shape["frames"], mesh.shape["heads"]
    total_frames = n * FR_DEV
    reach = min(reach_cap, (total_frames - 1) // 2)
    every = total_frames - (2 * reach + 1) < FR_DEV and heads == 4 and n == 2 * heads
    return jax.shard_map(
        on_device_ring if every else on_device_band,
        mesh=mesh,
        in_specs=in_specs,
        out_specs=out_specs,
        check_vma=False,
    )
```

```python
import functools
import math

import jax
import jax.numpy as jnp
from jax import lax
from jax.experimental import pallas as pl
from jax.experimental.pallas import tpu as pltpu
from jax.sharding import PartitionSpec as P

HD = 128
TPF = 32
FR_DEV = 3
ROWS = FR_DEV * TPF


reach_cap = 32


def from_behind(x, axis, by):
    devices = lax.axis_size(axis)
    return lax.ppermute(x, axis, [(i, (i + by) % devices) for i in range(devices)])


def on_device_band(queries, keys_values, out_weight):
    total_frames = lax.axis_size("frames") * FR_DEV
    reach = min(reach_cap, (total_frames - 1) // 2)
    steps = (reach + FR_DEV - 1) // FR_DEV
    width = keys_values.shape[2]
    span = FR_DEV + 2 * reach
    stacked = keys_values.reshape(2, FR_DEV, TPF, width)
    pieces = []
    for offset in range(-steps, steps + 1):
        if offset == 0:
            pieces.append(stacked)
        else:
            pieces.append(from_behind(stacked, "frames", -offset))
    window = jnp.concatenate(pieces, axis=1)
    lower_frame = steps * FR_DEV - reach
    extended = window[:, lower_frame : lower_frame + span]
    keys_ext = extended[0].reshape(span * TPF, width)
    values_ext = extended[1].reshape(span * TPF, width)
    row_frame = jnp.arange(FR_DEV * TPF, dtype=jnp.int32) // TPF
    col_frame = jnp.arange(span * TPF, dtype=jnp.int32) // TPF
    allowed = (col_frame[None, :] >= row_frame[:, None]) & (
        col_frame[None, :] <= row_frame[:, None] + 2 * reach
    )
    results = []
    for head in range(width // HD):
        lower = head * HD
        query_cols = queries[:, lower : lower + HD]
        key_cols = keys_ext[:, lower : lower + HD]
        scores = lax.dot_general(
            query_cols, key_cols, (((1,), (1,)), ((), ())), preferred_element_type=jnp.float32
        )
        scores = scores * HD ** (-0.5)
        top = jnp.max(jnp.where(allowed, scores, -1e30), axis=1, keepdims=True)
        weights = jnp.where(allowed, jnp.exp(scores - top), 0.0)
        probs = (weights / jnp.sum(weights, axis=1, keepdims=True)).astype(jnp.bfloat16)
        results.append(
            jnp.dot(
                probs, values_ext[:, lower : lower + HD], preferred_element_type=jnp.float32
            ).astype(jnp.bfloat16)
        )
    attended = jnp.concatenate(results, axis=1)
    partial_rows = jnp.dot(
        attended,
        lax.all_gather(out_weight, "frames", axis=1, tiled=True),
        preferred_element_type=jnp.float32,
    )
    return lax.psum_scatter(
        partial_rows.astype(jnp.bfloat16), "heads", scatter_dimension=1, tiled=True
    )


def ring_order(n):
    return list(range(0, n, 2)) + list(range(n - 1, 0, -2))


def ring_place(f, n):
    return f // 2 + f % 2 * (n - 1 - f // 2 * 2)


def hop(x, n, by):
    order = ring_order(n)
    return lax.ppermute(x, "frames", [(order[i], order[(i + by) % n]) for i in range(n)])


def gather_ring(parts, n):
    found = [[p] + [None] * (n - 1) for p in parts]
    for step in range(1, n // 2 + 1):
        last = step == n // 2
        for j in range(len(parts)):
            for by in (1, -1):
                if last and (j % 2 == 0) == (by > 0):
                    continue
                found[j][by * step % n] = hop(found[j][by * (step - 1) % n], n, by)
    return [jnp.stack(pieces) for pieces in found]


def attend_kernel(heads, n, at_ref, q_ref, kv_ref, w_ref, out_ref):
    place, first = at_ref[0], at_ref[1]
    count = n // 2
    scale = HD ** (-0.5) * math.log2(math.e)

    def slots(parity):
        return [(place - (i + parity * (n - 1 - 2 * i)) + n) % n for i in range(count)]

    mine = slots(first)
    order = mine + slots(1 - first)
    ones = jnp.ones((n * ROWS, HD), jnp.bfloat16)
    attended = []
    for head in range(heads):
        cols = slice(head * HD, (head + 1) * HD)
        rows = jnp.concatenate([q_ref[o, :, cols] for o in mine], axis=0)
        keys = jnp.concatenate([kv_ref[o, 0, :, cols] for o in order], axis=0)
        values = jnp.concatenate([kv_ref[o, 1, :, cols] for o in order], axis=0)
        scores = lax.dot_general(rows, keys, (((1,), (1,)), ((), ())), preferred_element_type=jnp.float32)
        groups = []
        for g in range(count * FR_DEV):
            tall = slice(g * TPF, (g + 1) * TPF)
            parts = [scores[tall, c : c + HD] for c in range(0, n * ROWS, HD)]
            away = (g + count // 2 * FR_DEV) % (count * FR_DEV) * TPF
            lane = lax.broadcasted_iota(jnp.int32, (TPF, HD), 1)
            out_of_band = (lane >= away % HD) & (lane < away % HD + TPF)
            parts[away // HD] = jnp.where(out_of_band, -1e30, parts[away // HD])
            top = jnp.max(functools.reduce(jnp.maximum, parts), axis=1, keepdims=True)
            groups.append(
                jnp.concatenate([jnp.exp2((p - top) * scale).astype(jnp.bfloat16) for p in parts], axis=1)
            )
        weights = jnp.concatenate(groups, axis=0)
        mixed = jnp.dot(weights, jnp.concatenate([values, ones], axis=1), preferred_element_type=jnp.float32)
        attended.append((mixed[:, :HD] / mixed[:, HD:]).astype(jnp.bfloat16))
    result = jnp.dot(jnp.concatenate(attended, axis=1), w_ref[...], preferred_element_type=jnp.float32)
    for i in range(count):
        out_ref[i] = result[i * ROWS : (i + 1) * ROWS].astype(out_ref.dtype)


def attend(first, q_all, kv_all, out_weight, out_dtype):
    n, rows, width = q_all.shape
    count = n // 2
    cols = out_weight.shape[1]
    place = ring_place(lax.axis_index("frames"), n)
    vmem = pl.BlockSpec(memory_space=pltpu.VMEM)
    return pl.pallas_call(
        functools.partial(attend_kernel, width // HD, n),
        out_shape=jax.ShapeDtypeStruct((count, rows, cols), out_dtype),
        in_specs=[pl.BlockSpec(memory_space=pltpu.SMEM), vmem, vmem, vmem],
        out_specs=vmem,
        compiler_params=pltpu.CompilerParams(vmem_limit_bytes=32 * 1024 * 1024),
        cost_estimate=pl.CostEstimate(
            flops=count * rows * width * (4 * n * rows + 2 * cols),
            bytes_accessed=2 * (3 * q_all.size + out_weight.size),
            transcendentals=count * rows * n * rows * (width // HD),
        ),
    )(jnp.stack([place, first]).astype(jnp.int32), q_all, kv_all, out_weight)


def on_device_ring(queries, keys_values, out_weight):
    n = lax.axis_size("frames")
    cores = 2
    frame, head = lax.axis_index("frames"), lax.axis_index("heads")
    wide = lax.axis_size("heads") // cores
    x, core = head // cores, head % cores
    kv_all, q_all = gather_ring([keys_values, queries], n)
    given = attend(1 - core, q_all, kv_all, out_weight, jnp.bfloat16)
    taken = lax.ppermute(
        given, "heads", [(h, h // cores * cores + (h + 1) % cores) for h in range(wide * cores)]
    )
    kept = attend(core, q_all, kv_all, out_weight, jnp.float32)
    sources = 2 * wide
    source = frame % 2 * wide + x
    arrived = []
    for slot in range(sources):
        pairs = []
        for f in range(n):
            for h in range(wide * cores):
                block = slot ^ (f % 2 * wide + h // cores)
                pairs.append((f * wide * cores + h, (2 * block + h % cores) * wide * cores + f // 2))
        which = slot ^ source
        total = kept[which] + taken[which].astype(jnp.float32)
        arrived.append(lax.ppermute(total.astype(jnp.bfloat16), ("frames", "heads"), pairs))
    stack = jnp.stack(arrived)
    mine = frame // 2
    halves = []
    for y in range(2):
        total = sum(stack[mine ^ (y * wide + other)].astype(jnp.float32) for other in range(wide))
        halves.append(total.astype(jnp.bfloat16))
    return jnp.concatenate(halves, axis=1)


def solution(mesh):
    in_specs = (P("frames", "heads"), P(None, "frames", "heads"), P("heads", "frames"))
    out_specs = P("frames", "heads")
    n, heads = mesh.shape["frames"], mesh.shape["heads"]
    total_frames = n * FR_DEV
    reach = min(reach_cap, (total_frames - 1) // 2)
    every = total_frames == 2 * reach + 2 and heads == 4 and n == 2 * heads
    return jax.shard_map(
        on_device_ring if every else on_device_band,
        mesh=mesh,
        in_specs=in_specs,
        out_specs=out_specs,
        check_vma=False,
    )
```

```python
import functools
import math

import jax
import jax.numpy as jnp
from jax import lax
from jax.experimental import pallas as pl
from jax.experimental.pallas import tpu as pltpu
from jax.sharding import PartitionSpec as P

HD = 128
TPF = 32
FR_DEV = 3
ROWS = FR_DEV * TPF


reach_cap = 32


def from_behind(x, axis, by):
    devices = lax.axis_size(axis)
    return lax.ppermute(x, axis, [(i, (i + by) % devices) for i in range(devices)])


def on_device_band(queries, keys_values, out_weight):
    total_frames = lax.axis_size("frames") * FR_DEV
    reach = min(reach_cap, (total_frames - 1) // 2)
    steps = (reach + FR_DEV - 1) // FR_DEV
    width = keys_values.shape[2]
    span = FR_DEV + 2 * reach
    stacked = keys_values.reshape(2, FR_DEV, TPF, width)
    pieces = []
    for offset in range(-steps, steps + 1):
        if offset == 0:
            pieces.append(stacked)
        else:
            pieces.append(from_behind(stacked, "frames", -offset))
    window = jnp.concatenate(pieces, axis=1)
    lower_frame = steps * FR_DEV - reach
    extended = window[:, lower_frame : lower_frame + span]
    keys_ext = extended[0].reshape(span * TPF, width)
    values_ext = extended[1].reshape(span * TPF, width)
    row_frame = jnp.arange(FR_DEV * TPF, dtype=jnp.int32) // TPF
    col_frame = jnp.arange(span * TPF, dtype=jnp.int32) // TPF
    allowed = (col_frame[None, :] >= row_frame[:, None]) & (
        col_frame[None, :] <= row_frame[:, None] + 2 * reach
    )
    results = []
    for head in range(width // HD):
        lower = head * HD
        query_cols = queries[:, lower : lower + HD]
        key_cols = keys_ext[:, lower : lower + HD]
        scores = lax.dot_general(
            query_cols, key_cols, (((1,), (1,)), ((), ())), preferred_element_type=jnp.float32
        )
        scores = scores * HD ** (-0.5)
        top = jnp.max(jnp.where(allowed, scores, -1e30), axis=1, keepdims=True)
        weights = jnp.where(allowed, jnp.exp(scores - top), 0.0)
        probs = (weights / jnp.sum(weights, axis=1, keepdims=True)).astype(jnp.bfloat16)
        results.append(
            jnp.dot(
                probs, values_ext[:, lower : lower + HD], preferred_element_type=jnp.float32
            ).astype(jnp.bfloat16)
        )
    attended = jnp.concatenate(results, axis=1)
    partial_rows = jnp.dot(
        attended,
        lax.all_gather(out_weight, "frames", axis=1, tiled=True),
        preferred_element_type=jnp.float32,
    )
    return lax.psum_scatter(
        partial_rows.astype(jnp.bfloat16), "heads", scatter_dimension=1, tiled=True
    )


def ring_order(n):
    return list(range(0, n, 2)) + list(range(n - 1, 0, -2))


def ring_place(f, n):
    return (f >> 1) + (f & 1) * (n - 1 - (f >> 1) * 2)


def hop(x, n, by):
    order = ring_order(n)
    return lax.ppermute(x, "frames", [(order[i], order[(i + by) % n]) for i in range(n)])


def gather_ring(streams, n):
    found = [[block] + [None] * (n - 1) for block in streams]
    for step in range(1, n // 2 + 1):
        for j, blocks in enumerate(found):
            for by in (1, -1):
                if step < n // 2 or (j == 0) == (by == 1):
                    blocks[by * step % n] = hop(blocks[by * (step - 1) % n], n, by)
    return found


def pick(options, index):
    low = jnp.where(index & 1 == 0, options[0], options[1])
    high = jnp.where(index & 1 == 0, options[2], options[3])
    return jnp.where(index & 2 == 0, low, high)


def attend_kernel(heads, n, flip, at_ref, *refs):
    first, second, w_ref, out_ref = refs[:n], refs[n : 2 * n], refs[2 * n], refs[-1]
    place, at = at_ref[0], at_ref[1] ^ flip
    count = n // 4
    half = ROWS // 2
    scale = HD ** (-0.5) * math.log2(math.e)
    two = jnp.where((place - at + n) & 2 == 0, n - 2, 2)
    away = [FR_DEV * ((at + 4 * i + two) & (n - 1)) for i in range(count)]
    lane_frame = lax.broadcasted_iota(jnp.int32, (TPF, HD), 1) // TPF
    ones = jnp.ones((n * ROWS, HD), jnp.bfloat16)
    attended = []
    for head in range(heads):
        cols = slice(head * HD, (head + 1) * HD)
        rows = jnp.concatenate(
            [
                pick([half_ref[ROWS:, cols] for half_ref in part[4 * i : 4 * i + 4]], at)
                for i in range(count)
                for part in (first, second)
            ],
            axis=0,
        )
        keys = jnp.concatenate([ref[:ROWS, cols] for ref in first], axis=0)
        values = jnp.concatenate([ref[:ROWS, cols] for ref in second], axis=0)
        scores = lax.dot_general(rows, keys, (((1,), (1,)), ((), ())), preferred_element_type=jnp.float32)
        groups = []
        for g in range(count * FR_DEV):
            out_frame = away[g // FR_DEV] + g % FR_DEV
            parts = []
            for c in range(0, n * ROWS, HD):
                part = scores[g * TPF : (g + 1) * TPF, c : c + HD]
                parts.append(jnp.where(lane_frame == out_frame - c // TPF, -1e30, part))
            top = jnp.max(functools.reduce(jnp.maximum, parts), axis=1, keepdims=True)
            groups.append(
                jnp.concatenate([jnp.exp2((p - top) * scale).astype(jnp.bfloat16) for p in parts], axis=1)
            )
        weights = jnp.concatenate(groups, axis=0)
        mixed = jnp.dot(weights, jnp.concatenate([values, ones], axis=1), preferred_element_type=jnp.float32)
        attended.append((mixed[:, :HD] / mixed[:, HD:]).astype(jnp.bfloat16))
    result = jnp.dot(jnp.concatenate(attended, axis=1), w_ref[...], preferred_element_type=jnp.float32)
    for i in range(count):
        out_ref[i] = result[i * ROWS : (i + 1) * ROWS].astype(out_ref.dtype)


def attend(where, flip, found, out_weight, out_dtype, after=()):
    n = len(found[0])
    count = n // 4
    width, cols = out_weight.shape
    vmem = pl.BlockSpec(memory_space=pltpu.VMEM)
    return pl.pallas_call(
        functools.partial(attend_kernel, width // HD, n, flip),
        out_shape=jax.ShapeDtypeStruct((count, ROWS, cols), out_dtype),
        in_specs=[pl.BlockSpec(memory_space=pltpu.SMEM)]
        + [vmem] * (2 * n + 1)
        + [pl.BlockSpec(memory_space=pl.ANY)] * len(after),
        out_specs=vmem,
        compiler_params=pltpu.CompilerParams(vmem_limit_bytes=16 * 1024 * 1024),
        cost_estimate=pl.CostEstimate(
            flops=count * ROWS * width * (4 * n * ROWS + 2 * cols),
            bytes_accessed=2 * (3 * n * ROWS * width + out_weight.size),
            transcendentals=count * ROWS * n * ROWS * (width // HD),
        ),
    )(where, *found[0], *found[1], out_weight, *after)


def on_device_ring(queries, keys_values, out_weight):
    n = lax.axis_size("frames")
    frame, head = lax.axis_index("frames"), lax.axis_index("heads")
    where = jnp.stack([ring_place(frame, n), head]).astype(jnp.int32)
    half = ROWS // 2
    streams = [
        jnp.concatenate([keys_values[0], queries[:half]], axis=0),
        jnp.concatenate([keys_values[1], queries[half:]], axis=0),
    ]
    found = gather_ring(streams, n)
    to_core = [(h, h ^ 1) for h in range(4)]
    to_x = [(h, h ^ 2) for h in range(4)]
    f32 = jnp.float32
    from_core = lax.ppermute(attend(where, 3, found, out_weight, jnp.bfloat16), "heads", to_core)
    given = attend(where, 2, found, out_weight, f32)
    given = (given + from_core.astype(f32)).astype(jnp.bfloat16)
    from_x = lax.ppermute(given, "heads", to_x)
    last_given = attend(where, 1, found, out_weight, jnp.bfloat16, (given,))
    from_core = lax.ppermute(last_given, "heads", to_core)
    kept = attend(where, 0, found, out_weight, f32, (last_given,))
    order = ring_order(n)
    z, y = frame >> 1, frame & 1

    def flip(z, y, head):
        return y & (1 ^ ((head + 2 * z + 1) >> 2 & 1))

    arrived = []
    for slot in range(2):
        pairs = []
        for f in range(n):
            for h in range(4):
                distance = 4 * (slot ^ flip(f >> 1, f & 1, h)) + h
                owner = order[(ring_place(f, n) - distance) % n]
                pairs.append((f * 4 + h, owner * 4 + f // 2))
        j = slot ^ flip(z, y, head)
        total = kept[j] + from_core[j].astype(f32) + from_x[j].astype(f32)
        arrived.append(lax.ppermute(total.astype(jnp.bfloat16), ("frames", "heads"), pairs))
    straight = (head - where[0]) & 4 == 0
    return jnp.concatenate(
        [jnp.where(straight, arrived[0], arrived[1]), jnp.where(straight, arrived[1], arrived[0])], axis=1
    )


def solution(mesh):
    in_specs = (P("frames", "heads"), P(None, "frames", "heads"), P("heads", "frames"))
    out_specs = P("frames", "heads")
    n, heads = mesh.shape["frames"], mesh.shape["heads"]
    total_frames = n * FR_DEV
    reach = min(reach_cap, (total_frames - 1) // 2)
    every = total_frames == 2 * reach + 2 and heads == 4 and n == 2 * heads
    return jax.shard_map(
        on_device_ring if every else on_device_band,
        mesh=mesh,
        in_specs=in_specs,
        out_specs=out_specs,
        check_vma=False,
    )
```

```python
import functools
import math

import jax
import jax.numpy as jnp
from jax import lax
from jax.experimental import pallas as pl
from jax.experimental.pallas import tpu as pltpu
from jax.sharding import PartitionSpec as P

HD = 128
TPF = 32
FR_DEV = 3
ROWS = FR_DEV * TPF


reach_cap = 32


def from_behind(x, axis, by):
    devices = lax.axis_size(axis)
    return lax.ppermute(x, axis, [(i, (i + by) % devices) for i in range(devices)])


def on_device_band(queries, keys_values, out_weight):
    total_frames = lax.axis_size("frames") * FR_DEV
    reach = min(reach_cap, (total_frames - 1) // 2)
    steps = (reach + FR_DEV - 1) // FR_DEV
    width = keys_values.shape[2]
    span = FR_DEV + 2 * reach
    stacked = keys_values.reshape(2, FR_DEV, TPF, width)
    pieces = []
    for offset in range(-steps, steps + 1):
        if offset == 0:
            pieces.append(stacked)
        else:
            pieces.append(from_behind(stacked, "frames", -offset))
    window = jnp.concatenate(pieces, axis=1)
    lower_frame = steps * FR_DEV - reach
    extended = window[:, lower_frame : lower_frame + span]
    keys_ext = extended[0].reshape(span * TPF, width)
    values_ext = extended[1].reshape(span * TPF, width)
    row_frame = jnp.arange(FR_DEV * TPF, dtype=jnp.int32) // TPF
    col_frame = jnp.arange(span * TPF, dtype=jnp.int32) // TPF
    allowed = (col_frame[None, :] >= row_frame[:, None]) & (
        col_frame[None, :] <= row_frame[:, None] + 2 * reach
    )
    results = []
    for head in range(width // HD):
        lower = head * HD
        query_cols = queries[:, lower : lower + HD]
        key_cols = keys_ext[:, lower : lower + HD]
        scores = lax.dot_general(
            query_cols, key_cols, (((1,), (1,)), ((), ())), preferred_element_type=jnp.float32
        )
        scores = scores * HD ** (-0.5)
        top = jnp.max(jnp.where(allowed, scores, -1e30), axis=1, keepdims=True)
        weights = jnp.where(allowed, jnp.exp(scores - top), 0.0)
        probs = (weights / jnp.sum(weights, axis=1, keepdims=True)).astype(jnp.bfloat16)
        results.append(
            jnp.dot(
                probs, values_ext[:, lower : lower + HD], preferred_element_type=jnp.float32
            ).astype(jnp.bfloat16)
        )
    attended = jnp.concatenate(results, axis=1)
    partial_rows = jnp.dot(
        attended,
        lax.all_gather(out_weight, "frames", axis=1, tiled=True),
        preferred_element_type=jnp.float32,
    )
    return lax.psum_scatter(
        partial_rows.astype(jnp.bfloat16), "heads", scatter_dimension=1, tiled=True
    )


def ring_order(n):
    return list(range(0, n, 2)) + list(range(n - 1, 0, -2))


def ring_place(f, n):
    return (f >> 1) + (f & 1) * (n - 1 - (f >> 1) * 2)


def hop(x, n, by):
    order = ring_order(n)
    return lax.ppermute(x, "frames", [(order[i], order[(i + by) % n]) for i in range(n)])


def gather_ring(streams, n):
    found = [[block] + [None] * (n - 1) for block in streams]
    for step in range(1, n // 2 + 1):
        for j, blocks in enumerate(found):
            for by in (1, -1):
                if step < n // 2 or (j == 0) == (by == 1):
                    blocks[by * step % n] = hop(blocks[by * (step - 1) % n], n, by)
    return found


def pick(options, index):
    while len(options) > 1:
        pairs = zip(options[::2], options[1::2])
        options = [jnp.where(index & 1 == 0, even, odd) for even, odd in pairs]
        index = index >> 1
    return options[0]


def attend_kernel(heads, n, flips, at_ref, *refs):
    first, second, w_ref, out_ref = refs[:n], refs[n : 2 * n], refs[2 * n], refs[-1]
    place, x, y, core = (at_ref[i] for i in range(4))
    half = ROWS // 2
    scale = HD ** (-0.5) * math.log2(math.e)
    blocks, away = [], []
    for flip_x, flip_y, flip_core in flips:
        z = 2 * (core ^ flip_core) + (x ^ flip_x)
        owner = z + (y ^ flip_y) * (n - 1 - 2 * z)
        blocks.append((place - owner) & (n - 1))
        away.append(FR_DEV * ((place - (owner ^ 2)) & (n - 1)))
    lane_frame = lax.broadcasted_iota(jnp.int32, (TPF, HD), 1) // TPF
    ones = jnp.ones((n * ROWS, HD), jnp.bfloat16)
    attended = []
    for head in range(heads):
        cols = slice(head * HD, (head + 1) * HD)
        rows = jnp.concatenate(
            [pick([ref[ROWS:, cols] for ref in part], block) for block in blocks for part in (first, second)], axis=0
        )
        keys = jnp.concatenate([ref[:ROWS, cols] for ref in first], axis=0)
        values = jnp.concatenate([ref[:ROWS, cols] for ref in second], axis=0)
        scores = lax.dot_general(rows, keys, (((1,), (1,)), ((), ())), preferred_element_type=jnp.float32)
        groups = []
        for g in range(len(flips) * FR_DEV):
            out_frame = away[g // FR_DEV] + g % FR_DEV
            parts = []
            for c in range(0, n * ROWS, HD):
                part = scores[g * TPF : (g + 1) * TPF, c : c + HD]
                parts.append(jnp.where(lane_frame == out_frame - c // TPF, -1e30, part))
            top = jnp.max(functools.reduce(jnp.maximum, parts), axis=1, keepdims=True)
            groups.append(
                jnp.concatenate([jnp.exp2((p - top) * scale).astype(jnp.bfloat16) for p in parts], axis=1)
            )
        weights = jnp.concatenate(groups, axis=0)
        mixed = jnp.dot(weights, jnp.concatenate([values, ones], axis=1), preferred_element_type=jnp.float32)
        attended.append((mixed[:, :HD] / mixed[:, HD:]).astype(jnp.bfloat16))
    result = jnp.dot(jnp.concatenate(attended, axis=1), w_ref[...], preferred_element_type=jnp.float32)
    out_ref[...] = result.astype(out_ref.dtype)


def attend(where, flips, found, out_weight, out_dtype, after=()):
    n = len(found[0])
    count = len(flips)
    width, cols = out_weight.shape
    vmem = pl.BlockSpec(memory_space=pltpu.VMEM)
    return pl.pallas_call(
        functools.partial(attend_kernel, width // HD, n, flips),
        out_shape=jax.ShapeDtypeStruct((count * ROWS, cols), out_dtype),
        in_specs=[pl.BlockSpec(memory_space=pltpu.SMEM)]
        + [vmem] * (2 * n + 1)
        + [pl.BlockSpec(memory_space=pl.ANY)] * len(after),
        out_specs=vmem,
        compiler_params=pltpu.CompilerParams(vmem_limit_bytes=16 * 1024 * 1024),
        cost_estimate=pl.CostEstimate(
            flops=count * ROWS * width * (4 * n * ROWS + 2 * cols),
            bytes_accessed=2 * (3 * n * ROWS * width + out_weight.size),
            transcendentals=count * ROWS * n * ROWS * (width // HD),
        ),
    )(where, *found[0], *found[1], out_weight, *after)


def on_device_ring(queries, keys_values, out_weight):
    n = lax.axis_size("frames")
    frame, head = lax.axis_index("frames"), lax.axis_index("heads")
    x, y, core = head >> 1, frame & 1, head & 1
    where = jnp.stack([ring_place(frame, n), x, y, core]).astype(jnp.int32)
    half = ROWS // 2
    streams = [
        jnp.concatenate([keys_values[0], queries[:half]], axis=0),
        jnp.concatenate([keys_values[1], queries[half:]], axis=0),
    ]
    found = gather_ring(streams, n)
    devices = [(f, h) for f in range(n) for h in range(4)]
    f32, bf16 = jnp.float32, jnp.bfloat16

    def swap(block, flip_x, flip_y, flip_core):
        pairs = [(4 * f + h, 4 * (f ^ flip_y) + (h ^ (2 * flip_x + flip_core))) for f, h in devices]
        return lax.ppermute(block, ("frames", "heads"), pairs)

    flips = [(1, 1), (1, 0), (0, 1)]
    given = attend(where, [(*flip, 1) for flip in flips + [(0, 0)]], found, out_weight, bf16)
    from_core = swap(given, 0, 0, 1).reshape(len(flips) + 1, ROWS, -1)
    kept = attend(where, [(*flip, 0) for flip in flips], found, out_weight, f32, (given,))
    kept = kept.reshape(len(flips), ROWS, -1)
    sums = [(kept[i] + from_core[i].astype(f32)).astype(bf16) for i in range(len(flips))]
    diagonal, beside, across = (swap(block, *flip, 0) for block, flip in zip(sums, flips))
    kept = attend(where, [(0, 0, 0)], found, out_weight, f32, tuple(sums))
    same = (kept + from_core[-1].astype(f32) + beside.astype(f32)).astype(bf16)
    other = (across.astype(f32) + diagonal.astype(f32)).astype(bf16)
    block = jnp.concatenate([jnp.where(y == 0, same, other), jnp.where(y == 0, other, same)], axis=1)
    pairs = [(4 * f + h, 4 * (2 * (2 * (h & 1) + (h >> 1)) + (f & 1)) + (f >> 1)) for f, h in devices]
    return lax.ppermute(block, ("frames", "heads"), pairs)


def solution(mesh):
    in_specs = (P("frames", "heads"), P(None, "frames", "heads"), P("heads", "frames"))
    out_specs = P("frames", "heads")
    n, heads = mesh.shape["frames"], mesh.shape["heads"]
    total_frames = n * FR_DEV
    reach = min(reach_cap, (total_frames - 1) // 2)
    every = total_frames == 2 * reach + 2 and heads == 4 and n == 2 * heads
    return jax.shard_map(
        on_device_ring if every else on_device_band,
        mesh=mesh,
        in_specs=in_specs,
        out_specs=out_specs,
        check_vma=False,
    )
```

```python
import functools
import math

import jax
import jax.numpy as jnp
from jax import lax
from jax.experimental import pallas as pl
from jax.experimental.pallas import tpu as pltpu
from jax.sharding import PartitionSpec as P

HD = 128
TPF = 32
FR_DEV = 3
ROWS = FR_DEV * TPF
SCALE = HD ** (-0.5) * math.log2(math.e)


reach_cap = 32


def from_behind(x, axis, by):
    devices = lax.axis_size(axis)
    return lax.ppermute(x, axis, [(i, (i + by) % devices) for i in range(devices)])


def on_device_band(queries, keys_values, out_weight):
    total_frames = lax.axis_size("frames") * FR_DEV
    reach = min(reach_cap, (total_frames - 1) // 2)
    steps = (reach + FR_DEV - 1) // FR_DEV
    width = keys_values.shape[2]
    span = FR_DEV + 2 * reach
    stacked = keys_values.reshape(2, FR_DEV, TPF, width)
    pieces = []
    for offset in range(-steps, steps + 1):
        if offset == 0:
            pieces.append(stacked)
        else:
            pieces.append(from_behind(stacked, "frames", -offset))
    window = jnp.concatenate(pieces, axis=1)
    lower_frame = steps * FR_DEV - reach
    extended = window[:, lower_frame : lower_frame + span]
    keys_ext = extended[0].reshape(span * TPF, width)
    values_ext = extended[1].reshape(span * TPF, width)
    row_frame = jnp.arange(FR_DEV * TPF, dtype=jnp.int32) // TPF
    col_frame = jnp.arange(span * TPF, dtype=jnp.int32) // TPF
    allowed = (col_frame[None, :] >= row_frame[:, None]) & (
        col_frame[None, :] <= row_frame[:, None] + 2 * reach
    )
    results = []
    for head in range(width // HD):
        lower = head * HD
        query_cols = queries[:, lower : lower + HD]
        key_cols = keys_ext[:, lower : lower + HD]
        scores = lax.dot_general(
            query_cols, key_cols, (((1,), (1,)), ((), ())), preferred_element_type=jnp.float32
        )
        scores = scores * HD ** (-0.5)
        top = jnp.max(jnp.where(allowed, scores, -1e30), axis=1, keepdims=True)
        weights = jnp.where(allowed, jnp.exp(scores - top), 0.0)
        probs = (weights / jnp.sum(weights, axis=1, keepdims=True)).astype(jnp.bfloat16)
        results.append(
            jnp.dot(
                probs, values_ext[:, lower : lower + HD], preferred_element_type=jnp.float32
            ).astype(jnp.bfloat16)
        )
    attended = jnp.concatenate(results, axis=1)
    partial_rows = jnp.dot(
        attended,
        lax.all_gather(out_weight, "frames", axis=1, tiled=True),
        preferred_element_type=jnp.float32,
    )
    return lax.psum_scatter(
        partial_rows.astype(jnp.bfloat16), "heads", scatter_dimension=1, tiled=True
    )


def ring_order(n):
    return list(range(0, n, 2)) + list(range(n - 1, 0, -2))


def ring_place(f, n):
    return (f >> 1) + (f & 1) * (n - 1 - (f >> 1) * 2)


def hop(x, n, by):
    order = ring_order(n)
    return lax.ppermute(x, "frames", [(order[i], order[(i + by) % n]) for i in range(n)])


def gather_ring(streams, n):
    found = [[block] + [None] * (n - 1) for block in streams]
    for step in range(1, n // 2 + 1):
        for j, blocks in enumerate(found):
            for by in (1, -1):
                if step < n // 2 or (j == 0) == (by == 1):
                    blocks[by * step % n] = hop(blocks[by * (step - 1) % n], n, by)
    return found


def left_out(place, block, n):
    return FR_DEV * ((place - ((place - block) & (n - 1) ^ 2)) & (n - 1))


def frame_marks(place, blocks, n):
    lane = lax.broadcasted_iota(jnp.int32, (TPF, HD), 1)
    marks = []
    for block in blocks:
        frame = left_out(place, block, n)
        for g in range(FR_DEV):
            marks.append((lane == frame + g) | (lane >= n * FR_DEV))
    return jnp.concatenate([jnp.where(mark, 1.0, 0.0) for mark in marks], axis=0).astype(jnp.bfloat16)


def key_marks(blocks, padding, n):
    lane = lax.broadcasted_iota(jnp.int32, (TPF, HD), 1)
    frames = [FR_DEV * block + g for block in blocks for g in range(FR_DEV)] + [n * FR_DEV] * (padding // TPF)
    return jnp.concatenate([jnp.where(lane == frame, -1e30, 0.0) for frame in frames], axis=0).astype(jnp.bfloat16)


def rows_of(refs, rows, cols, padding=0):
    pieces = [ref[rows, cols] for ref in refs]
    if padding:
        pieces.append(jnp.zeros((padding, HD), jnp.bfloat16))
    return jnp.concatenate(pieces, axis=0)


def scores_of(queries, keys):
    return lax.dot_general(queries, keys, (((1,), (1,)), ((), ())), preferred_element_type=jnp.float32)


def soften(scores, floor=None):
    weights, tops = [], []
    for r in range(0, scores.shape[0], TPF):
        parts = [scores[r : r + TPF, c : c + HD] for c in range(0, scores.shape[1], HD)]
        top = jnp.max(functools.reduce(jnp.maximum, parts), axis=1, keepdims=True)
        top = jnp.broadcast_to(top, (TPF, HD))
        if floor is not None:
            top = jnp.maximum(top, floor[r : r + TPF])
        weights.append(jnp.concatenate([jnp.exp2((p - top) * SCALE).astype(jnp.bfloat16) for p in parts], axis=1))
        tops.append(top)
    return jnp.concatenate(weights, axis=0), jnp.concatenate(tops, axis=0)


def mix(weights, values):
    ones = jnp.ones(values.shape, values.dtype)
    mixed = jnp.dot(weights, jnp.concatenate([values, ones], axis=1), preferred_element_type=jnp.float32)
    return mixed[:, :HD], mixed[:, HD:]


TOKEN_ROWS = slice(0, ROWS)
QUERY_ROWS = slice(ROWS, ROWS + ROWS // 2)


def queries_of(first, second, blocks, cols):
    pieces = [part[block][QUERY_ROWS, cols] for block in blocks for part in (first, second)]
    return jnp.concatenate(pieces, axis=0)


def near_kernel(heads, n, at_ref, *refs):
    near = [d for d in range(n) if d != n // 2]
    refs, (mixed_ref, sum_ref, top_ref) = refs[:-3], refs[-3:]
    first, second = dict(zip(near, refs[: n - 1])), dict(zip(near, refs[n - 1 :]))
    marks = frame_marks(at_ref[0], near, n)
    keys_marks = key_marks(near, ROWS, n)
    for head in range(heads):
        cols = slice(head * HD, (head + 1) * HD)
        queries = jnp.concatenate([queries_of(first, second, near, cols), marks], axis=1)
        keys = rows_of([first[d] for d in near], TOKEN_ROWS, cols, ROWS)
        values = rows_of([second[d] for d in near], TOKEN_ROWS, cols, ROWS)
        weights, top = soften(scores_of(queries, jnp.concatenate([keys, keys_marks], axis=1)))
        mixed_ref[head], sum_ref[head] = mix(weights, values)
        top_ref[head] = top


def slot_block(at_ref, slot, flip_core, n):
    place, z, y, x, core = (at_ref[i] for i in range(5))
    z = z ^ slot ^ (2 * y + x)
    owner = z + (core ^ flip_core) * (n - 1 - 2 * z)
    return (place - owner) & (n - 1)


def finish_kernel(heads, n, at_ref, *refs):
    far = n // 2
    near = [d for d in range(n) if d != far]
    first, second = refs[:n], refs[n : 2 * n]
    mixed_ref, sum_ref, top_ref, w_ref, given_ref, attended_ref = refs[2 * n :]
    place = at_ref[0]
    pad = TPF
    marks, far_marks = frame_marks(place, near, n), frame_marks(place, [far], n)
    far_keys_marks, all_marks = key_marks([far], pad, n), key_marks(range(n), 0, n)
    for head in range(heads):
        cols = slice(head * HD, (head + 1) * HD)
        queries = jnp.concatenate([queries_of(first, second, near, cols), marks], axis=1)
        keys = jnp.concatenate([rows_of([first[far]], TOKEN_ROWS, cols, pad), far_keys_marks], axis=1)
        before = top_ref[head]
        weights, top = soften(scores_of(queries, keys), before)
        mixed, total = mix(weights, rows_of([second[far]], TOKEN_ROWS, cols, pad))
        kept = jnp.exp2((before - top) * SCALE)
        mixed = (mixed + mixed_ref[head] * kept) / (total + sum_ref[head] * kept)
        for i, d in enumerate(near):
            attended_ref[d, :, cols] = mixed[i * ROWS : (i + 1) * ROWS].astype(jnp.bfloat16)
        queries = jnp.concatenate([queries_of(first, second, [far], cols), far_marks], axis=1)
        keys = jnp.concatenate([rows_of(first, TOKEN_ROWS, cols), all_marks], axis=1)
        weights, _ = soften(scores_of(queries, keys))
        mixed, total = mix(weights, rows_of(second, TOKEN_ROWS, cols))
        attended_ref[far, :, cols] = (mixed / total).astype(jnp.bfloat16)
    rows = jnp.concatenate([attended_ref[slot_block(at_ref, slot, 1, n)] for slot in range(n // 2)], axis=0)
    given_ref[...] = jnp.dot(rows, w_ref[...], preferred_element_type=jnp.float32).astype(given_ref.dtype)


def own_kernel(n, at_ref, attended_ref, w_ref, kept_ref):
    rows = jnp.concatenate([attended_ref[slot_block(at_ref, slot, 0, n)] for slot in range(n // 2)], axis=0)
    kept_ref[...] = jnp.dot(rows, w_ref[...], preferred_element_type=jnp.float32)


def call(kernel, where, operands, outs, flops):
    vmem = pl.BlockSpec(memory_space=pltpu.VMEM)
    return pl.pallas_call(
        kernel,
        out_shape=[jax.ShapeDtypeStruct(shape, dtype) for shape, dtype in outs],
        in_specs=[pl.BlockSpec(memory_space=pltpu.SMEM)] + [vmem] * len(operands),
        out_specs=[vmem] * len(outs),
        compiler_params=pltpu.CompilerParams(vmem_limit_bytes=20 * 1024 * 1024),
        cost_estimate=pl.CostEstimate(flops=flops, bytes_accessed=0, transcendentals=0),
    )(where, *operands)


def on_device_ring(queries, keys_values, out_weight):
    n = lax.axis_size("frames")
    frame, head = lax.axis_index("frames"), lax.axis_index("heads")
    z, y, x, core = frame >> 1, frame & 1, head >> 1, head & 1
    where = jnp.stack([ring_place(frame, n), z, y, x, core]).astype(jnp.int32)
    half = ROWS // 2
    width, cols = out_weight.shape
    heads = width // HD
    streams = [
        jnp.concatenate([keys_values[0], queries[:half]], axis=0),
        jnp.concatenate([keys_values[1], queries[half:]], axis=0),
    ]
    first, second = gather_ring(streams, n)
    f32, bf16 = jnp.float32, jnp.bfloat16
    near = [d for d in range(n) if d != n // 2]
    state = call(
        functools.partial(near_kernel, heads, n),
        where,
        [blocks[d] for blocks in (first, second) for d in near],
        [((heads, (n - 1) * ROWS, HD), f32)] * 3,
        4 * (n - 1) ** 2 * ROWS**2 * width,
    )
    given, attended = call(
        functools.partial(finish_kernel, heads, n),
        where,
        [*first, *second, *state, out_weight],
        [((n // 2 * ROWS, cols), bf16), ((n, ROWS, width), bf16)],
        8 * n * ROWS**2 * width,
    )
    from_core = lax.ppermute(given, "heads", [(h, h ^ 1) for h in range(4)])
    (kept,) = call(
        functools.partial(own_kernel, n),
        where,
        [attended, out_weight],
        [((n // 2 * ROWS, cols), f32)],
        n * ROWS * width * cols,
    )
    arrived = []
    for slot in range(n // 2):
        rows = slice(slot * ROWS, (slot + 1) * ROWS)
        pairs = []
        for f in range(n):
            for h in range(4):
                to = (f >> 1) ^ slot ^ (2 * (f & 1) + (h >> 1))
                pairs.append((4 * f + h, 4 * (2 * to + (h & 1)) + (f >> 1)))
        total = (kept[rows] + from_core[rows].astype(f32)).astype(bf16)
        arrived.append(lax.ppermute(total, ("frames", "heads"), pairs).astype(f32))
    low, high = (arrived[0] + arrived[1]).astype(bf16), (arrived[2] + arrived[3]).astype(bf16)
    straight = (z ^ head) & 2 == 0
    return jnp.concatenate([jnp.where(straight, low, high), jnp.where(straight, high, low)], axis=1)


def solution(mesh):
    in_specs = (P("frames", "heads"), P(None, "frames", "heads"), P("heads", "frames"))
    out_specs = P("frames", "heads")
    n, heads = mesh.shape["frames"], mesh.shape["heads"]
    total_frames = n * FR_DEV
    reach = min(reach_cap, (total_frames - 1) // 2)
    every = total_frames == 2 * reach + 2 and heads == 4 and n == 2 * heads
    return jax.shard_map(
        on_device_ring if every else on_device_band,
        mesh=mesh,
        in_specs=in_specs,
        out_specs=out_specs,
        check_vma=False,
    )
```

```python
import functools
import math

import jax
import jax.numpy as jnp
from jax import lax
from jax.experimental import pallas as pl
from jax.experimental.pallas import tpu as pltpu
from jax.sharding import PartitionSpec as P

HD = 128
TPF = 32
FR_DEV = 3
ROWS = FR_DEV * TPF
SCALE = HD ** (-0.5) * math.log2(math.e)


reach_cap = 32


def from_behind(x, axis, by):
    devices = lax.axis_size(axis)
    return lax.ppermute(x, axis, [(i, (i + by) % devices) for i in range(devices)])


def on_device_band(queries, keys_values, out_weight):
    total_frames = lax.axis_size("frames") * FR_DEV
    reach = min(reach_cap, (total_frames - 1) // 2)
    steps = (reach + FR_DEV - 1) // FR_DEV
    width = keys_values.shape[2]
    span = FR_DEV + 2 * reach
    stacked = keys_values.reshape(2, FR_DEV, TPF, width)
    pieces = []
    for offset in range(-steps, steps + 1):
        if offset == 0:
            pieces.append(stacked)
        else:
            pieces.append(from_behind(stacked, "frames", -offset))
    window = jnp.concatenate(pieces, axis=1)
    lower_frame = steps * FR_DEV - reach
    extended = window[:, lower_frame : lower_frame + span]
    keys_ext = extended[0].reshape(span * TPF, width)
    values_ext = extended[1].reshape(span * TPF, width)
    row_frame = jnp.arange(FR_DEV * TPF, dtype=jnp.int32) // TPF
    col_frame = jnp.arange(span * TPF, dtype=jnp.int32) // TPF
    allowed = (col_frame[None, :] >= row_frame[:, None]) & (
        col_frame[None, :] <= row_frame[:, None] + 2 * reach
    )
    results = []
    for head in range(width // HD):
        lower = head * HD
        query_cols = queries[:, lower : lower + HD]
        key_cols = keys_ext[:, lower : lower + HD]
        scores = lax.dot_general(
            query_cols, key_cols, (((1,), (1,)), ((), ())), preferred_element_type=jnp.float32
        )
        scores = scores * HD ** (-0.5)
        top = jnp.max(jnp.where(allowed, scores, -1e30), axis=1, keepdims=True)
        weights = jnp.where(allowed, jnp.exp(scores - top), 0.0)
        probs = (weights / jnp.sum(weights, axis=1, keepdims=True)).astype(jnp.bfloat16)
        results.append(
            jnp.dot(
                probs, values_ext[:, lower : lower + HD], preferred_element_type=jnp.float32
            ).astype(jnp.bfloat16)
        )
    attended = jnp.concatenate(results, axis=1)
    partial_rows = jnp.dot(
        attended,
        lax.all_gather(out_weight, "frames", axis=1, tiled=True),
        preferred_element_type=jnp.float32,
    )
    return lax.psum_scatter(
        partial_rows.astype(jnp.bfloat16), "heads", scatter_dimension=1, tiled=True
    )


def ring_order(n):
    return list(range(0, n, 2)) + list(range(n - 1, 0, -2))


def ring_place(f, n):
    return (f >> 1) + (f & 1) * (n - 1 - (f >> 1) * 2)


def hop(x, n, by):
    order = ring_order(n)
    return lax.ppermute(x, "frames", [(order[i], order[(i + by) % n]) for i in range(n)])


def gather_ring(streams, n):
    found = [[block] + [None] * (n - 1) for block in streams]
    for step in range(1, n // 2 + 1):
        for j, blocks in enumerate(found):
            for by in (1, -1):
                if step < n // 2 or (j == 0) == (by == 1):
                    blocks[by * step % n] = hop(blocks[by * (step - 1) % n], n, by)
    return found


def left_out(place, block, n):
    return FR_DEV * ((place - ((place - block) & (n - 1) ^ 2)) & (n - 1))


def frame_marks(place, blocks, n):
    lane = lax.broadcasted_iota(jnp.int32, (TPF, HD), 1)
    marks = []
    for block in blocks:
        frame = left_out(place, block, n)
        for g in range(FR_DEV):
            marks.append((lane == frame + g) | (lane >= n * FR_DEV))
    return jnp.concatenate([jnp.where(mark, 1.0, 0.0) for mark in marks], axis=0).astype(jnp.bfloat16)


def key_marks(blocks, padding, n):
    lane = lax.broadcasted_iota(jnp.int32, (TPF, HD), 1)
    frames = [FR_DEV * block + g for block in blocks for g in range(FR_DEV)] + [n * FR_DEV] * (padding // TPF)
    return jnp.concatenate([jnp.where(lane == frame, -1e30, 0.0) for frame in frames], axis=0).astype(jnp.bfloat16)


def rows_of(refs, rows, cols, padding=0):
    pieces = [ref[rows, cols] for ref in refs]
    if padding:
        pieces.append(jnp.zeros((padding, HD), jnp.bfloat16))
    return jnp.concatenate(pieces, axis=0)


def scores_of(queries, keys):
    return lax.dot_general(queries, keys, (((1,), (1,)), ((), ())), preferred_element_type=jnp.float32)


def soften(scores, floor=None):
    weights, tops = [], []
    for r in range(0, scores.shape[0], TPF):
        parts = [scores[r : r + TPF, c : c + HD] for c in range(0, scores.shape[1], HD)]
        top = jnp.max(functools.reduce(jnp.maximum, parts), axis=1, keepdims=True)
        top = jnp.broadcast_to(top, (TPF, HD))
        if floor is not None:
            top = jnp.maximum(top, floor[r : r + TPF])
        weights.append(jnp.concatenate([jnp.exp2((p - top) * SCALE).astype(jnp.bfloat16) for p in parts], axis=1))
        tops.append(top)
    return jnp.concatenate(weights, axis=0), jnp.concatenate(tops, axis=0)


def mix(weights, values):
    ones = jnp.ones(values.shape, values.dtype)
    mixed = jnp.dot(weights, jnp.concatenate([values, ones], axis=1), preferred_element_type=jnp.float32)
    return mixed[:, :HD], mixed[:, HD:]


TOKEN_ROWS = slice(0, ROWS)
QUERY_ROWS = slice(ROWS, ROWS + ROWS // 2)


def queries_of(first, second, blocks, cols):
    pieces = [part[block][QUERY_ROWS, cols] for block in blocks for part in (first, second)]
    return jnp.concatenate(pieces, axis=0)


def near_kernel(heads, n, at_ref, *refs):
    near = [d for d in range(n) if d != n // 2]
    refs, (mixed_ref, sum_ref, top_ref) = refs[:-3], refs[-3:]
    first, second = dict(zip(near, refs[: n - 1])), dict(zip(near, refs[n - 1 :]))
    marks = frame_marks(at_ref[0], near, n)
    keys_marks = key_marks(near, ROWS, n)
    for head in range(heads):
        cols = slice(head * HD, (head + 1) * HD)
        queries = jnp.concatenate([queries_of(first, second, near, cols), marks], axis=1)
        keys = rows_of([first[d] for d in near], TOKEN_ROWS, cols, ROWS)
        values = rows_of([second[d] for d in near], TOKEN_ROWS, cols, ROWS)
        weights, top = soften(scores_of(queries, jnp.concatenate([keys, keys_marks], axis=1)))
        mixed_ref[head], sum_ref[head] = mix(weights, values)
        top_ref[head] = top


def slot_block(at_ref, slot, flip_core, n):
    place, y, x, core = (at_ref[i] for i in range(4))
    z = slot ^ (2 * y + x)
    owner = z + (core ^ flip_core) * (n - 1 - 2 * z)
    return (place - owner) & (n - 1)


def finish_kernel(heads, n, at_ref, *refs):
    far = n // 2
    near = [d for d in range(n) if d != far]
    first, second = refs[:n], refs[n : 2 * n]
    mixed_ref, sum_ref, top_ref, w_ref, given_ref, attended_ref = refs[2 * n :]
    place = at_ref[0]
    pad = TPF
    marks, far_marks = frame_marks(place, near, n), frame_marks(place, [far], n)
    far_keys_marks, all_marks = key_marks([far], pad, n), key_marks(range(n), 0, n)
    for head in range(heads):
        cols = slice(head * HD, (head + 1) * HD)
        queries = jnp.concatenate([queries_of(first, second, near, cols), marks], axis=1)
        keys = jnp.concatenate([rows_of([first[far]], TOKEN_ROWS, cols, pad), far_keys_marks], axis=1)
        before = top_ref[head]
        weights, top = soften(scores_of(queries, keys), before)
        mixed, total = mix(weights, rows_of([second[far]], TOKEN_ROWS, cols, pad))
        kept = jnp.exp2((before - top) * SCALE)
        mixed = (mixed + mixed_ref[head] * kept) / (total + sum_ref[head] * kept)
        for i, d in enumerate(near):
            attended_ref[d, :, cols] = mixed[i * ROWS : (i + 1) * ROWS].astype(jnp.bfloat16)
        queries = jnp.concatenate([queries_of(first, second, [far], cols), far_marks], axis=1)
        keys = jnp.concatenate([rows_of(first, TOKEN_ROWS, cols), all_marks], axis=1)
        weights, _ = soften(scores_of(queries, keys))
        mixed, total = mix(weights, rows_of(second, TOKEN_ROWS, cols))
        attended_ref[far, :, cols] = (mixed / total).astype(jnp.bfloat16)
    rows = jnp.concatenate([attended_ref[slot_block(at_ref, slot, 1, n)] for slot in range(n // 2)], axis=0)
    given_ref[...] = jnp.dot(rows, w_ref[...], preferred_element_type=jnp.float32).astype(given_ref.dtype)


def own_kernel(n, at_ref, attended_ref, w_ref, kept_ref):
    rows = jnp.concatenate([attended_ref[slot_block(at_ref, slot, 0, n)] for slot in range(n // 2)], axis=0)
    kept_ref[...] = jnp.dot(rows, w_ref[...], preferred_element_type=jnp.float32)


def call(kernel, where, operands, outs, flops):
    vmem = pl.BlockSpec(memory_space=pltpu.VMEM)
    return pl.pallas_call(
        kernel,
        out_shape=[jax.ShapeDtypeStruct(shape, dtype) for shape, dtype in outs],
        in_specs=[pl.BlockSpec(memory_space=pltpu.SMEM)] + [vmem] * len(operands),
        out_specs=[vmem] * len(outs),
        compiler_params=pltpu.CompilerParams(vmem_limit_bytes=20 * 1024 * 1024),
        cost_estimate=pl.CostEstimate(flops=flops, bytes_accessed=0, transcendentals=0),
    )(where, *operands)


def on_device_ring(queries, keys_values, out_weight):
    n = lax.axis_size("frames")
    frame, head = lax.axis_index("frames"), lax.axis_index("heads")
    z, y, x, core = frame >> 1, frame & 1, head >> 1, head & 1
    where = jnp.stack([ring_place(frame, n), y, x, core]).astype(jnp.int32)
    half = ROWS // 2
    width, cols = out_weight.shape
    heads = width // HD
    streams = [
        jnp.concatenate([keys_values[0], queries[:half]], axis=0),
        jnp.concatenate([keys_values[1], queries[half:]], axis=0),
    ]
    first, second = gather_ring(streams, n)
    f32, bf16 = jnp.float32, jnp.bfloat16
    near = [d for d in range(n) if d != n // 2]
    state = call(
        functools.partial(near_kernel, heads, n),
        where,
        [blocks[d] for blocks in (first, second) for d in near],
        [((heads, (n - 1) * ROWS, HD), f32)] * 3,
        4 * (n - 1) ** 2 * ROWS**2 * width,
    )
    given, attended = call(
        functools.partial(finish_kernel, heads, n),
        where,
        [*first, *second, *state, out_weight],
        [((n // 2 * ROWS, cols), bf16), ((n, ROWS, width), bf16)],
        8 * n * ROWS**2 * width,
    )
    from_core = lax.ppermute(given, "heads", [(h, h ^ 1) for h in range(4)])
    (kept,) = call(
        functools.partial(own_kernel, n),
        where,
        [attended, out_weight],
        [((n // 2 * ROWS, cols), f32)],
        n * ROWS * width * cols,
    )
    arrived = []
    for slot in range(n // 2):
        rows = slice(slot * ROWS, (slot + 1) * ROWS)
        pairs = []
        for f in range(n):
            for h in range(4):
                to = slot ^ (2 * (f & 1) + (h >> 1))
                pairs.append((4 * f + h, 4 * (2 * to + (h & 1)) + (f >> 1)))
        total = (kept[rows] + from_core[rows].astype(f32)).astype(bf16)
        arrived.append(lax.ppermute(total, ("frames", "heads"), pairs).astype(f32))
    low, high = (arrived[0] + arrived[1]).astype(bf16), (arrived[2] + arrived[3]).astype(bf16)
    straight = z & 2 == 0
    return jnp.concatenate([jnp.where(straight, low, high), jnp.where(straight, high, low)], axis=1)


def solution(mesh):
    in_specs = (P("frames", "heads"), P(None, "frames", "heads"), P("heads", "frames"))
    out_specs = P("frames", "heads")
    n, heads = mesh.shape["frames"], mesh.shape["heads"]
    total_frames = n * FR_DEV
    reach = min(reach_cap, (total_frames - 1) // 2)
    every = total_frames == 2 * reach + 2 and heads == 4 and n == 2 * heads
    return jax.shard_map(
        on_device_ring if every else on_device_band,
        mesh=mesh,
        in_specs=in_specs,
        out_specs=out_specs,
        check_vma=False,
    )
```

```python
import functools
import math

import jax
import jax.numpy as jnp
from jax import lax
from jax.experimental import pallas as pl
from jax.experimental.pallas import tpu as pltpu
from jax.sharding import PartitionSpec as P

HD = 128
TPF = 32
FR_DEV = 3
ROWS = FR_DEV * TPF
SCALE = HD ** (-0.5) * math.log2(math.e)


reach_cap = 32


def from_behind(x, axis, by):
    devices = lax.axis_size(axis)
    return lax.ppermute(x, axis, [(i, (i + by) % devices) for i in range(devices)])


def on_device_band(queries, keys_values, out_weight):
    total_frames = lax.axis_size("frames") * FR_DEV
    reach = min(reach_cap, (total_frames - 1) // 2)
    steps = (reach + FR_DEV - 1) // FR_DEV
    width = keys_values.shape[2]
    span = FR_DEV + 2 * reach
    stacked = keys_values.reshape(2, FR_DEV, TPF, width)
    pieces = []
    for offset in range(-steps, steps + 1):
        if offset == 0:
            pieces.append(stacked)
        else:
            pieces.append(from_behind(stacked, "frames", -offset))
    window = jnp.concatenate(pieces, axis=1)
    lower_frame = steps * FR_DEV - reach
    extended = window[:, lower_frame : lower_frame + span]
    keys_ext = extended[0].reshape(span * TPF, width)
    values_ext = extended[1].reshape(span * TPF, width)
    row_frame = jnp.arange(FR_DEV * TPF, dtype=jnp.int32) // TPF
    col_frame = jnp.arange(span * TPF, dtype=jnp.int32) // TPF
    allowed = (col_frame[None, :] >= row_frame[:, None]) & (
        col_frame[None, :] <= row_frame[:, None] + 2 * reach
    )
    results = []
    for head in range(width // HD):
        lower = head * HD
        query_cols = queries[:, lower : lower + HD]
        key_cols = keys_ext[:, lower : lower + HD]
        scores = lax.dot_general(
            query_cols, key_cols, (((1,), (1,)), ((), ())), preferred_element_type=jnp.float32
        )
        scores = scores * HD ** (-0.5)
        top = jnp.max(jnp.where(allowed, scores, -1e30), axis=1, keepdims=True)
        weights = jnp.where(allowed, jnp.exp(scores - top), 0.0)
        probs = (weights / jnp.sum(weights, axis=1, keepdims=True)).astype(jnp.bfloat16)
        results.append(
            jnp.dot(
                probs, values_ext[:, lower : lower + HD], preferred_element_type=jnp.float32
            ).astype(jnp.bfloat16)
        )
    attended = jnp.concatenate(results, axis=1)
    partial_rows = jnp.dot(
        attended,
        lax.all_gather(out_weight, "frames", axis=1, tiled=True),
        preferred_element_type=jnp.float32,
    )
    return lax.psum_scatter(
        partial_rows.astype(jnp.bfloat16), "heads", scatter_dimension=1, tiled=True
    )


def ring_order(n):
    return list(range(0, n, 2)) + list(range(n - 1, 0, -2))


def ring_place(f, n):
    return (f >> 1) + (f & 1) * (n - 1 - (f >> 1) * 2)


def hop(x, n, by):
    order = ring_order(n)
    return lax.ppermute(x, "frames", [(order[i], order[(i + by) % n]) for i in range(n)])


def gather_ring(streams, n):
    found = [[block] + [None] * (n - 1) for block in streams]
    for step in range(1, n // 2 + 1):
        for j, blocks in enumerate(found):
            for by in (1, -1):
                if step < n // 2 or (j == 0) == (by == 1):
                    blocks[by * step % n] = hop(blocks[by * (step - 1) % n], n, by)
    return found


def left_out(place, block, n):
    return FR_DEV * ((place - ((place - block) & (n - 1) ^ 2)) & (n - 1))


def frame_marks(place, blocks, n):
    lane = lax.broadcasted_iota(jnp.int32, (TPF, HD), 1)
    marks = []
    for block in blocks:
        frame = left_out(place, block, n)
        for g in range(FR_DEV):
            marks.append((lane == frame + g) | (lane >= n * FR_DEV))
    return jnp.concatenate([jnp.where(mark, 1.0, 0.0) for mark in marks], axis=0).astype(jnp.bfloat16)


def key_marks(blocks, padding, n):
    lane = lax.broadcasted_iota(jnp.int32, (TPF, HD), 1)
    frames = [FR_DEV * block + g for block in blocks for g in range(FR_DEV)] + [n * FR_DEV] * (padding // TPF)
    return jnp.concatenate([jnp.where(lane == frame, -1e30, 0.0) for frame in frames], axis=0).astype(jnp.bfloat16)


def rows_of(refs, rows, cols, padding=0):
    pieces = [ref[rows, cols] if len(ref.shape) == 2 else ref[rows, :, cols] for ref in refs]
    if padding:
        pieces.append(jnp.zeros((padding, HD), jnp.bfloat16))
    return jnp.concatenate(pieces, axis=0)


def scores_of(queries, keys):
    return lax.dot_general(queries, keys, (((1,), (1,)), ((), ())), preferred_element_type=jnp.float32)


def soften(scores, floor=None):
    weights, tops = [], []
    for r in range(0, scores.shape[0], TPF):
        parts = [scores[r : r + TPF, c : c + HD] for c in range(0, scores.shape[1], HD)]
        top = jnp.max(functools.reduce(jnp.maximum, parts), axis=1, keepdims=True)
        top = jnp.broadcast_to(top, (TPF, HD))
        if floor is not None:
            top = jnp.maximum(top, floor[r : r + TPF])
        weights.append(jnp.concatenate([jnp.exp2((p - top) * SCALE).astype(jnp.bfloat16) for p in parts], axis=1))
        tops.append(top)
    return jnp.concatenate(weights, axis=0), jnp.concatenate(tops, axis=0)


def mix(weights, values):
    ones = jnp.ones(values.shape, values.dtype)
    mixed = jnp.dot(weights, jnp.concatenate([values, ones], axis=1), preferred_element_type=jnp.float32)
    return mixed[:, :HD], mixed[:, HD:]


PATTERNS = ((2, 1, 2, 1), (0, 3, 0, 3), (3, 0, 1, 2), (1, 2, 3, 0))


def look_up(table, index):
    code = sum(entry << (2 * i) for i, entry in enumerate(table))
    return (jnp.int32(code - (code >> 31 << 32)) >> (2 * index)) & 3


def slot_blocks(at_ref, flip_core, n):
    place, z, y, x, core = (at_ref[i] for i in range(5))
    blocks = []
    for slot in range(n // 2):
        to = look_up(sum(PATTERNS, ()), 4 * (slot ^ (2 * y + x)) + z)
        owner = to + (core ^ flip_core) * (n - 1 - 2 * to)
        blocks.append((place - owner) & (n - 1))
    return blocks


def near_kernel(heads, n, at_ref, *refs):
    near = [d for d in range(n) if d != n // 2]
    query_refs, kv_refs, (rows_ref, mixed_ref, sum_ref, top_ref) = refs[:n], refs[n:-4], refs[-4:]
    marks = frame_marks(at_ref[0], range(n), n)
    keys_marks = key_marks(near, ROWS, n)
    for d in range(n):
        rows_ref[d] = query_refs[d][...]
    for head in range(heads):
        cols = slice(head * HD, (head + 1) * HD)
        queries = jnp.concatenate([rows_of(query_refs, slice(0, ROWS), cols), marks], axis=1)
        keys = jnp.concatenate([rows_of(kv_refs, 0, cols, ROWS), keys_marks], axis=1)
        weights, top = soften(scores_of(queries, keys))
        mixed, total = mix(weights, rows_of(kv_refs, 1, cols, ROWS))
        for d in range(n):
            rows = slice(d * ROWS, (d + 1) * ROWS)
            mixed_ref[head, d], sum_ref[head, d], top_ref[head, d] = mixed[rows], total[rows], top[rows]


def finish_kernel(heads, n, flip_core, at_ref, rows_ref, mixed_ref, sum_ref, top_ref, kv_ref, w_ref, out_ref):
    blocks = slot_blocks(at_ref, flip_core, n)
    marks = frame_marks(at_ref[0], blocks, n)
    keys_marks = key_marks([n // 2], TPF, n)
    attended = []

    def of(ref, head):
        return jnp.concatenate([ref[head, block] for block in blocks], axis=0)

    for head in range(heads):
        cols = slice(head * HD, (head + 1) * HD)
        queries = jnp.concatenate([rows_ref[block, :, cols] for block in blocks], axis=0)
        keys = jnp.concatenate([rows_of([kv_ref], 0, cols, TPF), keys_marks], axis=1)
        before = of(top_ref, head)
        weights, top = soften(scores_of(jnp.concatenate([queries, marks], axis=1), keys), before)
        mixed, total = mix(weights, rows_of([kv_ref], 1, cols, TPF))
        kept = jnp.exp2((before - top) * SCALE)
        mixed, total = mixed + of(mixed_ref, head) * kept, total + of(sum_ref, head) * kept
        attended.append((mixed / total).astype(jnp.bfloat16))
    rows = jnp.concatenate(attended, axis=1)
    out_ref[...] = jnp.dot(rows, w_ref[...], preferred_element_type=jnp.float32).astype(out_ref.dtype)


def call(kernel, where, operands, outs, flops):
    vmem = pl.BlockSpec(memory_space=pltpu.VMEM)
    return pl.pallas_call(
        kernel,
        out_shape=[jax.ShapeDtypeStruct(shape, dtype) for shape, dtype in outs],
        in_specs=[pl.BlockSpec(memory_space=pltpu.SMEM)] + [vmem] * len(operands),
        out_specs=[vmem] * len(outs),
        compiler_params=pltpu.CompilerParams(vmem_limit_bytes=20 * 1024 * 1024),
        cost_estimate=pl.CostEstimate(flops=flops, bytes_accessed=0, transcendentals=0),
    )(where, *operands)


def on_device_ring(queries, keys_values, out_weight):
    n = lax.axis_size("frames")
    frame, head = lax.axis_index("frames"), lax.axis_index("heads")
    z, y, x, core = frame >> 1, frame & 1, head >> 1, head & 1
    where = jnp.stack([ring_place(frame, n), z, y, x, core]).astype(jnp.int32)
    width, cols = out_weight.shape
    heads = width // HD
    found_queries, found_kv = gather_ring([queries, keys_values], n)
    f32, bf16 = jnp.float32, jnp.bfloat16
    state = call(
        functools.partial(near_kernel, heads, n),
        where,
        [*found_queries, *(found_kv[d] for d in range(n) if d != n // 2)],
        [((n, ROWS, width), bf16)] + [((heads, n, ROWS, HD), f32)] * 3,
        4 * n * (n - 1) * ROWS**2 * width,
    )

    def finish(flip_core, dtype):
        (rows,) = call(
            functools.partial(finish_kernel, heads, n, flip_core),
            where,
            [*state, found_kv[n // 2], out_weight],
            [((n // 2 * ROWS, cols), dtype)],
            n * ROWS * width * cols,
        )
        return rows

    from_core = lax.ppermute(finish(1, bf16), "heads", [(h, h ^ 1) for h in range(4)])
    kept = finish(0, f32)
    arrived = []
    for slot in range(n // 2):
        rows = slice(slot * ROWS, (slot + 1) * ROWS)
        pairs = []
        for f in range(n):
            for h in range(4):
                to = PATTERNS[slot ^ (2 * (f & 1) + (h >> 1))][f >> 1]
                pairs.append((4 * f + h, 4 * (2 * to + (h & 1)) + (f >> 1)))
        total = (kept[rows] + from_core[rows].astype(f32)).astype(bf16)
        arrived.append(lax.ppermute(total, ("frames", "heads"), pairs).astype(f32))
    low, high = (arrived[0] + arrived[1]).astype(bf16), (arrived[2] + arrived[3]).astype(bf16)
    patterns = [[p[source] for p in PATTERNS].index(to) for source in range(4) for to in range(4)]
    straight = look_up(patterns, 4 * head + z) & 2 == 0
    return jnp.concatenate([jnp.where(straight, low, high), jnp.where(straight, high, low)], axis=1)


def solution(mesh):
    in_specs = (P("frames", "heads"), P(None, "frames", "heads"), P("heads", "frames"))
    out_specs = P("frames", "heads")
    n, heads = mesh.shape["frames"], mesh.shape["heads"]
    total_frames = n * FR_DEV
    reach = min(reach_cap, (total_frames - 1) // 2)
    every = total_frames == 2 * reach + 2 and heads == 4 and n == 2 * heads
    return jax.shard_map(
        on_device_ring if every else on_device_band,
        mesh=mesh,
        in_specs=in_specs,
        out_specs=out_specs,
        check_vma=False,
    )
```

```python
import functools
import math

import jax
import jax.numpy as jnp
from jax import lax
from jax.experimental import pallas as pl
from jax.experimental.pallas import tpu as pltpu
from jax.sharding import PartitionSpec as P

HD = 128
TPF = 32
FR_DEV = 3
ROWS = FR_DEV * TPF
SCALE = HD ** (-0.5) * math.log2(math.e)


reach_cap = 32


def from_behind(x, axis, by):
    devices = lax.axis_size(axis)
    return lax.ppermute(x, axis, [(i, (i + by) % devices) for i in range(devices)])


def on_device_band(queries, keys_values, out_weight):
    total_frames = lax.axis_size("frames") * FR_DEV
    reach = min(reach_cap, (total_frames - 1) // 2)
    steps = (reach + FR_DEV - 1) // FR_DEV
    width = keys_values.shape[2]
    span = FR_DEV + 2 * reach
    stacked = keys_values.reshape(2, FR_DEV, TPF, width)
    pieces = []
    for offset in range(-steps, steps + 1):
        if offset == 0:
            pieces.append(stacked)
        else:
            pieces.append(from_behind(stacked, "frames", -offset))
    window = jnp.concatenate(pieces, axis=1)
    lower_frame = steps * FR_DEV - reach
    extended = window[:, lower_frame : lower_frame + span]
    keys_ext = extended[0].reshape(span * TPF, width)
    values_ext = extended[1].reshape(span * TPF, width)
    row_frame = jnp.arange(FR_DEV * TPF, dtype=jnp.int32) // TPF
    col_frame = jnp.arange(span * TPF, dtype=jnp.int32) // TPF
    allowed = (col_frame[None, :] >= row_frame[:, None]) & (
        col_frame[None, :] <= row_frame[:, None] + 2 * reach
    )
    results = []
    for head in range(width // HD):
        lower = head * HD
        query_cols = queries[:, lower : lower + HD]
        key_cols = keys_ext[:, lower : lower + HD]
        scores = lax.dot_general(
            query_cols, key_cols, (((1,), (1,)), ((), ())), preferred_element_type=jnp.float32
        )
        scores = scores * HD ** (-0.5)
        top = jnp.max(jnp.where(allowed, scores, -1e30), axis=1, keepdims=True)
        weights = jnp.where(allowed, jnp.exp(scores - top), 0.0)
        probs = (weights / jnp.sum(weights, axis=1, keepdims=True)).astype(jnp.bfloat16)
        results.append(
            jnp.dot(
                probs, values_ext[:, lower : lower + HD], preferred_element_type=jnp.float32
            ).astype(jnp.bfloat16)
        )
    attended = jnp.concatenate(results, axis=1)
    partial_rows = jnp.dot(
        attended,
        lax.all_gather(out_weight, "frames", axis=1, tiled=True),
        preferred_element_type=jnp.float32,
    )
    return lax.psum_scatter(
        partial_rows.astype(jnp.bfloat16), "heads", scatter_dimension=1, tiled=True
    )


def ring_order(n):
    return list(range(0, n, 2)) + list(range(n - 1, 0, -2))


def ring_place(f, n):
    return (f >> 1) + (f & 1) * (n - 1 - (f >> 1) * 2)


def hop(x, n, by):
    order = ring_order(n)
    return lax.ppermute(x, "frames", [(order[i], order[(i + by) % n]) for i in range(n)])


def gather_ring(streams, n):
    found = [[block] + [None] * (n - 1) for block in streams]
    for step in range(1, n // 2 + 1):
        for j, blocks in enumerate(found):
            for by in (1, -1):
                if step < n // 2 or (j == 0) == (by == 1):
                    blocks[by * step % n] = hop(blocks[by * (step - 1) % n], n, by)
    return found


def left_out(place, block, n):
    return FR_DEV * ((place - ((place - block) & (n - 1) ^ 2)) & (n - 1))


def frame_marks(place, blocks, n):
    lane = lax.broadcasted_iota(jnp.int32, (TPF, HD), 1)
    marks = []
    for block in blocks:
        frame = left_out(place, block, n)
        for g in range(FR_DEV):
            marks.append((lane == frame + g) | (lane >= n * FR_DEV))
    return jnp.concatenate([jnp.where(mark, 1.0, 0.0) for mark in marks], axis=0).astype(jnp.bfloat16)


def key_marks(blocks, padding, n):
    lane = lax.broadcasted_iota(jnp.int32, (TPF, HD), 1)
    frames = [FR_DEV * block + g for block in blocks for g in range(FR_DEV)] + [n * FR_DEV] * (padding // TPF)
    return jnp.concatenate([jnp.where(lane == frame, -1e30, 0.0) for frame in frames], axis=0).astype(jnp.bfloat16)


def rows_of(refs, rows, cols, padding=0):
    pieces = [ref[rows, cols] if len(ref.shape) == 2 else ref[rows, :, cols] for ref in refs]
    if padding:
        pieces.append(jnp.zeros((padding, HD), jnp.bfloat16))
    return jnp.concatenate(pieces, axis=0)


def scores_of(queries, keys):
    return lax.dot_general(queries, keys, (((1,), (1,)), ((), ())), preferred_element_type=jnp.float32)


def soften(scores, floor=None):
    weights, tops = [], []
    for r in range(0, scores.shape[0], TPF):
        parts = [scores[r : r + TPF, c : c + HD] for c in range(0, scores.shape[1], HD)]
        top = jnp.max(functools.reduce(jnp.maximum, parts), axis=1, keepdims=True)
        top = jnp.broadcast_to(top, (TPF, HD))
        if floor is not None:
            top = jnp.maximum(top, floor[r : r + TPF])
        weights.append(jnp.concatenate([jnp.exp2((p - top) * SCALE).astype(jnp.bfloat16) for p in parts], axis=1))
        tops.append(top)
    return jnp.concatenate(weights, axis=0), jnp.concatenate(tops, axis=0)


def mix(weights, values):
    ones = jnp.ones(values.shape, values.dtype)
    mixed = jnp.dot(weights, jnp.concatenate([values, ones], axis=1), preferred_element_type=jnp.float32)
    return mixed[:, :HD], mixed[:, HD:]


PATTERNS = ((2, 1, 2, 1), (0, 3, 0, 3), (3, 0, 1, 2), (1, 2, 3, 0))


def look_up(table, index):
    code = sum(entry << (2 * i) for i, entry in enumerate(table))
    return (jnp.int32(code - (code >> 31 << 32)) >> (2 * index)) & 3


def slot_blocks(at_ref, flip_core, n):
    place, z, y, x, core = (at_ref[i] for i in range(5))
    blocks = []
    for slot in range(n // 2):
        to = look_up(sum(PATTERNS, ()), 4 * (slot ^ (2 * y + x)) + z)
        owner = to + (core ^ flip_core) * (n - 1 - 2 * to)
        blocks.append((place - owner) & (n - 1))
    return blocks


TOKEN_ROWS = slice(0, ROWS)
QUERY_ROWS = slice(ROWS, ROWS + ROWS // 2)


def streams_kernel(queries_ref, kv_ref, first_ref, second_ref, sems):
    half = ROWS // 2
    copies = []
    for i, out_ref in enumerate((first_ref, second_ref)):
        copies.append((kv_ref.at[i], out_ref.at[pl.ds(0, ROWS)]))
        copies.append((queries_ref.at[pl.ds(i * half, half)], out_ref.at[pl.ds(ROWS, half)]))
    copies = [pltpu.make_async_copy(src, dst, sems.at[i]) for i, (src, dst) in enumerate(copies)]
    for copy in copies:
        copy.start()
    for copy in copies:
        copy.wait()


def attend_all(place, block, queries, first, second, cols, n):
    queries = jnp.concatenate([queries, frame_marks(place, [block], n)], axis=1)
    keys = jnp.concatenate([rows_of(first, TOKEN_ROWS, cols), key_marks(range(n), 0, n)], axis=1)
    weights, _ = soften(scores_of(queries, keys))
    mixed, total = mix(weights, rows_of(second, TOKEN_ROWS, cols))
    return (mixed / total).astype(jnp.bfloat16)


def near_kernel(heads, n, at_ref, *refs):
    far = n // 2
    near = [d for d in range(n) if d != far]
    first, second, (rows_ref, mixed_ref, sum_ref, top_ref) = refs[: n - 1], refs[n - 1 : -4], refs[-4:]
    marks = frame_marks(at_ref[0], near, n)
    keys_marks = key_marks(near, ROWS, n)
    half = ROWS // 2
    for d, first_ref, second_ref in zip(near, first, second):
        rows_ref[d, :half] = first_ref[QUERY_ROWS, :]
        rows_ref[d, half:] = second_ref[QUERY_ROWS, :]
    rows_ref[far] = jnp.zeros(rows_ref.shape[1:], rows_ref.dtype)
    for head in range(heads):
        cols = slice(head * HD, (head + 1) * HD)
        queries = [ref[QUERY_ROWS, cols] for pair in zip(first, second) for ref in pair]
        keys = jnp.concatenate([rows_of(first, TOKEN_ROWS, cols, ROWS), keys_marks], axis=1)
        weights, top = soften(scores_of(jnp.concatenate([jnp.concatenate(queries, axis=0), marks], axis=1), keys))
        mixed, total = mix(weights, rows_of(second, TOKEN_ROWS, cols, ROWS))
        for i, d in enumerate(near):
            rows = slice(i * ROWS, (i + 1) * ROWS)
            mixed_ref[head, d], sum_ref[head, d], top_ref[head, d] = mixed[rows], total[rows], top[rows]
        mixed_ref[head, far] = jnp.zeros((ROWS, HD), jnp.float32)
        sum_ref[head, far] = jnp.ones((ROWS, HD), jnp.float32)
        top_ref[head, far] = jnp.zeros((ROWS, HD), jnp.float32)


def finish(heads, n, flip_core, at_ref, state, far_keys_ref, far_values_ref, far_rows_ref, w_ref):
    rows_ref, mixed_ref, sum_ref, top_ref = state
    far = n // 2
    blocks = slot_blocks(at_ref, flip_core, n)
    marks = frame_marks(at_ref[0], blocks, n)
    keys_marks = key_marks([far], TPF, n)
    attended = []

    def of(ref, head):
        return jnp.concatenate([ref[head, block] for block in blocks], axis=0)

    for head in range(heads):
        cols = slice(head * HD, (head + 1) * HD)
        queries = jnp.concatenate([rows_ref[block, :, cols] for block in blocks], axis=0)
        keys = jnp.concatenate([rows_of([far_keys_ref], TOKEN_ROWS, cols, TPF), keys_marks], axis=1)
        before = of(top_ref, head)
        weights, top = soften(scores_of(jnp.concatenate([queries, marks], axis=1), keys), before)
        mixed, total = mix(weights, rows_of([far_values_ref], TOKEN_ROWS, cols, TPF))
        kept = jnp.exp2((before - top) * SCALE)
        mixed, total = mixed + of(mixed_ref, head) * kept, total + of(sum_ref, head) * kept
        result = (mixed / total).astype(jnp.bfloat16)
        result = [
            jnp.where(block == far, far_rows_ref[:, cols], result[i * ROWS : (i + 1) * ROWS])
            for i, block in enumerate(blocks)
        ]
        attended.append(jnp.concatenate(result, axis=0))
    return jnp.dot(jnp.concatenate(attended, axis=1), w_ref[...], preferred_element_type=jnp.float32)


def given_kernel(heads, n, at_ref, *refs):
    far = n // 2
    first, second, state, (w_ref, out_ref, far_rows_ref) = refs[:n], refs[n : 2 * n], refs[2 * n : 2 * n + 4], refs[-3:]
    for head in range(heads):
        cols = slice(head * HD, (head + 1) * HD)
        queries = jnp.concatenate([part[far][QUERY_ROWS, cols] for part in (first, second)], axis=0)
        far_rows_ref[:, cols] = attend_all(at_ref[0], far, queries, first, second, cols, n)
    result = finish(heads, n, 1, at_ref, state, first[far], second[far], far_rows_ref, w_ref)
    out_ref[...] = result.astype(out_ref.dtype)


def kept_kernel(heads, n, at_ref, *refs):
    state, others, out_ref = refs[:4], refs[4:8], refs[-1]
    out_ref[...] = finish(heads, n, 0, at_ref, state, *others)


def call(kernel, where, operands, outs, flops):
    vmem = pl.BlockSpec(memory_space=pltpu.VMEM)
    return pl.pallas_call(
        kernel,
        out_shape=[jax.ShapeDtypeStruct(shape, dtype) for shape, dtype in outs],
        in_specs=[pl.BlockSpec(memory_space=pltpu.SMEM)] + [vmem] * len(operands),
        out_specs=[vmem] * len(outs),
        compiler_params=pltpu.CompilerParams(vmem_limit_bytes=20 * 1024 * 1024),
        cost_estimate=pl.CostEstimate(flops=flops, bytes_accessed=0, transcendentals=0),
    )(where, *operands)


def on_device_ring(queries, keys_values, out_weight):
    n = lax.axis_size("frames")
    frame, head = lax.axis_index("frames"), lax.axis_index("heads")
    z, y, x, core = frame >> 1, frame & 1, head >> 1, head & 1
    where = jnp.stack([ring_place(frame, n), z, y, x, core]).astype(jnp.int32)
    width, cols = out_weight.shape
    heads = width // HD
    f32, bf16 = jnp.float32, jnp.bfloat16
    hbm, vmem = pl.BlockSpec(memory_space=pltpu.HBM), pl.BlockSpec(memory_space=pltpu.VMEM)
    streams = pl.pallas_call(
        streams_kernel,
        out_shape=[jax.ShapeDtypeStruct((ROWS + ROWS // 2, width), bf16)] * 2,
        in_specs=[hbm] * 2,
        out_specs=[vmem] * 2,
        scratch_shapes=[pltpu.SemaphoreType.DMA((4,))],
    )(queries, keys_values)
    first, second = gather_ring(streams, n)
    far = n // 2
    state = call(
        functools.partial(near_kernel, heads, n),
        where,
        [blocks[d] for blocks in (first, second) for d in range(n) if d != far],
        [((n, ROWS, width), bf16)] + [((heads, n, ROWS, HD), f32)] * 3,
        4 * (n - 1) ** 2 * ROWS**2 * width,
    )
    given, far_rows = call(
        functools.partial(given_kernel, heads, n),
        where,
        [*first, *second, *state, out_weight],
        [((n // 2 * ROWS, cols), bf16), ((ROWS, width), bf16)],
        n * ROWS * width * cols,
    )
    from_core = lax.ppermute(given, "heads", [(h, h ^ 1) for h in range(4)])
    (kept,) = call(
        functools.partial(kept_kernel, heads, n),
        where,
        [*state, first[far], second[far], far_rows, out_weight],
        [((n // 2 * ROWS, cols), f32)],
        n * ROWS * width * cols,
    )
    arrived = []
    for slot in range(n // 2):
        rows = slice(slot * ROWS, (slot + 1) * ROWS)
        pairs = []
        for f in range(n):
            for h in range(4):
                to = PATTERNS[slot ^ (2 * (f & 1) + (h >> 1))][f >> 1]
                pairs.append((4 * f + h, 4 * (2 * to + (h & 1)) + (f >> 1)))
        total = (kept[rows] + from_core[rows].astype(f32)).astype(bf16)
        arrived.append(lax.ppermute(total, ("frames", "heads"), pairs).astype(f32))
    low, high = (arrived[0] + arrived[1]).astype(bf16), (arrived[2] + arrived[3]).astype(bf16)
    patterns = [[p[source] for p in PATTERNS].index(to) for source in range(4) for to in range(4)]
    straight = look_up(patterns, 4 * head + z) & 2 == 0
    return jnp.concatenate([jnp.where(straight, low, high), jnp.where(straight, high, low)], axis=1)


def solution(mesh):
    in_specs = (P("frames", "heads"), P(None, "frames", "heads"), P("heads", "frames"))
    out_specs = P("frames", "heads")
    n, heads = mesh.shape["frames"], mesh.shape["heads"]
    total_frames = n * FR_DEV
    reach = min(reach_cap, (total_frames - 1) // 2)
    every = total_frames == 2 * reach + 2 and heads == 4 and n == 2 * heads
    return jax.shard_map(
        on_device_ring if every else on_device_band,
        mesh=mesh,
        in_specs=in_specs,
        out_specs=out_specs,
        check_vma=False,
    )
```

```python
import functools
import math

import jax
import jax.numpy as jnp
from jax import lax
from jax.experimental import pallas as pl
from jax.experimental.pallas import tpu as pltpu
from jax.sharding import PartitionSpec as P

HD = 128
TPF = 32
FR_DEV = 3
ROWS = FR_DEV * TPF
SCALE = HD ** (-0.5) * math.log2(math.e)


reach_cap = 32


def from_behind(x, axis, by):
    devices = lax.axis_size(axis)
    return lax.ppermute(x, axis, [(i, (i + by) % devices) for i in range(devices)])


def on_device_band(queries, keys_values, out_weight):
    total_frames = lax.axis_size("frames") * FR_DEV
    reach = min(reach_cap, (total_frames - 1) // 2)
    steps = (reach + FR_DEV - 1) // FR_DEV
    width = keys_values.shape[2]
    span = FR_DEV + 2 * reach
    stacked = keys_values.reshape(2, FR_DEV, TPF, width)
    pieces = []
    for offset in range(-steps, steps + 1):
        if offset == 0:
            pieces.append(stacked)
        else:
            pieces.append(from_behind(stacked, "frames", -offset))
    window = jnp.concatenate(pieces, axis=1)
    lower_frame = steps * FR_DEV - reach
    extended = window[:, lower_frame : lower_frame + span]
    keys_ext = extended[0].reshape(span * TPF, width)
    values_ext = extended[1].reshape(span * TPF, width)
    row_frame = jnp.arange(FR_DEV * TPF, dtype=jnp.int32) // TPF
    col_frame = jnp.arange(span * TPF, dtype=jnp.int32) // TPF
    allowed = (col_frame[None, :] >= row_frame[:, None]) & (
        col_frame[None, :] <= row_frame[:, None] + 2 * reach
    )
    results = []
    for head in range(width // HD):
        lower = head * HD
        query_cols = queries[:, lower : lower + HD]
        key_cols = keys_ext[:, lower : lower + HD]
        scores = lax.dot_general(
            query_cols, key_cols, (((1,), (1,)), ((), ())), preferred_element_type=jnp.float32
        )
        scores = scores * HD ** (-0.5)
        top = jnp.max(jnp.where(allowed, scores, -1e30), axis=1, keepdims=True)
        weights = jnp.where(allowed, jnp.exp(scores - top), 0.0)
        probs = (weights / jnp.sum(weights, axis=1, keepdims=True)).astype(jnp.bfloat16)
        results.append(
            jnp.dot(
                probs, values_ext[:, lower : lower + HD], preferred_element_type=jnp.float32
            ).astype(jnp.bfloat16)
        )
    attended = jnp.concatenate(results, axis=1)
    partial_rows = jnp.dot(
        attended,
        lax.all_gather(out_weight, "frames", axis=1, tiled=True),
        preferred_element_type=jnp.float32,
    )
    return lax.psum_scatter(
        partial_rows.astype(jnp.bfloat16), "heads", scatter_dimension=1, tiled=True
    )


def ring_order(n):
    return list(range(0, n, 2)) + list(range(n - 1, 0, -2))


def ring_place(f, n):
    return (f >> 1) + (f & 1) * (n - 1 - (f >> 1) * 2)


def hop(x, n, by):
    order = ring_order(n)
    return lax.ppermute(x, "frames", [(order[i], order[(i + by) % n]) for i in range(n)])


def gather_ring(streams, n):
    found = [[block] + [None] * (n - 1) for block in streams]
    for step in range(1, n // 2 + 1):
        for j, blocks in enumerate(found):
            for by in (1, -1):
                if step < n // 2 or (j % 2 == 0) == (by == 1):
                    blocks[by * step % n] = hop(blocks[by * (step - 1) % n], n, by)
    return found


def left_out(place, block, n):
    return FR_DEV * ((place - ((place - block) & (n - 1) ^ 2)) & (n - 1))


def frame_marks(place, blocks, n):
    lane = lax.broadcasted_iota(jnp.int32, (TPF, HD), 1)
    marks = []
    for block in blocks:
        frame = left_out(place, block, n)
        for g in range(FR_DEV):
            marks.append((lane == frame + g) | (lane >= n * FR_DEV))
    return jnp.concatenate([jnp.where(mark, 1.0, 0.0) for mark in marks], axis=0).astype(jnp.bfloat16)


def key_marks(blocks, padding, n):
    lane = lax.broadcasted_iota(jnp.int32, (TPF, HD), 1)
    frames = [FR_DEV * block + g for block in blocks for g in range(FR_DEV)] + [n * FR_DEV] * (padding // TPF)
    return jnp.concatenate([jnp.where(lane == frame, -1e30, 0.0) for frame in frames], axis=0).astype(jnp.bfloat16)


def rows_of(refs, cols, padding=0):
    pieces = [ref[:, cols] for ref in refs]
    if padding:
        pieces.append(jnp.zeros((padding, HD), jnp.bfloat16))
    return jnp.concatenate(pieces, axis=0)


def scores_of(queries, keys):
    return lax.dot_general(queries, keys, (((1,), (1,)), ((), ())), preferred_element_type=jnp.float32)


def soften(scores, floor=None):
    weights, tops = [], []
    for r in range(0, scores.shape[0], TPF):
        parts = [scores[r : r + TPF, c : c + HD] for c in range(0, scores.shape[1], HD)]
        top = jnp.max(functools.reduce(jnp.maximum, parts), axis=1, keepdims=True)
        top = jnp.broadcast_to(top, (TPF, HD))
        if floor is not None:
            top = jnp.maximum(top, floor[r : r + TPF])
        weights.append(jnp.concatenate([jnp.exp2((p - top) * SCALE).astype(jnp.bfloat16) for p in parts], axis=1))
        tops.append(top)
    return jnp.concatenate(weights, axis=0), jnp.concatenate(tops, axis=0)


def mix(weights, values):
    ones = jnp.ones(values.shape, values.dtype)
    mixed = jnp.dot(weights, jnp.concatenate([values, ones], axis=1), preferred_element_type=jnp.float32)
    return mixed[:, :HD], mixed[:, HD:]


PATTERNS = ((2, 1, 2, 1), (0, 3, 0, 3), (3, 0, 1, 2), (1, 2, 3, 0))


def look_up(table, index):
    code = sum(entry << (2 * i) for i, entry in enumerate(table))
    return (jnp.int32(code - (code >> 31 << 32)) >> (2 * index)) & 3


def slot_blocks(at_ref, flip_core, n):
    place, z, y, x, core = (at_ref[i] for i in range(5))
    blocks = []
    for slot in range(n // 2):
        to = look_up(sum(PATTERNS, ()), 4 * (slot ^ (2 * y + x)) + z)
        owner = to + (core ^ flip_core) * (n - 1 - 2 * to)
        blocks.append((place - owner) & (n - 1))
    return blocks


def split_kernel(kv_ref, keys_ref, values_ref):
    keys_ref[...] = kv_ref[0]
    values_ref[...] = kv_ref[1]


def rows_kernel(n, *refs):
    for d in range(n):
        refs[n][d] = refs[d][...]


def near_kernel(heads, n, at_ref, rows_ref, *refs):
    near = [d for d in range(n) if d != n // 2]
    key_refs, value_refs, (mixed_ref, sum_ref, top_ref) = refs[: n - 1], refs[n - 1 : -3], refs[-3:]
    marks = frame_marks(at_ref[0], range(n), n)
    keys_marks = key_marks(near, ROWS, n)
    for head in range(heads):
        cols = slice(head * HD, (head + 1) * HD)
        queries = jnp.concatenate([rows_ref[:, :, cols].reshape(n * ROWS, HD), marks], axis=1)
        keys = jnp.concatenate([rows_of(key_refs, cols, ROWS), keys_marks], axis=1)
        weights, top = soften(scores_of(queries, keys))
        mixed, total = mix(weights, rows_of(value_refs, cols, ROWS))
        for d in range(n):
            rows = slice(d * ROWS, (d + 1) * ROWS)
            mixed_ref[head, d], sum_ref[head, d], top_ref[head, d] = mixed[rows], total[rows], top[rows]


def finish_kernel(heads, n, flip_core, at_ref, rows_ref, mixed_ref, sum_ref, top_ref, keys_ref, values_ref, w_ref, out_ref):
    blocks = slot_blocks(at_ref, flip_core, n)
    marks = frame_marks(at_ref[0], blocks, n)
    keys_marks = key_marks([n // 2], TPF, n)
    attended = []

    def of(ref, head):
        return jnp.concatenate([ref[head, block] for block in blocks], axis=0)

    for head in range(heads):
        cols = slice(head * HD, (head + 1) * HD)
        queries = jnp.concatenate([rows_ref[block, :, cols] for block in blocks], axis=0)
        keys = jnp.concatenate([rows_of([keys_ref], cols, TPF), keys_marks], axis=1)
        before = of(top_ref, head)
        weights, top = soften(scores_of(jnp.concatenate([queries, marks], axis=1), keys), before)
        mixed, total = mix(weights, rows_of([values_ref], cols, TPF))
        kept = jnp.exp2((before - top) * SCALE)
        mixed, total = mixed + of(mixed_ref, head) * kept, total + of(sum_ref, head) * kept
        attended.append((mixed / total).astype(jnp.bfloat16))
    rows = jnp.concatenate(attended, axis=1)
    out_ref[...] = jnp.dot(rows, w_ref[...], preferred_element_type=jnp.float32).astype(out_ref.dtype)


def call(kernel, scalars, operands, outs, flops):
    vmem = pl.BlockSpec(memory_space=pltpu.VMEM)
    return pl.pallas_call(
        kernel,
        out_shape=[jax.ShapeDtypeStruct(shape, dtype) for shape, dtype in outs],
        in_specs=[pl.BlockSpec(memory_space=pltpu.SMEM)] * len(scalars) + [vmem] * len(operands),
        out_specs=[vmem] * len(outs),
        compiler_params=pltpu.CompilerParams(vmem_limit_bytes=20 * 1024 * 1024),
        cost_estimate=pl.CostEstimate(flops=flops, bytes_accessed=0, transcendentals=0),
    )(*scalars, *operands)


def on_device_ring(queries, keys_values, out_weight):
    n = lax.axis_size("frames")
    frame, head = lax.axis_index("frames"), lax.axis_index("heads")
    z, y, x, core = frame >> 1, frame & 1, head >> 1, head & 1
    where = jnp.stack([ring_place(frame, n), z, y, x, core]).astype(jnp.int32)
    width, cols = out_weight.shape
    heads = width // HD
    f32, bf16 = jnp.float32, jnp.bfloat16
    block = (queries.shape, bf16)
    own = call(split_kernel, (), [keys_values], [block, block], 0)
    queries, keys, values = gather_ring([queries, *own], n)
    (rows,) = call(functools.partial(rows_kernel, n), (), queries, [((n, ROWS, width), bf16)], 0)
    far = n // 2
    state = call(
        functools.partial(near_kernel, heads, n),
        (where,),
        [rows, *(blocks[d] for blocks in (keys, values) for d in range(n) if d != far)],
        [((heads, n, ROWS, HD), f32)] * 3,
        4 * n * (n - 1) * ROWS**2 * width,
    )

    def finish(flip_core, dtype):
        (sums,) = call(
            functools.partial(finish_kernel, heads, n, flip_core),
            (where,),
            [rows, *state, keys[far], values[far], out_weight],
            [((n // 2 * ROWS, cols), dtype)],
            n * ROWS * width * cols,
        )
        return sums

    from_core = lax.ppermute(finish(1, bf16), "heads", [(h, h ^ 1) for h in range(4)])
    kept = finish(0, f32)
    arrived = []
    for slot in range(n // 2):
        rows = slice(slot * ROWS, (slot + 1) * ROWS)
        pairs = []
        for f in range(n):
            for h in range(4):
                to = PATTERNS[slot ^ (2 * (f & 1) + (h >> 1))][f >> 1]
                pairs.append((4 * f + h, 4 * (2 * to + (h & 1)) + (f >> 1)))
        total = (kept[rows] + from_core[rows].astype(f32)).astype(bf16)
        arrived.append(lax.ppermute(total, ("frames", "heads"), pairs).astype(f32))
    low, high = (arrived[0] + arrived[1]).astype(bf16), (arrived[2] + arrived[3]).astype(bf16)
    patterns = [[p[source] for p in PATTERNS].index(to) for source in range(4) for to in range(4)]
    straight = look_up(patterns, 4 * head + z) & 2 == 0
    return jnp.concatenate([jnp.where(straight, low, high), jnp.where(straight, high, low)], axis=1)


def solution(mesh):
    in_specs = (P("frames", "heads"), P(None, "frames", "heads"), P("heads", "frames"))
    out_specs = P("frames", "heads")
    n, heads = mesh.shape["frames"], mesh.shape["heads"]
    total_frames = n * FR_DEV
    reach = min(reach_cap, (total_frames - 1) // 2)
    every = total_frames == 2 * reach + 2 and heads == 4 and n == 2 * heads
    return jax.shard_map(
        on_device_ring if every else on_device_band,
        mesh=mesh,
        in_specs=in_specs,
        out_specs=out_specs,
        check_vma=False,
    )
```

```python
import functools
import math

import jax
import jax.numpy as jnp
from jax import lax
from jax.experimental import pallas as pl
from jax.experimental.pallas import tpu as pltpu
from jax.sharding import PartitionSpec as P

HD = 128
TPF = 32
FR_DEV = 3
ROWS = FR_DEV * TPF
SCALE = HD ** (-0.5) * math.log2(math.e)


reach_cap = 32


def from_behind(x, axis, by):
    devices = lax.axis_size(axis)
    return lax.ppermute(x, axis, [(i, (i + by) % devices) for i in range(devices)])


def on_device_band(queries, keys_values, out_weight):
    total_frames = lax.axis_size("frames") * FR_DEV
    reach = min(reach_cap, (total_frames - 1) // 2)
    steps = (reach + FR_DEV - 1) // FR_DEV
    width = keys_values.shape[2]
    span = FR_DEV + 2 * reach
    stacked = keys_values.reshape(2, FR_DEV, TPF, width)
    pieces = []
    for offset in range(-steps, steps + 1):
        if offset == 0:
            pieces.append(stacked)
        else:
            pieces.append(from_behind(stacked, "frames", -offset))
    window = jnp.concatenate(pieces, axis=1)
    lower_frame = steps * FR_DEV - reach
    extended = window[:, lower_frame : lower_frame + span]
    keys_ext = extended[0].reshape(span * TPF, width)
    values_ext = extended[1].reshape(span * TPF, width)
    row_frame = jnp.arange(FR_DEV * TPF, dtype=jnp.int32) // TPF
    col_frame = jnp.arange(span * TPF, dtype=jnp.int32) // TPF
    allowed = (col_frame[None, :] >= row_frame[:, None]) & (
        col_frame[None, :] <= row_frame[:, None] + 2 * reach
    )
    results = []
    for head in range(width // HD):
        lower = head * HD
        query_cols = queries[:, lower : lower + HD]
        key_cols = keys_ext[:, lower : lower + HD]
        scores = lax.dot_general(
            query_cols, key_cols, (((1,), (1,)), ((), ())), preferred_element_type=jnp.float32
        )
        scores = scores * HD ** (-0.5)
        top = jnp.max(jnp.where(allowed, scores, -1e30), axis=1, keepdims=True)
        weights = jnp.where(allowed, jnp.exp(scores - top), 0.0)
        probs = (weights / jnp.sum(weights, axis=1, keepdims=True)).astype(jnp.bfloat16)
        results.append(
            jnp.dot(
                probs, values_ext[:, lower : lower + HD], preferred_element_type=jnp.float32
            ).astype(jnp.bfloat16)
        )
    attended = jnp.concatenate(results, axis=1)
    partial_rows = jnp.dot(
        attended,
        lax.all_gather(out_weight, "frames", axis=1, tiled=True),
        preferred_element_type=jnp.float32,
    )
    return lax.psum_scatter(
        partial_rows.astype(jnp.bfloat16), "heads", scatter_dimension=1, tiled=True
    )


def ring_order(n):
    return list(range(0, n, 2)) + list(range(n - 1, 0, -2))


def ring_place(f, n):
    return (f >> 1) + (f & 1) * (n - 1 - (f >> 1) * 2)


def hop(x, n, by):
    order = ring_order(n)
    pairs = []
    for i in range(n):
        for h in range(4):
            pairs.append((4 * order[i] + h, 4 * order[(i + by * (1 - 2 * (h & 1))) % n] + h))
    return lax.ppermute(x, ("frames", "heads"), pairs)


def gather_ring(streams, n):
    found = [[block] + [None] * (n - 1) for block in streams]
    for step in range(1, n // 2 + 1):
        for j, blocks in enumerate(found):
            for by in (1, -1):
                if step < n // 2 or (j % 2 == 0) == (by == 1):
                    blocks[by * step % n] = hop(blocks[by * (step - 1) % n], n, by)
    return found


def ring_distance(at_ref, owner, n):
    place, core = at_ref[0], at_ref[4]
    return (place - owner) * (1 - 2 * core) & (n - 1)


def frame_marks(at_ref, blocks, n):
    place, core = at_ref[0], at_ref[4]
    lane = lax.broadcasted_iota(jnp.int32, (TPF, HD), 1)
    marks = []
    for block in blocks:
        owner = (place - block * (1 - 2 * core)) & (n - 1)
        frame = FR_DEV * ring_distance(at_ref, owner ^ 2, n)
        for g in range(FR_DEV):
            marks.append((lane == frame + g) | (lane >= n * FR_DEV))
    return jnp.concatenate([jnp.where(mark, 1.0, 0.0) for mark in marks], axis=0).astype(jnp.bfloat16)


def key_marks(blocks, padding, n):
    lane = lax.broadcasted_iota(jnp.int32, (TPF, HD), 1)
    frames = [FR_DEV * block + g for block in blocks for g in range(FR_DEV)] + [n * FR_DEV] * (padding // TPF)
    return jnp.concatenate([jnp.where(lane == frame, -1e30, 0.0) for frame in frames], axis=0).astype(jnp.bfloat16)


def rows_of(refs, cols, padding=0):
    pieces = [ref[:, cols] for ref in refs]
    if padding:
        pieces.append(jnp.zeros((padding, HD), jnp.bfloat16))
    return jnp.concatenate(pieces, axis=0)


def scores_of(queries, keys):
    return lax.dot_general(queries, keys, (((1,), (1,)), ((), ())), preferred_element_type=jnp.float32)


def soften(scores, floor=None):
    weights, tops = [], []
    for r in range(0, scores.shape[0], TPF):
        parts = [scores[r : r + TPF, c : c + HD] for c in range(0, scores.shape[1], HD)]
        top = jnp.max(functools.reduce(jnp.maximum, parts), axis=1, keepdims=True)
        top = jnp.broadcast_to(top, (TPF, HD))
        if floor is not None:
            top = jnp.maximum(top, floor[r : r + TPF])
        weights.append(jnp.concatenate([jnp.exp2((p - top) * SCALE).astype(jnp.bfloat16) for p in parts], axis=1))
        tops.append(top)
    return jnp.concatenate(weights, axis=0), jnp.concatenate(tops, axis=0)


def mix(weights, values):
    ones = jnp.ones(values.shape, values.dtype)
    mixed = jnp.dot(weights, jnp.concatenate([values, ones], axis=1), preferred_element_type=jnp.float32)
    return mixed[:, :HD], mixed[:, HD:]


PATTERNS = ((2, 1, 2, 1), (0, 3, 0, 3), (3, 0, 1, 2), (1, 2, 3, 0))


def look_up(table, index):
    code = sum(entry << (2 * i) for i, entry in enumerate(table))
    return (jnp.int32(code - (code >> 31 << 32)) >> (2 * index)) & 3


def slot_blocks(at_ref, flip_core, n):
    z, y, x, core = (at_ref[i] for i in range(1, 5))
    blocks = []
    for slot in range(n // 2):
        to = look_up(sum(PATTERNS, ()), 4 * (slot ^ (2 * y + x)) + z)
        owner = to + (core ^ flip_core) * (n - 1 - 2 * to)
        blocks.append(ring_distance(at_ref, owner, n))
    return blocks


def split_kernel(kv_ref, keys_ref, values_ref):
    keys_ref[...] = kv_ref[0]
    values_ref[...] = kv_ref[1]


def rows_kernel(n, *refs):
    for d in range(n):
        refs[n][d] = refs[d][...]


def near_kernel(heads, n, at_ref, rows_ref, *refs):
    near = [d for d in range(n) if d != n // 2]
    key_refs, value_refs, (mixed_ref, sum_ref, top_ref) = refs[: n - 1], refs[n - 1 : -3], refs[-3:]
    marks = frame_marks(at_ref, range(n), n)
    keys_marks = key_marks(near, ROWS, n)
    for head in range(heads):
        cols = slice(head * HD, (head + 1) * HD)
        queries = jnp.concatenate([rows_ref[:, :, cols].reshape(n * ROWS, HD), marks], axis=1)
        keys = jnp.concatenate([rows_of(key_refs, cols, ROWS), keys_marks], axis=1)
        weights, top = soften(scores_of(queries, keys))
        mixed, total = mix(weights, rows_of(value_refs, cols, ROWS))
        for d in range(n):
            rows = slice(d * ROWS, (d + 1) * ROWS)
            mixed_ref[head, d], sum_ref[head, d], top_ref[head, d] = mixed[rows], total[rows], top[rows]


def finish_kernel(heads, n, flip_core, at_ref, rows_ref, mixed_ref, sum_ref, top_ref, keys_ref, values_ref, w_ref, out_ref):
    blocks = slot_blocks(at_ref, flip_core, n)
    marks = frame_marks(at_ref, blocks, n)
    keys_marks = key_marks([n // 2], TPF, n)
    attended = []

    def of(ref, head):
        return jnp.concatenate([ref[head, block] for block in blocks], axis=0)

    for head in range(heads):
        cols = slice(head * HD, (head + 1) * HD)
        queries = jnp.concatenate([rows_ref[block, :, cols] for block in blocks], axis=0)
        keys = jnp.concatenate([rows_of([keys_ref], cols, TPF), keys_marks], axis=1)
        before = of(top_ref, head)
        weights, top = soften(scores_of(jnp.concatenate([queries, marks], axis=1), keys), before)
        mixed, total = mix(weights, rows_of([values_ref], cols, TPF))
        kept = jnp.exp2((before - top) * SCALE)
        mixed, total = mixed + of(mixed_ref, head) * kept, total + of(sum_ref, head) * kept
        attended.append((mixed / total).astype(jnp.bfloat16))
    rows = jnp.concatenate(attended, axis=1)
    out_ref[...] = jnp.dot(rows, w_ref[...], preferred_element_type=jnp.float32).astype(out_ref.dtype)


def call(kernel, scalars, operands, outs, flops):
    vmem = pl.BlockSpec(memory_space=pltpu.VMEM)
    return pl.pallas_call(
        kernel,
        out_shape=[jax.ShapeDtypeStruct(shape, dtype) for shape, dtype in outs],
        in_specs=[pl.BlockSpec(memory_space=pltpu.SMEM)] * len(scalars) + [vmem] * len(operands),
        out_specs=[vmem] * len(outs),
        compiler_params=pltpu.CompilerParams(vmem_limit_bytes=20 * 1024 * 1024),
        cost_estimate=pl.CostEstimate(flops=flops, bytes_accessed=0, transcendentals=0),
    )(*scalars, *operands)


def on_device_ring(queries, keys_values, out_weight):
    n = lax.axis_size("frames")
    frame, head = lax.axis_index("frames"), lax.axis_index("heads")
    z, y, x, core = frame >> 1, frame & 1, head >> 1, head & 1
    where = jnp.stack([ring_place(frame, n), z, y, x, core]).astype(jnp.int32)
    width, cols = out_weight.shape
    heads = width // HD
    f32, bf16 = jnp.float32, jnp.bfloat16
    block = (queries.shape, bf16)
    own = call(split_kernel, (), [keys_values], [block, block], 0)
    queries, keys, values = gather_ring([queries, *own], n)
    (rows,) = call(functools.partial(rows_kernel, n), (), queries, [((n, ROWS, width), bf16)], 0)
    far = n // 2
    state = call(
        functools.partial(near_kernel, heads, n),
        (where,),
        [rows, *(blocks[d] for blocks in (keys, values) for d in range(n) if d != far)],
        [((heads, n, ROWS, HD), f32)] * 3,
        4 * n * (n - 1) * ROWS**2 * width,
    )

    def finish(flip_core, dtype):
        (sums,) = call(
            functools.partial(finish_kernel, heads, n, flip_core),
            (where,),
            [rows, *state, keys[far], values[far], out_weight],
            [((n // 2 * ROWS, cols), dtype)],
            n * ROWS * width * cols,
        )
        return sums

    from_core = lax.ppermute(finish(1, bf16), "heads", [(h, h ^ 1) for h in range(4)])
    kept = finish(0, f32)
    arrived = []
    for slot in range(n // 2):
        rows = slice(slot * ROWS, (slot + 1) * ROWS)
        pairs = []
        for f in range(n):
            for h in range(4):
                to = PATTERNS[slot ^ (2 * (f & 1) + (h >> 1))][f >> 1]
                pairs.append((4 * f + h, 4 * (2 * to + (h & 1)) + (f >> 1)))
        total = (kept[rows] + from_core[rows].astype(f32)).astype(bf16)
        arrived.append(lax.ppermute(total, ("frames", "heads"), pairs).astype(f32))
    low, high = (arrived[0] + arrived[1]).astype(bf16), (arrived[2] + arrived[3]).astype(bf16)
    patterns = [[p[source] for p in PATTERNS].index(to) for source in range(4) for to in range(4)]
    straight = look_up(patterns, 4 * head + z) & 2 == 0
    return jnp.concatenate([jnp.where(straight, low, high), jnp.where(straight, high, low)], axis=1)


def solution(mesh):
    in_specs = (P("frames", "heads"), P(None, "frames", "heads"), P("heads", "frames"))
    out_specs = P("frames", "heads")
    n, heads = mesh.shape["frames"], mesh.shape["heads"]
    total_frames = n * FR_DEV
    reach = min(reach_cap, (total_frames - 1) // 2)
    every = total_frames == 2 * reach + 2 and heads == 4 and n == 2 * heads
    return jax.shard_map(
        on_device_ring if every else on_device_band,
        mesh=mesh,
        in_specs=in_specs,
        out_specs=out_specs,
        check_vma=False,
    )
```

```python
import functools
import math

import jax
import jax.numpy as jnp
from jax import lax
from jax.experimental import pallas as pl
from jax.experimental.pallas import tpu as pltpu
from jax.sharding import PartitionSpec as P

HD = 128
TPF = 32
FR_DEV = 3
ROWS = FR_DEV * TPF
SCALE = HD ** (-0.5) * math.log2(math.e)


reach_cap = 32


def from_behind(x, axis, by):
    devices = lax.axis_size(axis)
    return lax.ppermute(x, axis, [(i, (i + by) % devices) for i in range(devices)])


def on_device_band(queries, keys_values, out_weight):
    total_frames = lax.axis_size("frames") * FR_DEV
    reach = min(reach_cap, (total_frames - 1) // 2)
    steps = (reach + FR_DEV - 1) // FR_DEV
    width = keys_values.shape[2]
    span = FR_DEV + 2 * reach
    stacked = keys_values.reshape(2, FR_DEV, TPF, width)
    pieces = []
    for offset in range(-steps, steps + 1):
        if offset == 0:
            pieces.append(stacked)
        else:
            pieces.append(from_behind(stacked, "frames", -offset))
    window = jnp.concatenate(pieces, axis=1)
    lower_frame = steps * FR_DEV - reach
    extended = window[:, lower_frame : lower_frame + span]
    keys_ext = extended[0].reshape(span * TPF, width)
    values_ext = extended[1].reshape(span * TPF, width)
    row_frame = jnp.arange(FR_DEV * TPF, dtype=jnp.int32) // TPF
    col_frame = jnp.arange(span * TPF, dtype=jnp.int32) // TPF
    allowed = (col_frame[None, :] >= row_frame[:, None]) & (
        col_frame[None, :] <= row_frame[:, None] + 2 * reach
    )
    results = []
    for head in range(width // HD):
        lower = head * HD
        query_cols = queries[:, lower : lower + HD]
        key_cols = keys_ext[:, lower : lower + HD]
        scores = lax.dot_general(
            query_cols, key_cols, (((1,), (1,)), ((), ())), preferred_element_type=jnp.float32
        )
        scores = scores * HD ** (-0.5)
        top = jnp.max(jnp.where(allowed, scores, -1e30), axis=1, keepdims=True)
        weights = jnp.where(allowed, jnp.exp(scores - top), 0.0)
        probs = (weights / jnp.sum(weights, axis=1, keepdims=True)).astype(jnp.bfloat16)
        results.append(
            jnp.dot(
                probs, values_ext[:, lower : lower + HD], preferred_element_type=jnp.float32
            ).astype(jnp.bfloat16)
        )
    attended = jnp.concatenate(results, axis=1)
    partial_rows = jnp.dot(
        attended,
        lax.all_gather(out_weight, "frames", axis=1, tiled=True),
        preferred_element_type=jnp.float32,
    )
    return lax.psum_scatter(
        partial_rows.astype(jnp.bfloat16), "heads", scatter_dimension=1, tiled=True
    )


def ring_order(n):
    return list(range(0, n, 2)) + list(range(n - 1, 0, -2))


def ring_place(f, n):
    return (f >> 1) + (f & 1) * (n - 1 - (f >> 1) * 2)


def hop(x, n, by):
    order = ring_order(n)
    pairs = []
    for i in range(n):
        for h in range(4):
            pairs.append((4 * order[i] + h, 4 * order[(i + by * (1 - 2 * (h & 1))) % n] + h))
    return lax.ppermute(x, ("frames", "heads"), pairs)


def gather_ring(streams, n):
    found = [[block] + [None] * (n - 1) for block in streams]
    for step in range(1, n // 2 + 1):
        for j, blocks in enumerate(found):
            for by in (1, -1):
                if step < n // 2 or (j % 2 == 0) == (by == 1):
                    blocks[by * step % n] = hop(blocks[by * (step - 1) % n], n, by)
    return found


def ring_distance(at_ref, owner, n):
    place, core = at_ref[0], at_ref[4]
    return (place - owner) * (1 - 2 * core) & (n - 1)


def frame_marks(at_ref, blocks, n):
    place, core = at_ref[0], at_ref[4]
    lane = lax.broadcasted_iota(jnp.int32, (TPF, HD), 1)
    marks = []
    for block in blocks:
        owner = (place - block * (1 - 2 * core)) & (n - 1)
        frame = FR_DEV * ring_distance(at_ref, owner ^ 2, n)
        for g in range(FR_DEV):
            marks.append((lane == frame + g) | (lane >= n * FR_DEV))
    return jnp.concatenate([jnp.where(mark, 1.0, 0.0) for mark in marks], axis=0).astype(jnp.bfloat16)


def key_marks(blocks, padding, n):
    lane = lax.broadcasted_iota(jnp.int32, (TPF, HD), 1)
    frames = [FR_DEV * block + g for block in blocks for g in range(FR_DEV)] + [n * FR_DEV] * (padding // TPF)
    return jnp.concatenate([jnp.where(lane == frame, -1e30, 0.0) for frame in frames], axis=0).astype(jnp.bfloat16)


def rows_of(refs, cols, padding=0):
    pieces = [ref[:, cols] for ref in refs]
    if padding:
        pieces.append(jnp.zeros((padding, HD), jnp.bfloat16))
    return jnp.concatenate(pieces, axis=0)


def scores_of(queries, keys):
    return lax.dot_general(queries, keys, (((1,), (1,)), ((), ())), preferred_element_type=jnp.float32)


def soften(scores, floor=None):
    weights, tops = [], []
    for r in range(0, scores.shape[0], TPF):
        parts = [scores[r : r + TPF, c : c + HD] for c in range(0, scores.shape[1], HD)]
        top = jnp.max(functools.reduce(jnp.maximum, parts), axis=1, keepdims=True)
        top = jnp.broadcast_to(top, (TPF, HD))
        if floor is not None:
            top = jnp.maximum(top, floor[r : r + TPF])
        weights.append(jnp.concatenate([jnp.exp2((p - top) * SCALE).astype(jnp.bfloat16) for p in parts], axis=1))
        tops.append(top)
    return jnp.concatenate(weights, axis=0), jnp.concatenate(tops, axis=0)


def mix(weights, values):
    ones = jnp.ones(values.shape, values.dtype)
    mixed = jnp.dot(weights, jnp.concatenate([values, ones], axis=1), preferred_element_type=jnp.float32)
    return mixed[:, :HD], mixed[:, HD:]


PATTERNS = ((2, 1, 2, 1), (0, 3, 0, 3), (3, 0, 1, 2), (1, 2, 3, 0))


def look_up(table, index):
    code = sum(entry << (2 * i) for i, entry in enumerate(table))
    return (jnp.int32(code - (code >> 31 << 32)) >> (2 * index)) & 3


def slot_blocks(at_ref, flip_x, flip_core, n):
    z, y, x, core = (at_ref[i] for i in range(1, 5))
    blocks = []
    for slot in range(2):
        to = look_up(sum(PATTERNS, ()), 4 * ((slot ^ y) + 2 * (x ^ flip_x)) + z)
        owner = to + (core ^ flip_core) * (n - 1 - 2 * to)
        blocks.append(ring_distance(at_ref, owner, n))
    return blocks


def split_kernel(kv_ref, keys_ref, values_ref):
    keys_ref[...] = kv_ref[0]
    values_ref[...] = kv_ref[1]


def rows_kernel(n, *refs):
    for d in range(n):
        refs[n][d] = refs[d][...]


def near_kernel(heads, n, at_ref, rows_ref, *refs):
    near = [d for d in range(n) if d != n // 2]
    key_refs, value_refs, (mixed_ref, sum_ref, top_ref) = refs[: n - 1], refs[n - 1 : -3], refs[-3:]
    marks = frame_marks(at_ref, range(n), n)
    keys_marks = key_marks(near, ROWS, n)
    for head in range(heads):
        cols = slice(head * HD, (head + 1) * HD)
        queries = jnp.concatenate([rows_ref[:, :, cols].reshape(n * ROWS, HD), marks], axis=1)
        keys = jnp.concatenate([rows_of(key_refs, cols, ROWS), keys_marks], axis=1)
        weights, top = soften(scores_of(queries, keys))
        mixed, total = mix(weights, rows_of(value_refs, cols, ROWS))
        for d in range(n):
            rows = slice(d * ROWS, (d + 1) * ROWS)
            mixed_ref[head, d], sum_ref[head, d], top_ref[head, d] = mixed[rows], total[rows], top[rows]


def finish_kernel(heads, n, flips, at_ref, rows_ref, mixed_ref, sum_ref, top_ref, keys_ref, values_ref, w_ref, *refs):
    blocks = [block for flip in flips for block in slot_blocks(at_ref, *flip, n)]
    marks = frame_marks(at_ref, blocks, n)
    keys_marks = key_marks([n // 2], TPF, n)
    attended = []

    def of(ref, head):
        return jnp.concatenate([ref[head, block] for block in blocks], axis=0)

    for head in range(heads):
        cols = slice(head * HD, (head + 1) * HD)
        queries = jnp.concatenate([rows_ref[block, :, cols] for block in blocks], axis=0)
        keys = jnp.concatenate([rows_of([keys_ref], cols, TPF), keys_marks], axis=1)
        before = of(top_ref, head)
        weights, top = soften(scores_of(jnp.concatenate([queries, marks], axis=1), keys), before)
        mixed, total = mix(weights, rows_of([values_ref], cols, TPF))
        kept = jnp.exp2((before - top) * SCALE)
        mixed, total = mixed + of(mixed_ref, head) * kept, total + of(sum_ref, head) * kept
        attended.append((mixed / total).astype(jnp.bfloat16))
    rows = jnp.concatenate(attended, axis=1)
    refs[-1][...] = jnp.dot(rows, w_ref[...], preferred_element_type=jnp.float32).astype(refs[-1].dtype)


def call(kernel, scalars, operands, outs, flops, after=()):
    vmem = pl.BlockSpec(memory_space=pltpu.VMEM)
    return pl.pallas_call(
        kernel,
        out_shape=[jax.ShapeDtypeStruct(shape, dtype) for shape, dtype in outs],
        in_specs=[pl.BlockSpec(memory_space=pltpu.SMEM)] * len(scalars)
        + [vmem] * len(operands)
        + [pl.BlockSpec(memory_space=pl.ANY)] * len(after),
        out_specs=[vmem] * len(outs),
        compiler_params=pltpu.CompilerParams(vmem_limit_bytes=20 * 1024 * 1024),
        cost_estimate=pl.CostEstimate(flops=flops, bytes_accessed=0, transcendentals=0),
    )(*scalars, *operands, *after)


def on_device_ring(queries, keys_values, out_weight):
    n = lax.axis_size("frames")
    frame, head = lax.axis_index("frames"), lax.axis_index("heads")
    z, y, x, core = frame >> 1, frame & 1, head >> 1, head & 1
    where = jnp.stack([ring_place(frame, n), z, y, x, core]).astype(jnp.int32)
    width, cols = out_weight.shape
    heads = width // HD
    f32, bf16 = jnp.float32, jnp.bfloat16
    block = (queries.shape, bf16)
    own = call(split_kernel, (), [keys_values], [block, block], 0)
    queries, keys, values = gather_ring([queries, *own], n)
    (rows,) = call(functools.partial(rows_kernel, n), (), queries, [((n, ROWS, width), bf16)], 0)
    far = n // 2
    state = call(
        functools.partial(near_kernel, heads, n),
        (where,),
        [rows, *(blocks[d] for blocks in (keys, values) for d in range(n) if d != far)],
        [((heads, n, ROWS, HD), f32)] * 3,
        4 * n * (n - 1) * ROWS**2 * width,
    )

    def finish(flips, dtype, after=()):
        (sums,) = call(
            functools.partial(finish_kernel, heads, n, flips),
            (where,),
            [rows, *state, keys[far], values[far], out_weight],
            [((len(flips) * 2 * ROWS, cols), dtype)],
            n * ROWS * width * cols,
            after,
        )
        return sums.reshape(len(flips), 2 * ROWS, cols)

    given = finish([(1, 1), (0, 1)], bf16)
    from_core = lax.ppermute(given, "heads", [(h, h ^ 1) for h in range(4)])
    given = (finish([(1, 0)], f32, (given,))[0] + from_core[0].astype(f32)).astype(bf16)
    from_x = lax.ppermute(given, "heads", [(h, h ^ 2) for h in range(4)])
    kept = finish([(0, 0)], f32, (given,))[0]
    arrived = []
    for slot in range(2):
        part = slice(slot * ROWS, (slot + 1) * ROWS)
        pairs = []
        for f in range(n):
            for h in range(4):
                to = PATTERNS[(slot ^ (f & 1)) + 2 * (h >> 1)][f >> 1]
                pairs.append((4 * f + h, 4 * (2 * to + (h & 1)) + (f >> 1)))
        total = kept[part] + from_core[1, part].astype(f32) + from_x[part].astype(f32)
        arrived.append(lax.ppermute(total.astype(bf16), ("frames", "heads"), pairs))
    patterns = [[p[source] for p in PATTERNS].index(to) for source in range(4) for to in range(4)]
    straight = look_up(patterns, 4 * head + z) & 1 == 0
    low, high = arrived
    return jnp.concatenate([jnp.where(straight, low, high), jnp.where(straight, high, low)], axis=1)


def solution(mesh):
    in_specs = (P("frames", "heads"), P(None, "frames", "heads"), P("heads", "frames"))
    out_specs = P("frames", "heads")
    n, heads = mesh.shape["frames"], mesh.shape["heads"]
    total_frames = n * FR_DEV
    reach = min(reach_cap, (total_frames - 1) // 2)
    every = total_frames == 2 * reach + 2 and heads == 4 and n == 2 * heads
    return jax.shard_map(
        on_device_ring if every else on_device_band,
        mesh=mesh,
        in_specs=in_specs,
        out_specs=out_specs,
        check_vma=False,
    )
```

```python
import functools
import math

import jax
import jax.numpy as jnp
from jax import lax
from jax.experimental import pallas as pl
from jax.experimental.pallas import tpu as pltpu
from jax.sharding import PartitionSpec as P

HD = 128
TPF = 32
FR_DEV = 3
ROWS = FR_DEV * TPF
SCALE = HD ** (-0.5) * math.log2(math.e)


reach_cap = 32


def from_behind(x, axis, by):
    devices = lax.axis_size(axis)
    return lax.ppermute(x, axis, [(i, (i + by) % devices) for i in range(devices)])


def on_device_band(queries, keys_values, out_weight):
    total_frames = lax.axis_size("frames") * FR_DEV
    reach = min(reach_cap, (total_frames - 1) // 2)
    steps = (reach + FR_DEV - 1) // FR_DEV
    width = keys_values.shape[2]
    span = FR_DEV + 2 * reach
    stacked = keys_values.reshape(2, FR_DEV, TPF, width)
    pieces = []
    for offset in range(-steps, steps + 1):
        if offset == 0:
            pieces.append(stacked)
        else:
            pieces.append(from_behind(stacked, "frames", -offset))
    window = jnp.concatenate(pieces, axis=1)
    lower_frame = steps * FR_DEV - reach
    extended = window[:, lower_frame : lower_frame + span]
    keys_ext = extended[0].reshape(span * TPF, width)
    values_ext = extended[1].reshape(span * TPF, width)
    row_frame = jnp.arange(FR_DEV * TPF, dtype=jnp.int32) // TPF
    col_frame = jnp.arange(span * TPF, dtype=jnp.int32) // TPF
    allowed = (col_frame[None, :] >= row_frame[:, None]) & (
        col_frame[None, :] <= row_frame[:, None] + 2 * reach
    )
    results = []
    for head in range(width // HD):
        lower = head * HD
        query_cols = queries[:, lower : lower + HD]
        key_cols = keys_ext[:, lower : lower + HD]
        scores = lax.dot_general(
            query_cols, key_cols, (((1,), (1,)), ((), ())), preferred_element_type=jnp.float32
        )
        scores = scores * HD ** (-0.5)
        top = jnp.max(jnp.where(allowed, scores, -1e30), axis=1, keepdims=True)
        weights = jnp.where(allowed, jnp.exp(scores - top), 0.0)
        probs = (weights / jnp.sum(weights, axis=1, keepdims=True)).astype(jnp.bfloat16)
        results.append(
            jnp.dot(
                probs, values_ext[:, lower : lower + HD], preferred_element_type=jnp.float32
            ).astype(jnp.bfloat16)
        )
    attended = jnp.concatenate(results, axis=1)
    partial_rows = jnp.dot(
        attended,
        lax.all_gather(out_weight, "frames", axis=1, tiled=True),
        preferred_element_type=jnp.float32,
    )
    return lax.psum_scatter(
        partial_rows.astype(jnp.bfloat16), "heads", scatter_dimension=1, tiled=True
    )


def ring_order(n):
    return list(range(0, n, 2)) + list(range(n - 1, 0, -2))


def ring_place(f, n):
    return (f >> 1) + (f & 1) * (n - 1 - (f >> 1) * 2)


def hop(x, n, by):
    order = ring_order(n)
    pairs = []
    for i in range(n):
        for h in range(4):
            pairs.append((4 * order[i] + h, 4 * order[(i + by * (1 - 2 * (h & 1))) % n] + h))
    return lax.ppermute(x, ("frames", "heads"), pairs)


def gather_ring(streams, n):
    found = [[block] + [None] * (n - 1) for block in streams]
    for step in range(1, n // 2 + 1):
        for j, blocks in enumerate(found):
            for by in (1, -1):
                if step < n // 2 or (j % 2 == 0) == (by == 1):
                    blocks[by * step % n] = hop(blocks[by * (step - 1) % n], n, by)
    return found


def ring_distance(at_ref, owner, n):
    place, core = at_ref[0], at_ref[4]
    return (place - owner) * (1 - 2 * core) & (n - 1)


def frame_marks(at_ref, blocks, n):
    place, core = at_ref[0], at_ref[4]
    lane = lax.broadcasted_iota(jnp.int32, (TPF, HD), 1)
    marks = []
    for block in blocks:
        owner = (place - block * (1 - 2 * core)) & (n - 1)
        frame = FR_DEV * ring_distance(at_ref, owner ^ 2, n)
        for g in range(FR_DEV):
            marks.append((lane == frame + g) | (lane >= n * FR_DEV))
    return jnp.concatenate([jnp.where(mark, 1.0, 0.0) for mark in marks], axis=0).astype(jnp.bfloat16)


def key_marks(blocks, padding, n):
    lane = lax.broadcasted_iota(jnp.int32, (TPF, HD), 1)
    frames = [FR_DEV * block + g for block in blocks for g in range(FR_DEV)] + [n * FR_DEV] * (padding // TPF)
    return jnp.concatenate([jnp.where(lane == frame, -1e30, 0.0) for frame in frames], axis=0).astype(jnp.bfloat16)


def rows_of(refs, cols, padding=0):
    pieces = [ref[:, cols] for ref in refs]
    if padding:
        pieces.append(jnp.zeros((padding, HD), jnp.bfloat16))
    return jnp.concatenate(pieces, axis=0)


def scores_of(queries, keys):
    return lax.dot_general(queries, keys, (((1,), (1,)), ((), ())), preferred_element_type=jnp.float32)


def soften(scores, floor=None):
    weights, tops = [], []
    for r in range(0, scores.shape[0], TPF):
        parts = [scores[r : r + TPF, c : c + HD] for c in range(0, scores.shape[1], HD)]
        top = jnp.max(functools.reduce(jnp.maximum, parts), axis=1, keepdims=True)
        top = jnp.broadcast_to(top, (TPF, HD))
        if floor is not None:
            top = jnp.maximum(top, floor[r : r + TPF])
        weights.append(jnp.concatenate([jnp.exp2((p - top) * SCALE).astype(jnp.bfloat16) for p in parts], axis=1))
        tops.append(top)
    return jnp.concatenate(weights, axis=0), jnp.concatenate(tops, axis=0)


def mix(weights, values):
    ones = jnp.ones(values.shape, values.dtype)
    mixed = jnp.dot(weights, jnp.concatenate([values, ones], axis=1), preferred_element_type=jnp.float32)
    return mixed[:, :HD], mixed[:, HD:]


PATTERNS = ((2, 1, 2, 1), (0, 3, 0, 3), (3, 0, 1, 2), (1, 2, 3, 0))


def look_up(table, index):
    code = sum(entry << (2 * i) for i, entry in enumerate(table))
    return (jnp.int32(code - (code >> 31 << 32)) >> (2 * index)) & 3


def slot_blocks(at_ref, flip_x, flip_core, n):
    z, y, x, core = (at_ref[i] for i in range(1, 5))
    blocks = []
    for slot in range(2):
        to = look_up(sum(PATTERNS, ()), 4 * ((slot ^ y) + 2 * (x ^ flip_x)) + z)
        owner = to + (core ^ flip_core) * (n - 1 - 2 * to)
        blocks.append(ring_distance(at_ref, owner, n))
    return blocks


def split_kernel(kv_ref, keys_ref, values_ref):
    keys_ref[...] = kv_ref[0]
    values_ref[...] = kv_ref[1]


def rows_kernel(n, *refs):
    for d in range(n):
        refs[n][d] = refs[d][...]


def near_kernel(heads, n, at_ref, rows_ref, *refs):
    near = [d for d in range(n) if d != n // 2]
    key_refs, value_refs, (mixed_ref, sum_ref, top_ref) = refs[: n - 1], refs[n - 1 : -3], refs[-3:]
    marks = frame_marks(at_ref, range(n), n)
    keys_marks = key_marks(near, ROWS, n)
    for head in range(heads):
        cols = slice(head * HD, (head + 1) * HD)
        queries = jnp.concatenate([rows_ref[:, :, cols].reshape(n * ROWS, HD), marks], axis=1)
        keys = jnp.concatenate([rows_of(key_refs, cols, ROWS), keys_marks], axis=1)
        weights, top = soften(scores_of(queries, keys))
        mixed, total = mix(weights, rows_of(value_refs, cols, ROWS))
        for d in range(n):
            rows = slice(d * ROWS, (d + 1) * ROWS)
            mixed_ref[head, d], sum_ref[head, d], top_ref[head, d] = mixed[rows], total[rows], top[rows]


def finish_kernel(heads, n, flips, at_ref, rows_ref, mixed_ref, sum_ref, top_ref, keys_ref, values_ref, w_ref, *refs):
    blocks = [block for flip in flips for block in slot_blocks(at_ref, *flip, n)]
    marks = frame_marks(at_ref, blocks, n)
    keys_marks = key_marks([n // 2], TPF, n)
    attended = []

    def of(ref, head):
        return jnp.concatenate([ref[head, block] for block in blocks], axis=0)

    for head in range(heads):
        cols = slice(head * HD, (head + 1) * HD)
        queries = jnp.concatenate([rows_ref[block, :, cols] for block in blocks], axis=0)
        keys = jnp.concatenate([rows_of([keys_ref], cols, TPF), keys_marks], axis=1)
        before = of(top_ref, head)
        weights, top = soften(scores_of(jnp.concatenate([queries, marks], axis=1), keys), before)
        mixed, total = mix(weights, rows_of([values_ref], cols, TPF))
        kept = jnp.exp2((before - top) * SCALE)
        mixed, total = mixed + of(mixed_ref, head) * kept, total + of(sum_ref, head) * kept
        attended.append((mixed / total).astype(jnp.bfloat16))
    rows = jnp.concatenate(attended, axis=1)
    refs[-1][...] = jnp.dot(rows, w_ref[...], preferred_element_type=jnp.float32).astype(refs[-1].dtype)


def call(kernel, scalars, operands, outs, flops, after=()):
    vmem = pl.BlockSpec(memory_space=pltpu.VMEM)
    return pl.pallas_call(
        kernel,
        out_shape=[jax.ShapeDtypeStruct(shape, dtype) for shape, dtype in outs],
        in_specs=[pl.BlockSpec(memory_space=pltpu.SMEM)] * len(scalars)
        + [vmem] * len(operands)
        + [pl.BlockSpec(memory_space=pl.ANY)] * len(after),
        out_specs=[vmem] * len(outs),
        compiler_params=pltpu.CompilerParams(vmem_limit_bytes=20 * 1024 * 1024),
        cost_estimate=pl.CostEstimate(flops=flops, bytes_accessed=0, transcendentals=0),
    )(*scalars, *operands, *after)


def on_device_ring(queries, keys_values, out_weight):
    n = lax.axis_size("frames")
    frame, head = lax.axis_index("frames"), lax.axis_index("heads")
    z, y, x, core = frame >> 1, frame & 1, head >> 1, head & 1
    where = jnp.stack([ring_place(frame, n), z, y, x, core]).astype(jnp.int32)
    width, cols = out_weight.shape
    heads = width // HD
    f32, bf16 = jnp.float32, jnp.bfloat16
    block = (queries.shape, bf16)
    own = call(split_kernel, (), [keys_values], [block, block], 0)
    queries, keys, values = gather_ring([queries, *own], n)
    (rows,) = call(functools.partial(rows_kernel, n), (), queries, [((n, ROWS, width), bf16)], 0)
    far = n // 2
    state = call(
        functools.partial(near_kernel, heads, n),
        (where,),
        [rows, *(blocks[d] for blocks in (keys, values) for d in range(n) if d != far)],
        [((heads, n, ROWS, HD), f32)] * 3,
        4 * n * (n - 1) * ROWS**2 * width,
    )

    def finish(flips, dtype, after=()):
        (sums,) = call(
            functools.partial(finish_kernel, heads, n, flips),
            (where,),
            [rows, *state, keys[far], values[far], out_weight],
            [((len(flips) * 2 * ROWS, cols), dtype)],
            n * ROWS * width * cols,
            after,
        )
        return sums.reshape(len(flips), 2 * ROWS, cols)

    given = finish([(1, 1), (0, 1)], bf16)
    from_core = lax.ppermute(given, "heads", [(h, h ^ 1) for h in range(4)])
    sums = finish([(1, 0)], f32, (given,))[0]
    parts = [slice(slot * ROWS, (slot + 1) * ROWS) for slot in range(2)]
    given = [(sums[part] + from_core[0, part].astype(f32)).astype(bf16) for part in parts]
    from_x = [lax.ppermute(block, "heads", [(h, h ^ 2) for h in range(4)]) for block in given]
    kept = finish([(0, 0)], f32, given)[0]
    arrived = []
    for slot, part in enumerate(parts):
        pairs = []
        for f in range(n):
            for h in range(4):
                to = PATTERNS[(slot ^ (f & 1)) + 2 * (h >> 1)][f >> 1]
                pairs.append((4 * f + h, 4 * (2 * to + (h & 1)) + (f >> 1)))
        total = kept[part] + from_core[1, part].astype(f32) + from_x[slot].astype(f32)
        arrived.append(lax.ppermute(total.astype(bf16), ("frames", "heads"), pairs))
    patterns = [[p[source] for p in PATTERNS].index(to) for source in range(4) for to in range(4)]
    straight = look_up(patterns, 4 * head + z) & 1 == 0
    low, high = arrived
    return jnp.concatenate([jnp.where(straight, low, high), jnp.where(straight, high, low)], axis=1)


def solution(mesh):
    in_specs = (P("frames", "heads"), P(None, "frames", "heads"), P("heads", "frames"))
    out_specs = P("frames", "heads")
    n, heads = mesh.shape["frames"], mesh.shape["heads"]
    total_frames = n * FR_DEV
    reach = min(reach_cap, (total_frames - 1) // 2)
    every = total_frames == 2 * reach + 2 and heads == 4 and n == 2 * heads
    return jax.shard_map(
        on_device_ring if every else on_device_band,
        mesh=mesh,
        in_specs=in_specs,
        out_specs=out_specs,
        check_vma=False,
    )
```

```python
import functools
import math

import jax
import jax.numpy as jnp
from jax import lax
from jax.experimental import pallas as pl
from jax.experimental.pallas import tpu as pltpu
from jax.sharding import PartitionSpec as P

HD = 128
TPF = 32
FR_DEV = 3
ROWS = FR_DEV * TPF
SCALE = HD ** (-0.5) * math.log2(math.e)


reach_cap = 32


def from_behind(x, axis, by):
    devices = lax.axis_size(axis)
    return lax.ppermute(x, axis, [(i, (i + by) % devices) for i in range(devices)])


def on_device_band(queries, keys_values, out_weight):
    total_frames = lax.axis_size("frames") * FR_DEV
    reach = min(reach_cap, (total_frames - 1) // 2)
    steps = (reach + FR_DEV - 1) // FR_DEV
    width = keys_values.shape[2]
    span = FR_DEV + 2 * reach
    stacked = keys_values.reshape(2, FR_DEV, TPF, width)
    pieces = []
    for offset in range(-steps, steps + 1):
        if offset == 0:
            pieces.append(stacked)
        else:
            pieces.append(from_behind(stacked, "frames", -offset))
    window = jnp.concatenate(pieces, axis=1)
    lower_frame = steps * FR_DEV - reach
    extended = window[:, lower_frame : lower_frame + span]
    keys_ext = extended[0].reshape(span * TPF, width)
    values_ext = extended[1].reshape(span * TPF, width)
    row_frame = jnp.arange(FR_DEV * TPF, dtype=jnp.int32) // TPF
    col_frame = jnp.arange(span * TPF, dtype=jnp.int32) // TPF
    allowed = (col_frame[None, :] >= row_frame[:, None]) & (
        col_frame[None, :] <= row_frame[:, None] + 2 * reach
    )
    results = []
    for head in range(width // HD):
        lower = head * HD
        query_cols = queries[:, lower : lower + HD]
        key_cols = keys_ext[:, lower : lower + HD]
        scores = lax.dot_general(
            query_cols, key_cols, (((1,), (1,)), ((), ())), preferred_element_type=jnp.float32
        )
        scores = scores * HD ** (-0.5)
        top = jnp.max(jnp.where(allowed, scores, -1e30), axis=1, keepdims=True)
        weights = jnp.where(allowed, jnp.exp(scores - top), 0.0)
        probs = (weights / jnp.sum(weights, axis=1, keepdims=True)).astype(jnp.bfloat16)
        results.append(
            jnp.dot(
                probs, values_ext[:, lower : lower + HD], preferred_element_type=jnp.float32
            ).astype(jnp.bfloat16)
        )
    attended = jnp.concatenate(results, axis=1)
    partial_rows = jnp.dot(
        attended,
        lax.all_gather(out_weight, "frames", axis=1, tiled=True),
        preferred_element_type=jnp.float32,
    )
    return lax.psum_scatter(
        partial_rows.astype(jnp.bfloat16), "heads", scatter_dimension=1, tiled=True
    )


def ring_order(n):
    return list(range(0, n, 2)) + list(range(n - 1, 0, -2))


def ring_place(f, n):
    return (f >> 1) + (f & 1) * (n - 1 - (f >> 1) * 2)


def hop(x, n, by):
    order = ring_order(n)
    pairs = []
    for i in range(n):
        for h in range(4):
            pairs.append((4 * order[i] + h, 4 * order[(i + by * (1 - 2 * (h & 1))) % n] + h))
    return lax.ppermute(x, ("frames", "heads"), pairs)


def gather_ring(streams, n):
    found = [[block] + [None] * (n - 1) for block in streams]
    for step in range(1, n // 2 + 1):
        for j, blocks in enumerate(found):
            for by in (1, -1):
                if step < n // 2 or (j % 2 == 0) == (by == 1):
                    blocks[by * step % n] = hop(blocks[by * (step - 1) % n], n, by)
    return found


def ring_distance(at_ref, owner, n):
    place, core = at_ref[0], at_ref[4]
    return (place - owner) * (1 - 2 * core) & (n - 1)


def frame_marks(at_ref, blocks, n):
    place, core = at_ref[0], at_ref[4]
    lane = lax.broadcasted_iota(jnp.int32, (TPF, HD), 1)
    marks = []
    for block in blocks:
        owner = (place - block * (1 - 2 * core)) & (n - 1)
        frame = FR_DEV * ring_distance(at_ref, owner ^ 2, n)
        for g in range(FR_DEV):
            marks.append((lane == frame + g) | (lane >= n * FR_DEV))
    return jnp.concatenate([jnp.where(mark, 1.0, 0.0) for mark in marks], axis=0).astype(jnp.bfloat16)


def key_marks(blocks, padding, n):
    lane = lax.broadcasted_iota(jnp.int32, (TPF, HD), 1)
    frames = [FR_DEV * block + g for block in blocks for g in range(FR_DEV)] + [n * FR_DEV] * (padding // TPF)
    return jnp.concatenate([jnp.where(lane == frame, -1e30, 0.0) for frame in frames], axis=0).astype(jnp.bfloat16)


def rows_of(refs, cols, padding=0):
    pieces = [ref[:, cols] for ref in refs]
    if padding:
        pieces.append(jnp.zeros((padding, HD), jnp.bfloat16))
    return jnp.concatenate(pieces, axis=0)


def scores_of(queries, keys):
    return lax.dot_general(queries, keys, (((1,), (1,)), ((), ())), preferred_element_type=jnp.float32)


def soften(scores, floor=None):
    weights, tops = [], []
    for r in range(0, scores.shape[0], TPF):
        parts = [scores[r : r + TPF, c : c + HD] for c in range(0, scores.shape[1], HD)]
        top = jnp.max(functools.reduce(jnp.maximum, parts), axis=1, keepdims=True)
        top = jnp.broadcast_to(top, (TPF, HD))
        if floor is not None:
            top = jnp.maximum(top, floor[r : r + TPF])
        weights.append(jnp.concatenate([jnp.exp2((p - top) * SCALE).astype(jnp.bfloat16) for p in parts], axis=1))
        tops.append(top)
    return jnp.concatenate(weights, axis=0), jnp.concatenate(tops, axis=0)


def mix(weights, values):
    ones = jnp.ones(values.shape, values.dtype)
    mixed = jnp.dot(weights, jnp.concatenate([values, ones], axis=1), preferred_element_type=jnp.float32)
    return mixed[:, :HD], mixed[:, HD:]


PATTERNS = ((2, 1, 2, 1), (0, 3, 0, 3), (3, 0, 1, 2), (1, 2, 3, 0))


def look_up(table, index):
    code = sum(entry << (2 * i) for i, entry in enumerate(table))
    return (jnp.int32(code - (code >> 31 << 32)) >> (2 * index)) & 3


def slot_blocks(at_ref, flip_x, flip_core, n):
    z, y, x, core = (at_ref[i] for i in range(1, 5))
    blocks = []
    for slot in range(2):
        to = look_up(sum(PATTERNS, ()), 4 * ((slot ^ y) + 2 * (x ^ flip_x)) + z)
        owner = to + (core ^ flip_core) * (n - 1 - 2 * to)
        blocks.append(ring_distance(at_ref, owner, n))
    return blocks


def split_kernel(kv_ref, keys_ref, values_ref):
    keys_ref[...] = kv_ref[0]
    values_ref[...] = kv_ref[1]


def rows_kernel(n, *refs):
    for d in range(n):
        refs[n][d] = refs[d][...]


def near_kernel(heads, n, at_ref, rows_ref, *refs):
    near = [d for d in range(n) if d != n // 2]
    key_refs, value_refs, (mixed_ref, sum_ref, top_ref) = refs[: n - 1], refs[n - 1 : -3], refs[-3:]
    marks = frame_marks(at_ref, range(n), n)
    keys_marks = key_marks(near, ROWS, n)
    for head in range(heads):
        cols = slice(head * HD, (head + 1) * HD)
        queries = jnp.concatenate([rows_ref[:, :, cols].reshape(n * ROWS, HD), marks], axis=1)
        keys = jnp.concatenate([rows_of(key_refs, cols, ROWS), keys_marks], axis=1)
        weights, top = soften(scores_of(queries, keys))
        mixed, total = mix(weights, rows_of(value_refs, cols, ROWS))
        for d in range(n):
            rows = slice(d * ROWS, (d + 1) * ROWS)
            mixed_ref[head, d], sum_ref[head, d], top_ref[head, d] = mixed[rows], total[rows], top[rows]


def finish_kernel(heads, n, flips, at_ref, rows_ref, mixed_ref, sum_ref, top_ref, keys_ref, values_ref, w_ref, *refs):
    blocks = [block for flip in flips for block in slot_blocks(at_ref, *flip, n)]
    marks = frame_marks(at_ref, blocks, n)
    keys_marks = key_marks([n // 2], TPF, n)
    attended = []

    def of(ref, head):
        return jnp.concatenate([ref[head, block] for block in blocks], axis=0)

    for head in range(heads):
        cols = slice(head * HD, (head + 1) * HD)
        queries = jnp.concatenate([rows_ref[block, :, cols] for block in blocks], axis=0)
        keys = jnp.concatenate([rows_of([keys_ref], cols, TPF), keys_marks], axis=1)
        before = of(top_ref, head)
        weights, top = soften(scores_of(jnp.concatenate([queries, marks], axis=1), keys), before)
        mixed, total = mix(weights, rows_of([values_ref], cols, TPF))
        kept = jnp.exp2((before - top) * SCALE)
        mixed, total = mixed + of(mixed_ref, head) * kept, total + of(sum_ref, head) * kept
        attended.append((mixed / total).astype(jnp.bfloat16))
    rows = jnp.concatenate(attended, axis=1)
    refs[-1][...] = jnp.dot(rows, w_ref[...], preferred_element_type=jnp.float32).astype(refs[-1].dtype)


def sum_kernel(rows, kept_ref, from_core_ref, from_x_ref, total_ref):
    total = kept_ref[rows] + from_core_ref[1, rows].astype(jnp.float32) + from_x_ref[...].astype(jnp.float32)
    total_ref[...] = total.astype(total_ref.dtype)


def call(kernel, scalars, operands, outs, flops, after=()):
    vmem = pl.BlockSpec(memory_space=pltpu.VMEM)
    return pl.pallas_call(
        kernel,
        out_shape=[jax.ShapeDtypeStruct(shape, dtype) for shape, dtype in outs],
        in_specs=[pl.BlockSpec(memory_space=pltpu.SMEM)] * len(scalars)
        + [vmem] * len(operands)
        + [pl.BlockSpec(memory_space=pl.ANY)] * len(after),
        out_specs=[vmem] * len(outs),
        compiler_params=pltpu.CompilerParams(vmem_limit_bytes=20 * 1024 * 1024),
        cost_estimate=pl.CostEstimate(flops=flops, bytes_accessed=0, transcendentals=0),
    )(*scalars, *operands, *after)


def on_device_ring(queries, keys_values, out_weight):
    n = lax.axis_size("frames")
    frame, head = lax.axis_index("frames"), lax.axis_index("heads")
    z, y, x, core = frame >> 1, frame & 1, head >> 1, head & 1
    where = jnp.stack([ring_place(frame, n), z, y, x, core]).astype(jnp.int32)
    width, cols = out_weight.shape
    heads = width // HD
    f32, bf16 = jnp.float32, jnp.bfloat16
    block = (queries.shape, bf16)
    own = call(split_kernel, (), [keys_values], [block, block], 0)
    queries, keys, values = gather_ring([queries, *own], n)
    (rows,) = call(functools.partial(rows_kernel, n), (), queries, [((n, ROWS, width), bf16)], 0)
    far = n // 2
    state = call(
        functools.partial(near_kernel, heads, n),
        (where,),
        [rows, *(blocks[d] for blocks in (keys, values) for d in range(n) if d != far)],
        [((heads, n, ROWS, HD), f32)] * 3,
        4 * n * (n - 1) * ROWS**2 * width,
    )

    def finish(flips, dtype, after=()):
        (sums,) = call(
            functools.partial(finish_kernel, heads, n, flips),
            (where,),
            [rows, *state, keys[far], values[far], out_weight],
            [((len(flips) * 2 * ROWS, cols), dtype)],
            n * ROWS * width * cols,
            after,
        )
        return sums.reshape(len(flips), 2 * ROWS, cols)

    given = finish([(1, 1), (0, 1)], bf16)
    from_core = lax.ppermute(given, "heads", [(h, h ^ 1) for h in range(4)])
    sums = finish([(1, 0)], f32, (given,))[0]
    parts = [slice(slot * ROWS, (slot + 1) * ROWS) for slot in range(2)]
    given = [(sums[part] + from_core[0, part].astype(f32)).astype(bf16) for part in parts]
    from_x = [lax.ppermute(block, "heads", [(h, h ^ 2) for h in range(4)]) for block in given]
    kept = finish([(0, 0)], f32, given)[0]
    arrived = []
    for slot, part in enumerate(parts):
        pairs = []
        for f in range(n):
            for h in range(4):
                to = PATTERNS[(slot ^ (f & 1)) + 2 * (h >> 1)][f >> 1]
                pairs.append((4 * f + h, 4 * (2 * to + (h & 1)) + (f >> 1)))
        (total,) = call(
            functools.partial(sum_kernel, part), (), [kept, from_core, from_x[slot]], [((ROWS, cols), bf16)], 0
        )
        arrived.append(lax.ppermute(total, ("frames", "heads"), pairs))
    patterns = [[p[source] for p in PATTERNS].index(to) for source in range(4) for to in range(4)]
    straight = look_up(patterns, 4 * head + z) & 1 == 0
    low, high = arrived
    return jnp.concatenate([jnp.where(straight, low, high), jnp.where(straight, high, low)], axis=1)


def solution(mesh):
    in_specs = (P("frames", "heads"), P(None, "frames", "heads"), P("heads", "frames"))
    out_specs = P("frames", "heads")
    n, heads = mesh.shape["frames"], mesh.shape["heads"]
    total_frames = n * FR_DEV
    reach = min(reach_cap, (total_frames - 1) // 2)
    every = total_frames == 2 * reach + 2 and heads == 4 and n == 2 * heads
    return jax.shard_map(
        on_device_ring if every else on_device_band,
        mesh=mesh,
        in_specs=in_specs,
        out_specs=out_specs,
        check_vma=False,
    )
```

```python
import functools
import math

import jax
import jax.numpy as jnp
from jax import lax
from jax.experimental import pallas as pl
from jax.experimental.pallas import tpu as pltpu
from jax.sharding import PartitionSpec as P

HD = 128
TPF = 32
FR_DEV = 3
ROWS = FR_DEV * TPF
SCALE = HD ** (-0.5) * math.log2(math.e)


reach_cap = 32


def from_behind(x, axis, by):
    devices = lax.axis_size(axis)
    return lax.ppermute(x, axis, [(i, (i + by) % devices) for i in range(devices)])


def on_device_band(queries, keys_values, out_weight):
    total_frames = lax.axis_size("frames") * FR_DEV
    reach = min(reach_cap, (total_frames - 1) // 2)
    steps = (reach + FR_DEV - 1) // FR_DEV
    width = keys_values.shape[2]
    span = FR_DEV + 2 * reach
    stacked = keys_values.reshape(2, FR_DEV, TPF, width)
    pieces = []
    for offset in range(-steps, steps + 1):
        if offset == 0:
            pieces.append(stacked)
        else:
            pieces.append(from_behind(stacked, "frames", -offset))
    window = jnp.concatenate(pieces, axis=1)
    lower_frame = steps * FR_DEV - reach
    extended = window[:, lower_frame : lower_frame + span]
    keys_ext = extended[0].reshape(span * TPF, width)
    values_ext = extended[1].reshape(span * TPF, width)
    row_frame = jnp.arange(FR_DEV * TPF, dtype=jnp.int32) // TPF
    col_frame = jnp.arange(span * TPF, dtype=jnp.int32) // TPF
    allowed = (col_frame[None, :] >= row_frame[:, None]) & (
        col_frame[None, :] <= row_frame[:, None] + 2 * reach
    )
    results = []
    for head in range(width // HD):
        lower = head * HD
        query_cols = queries[:, lower : lower + HD]
        key_cols = keys_ext[:, lower : lower + HD]
        scores = lax.dot_general(
            query_cols, key_cols, (((1,), (1,)), ((), ())), preferred_element_type=jnp.float32
        )
        scores = scores * HD ** (-0.5)
        top = jnp.max(jnp.where(allowed, scores, -1e30), axis=1, keepdims=True)
        weights = jnp.where(allowed, jnp.exp(scores - top), 0.0)
        probs = (weights / jnp.sum(weights, axis=1, keepdims=True)).astype(jnp.bfloat16)
        results.append(
            jnp.dot(
                probs, values_ext[:, lower : lower + HD], preferred_element_type=jnp.float32
            ).astype(jnp.bfloat16)
        )
    attended = jnp.concatenate(results, axis=1)
    partial_rows = jnp.dot(
        attended,
        lax.all_gather(out_weight, "frames", axis=1, tiled=True),
        preferred_element_type=jnp.float32,
    )
    return lax.psum_scatter(
        partial_rows.astype(jnp.bfloat16), "heads", scatter_dimension=1, tiled=True
    )


def ring_order(n):
    return list(range(0, n, 2)) + list(range(n - 1, 0, -2))


def ring_place(f, n):
    return (f >> 1) + (f & 1) * (n - 1 - (f >> 1) * 2)


def hop(x, n, by):
    order = ring_order(n)
    pairs = []
    for i in range(n):
        for h in range(4):
            pairs.append((4 * order[i] + h, 4 * order[(i + by * (1 - 2 * (h & 1))) % n] + h))
    return lax.ppermute(x, ("frames", "heads"), pairs)


def gather_ring(streams, n):
    found = [[block] + [None] * (n - 1) for block in streams]
    for step in range(1, n // 2 + 1):
        for j, blocks in enumerate(found):
            for by in (1, -1):
                if step < n // 2 or (j % 2 == 0) == (by == 1):
                    blocks[by * step % n] = hop(blocks[by * (step - 1) % n], n, by)
    return found


def ring_distance(at_ref, owner, n):
    place, core = at_ref[0], at_ref[4]
    return (place - owner) * (1 - 2 * core) & (n - 1)


def frame_marks(at_ref, blocks, n):
    place, core = at_ref[0], at_ref[4]
    lane = lax.broadcasted_iota(jnp.int32, (TPF, HD), 1)
    marks = []
    for block in blocks:
        owner = (place - block * (1 - 2 * core)) & (n - 1)
        frame = FR_DEV * ring_distance(at_ref, owner ^ 2, n)
        for g in range(FR_DEV):
            marks.append((lane == frame + g) | (lane >= n * FR_DEV))
    return jnp.concatenate([jnp.where(mark, 1.0, 0.0) for mark in marks], axis=0).astype(jnp.bfloat16)


def key_marks(blocks, padding, n):
    lane = lax.broadcasted_iota(jnp.int32, (TPF, HD), 1)
    frames = [FR_DEV * block + g for block in blocks for g in range(FR_DEV)] + [n * FR_DEV] * (padding // TPF)
    return jnp.concatenate([jnp.where(lane == frame, -1e30, 0.0) for frame in frames], axis=0).astype(jnp.bfloat16)


def rows_of(refs, cols, padding=0):
    pieces = [ref[:, cols] for ref in refs]
    if padding:
        pieces.append(jnp.zeros((padding, HD), jnp.bfloat16))
    return jnp.concatenate(pieces, axis=0)


def scores_of(queries, keys):
    return lax.dot_general(queries, keys, (((1,), (1,)), ((), ())), preferred_element_type=jnp.float32)


def soften(scores, floor=None):
    weights, tops = [], []
    for r in range(0, scores.shape[0], TPF):
        parts = [scores[r : r + TPF, c : c + HD] for c in range(0, scores.shape[1], HD)]
        top = jnp.max(functools.reduce(jnp.maximum, parts), axis=1, keepdims=True)
        top = jnp.broadcast_to(top, (TPF, HD))
        if floor is not None:
            top = jnp.maximum(top, floor[r : r + TPF])
        weights.append(jnp.concatenate([jnp.exp2((p - top) * SCALE).astype(jnp.bfloat16) for p in parts], axis=1))
        tops.append(top)
    return jnp.concatenate(weights, axis=0), jnp.concatenate(tops, axis=0)


def mix(weights, values):
    ones = jnp.ones(values.shape, values.dtype)
    mixed = jnp.dot(weights, jnp.concatenate([values, ones], axis=1), preferred_element_type=jnp.float32)
    return mixed[:, :HD], mixed[:, HD:]


PATTERNS = ((2, 1, 2, 1), (0, 3, 0, 3), (3, 0, 1, 2), (1, 2, 3, 0))


def look_up(table, index):
    code = sum(entry << (2 * i) for i, entry in enumerate(table))
    return (jnp.int32(code - (code >> 31 << 32)) >> (2 * index)) & 3


def slot_blocks(at_ref, flip_x, flip_core, n):
    z, y, x, core = (at_ref[i] for i in range(1, 5))
    blocks = []
    for slot in range(2):
        to = look_up(sum(PATTERNS, ()), 4 * ((slot ^ y) + 2 * (x ^ flip_x)) + z)
        owner = to + (core ^ flip_core) * (n - 1 - 2 * to)
        blocks.append(ring_distance(at_ref, owner, n))
    return blocks


def ahead(scores, heads):
    columns = [slice(head * HD, (head + 1) * HD) for head in range(heads)]
    now = scores(columns[0])
    for head, cols in enumerate(columns):
        later = scores(columns[head + 1]) if head + 1 < heads else None
        yield head, cols, now
        now = later


def split_kernel(kv_ref, keys_ref, values_ref):
    keys_ref[...] = kv_ref[0]
    values_ref[...] = kv_ref[1]


def rows_kernel(n, *refs):
    for d in range(n):
        refs[n][d] = refs[d][...]


def near_kernel(heads, n, at_ref, rows_ref, *refs):
    near = [d for d in range(n) if d != n // 2]
    key_refs, value_refs, (mixed_ref, sum_ref, top_ref) = refs[: n - 1], refs[n - 1 : -3], refs[-3:]
    marks = frame_marks(at_ref, range(n), n)
    keys_marks = key_marks(near, ROWS, n)

    def scores(cols):
        queries = jnp.concatenate([rows_ref[:, :, cols].reshape(n * ROWS, HD), marks], axis=1)
        return scores_of(queries, jnp.concatenate([rows_of(key_refs, cols, ROWS), keys_marks], axis=1))

    for head, cols, now in ahead(scores, heads):
        weights, top = soften(now)
        mixed, total = mix(weights, rows_of(value_refs, cols, ROWS))
        for d in range(n):
            rows = slice(d * ROWS, (d + 1) * ROWS)
            mixed_ref[head, d], sum_ref[head, d], top_ref[head, d] = mixed[rows], total[rows], top[rows]


def finish_kernel(heads, n, flips, at_ref, rows_ref, mixed_ref, sum_ref, top_ref, keys_ref, values_ref, w_ref, *refs):
    blocks = [block for flip in flips for block in slot_blocks(at_ref, *flip, n)]
    marks = frame_marks(at_ref, blocks, n)
    keys_marks = key_marks([n // 2], TPF, n)
    attended = []

    def of(ref, head):
        return jnp.concatenate([ref[head, block] for block in blocks], axis=0)

    def scores(cols):
        queries = jnp.concatenate([rows_ref[block, :, cols] for block in blocks], axis=0)
        keys = jnp.concatenate([rows_of([keys_ref], cols, TPF), keys_marks], axis=1)
        return scores_of(jnp.concatenate([queries, marks], axis=1), keys)

    for head, cols, now in ahead(scores, heads):
        before = of(top_ref, head)
        weights, top = soften(now, before)
        mixed, total = mix(weights, rows_of([values_ref], cols, TPF))
        kept = jnp.exp2((before - top) * SCALE)
        mixed, total = mixed + of(mixed_ref, head) * kept, total + of(sum_ref, head) * kept
        attended.append((mixed / total).astype(jnp.bfloat16))
    rows = jnp.concatenate(attended, axis=1)
    refs[-1][...] = jnp.dot(rows, w_ref[...], preferred_element_type=jnp.float32).astype(refs[-1].dtype)


def sum_kernel(rows, kept_ref, from_core_ref, from_x_ref, total_ref):
    total = kept_ref[rows] + from_core_ref[1, rows].astype(jnp.float32) + from_x_ref[...].astype(jnp.float32)
    total_ref[...] = total.astype(total_ref.dtype)


def call(kernel, scalars, operands, outs, flops, after=()):
    vmem = pl.BlockSpec(memory_space=pltpu.VMEM)
    return pl.pallas_call(
        kernel,
        out_shape=[jax.ShapeDtypeStruct(shape, dtype) for shape, dtype in outs],
        in_specs=[pl.BlockSpec(memory_space=pltpu.SMEM)] * len(scalars)
        + [vmem] * len(operands)
        + [pl.BlockSpec(memory_space=pl.ANY)] * len(after),
        out_specs=[vmem] * len(outs),
        compiler_params=pltpu.CompilerParams(vmem_limit_bytes=20 * 1024 * 1024),
        cost_estimate=pl.CostEstimate(flops=flops, bytes_accessed=0, transcendentals=0),
    )(*scalars, *operands, *after)


def on_device_ring(queries, keys_values, out_weight):
    n = lax.axis_size("frames")
    frame, head = lax.axis_index("frames"), lax.axis_index("heads")
    z, y, x, core = frame >> 1, frame & 1, head >> 1, head & 1
    where = jnp.stack([ring_place(frame, n), z, y, x, core]).astype(jnp.int32)
    width, cols = out_weight.shape
    heads = width // HD
    f32, bf16 = jnp.float32, jnp.bfloat16
    block = (queries.shape, bf16)
    own = call(split_kernel, (), [keys_values], [block, block], 0)
    queries, keys, values = gather_ring([queries, *own], n)
    (rows,) = call(functools.partial(rows_kernel, n), (), queries, [((n, ROWS, width), bf16)], 0)
    far = n // 2
    state = call(
        functools.partial(near_kernel, heads, n),
        (where,),
        [rows, *(blocks[d] for blocks in (keys, values) for d in range(n) if d != far)],
        [((heads, n, ROWS, HD), f32)] * 3,
        4 * n * (n - 1) * ROWS**2 * width,
    )

    def finish(flips, dtype, after=()):
        (sums,) = call(
            functools.partial(finish_kernel, heads, n, flips),
            (where,),
            [rows, *state, keys[far], values[far], out_weight],
            [((len(flips) * 2 * ROWS, cols), dtype)],
            n * ROWS * width * cols,
            after,
        )
        return sums.reshape(len(flips), 2 * ROWS, cols)

    given = finish([(1, 1), (0, 1)], bf16)
    from_core = lax.ppermute(given, "heads", [(h, h ^ 1) for h in range(4)])
    sums = finish([(1, 0)], f32, (given,))[0]
    parts = [slice(slot * ROWS, (slot + 1) * ROWS) for slot in range(2)]
    given = [(sums[part] + from_core[0, part].astype(f32)).astype(bf16) for part in parts]
    from_x = [lax.ppermute(block, "heads", [(h, h ^ 2) for h in range(4)]) for block in given]
    kept = finish([(0, 0)], f32, given)[0]
    arrived = []
    for slot, part in enumerate(parts):
        pairs = []
        for f in range(n):
            for h in range(4):
                to = PATTERNS[(slot ^ (f & 1)) + 2 * (h >> 1)][f >> 1]
                pairs.append((4 * f + h, 4 * (2 * to + (h & 1)) + (f >> 1)))
        (total,) = call(
            functools.partial(sum_kernel, part), (), [kept, from_core, from_x[slot]], [((ROWS, cols), bf16)], 0
        )
        arrived.append(lax.ppermute(total, ("frames", "heads"), pairs))
    patterns = [[p[source] for p in PATTERNS].index(to) for source in range(4) for to in range(4)]
    straight = look_up(patterns, 4 * head + z) & 1 == 0
    low, high = arrived
    return jnp.concatenate([jnp.where(straight, low, high), jnp.where(straight, high, low)], axis=1)


def solution(mesh):
    in_specs = (P("frames", "heads"), P(None, "frames", "heads"), P("heads", "frames"))
    out_specs = P("frames", "heads")
    n, heads = mesh.shape["frames"], mesh.shape["heads"]
    total_frames = n * FR_DEV
    reach = min(reach_cap, (total_frames - 1) // 2)
    every = total_frames == 2 * reach + 2 and heads == 4 and n == 2 * heads
    return jax.shard_map(
        on_device_ring if every else on_device_band,
        mesh=mesh,
        in_specs=in_specs,
        out_specs=out_specs,
        check_vma=False,
    )
```

```python
import functools
import math

import jax
import jax.numpy as jnp
from jax import lax
from jax.experimental import pallas as pl
from jax.experimental.pallas import tpu as pltpu
from jax.sharding import PartitionSpec as P

HD = 128
TPF = 32
FR_DEV = 3
ROWS = FR_DEV * TPF
SCALE = HD ** (-0.5) * math.log2(math.e)


reach_cap = 32


def from_behind(x, axis, by):
    devices = lax.axis_size(axis)
    return lax.ppermute(x, axis, [(i, (i + by) % devices) for i in range(devices)])


def on_device_band(queries, keys_values, out_weight):
    total_frames = lax.axis_size("frames") * FR_DEV
    reach = min(reach_cap, (total_frames - 1) // 2)
    steps = (reach + FR_DEV - 1) // FR_DEV
    width = keys_values.shape[2]
    span = FR_DEV + 2 * reach
    stacked = keys_values.reshape(2, FR_DEV, TPF, width)
    pieces = []
    for offset in range(-steps, steps + 1):
        if offset == 0:
            pieces.append(stacked)
        else:
            pieces.append(from_behind(stacked, "frames", -offset))
    window = jnp.concatenate(pieces, axis=1)
    lower_frame = steps * FR_DEV - reach
    extended = window[:, lower_frame : lower_frame + span]
    keys_ext = extended[0].reshape(span * TPF, width)
    values_ext = extended[1].reshape(span * TPF, width)
    row_frame = jnp.arange(FR_DEV * TPF, dtype=jnp.int32) // TPF
    col_frame = jnp.arange(span * TPF, dtype=jnp.int32) // TPF
    allowed = (col_frame[None, :] >= row_frame[:, None]) & (
        col_frame[None, :] <= row_frame[:, None] + 2 * reach
    )
    results = []
    for head in range(width // HD):
        lower = head * HD
        query_cols = queries[:, lower : lower + HD]
        key_cols = keys_ext[:, lower : lower + HD]
        scores = lax.dot_general(
            query_cols, key_cols, (((1,), (1,)), ((), ())), preferred_element_type=jnp.float32
        )
        scores = scores * HD ** (-0.5)
        top = jnp.max(jnp.where(allowed, scores, -1e30), axis=1, keepdims=True)
        weights = jnp.where(allowed, jnp.exp(scores - top), 0.0)
        probs = (weights / jnp.sum(weights, axis=1, keepdims=True)).astype(jnp.bfloat16)
        results.append(
            jnp.dot(
                probs, values_ext[:, lower : lower + HD], preferred_element_type=jnp.float32
            ).astype(jnp.bfloat16)
        )
    attended = jnp.concatenate(results, axis=1)
    partial_rows = jnp.dot(
        attended,
        lax.all_gather(out_weight, "frames", axis=1, tiled=True),
        preferred_element_type=jnp.float32,
    )
    return lax.psum_scatter(
        partial_rows.astype(jnp.bfloat16), "heads", scatter_dimension=1, tiled=True
    )


def ring_order(n):
    return list(range(0, n, 2)) + list(range(n - 1, 0, -2))


def ring_place(f, n):
    return (f >> 1) + (f & 1) * (n - 1 - (f >> 1) * 2)


def hop(x, n, by):
    order = ring_order(n)
    pairs = []
    for i in range(n):
        for h in range(4):
            pairs.append((4 * order[i] + h, 4 * order[(i + by * (1 - 2 * (h & 1))) % n] + h))
    return lax.ppermute(x, ("frames", "heads"), pairs)


def gather_ring(streams, n):
    found = [[block] + [None] * (n - 1) for block in streams]
    for step in range(1, n // 2 + 1):
        for j, blocks in enumerate(found):
            for by in (1, -1):
                if step < n // 2 or (j % 2 == 0) == (by == 1):
                    blocks[by * step % n] = hop(blocks[by * (step - 1) % n], n, by)
    return found


def ring_distance(at_ref, owner, n):
    place, core = at_ref[0], at_ref[4]
    return (place - owner) * (1 - 2 * core) & (n - 1)


def frame_marks(at_ref, blocks, n):
    place, core = at_ref[0], at_ref[4]
    lane = lax.broadcasted_iota(jnp.int32, (TPF, HD), 1)
    marks = []
    for block in blocks:
        owner = (place - block * (1 - 2 * core)) & (n - 1)
        frame = FR_DEV * ring_distance(at_ref, owner ^ 2, n)
        for g in range(FR_DEV):
            marks.append((lane == frame + g) | (lane >= n * FR_DEV))
    return jnp.concatenate([jnp.where(mark, 1.0, 0.0) for mark in marks], axis=0).astype(jnp.bfloat16)


def key_marks(blocks, padding, n):
    lane = lax.broadcasted_iota(jnp.int32, (TPF, HD), 1)
    frames = [FR_DEV * block + g for block in blocks for g in range(FR_DEV)] + [n * FR_DEV] * (padding // TPF)
    return jnp.concatenate([jnp.where(lane == frame, -1e30, 0.0) for frame in frames], axis=0).astype(jnp.bfloat16)


def rows_of(refs, cols, padding=0):
    pieces = [ref[:, cols] for ref in refs]
    if padding:
        pieces.append(jnp.zeros((padding, HD), jnp.bfloat16))
    return jnp.concatenate(pieces, axis=0)


def scores_of(queries, keys):
    return lax.dot_general(queries, keys, (((1,), (1,)), ((), ())), preferred_element_type=jnp.float32)


def soften(scores, floor=None):
    weights, tops = [], []
    for r in range(0, scores.shape[0], TPF):
        parts = [scores[r : r + TPF, c : c + HD] for c in range(0, scores.shape[1], HD)]
        top = jnp.max(functools.reduce(jnp.maximum, parts), axis=1, keepdims=True)
        top = jnp.broadcast_to(top, (TPF, HD))
        if floor is not None:
            top = jnp.maximum(top, floor[r : r + TPF])
        weights.append(jnp.concatenate([jnp.exp2((p - top) * SCALE).astype(jnp.bfloat16) for p in parts], axis=1))
        tops.append(top)
    return jnp.concatenate(weights, axis=0), jnp.concatenate(tops, axis=0)


def mix(weights, values):
    ones = jnp.ones(values.shape, values.dtype)
    mixed = jnp.dot(weights, jnp.concatenate([values, ones], axis=1), preferred_element_type=jnp.float32)
    return mixed[:, :HD], mixed[:, HD:]


PATTERNS = ((2, 1, 2, 1), (0, 3, 0, 3), (3, 0, 1, 2), (1, 2, 3, 0))


def look_up(table, index):
    code = sum(entry << (2 * i) for i, entry in enumerate(table))
    return (jnp.int32(code - (code >> 31 << 32)) >> (2 * index)) & 3


def slot_blocks(at_ref, flip_x, flip_core, n):
    z, y, x, core = (at_ref[i] for i in range(1, 5))
    blocks = []
    for slot in range(2):
        to = look_up(sum(PATTERNS, ()), 4 * ((slot ^ y) + 2 * (x ^ flip_x)) + z)
        owner = to + (core ^ flip_core) * (n - 1 - 2 * to)
        blocks.append(ring_distance(at_ref, owner, n))
    return blocks


def add_keys(mixed, total, before, scores, values):
    weights, top = soften(scores, before)
    more, more_total = mix(weights, values)
    kept = jnp.exp2((before - top) * SCALE)
    return more + mixed * kept, more_total + total * kept, top


def ahead(scores, heads):
    columns = [slice(head * HD, (head + 1) * HD) for head in range(heads)]
    now = scores(columns[0])
    for head, cols in enumerate(columns):
        later = scores(columns[head + 1]) if head + 1 < heads else None
        yield head, cols, now
        now = later


def split_kernel(queries_ref, kv_ref, copy_ref, keys_ref, values_ref):
    copy_ref[...] = queries_ref[...]
    keys_ref[...] = kv_ref[0]
    values_ref[...] = kv_ref[1]


def rows_kernel(n, *refs):
    for d in range(n):
        refs[n][d] = refs[d][...]


def near_kernel(heads, n, blocks, at_ref, rows_ref, *refs):
    count = len(blocks)
    key_refs, value_refs, state, outs = refs[:count], refs[count : 2 * count], refs[2 * count : -3], refs[-3:]
    padding = -count * ROWS % (2 * HD)
    marks = frame_marks(at_ref, range(n), n)
    keys_marks = key_marks(blocks, padding, n)

    def scores(cols):
        queries = jnp.concatenate([rows_ref[:, :, cols].reshape(n * ROWS, HD), marks], axis=1)
        return scores_of(queries, jnp.concatenate([rows_of(key_refs, cols, padding), keys_marks], axis=1))

    for head, cols, now in ahead(scores, heads):
        values = rows_of(value_refs, cols, padding)
        if state:
            mixed, total, before = (ref[head].reshape(n * ROWS, HD) for ref in state)
            mixed, total, top = add_keys(mixed, total, before, now, values)
        else:
            weights, top = soften(now)
            mixed, total = mix(weights, values)
        for ref, result in zip(outs, (mixed, total, top)):
            ref[head] = result.reshape(n, ROWS, HD)


def finish_kernel(heads, n, flips, at_ref, rows_ref, mixed_ref, sum_ref, top_ref, keys_ref, values_ref, w_ref, *refs):
    blocks = [block for flip in flips for block in slot_blocks(at_ref, *flip, n)]
    marks = frame_marks(at_ref, blocks, n)
    keys_marks = key_marks([n // 2], TPF, n)
    attended = []

    def of(ref, head):
        return jnp.concatenate([ref[head, block] for block in blocks], axis=0)

    def scores(cols):
        queries = jnp.concatenate([rows_ref[block, :, cols] for block in blocks], axis=0)
        keys = jnp.concatenate([rows_of([keys_ref], cols, TPF), keys_marks], axis=1)
        return scores_of(jnp.concatenate([queries, marks], axis=1), keys)

    for head, cols, now in ahead(scores, heads):
        values = rows_of([values_ref], cols, TPF)
        mixed, total, _ = add_keys(of(mixed_ref, head), of(sum_ref, head), of(top_ref, head), now, values)
        attended.append((mixed / total).astype(jnp.bfloat16))
    rows = jnp.concatenate(attended, axis=1)
    refs[-1][...] = jnp.dot(rows, w_ref[...], preferred_element_type=jnp.float32).astype(refs[-1].dtype)


def sum_kernel(half, rows, others, own_ref, from_core_ref, *refs):
    total = own_ref[rows] + from_core_ref[half, rows].astype(jnp.float32)
    for ref in refs[:others]:
        total += ref[...].astype(jnp.float32)
    refs[-1][...] = total.astype(refs[-1].dtype)


def call(kernel, scalars, operands, outs, flops, after=()):
    vmem = pl.BlockSpec(memory_space=pltpu.VMEM)
    return pl.pallas_call(
        kernel,
        out_shape=[jax.ShapeDtypeStruct(shape, dtype) for shape, dtype in outs],
        in_specs=[pl.BlockSpec(memory_space=pltpu.SMEM)] * len(scalars)
        + [vmem] * len(operands)
        + [pl.BlockSpec(memory_space=pl.ANY)] * len(after),
        out_specs=[vmem] * len(outs),
        compiler_params=pltpu.CompilerParams(vmem_limit_bytes=20 * 1024 * 1024),
        cost_estimate=pl.CostEstimate(flops=flops, bytes_accessed=0, transcendentals=0),
    )(*scalars, *operands, *after)


def on_device_ring(queries, keys_values, out_weight):
    n = lax.axis_size("frames")
    frame, head = lax.axis_index("frames"), lax.axis_index("heads")
    z, y, x, core = frame >> 1, frame & 1, head >> 1, head & 1
    where = jnp.stack([ring_place(frame, n), z, y, x, core]).astype(jnp.int32)
    width, cols = out_weight.shape
    heads = width // HD
    f32, bf16 = jnp.float32, jnp.bfloat16
    block = (queries.shape, bf16)
    own_queries, *own = call(split_kernel, (), [queries, keys_values], [block] * 3, 0)
    queries, keys, values = gather_ring([queries, *own], n)
    (rows,) = call(functools.partial(rows_kernel, n), (), [own_queries, *queries[1:]], [((n, ROWS, width), bf16)], 0)
    far = n // 2
    state = []
    for blocks in ([0, 1, 2, n - 2, n - 1], list(range(3, far)) + list(range(far + 1, n - 2))):
        state = call(
            functools.partial(near_kernel, heads, n, blocks),
            (where,),
            [rows, *(keys[d] for d in blocks), *(values[d] for d in blocks), *state],
            [((heads, n, ROWS, HD), f32)] * 3,
            4 * n * len(blocks) * ROWS**2 * width,
        )

    def finish(flips, dtype, after=()):
        (sums,) = call(
            functools.partial(finish_kernel, heads, n, flips),
            (where,),
            [rows, *state, keys[far], values[far], out_weight],
            [((len(flips) * 2 * ROWS, cols), dtype)],
            n * ROWS * width * cols,
            after,
        )
        return sums.reshape(len(flips), 2 * ROWS, cols)

    given = finish([(1, 1), (0, 1)], bf16)
    from_core = lax.ppermute(given, "heads", [(h, h ^ 1) for h in range(4)])
    sums = finish([(1, 0)], f32, (given,))[0]
    parts = [slice(slot * ROWS, (slot + 1) * ROWS) for slot in range(2)]

    def add(half, part, own, others=(), after=()):
        kernel = functools.partial(sum_kernel, half, part, len(others))
        return call(kernel, (), [own, from_core, *others], [((ROWS, cols), bf16)], 0, after)[0]

    to_x = [(h, h ^ 2) for h in range(4)]
    given = add(0, parts[0], sums)
    from_x = [lax.ppermute(given, "heads", to_x)]
    kept = finish([(0, 0)], f32, (given,))[0]
    from_x.append(lax.ppermute(add(0, parts[1], sums, (), (kept,)), "heads", to_x))
    arrived = []
    for slot, part in enumerate(parts):
        pairs = []
        for f in range(n):
            for h in range(4):
                to = PATTERNS[(slot ^ (f & 1)) + 2 * (h >> 1)][f >> 1]
                pairs.append((4 * f + h, 4 * (2 * to + (h & 1)) + (f >> 1)))
        total = add(1, part, kept, [from_x[slot]])
        arrived.append(lax.ppermute(total, ("frames", "heads"), pairs))
    patterns = [[p[source] for p in PATTERNS].index(to) for source in range(4) for to in range(4)]
    straight = look_up(patterns, 4 * head + z) & 1 == 0
    low, high = arrived
    return jnp.concatenate([jnp.where(straight, low, high), jnp.where(straight, high, low)], axis=1)


def solution(mesh):
    in_specs = (P("frames", "heads"), P(None, "frames", "heads"), P("heads", "frames"))
    out_specs = P("frames", "heads")
    n, heads = mesh.shape["frames"], mesh.shape["heads"]
    total_frames = n * FR_DEV
    reach = min(reach_cap, (total_frames - 1) // 2)
    every = total_frames == 2 * reach + 2 and heads == 4 and n == 2 * heads
    return jax.shard_map(
        on_device_ring if every else on_device_band,
        mesh=mesh,
        in_specs=in_specs,
        out_specs=out_specs,
        check_vma=False,
    )
```

```python
import functools
import math

import jax
import jax.numpy as jnp
from jax import lax
from jax.experimental import pallas as pl
from jax.experimental.pallas import tpu as pltpu
from jax.sharding import PartitionSpec as P

HD = 128
TPF = 32
FR_DEV = 3
ROWS = FR_DEV * TPF
SCALE = HD ** (-0.5) * math.log2(math.e)


reach_cap = 32


def from_behind(x, axis, by):
    devices = lax.axis_size(axis)
    return lax.ppermute(x, axis, [(i, (i + by) % devices) for i in range(devices)])


def on_device_band(queries, keys_values, out_weight):
    total_frames = lax.axis_size("frames") * FR_DEV
    reach = min(reach_cap, (total_frames - 1) // 2)
    steps = (reach + FR_DEV - 1) // FR_DEV
    width = keys_values.shape[2]
    span = FR_DEV + 2 * reach
    stacked = keys_values.reshape(2, FR_DEV, TPF, width)
    pieces = []
    for offset in range(-steps, steps + 1):
        if offset == 0:
            pieces.append(stacked)
        else:
            pieces.append(from_behind(stacked, "frames", -offset))
    window = jnp.concatenate(pieces, axis=1)
    lower_frame = steps * FR_DEV - reach
    extended = window[:, lower_frame : lower_frame + span]
    keys_ext = extended[0].reshape(span * TPF, width)
    values_ext = extended[1].reshape(span * TPF, width)
    row_frame = jnp.arange(FR_DEV * TPF, dtype=jnp.int32) // TPF
    col_frame = jnp.arange(span * TPF, dtype=jnp.int32) // TPF
    allowed = (col_frame[None, :] >= row_frame[:, None]) & (
        col_frame[None, :] <= row_frame[:, None] + 2 * reach
    )
    results = []
    for head in range(width // HD):
        lower = head * HD
        query_cols = queries[:, lower : lower + HD]
        key_cols = keys_ext[:, lower : lower + HD]
        scores = lax.dot_general(
            query_cols, key_cols, (((1,), (1,)), ((), ())), preferred_element_type=jnp.float32
        )
        scores = scores * HD ** (-0.5)
        top = jnp.max(jnp.where(allowed, scores, -1e30), axis=1, keepdims=True)
        weights = jnp.where(allowed, jnp.exp(scores - top), 0.0)
        probs = (weights / jnp.sum(weights, axis=1, keepdims=True)).astype(jnp.bfloat16)
        results.append(
            jnp.dot(
                probs, values_ext[:, lower : lower + HD], preferred_element_type=jnp.float32
            ).astype(jnp.bfloat16)
        )
    attended = jnp.concatenate(results, axis=1)
    partial_rows = jnp.dot(
        attended,
        lax.all_gather(out_weight, "frames", axis=1, tiled=True),
        preferred_element_type=jnp.float32,
    )
    return lax.psum_scatter(
        partial_rows.astype(jnp.bfloat16), "heads", scatter_dimension=1, tiled=True
    )


def ring_order(n):
    return list(range(0, n, 2)) + list(range(n - 1, 0, -2))


def ring_place(f, n):
    return (f >> 1) + (f & 1) * (n - 1 - (f >> 1) * 2)


def hop(x, n, by):
    order = ring_order(n)
    pairs = []
    for i in range(n):
        for h in range(4):
            pairs.append((4 * order[i] + h, 4 * order[(i + by * (1 - 2 * (h & 1))) % n] + h))
    return lax.ppermute(x, ("frames", "heads"), pairs)


def gather_ring(streams, n):
    found = [[block] + [None] * (n - 1) for block in streams]
    for step in range(1, n // 2 + 1):
        for j, blocks in enumerate(found):
            for by in (1, -1):
                if step < n // 2 or (j % 2 == 0) == (by == 1):
                    blocks[by * step % n] = hop(blocks[by * (step - 1) % n], n, by)
    return found


def ring_distance(at_ref, owner, n):
    place, core = at_ref[0], at_ref[4]
    return (place - owner) * (1 - 2 * core) & (n - 1)


def frame_marks(at_ref, blocks, n):
    place, core = at_ref[0], at_ref[4]
    lane = lax.broadcasted_iota(jnp.int32, (TPF, HD), 1)
    marks = []
    for block in blocks:
        owner = (place - block * (1 - 2 * core)) & (n - 1)
        frame = FR_DEV * ring_distance(at_ref, owner ^ 2, n)
        for g in range(FR_DEV):
            marks.append((lane == frame + g) | (lane >= n * FR_DEV))
    return jnp.concatenate([jnp.where(mark, 1.0, 0.0) for mark in marks], axis=0).astype(jnp.bfloat16)


def key_marks(blocks, padding, n):
    lane = lax.broadcasted_iota(jnp.int32, (TPF, HD), 1)
    frames = [FR_DEV * block + g for block in blocks for g in range(FR_DEV)] + [n * FR_DEV] * (padding // TPF)
    return jnp.concatenate([jnp.where(lane == frame, -1e30, 0.0) for frame in frames], axis=0).astype(jnp.bfloat16)


def rows_of(refs, cols, padding=0):
    pieces = [ref[:, cols] for ref in refs]
    if padding:
        pieces.append(jnp.zeros((padding, HD), jnp.bfloat16))
    return jnp.concatenate(pieces, axis=0)


def scores_of(queries, keys):
    return lax.dot_general(queries, keys, (((1,), (1,)), ((), ())), preferred_element_type=jnp.float32)


def soften(scores, floor=None):
    weights, tops = [], []
    for r in range(0, scores.shape[0], TPF):
        parts = [scores[r : r + TPF, c : c + HD] for c in range(0, scores.shape[1], HD)]
        top = jnp.max(functools.reduce(jnp.maximum, parts), axis=1, keepdims=True)
        top = jnp.broadcast_to(top, (TPF, HD))
        if floor is not None:
            top = jnp.maximum(top, floor[r : r + TPF])
        weights.append(jnp.concatenate([jnp.exp2((p - top) * SCALE).astype(jnp.bfloat16) for p in parts], axis=1))
        tops.append(top)
    return jnp.concatenate(weights, axis=0), jnp.concatenate(tops, axis=0)


def mix(weights, values):
    ones = jnp.ones(values.shape, values.dtype)
    mixed = jnp.dot(weights, jnp.concatenate([values, ones], axis=1), preferred_element_type=jnp.float32)
    return mixed[:, :HD], mixed[:, HD:]


def ahead(scores, heads):
    columns = [slice(head * HD, (head + 1) * HD) for head in range(heads)]
    now = scores(columns[0])
    for head, cols in enumerate(columns):
        later = scores(columns[head + 1]) if head + 1 < heads else None
        yield head, cols, now
        now = later


def split_kernel(kv_ref, keys_ref, values_ref):
    keys_ref[...] = kv_ref[0]
    values_ref[...] = kv_ref[1]


def blocks_for(at_ref, parity, flips):
    x, core = at_ref[3], at_ref[4]
    found = []
    for flip_x, flip_core in flips:
        m = 2 * (core ^ flip_core) + (x ^ flip_x)
        found.append(jnp.where(core == 0, m, (-m - parity) & 3))
    return found


def attend_kernel(heads, n, blocks, before, flips, at_ref, *refs):
    count = len(blocks)
    query_refs, refs = refs[:count], refs[count:]
    key_refs, value_refs, refs = refs[:n], refs[n : 2 * n], refs[2 * n :]
    attended_ref = refs[-2] if flips else refs[-1]
    marks = frame_marks(at_ref, blocks, n)
    keys_marks = key_marks(range(n), 0, n)
    places = list(range(count))
    if before:
        places = [2]
        for source, place in enumerate((0, 1, 3)):
            attended_ref[place] = refs[0][source]

    def scores(cols):
        queries = jnp.concatenate([rows_of(query_refs, cols), marks], axis=1)
        return scores_of(queries, jnp.concatenate([rows_of(key_refs, cols), keys_marks], axis=1))

    for _, cols, now in ahead(scores, heads):
        weights, _ = soften(now)
        mixed, total = mix(weights, rows_of(value_refs, cols))
        result = (mixed / total).astype(jnp.bfloat16)
        for i, place in enumerate(places):
            attended_ref[place, :, cols] = result[i * ROWS : (i + 1) * ROWS]
    if flips:
        w_ref, out_ref = refs[1 if before else 0], refs[-1]
        out_ref[...] = times_w(at_ref, blocks[0] % 2, flips, attended_ref, w_ref).astype(out_ref.dtype)


def times_w(at_ref, parity, flips, attended_ref, w_ref):
    rows = jnp.concatenate([attended_ref[block] for block in blocks_for(at_ref, parity, flips)], axis=0)
    return jnp.dot(rows, w_ref[...], preferred_element_type=jnp.float32)


def kept_kernel(parity, at_ref, attended_ref, w_ref, out_ref):
    out_ref[...] = times_w(at_ref, parity, [(1, 0), (0, 0)], attended_ref, w_ref)


def sum_kernel(half, others, own_ref, from_core_ref, *refs):
    rows = slice(half * ROWS, (half + 1) * ROWS)
    total = own_ref[rows] + from_core_ref[rows].astype(jnp.float32)
    for ref in refs[:others]:
        total += ref[...].astype(jnp.float32)
    refs[-1][...] = total.astype(refs[-1].dtype)


def call(kernel, scalars, operands, outs, flops, after=()):
    vmem = pl.BlockSpec(memory_space=pltpu.VMEM)
    return pl.pallas_call(
        kernel,
        out_shape=[jax.ShapeDtypeStruct(shape, dtype) for shape, dtype in outs],
        in_specs=[pl.BlockSpec(memory_space=pltpu.SMEM)] * len(scalars)
        + [vmem] * len(operands)
        + [pl.BlockSpec(memory_space=pl.ANY)] * len(after),
        out_specs=[vmem] * len(outs),
        compiler_params=pltpu.CompilerParams(vmem_limit_bytes=20 * 1024 * 1024),
        cost_estimate=pl.CostEstimate(flops=flops, bytes_accessed=0, transcendentals=0),
    )(*scalars, *operands, *after)


def on_device_ring(queries, keys_values, out_weight):
    n = lax.axis_size("frames")
    frame, head = lax.axis_index("frames"), lax.axis_index("heads")
    z, y, x, core = frame >> 1, frame & 1, head >> 1, head & 1
    where = jnp.stack([ring_place(frame, n), z, y, x, core]).astype(jnp.int32)
    width, cols = out_weight.shape
    heads = width // HD
    f32, bf16 = jnp.float32, jnp.bfloat16
    block = (queries.shape, bf16)
    own = call(split_kernel, (), [keys_values], [block, block], 0)
    keys, values, queries = gather_ring([*own, queries], n)

    def attend(blocks, before=(), flips=(), after=()):
        outs = [((4 if before else len(blocks), ROWS, width), bf16)]
        if flips:
            outs.append(((len(flips) * ROWS, cols), bf16))
        return call(
            functools.partial(attend_kernel, heads, n, blocks, bool(before), flips),
            (where,),
            [*(queries[d] for d in blocks), *keys, *values, *before, *([out_weight] if flips else [])],
            outs,
            4 * len(blocks) * n * ROWS**2 * width,
            after,
        )

    def add(half, own, from_core, *others):
        kernel = functools.partial(sum_kernel, half, len(others))
        return call(kernel, (), [own, from_core, *others], [((ROWS, cols), bf16)], 0)[0]

    def sums(parity, attended, given, after=()):
        from_core = lax.ppermute(given, "heads", [(h, h ^ 1) for h in range(4)])
        (kept,) = call(
            functools.partial(kept_kernel, parity),
            (where,),
            [attended, out_weight],
            [((2 * ROWS, cols), f32)],
            2 * ROWS * width * cols,
            after,
        )
        from_x = lax.ppermute(add(0, kept, from_core), "heads", [(h, h ^ 2) for h in range(4)])
        return add(1, kept, from_core, from_x)

    def send(parity, total):
        order = ring_order(n)
        pairs = []
        for f in range(n):
            for h in range(4):
                distance = 2 * (2 * (h & 1) + (h >> 1)) + parity
                pairs.append((4 * f + h, 4 * order[(ring_place(f, n) - distance) % n] + (f >> 1)))
        return lax.ppermute(total, ("frames", "heads"), pairs)

    others = [(1, 1), (0, 1)]
    (some,) = attend([0, 2, n - 2])
    attended, given = attend([1, 3, n - 3, n - 1], (), others, (some,))
    odd = send(1, sums(1, attended, given))
    attended, given = attend([n // 2], (some,), others, (attended,))
    even = send(0, sums(0, attended, given))
    straight = (head - where[0]) & 1 == 0
    return jnp.concatenate([jnp.where(straight, even, odd), jnp.where(straight, odd, even)], axis=1)


def solution(mesh):
    in_specs = (P("frames", "heads"), P(None, "frames", "heads"), P("heads", "frames"))
    out_specs = P("frames", "heads")
    n, heads = mesh.shape["frames"], mesh.shape["heads"]
    total_frames = n * FR_DEV
    reach = min(reach_cap, (total_frames - 1) // 2)
    every = total_frames == 2 * reach + 2 and heads == 4 and n == 2 * heads
    return jax.shard_map(
        on_device_ring if every else on_device_band,
        mesh=mesh,
        in_specs=in_specs,
        out_specs=out_specs,
        check_vma=False,
    )
```

```python
import functools
import math

import jax
import jax.numpy as jnp
from jax import lax
from jax.experimental import pallas as pl
from jax.experimental.pallas import tpu as pltpu
from jax.sharding import PartitionSpec as P

HD = 128
TPF = 32
FR_DEV = 3
ROWS = FR_DEV * TPF
SCALE = HD ** (-0.5) * math.log2(math.e)


reach_cap = 32


def from_behind(x, axis, by):
    devices = lax.axis_size(axis)
    return lax.ppermute(x, axis, [(i, (i + by) % devices) for i in range(devices)])


def on_device_band(queries, keys_values, out_weight):
    total_frames = lax.axis_size("frames") * FR_DEV
    reach = min(reach_cap, (total_frames - 1) // 2)
    steps = (reach + FR_DEV - 1) // FR_DEV
    width = keys_values.shape[2]
    span = FR_DEV + 2 * reach
    stacked = keys_values.reshape(2, FR_DEV, TPF, width)
    pieces = []
    for offset in range(-steps, steps + 1):
        if offset == 0:
            pieces.append(stacked)
        else:
            pieces.append(from_behind(stacked, "frames", -offset))
    window = jnp.concatenate(pieces, axis=1)
    lower_frame = steps * FR_DEV - reach
    extended = window[:, lower_frame : lower_frame + span]
    keys_ext = extended[0].reshape(span * TPF, width)
    values_ext = extended[1].reshape(span * TPF, width)
    row_frame = jnp.arange(FR_DEV * TPF, dtype=jnp.int32) // TPF
    col_frame = jnp.arange(span * TPF, dtype=jnp.int32) // TPF
    allowed = (col_frame[None, :] >= row_frame[:, None]) & (
        col_frame[None, :] <= row_frame[:, None] + 2 * reach
    )
    results = []
    for head in range(width // HD):
        lower = head * HD
        query_cols = queries[:, lower : lower + HD]
        key_cols = keys_ext[:, lower : lower + HD]
        scores = lax.dot_general(
            query_cols, key_cols, (((1,), (1,)), ((), ())), preferred_element_type=jnp.float32
        )
        scores = scores * HD ** (-0.5)
        top = jnp.max(jnp.where(allowed, scores, -1e30), axis=1, keepdims=True)
        weights = jnp.where(allowed, jnp.exp(scores - top), 0.0)
        probs = (weights / jnp.sum(weights, axis=1, keepdims=True)).astype(jnp.bfloat16)
        results.append(
            jnp.dot(
                probs, values_ext[:, lower : lower + HD], preferred_element_type=jnp.float32
            ).astype(jnp.bfloat16)
        )
    attended = jnp.concatenate(results, axis=1)
    partial_rows = jnp.dot(
        attended,
        lax.all_gather(out_weight, "frames", axis=1, tiled=True),
        preferred_element_type=jnp.float32,
    )
    return lax.psum_scatter(
        partial_rows.astype(jnp.bfloat16), "heads", scatter_dimension=1, tiled=True
    )


def ring_order(n):
    return list(range(0, n, 2)) + list(range(n - 1, 0, -2))


def ring_place(f, n):
    return (f >> 1) + (f & 1) * (n - 1 - (f >> 1) * 2)


def hop(x, n, by):
    order = ring_order(n)
    pairs = []
    for i in range(n):
        for h in range(4):
            pairs.append((4 * order[i] + h, 4 * order[(i + by * (1 - 2 * (h & 1))) % n] + h))
    return lax.ppermute(x, ("frames", "heads"), pairs)


def held(block, after):
    return call(copy_kernel, (), [block], [(block.shape, block.dtype)], 0, after)[0]


def gather_ring(keys, values, queries, n):
    found = [[block] + [None] * (n - 1) for block in (keys, values, queries)]
    far = n // 2
    for j, blocks in enumerate(found):
        for step in range(1, far + 1):
            for by in (1, -1):
                if step < far or by == (1, -1, None)[j]:
                    block = blocks[by * (step - 1) % n]
                    if j == 2 and step > 1:
                        near = (far - 1, far + 1) if step == 2 else (far,)
                        block = held(block, [found[i][d] for i in range(2) for d in near])
                    blocks[by * step % n] = hop(block, n, by)
    return found


def ring_distance(at_ref, owner, n):
    place, core = at_ref[0], at_ref[4]
    return (place - owner) * (1 - 2 * core) & (n - 1)


def frame_marks(at_ref, blocks, n):
    place, core = at_ref[0], at_ref[4]
    lane = lax.broadcasted_iota(jnp.int32, (TPF, HD), 1)
    marks = []
    for block in blocks:
        owner = (place - block * (1 - 2 * core)) & (n - 1)
        frame = FR_DEV * ring_distance(at_ref, owner ^ 2, n)
        for g in range(FR_DEV):
            marks.append((lane == frame + g) | (lane >= n * FR_DEV))
    return jnp.concatenate([jnp.where(mark, 1.0, 0.0) for mark in marks], axis=0).astype(jnp.bfloat16)


def key_marks(blocks, padding, n):
    lane = lax.broadcasted_iota(jnp.int32, (TPF, HD), 1)
    frames = [FR_DEV * block + g for block in blocks for g in range(FR_DEV)] + [n * FR_DEV] * (padding // TPF)
    return jnp.concatenate([jnp.where(lane == frame, -1e30, 0.0) for frame in frames], axis=0).astype(jnp.bfloat16)


def rows_of(refs, cols, padding=0):
    pieces = [ref[:, cols] for ref in refs]
    if padding:
        pieces.append(jnp.zeros((padding, HD), jnp.bfloat16))
    return jnp.concatenate(pieces, axis=0)


def scores_of(queries, keys):
    return lax.dot_general(queries, keys, (((1,), (1,)), ((), ())), preferred_element_type=jnp.float32)


def soften(scores, floor=None):
    weights, tops = [], []
    for r in range(0, scores.shape[0], TPF):
        parts = [scores[r : r + TPF, c : c + HD] for c in range(0, scores.shape[1], HD)]
        top = jnp.max(functools.reduce(jnp.maximum, parts), axis=1, keepdims=True)
        top = jnp.broadcast_to(top, (TPF, HD))
        if floor is not None:
            top = jnp.maximum(top, floor[r : r + TPF])
        weights.append(jnp.concatenate([jnp.exp2((p - top) * SCALE).astype(jnp.bfloat16) for p in parts], axis=1))
        tops.append(top)
    return jnp.concatenate(weights, axis=0), jnp.concatenate(tops, axis=0)


def mix(weights, values):
    ones = jnp.ones(values.shape, values.dtype)
    mixed = jnp.dot(weights, jnp.concatenate([values, ones], axis=1), preferred_element_type=jnp.float32)
    return mixed[:, :HD], mixed[:, HD:]


def ahead(scores, heads):
    columns = [slice(head * HD, (head + 1) * HD) for head in range(heads)]
    now = scores(columns[0])
    for head, cols in enumerate(columns):
        later = scores(columns[head + 1]) if head + 1 < heads else None
        yield head, cols, now
        now = later


def copy_kernel(from_ref, *refs):
    refs[-1][...] = from_ref[...]


def split_kernel(kv_ref, keys_ref, values_ref):
    keys_ref[...] = kv_ref[0]
    values_ref[...] = kv_ref[1]


def blocks_for(at_ref, parity, flips):
    x, core = at_ref[3], at_ref[4]
    found = []
    for flip_x, flip_core in flips:
        m = 2 * (core ^ flip_core) + (x ^ flip_x)
        found.append(jnp.where(core == 0, m, (-m - parity) & 3))
    return found


def attend_kernel(heads, n, blocks, before, flips, at_ref, *refs):
    count = len(blocks)
    query_refs, refs = refs[:count], refs[count:]
    key_refs, value_refs, refs = refs[:n], refs[n : 2 * n], refs[2 * n :]
    attended_ref = refs[-2] if flips else refs[-1]
    marks = frame_marks(at_ref, blocks, n)
    keys_marks = key_marks(range(n), 0, n)
    for source, place in before:
        attended_ref[place] = refs[0][source]
    taken = [place for _, place in before]
    places = [place for place in range(attended_ref.shape[0]) if place not in taken]

    def scores(cols):
        queries = jnp.concatenate([rows_of(query_refs, cols), marks], axis=1)
        return scores_of(queries, jnp.concatenate([rows_of(key_refs, cols), keys_marks], axis=1))

    for _, cols, now in ahead(scores, heads):
        weights, _ = soften(now)
        mixed, total = mix(weights, rows_of(value_refs, cols))
        result = (mixed / total).astype(jnp.bfloat16)
        for i, place in enumerate(places):
            attended_ref[place, :, cols] = result[i * ROWS : (i + 1) * ROWS]
    if flips:
        w_ref, out_ref = refs[1 if before else 0], refs[-1]
        out_ref[...] = times_w(at_ref, blocks[0] % 2, flips, attended_ref, w_ref).astype(out_ref.dtype)


def times_w(at_ref, parity, flips, attended_ref, w_ref):
    rows = jnp.concatenate([attended_ref[block] for block in blocks_for(at_ref, parity, flips)], axis=0)
    return jnp.dot(rows, w_ref[...], preferred_element_type=jnp.float32)


def kept_kernel(parity, at_ref, attended_ref, w_ref, out_ref):
    out_ref[...] = times_w(at_ref, parity, [(1, 0), (0, 0)], attended_ref, w_ref)


def sum_kernel(half, others, own_ref, from_core_ref, *refs):
    rows = slice(half * ROWS, (half + 1) * ROWS)
    total = own_ref[rows] + from_core_ref[rows].astype(jnp.float32)
    for ref in refs[:others]:
        total += ref[...].astype(jnp.float32)
    refs[-1][...] = total.astype(refs[-1].dtype)


def call(kernel, scalars, operands, outs, flops, after=()):
    vmem = pl.BlockSpec(memory_space=pltpu.VMEM)
    return pl.pallas_call(
        kernel,
        out_shape=[jax.ShapeDtypeStruct(shape, dtype) for shape, dtype in outs],
        in_specs=[pl.BlockSpec(memory_space=pltpu.SMEM)] * len(scalars)
        + [vmem] * len(operands)
        + [pl.BlockSpec(memory_space=pl.ANY)] * len(after),
        out_specs=[vmem] * len(outs),
        compiler_params=pltpu.CompilerParams(vmem_limit_bytes=20 * 1024 * 1024),
        cost_estimate=pl.CostEstimate(flops=flops, bytes_accessed=0, transcendentals=0),
    )(*scalars, *operands, *after)


def on_device_ring(queries, keys_values, out_weight):
    n = lax.axis_size("frames")
    frame, head = lax.axis_index("frames"), lax.axis_index("heads")
    z, y, x, core = frame >> 1, frame & 1, head >> 1, head & 1
    where = jnp.stack([ring_place(frame, n), z, y, x, core]).astype(jnp.int32)
    width, cols = out_weight.shape
    heads = width // HD
    f32, bf16 = jnp.float32, jnp.bfloat16
    block = (queries.shape, bf16)
    own = call(split_kernel, (), [keys_values], [block, block], 0)
    keys, values, queries = gather_ring(*own, queries, n)

    def attend(blocks, results=(), before=(), flips=(), after=()):
        outs = [((len(before) + len(blocks), ROWS, width), bf16)]
        if flips:
            outs.append(((len(flips) * ROWS, cols), bf16))
        return call(
            functools.partial(attend_kernel, heads, n, blocks, before, flips),
            (where,),
            [*(queries[d] for d in blocks), *keys, *values, *results, *([out_weight] if flips else [])],
            outs,
            4 * len(blocks) * n * ROWS**2 * width,
            after,
        )

    def add(half, own, from_core, *others):
        kernel = functools.partial(sum_kernel, half, len(others))
        return call(kernel, (), [own, from_core, *others], [((ROWS, cols), bf16)], 0)[0]

    def sums(parity, attended, given, after=()):
        from_core = lax.ppermute(given, "heads", [(h, h ^ 1) for h in range(4)])
        (kept,) = call(
            functools.partial(kept_kernel, parity),
            (where,),
            [attended, out_weight],
            [((2 * ROWS, cols), f32)],
            2 * ROWS * width * cols,
            after,
        )
        from_x = lax.ppermute(add(0, kept, from_core), "heads", [(h, h ^ 2) for h in range(4)])
        return add(1, kept, from_core, from_x)

    def send(parity, total):
        order = ring_order(n)
        pairs = []
        for f in range(n):
            for h in range(4):
                distance = 2 * (2 * (h & 1) + (h >> 1)) + parity
                pairs.append((4 * f + h, 4 * order[(ring_place(f, n) - distance) % n] + (f >> 1)))
        return lax.ppermute(total, ("frames", "heads"), pairs)

    others = [(1, 1), (0, 1)]
    near = attend([0, 1, n - 1])
    queries[n // 2] = hop(held(queries[n // 2 - 1], near), n, 1)
    attended, given = attend([3, n - 3], near, [(1, 0), (2, 3)], others)
    odd = send(1, sums(1, attended, given))
    even = attend([2, n - 2], near, [(0, 0)])
    attended, given = attend([n // 2], even, [(0, 0), (1, 1), (2, 3)], others, (attended,))
    even = send(0, sums(0, attended, given))
    straight = (head - where[0]) & 1 == 0
    return jnp.concatenate([jnp.where(straight, even, odd), jnp.where(straight, odd, even)], axis=1)


def solution(mesh):
    in_specs = (P("frames", "heads"), P(None, "frames", "heads"), P("heads", "frames"))
    out_specs = P("frames", "heads")
    n, heads = mesh.shape["frames"], mesh.shape["heads"]
    total_frames = n * FR_DEV
    reach = min(reach_cap, (total_frames - 1) // 2)
    every = total_frames == 2 * reach + 2 and heads == 4 and n == 2 * heads
    return jax.shard_map(
        on_device_ring if every else on_device_band,
        mesh=mesh,
        in_specs=in_specs,
        out_specs=out_specs,
        check_vma=False,
    )
```

```python
import functools
import math

import jax
import jax.numpy as jnp
from jax import lax
from jax.experimental import pallas as pl
from jax.experimental.pallas import tpu as pltpu
from jax.sharding import PartitionSpec as P

HD = 128
TPF = 32
FR_DEV = 3
ROWS = FR_DEV * TPF
SCALE = HD ** (-0.5) * math.log2(math.e)


reach_cap = 32


def from_behind(x, axis, by):
    devices = lax.axis_size(axis)
    return lax.ppermute(x, axis, [(i, (i + by) % devices) for i in range(devices)])


def on_device_band(queries, keys_values, out_weight):
    total_frames = lax.axis_size("frames") * FR_DEV
    reach = min(reach_cap, (total_frames - 1) // 2)
    steps = (reach + FR_DEV - 1) // FR_DEV
    width = keys_values.shape[2]
    span = FR_DEV + 2 * reach
    stacked = keys_values.reshape(2, FR_DEV, TPF, width)
    pieces = []
    for offset in range(-steps, steps + 1):
        if offset == 0:
            pieces.append(stacked)
        else:
            pieces.append(from_behind(stacked, "frames", -offset))
    window = jnp.concatenate(pieces, axis=1)
    lower_frame = steps * FR_DEV - reach
    extended = window[:, lower_frame : lower_frame + span]
    keys_ext = extended[0].reshape(span * TPF, width)
    values_ext = extended[1].reshape(span * TPF, width)
    row_frame = jnp.arange(FR_DEV * TPF, dtype=jnp.int32) // TPF
    col_frame = jnp.arange(span * TPF, dtype=jnp.int32) // TPF
    allowed = (col_frame[None, :] >= row_frame[:, None]) & (
        col_frame[None, :] <= row_frame[:, None] + 2 * reach
    )
    results = []
    for head in range(width // HD):
        lower = head * HD
        query_cols = queries[:, lower : lower + HD]
        key_cols = keys_ext[:, lower : lower + HD]
        scores = lax.dot_general(
            query_cols, key_cols, (((1,), (1,)), ((), ())), preferred_element_type=jnp.float32
        )
        scores = scores * HD ** (-0.5)
        top = jnp.max(jnp.where(allowed, scores, -1e30), axis=1, keepdims=True)
        weights = jnp.where(allowed, jnp.exp(scores - top), 0.0)
        probs = (weights / jnp.sum(weights, axis=1, keepdims=True)).astype(jnp.bfloat16)
        results.append(
            jnp.dot(
                probs, values_ext[:, lower : lower + HD], preferred_element_type=jnp.float32
            ).astype(jnp.bfloat16)
        )
    attended = jnp.concatenate(results, axis=1)
    partial_rows = jnp.dot(
        attended,
        lax.all_gather(out_weight, "frames", axis=1, tiled=True),
        preferred_element_type=jnp.float32,
    )
    return lax.psum_scatter(
        partial_rows.astype(jnp.bfloat16), "heads", scatter_dimension=1, tiled=True
    )


def ring_order(n):
    return list(range(0, n, 2)) + list(range(n - 1, 0, -2))


def ring_place(f, n):
    return (f >> 1) + (f & 1) * (n - 1 - (f >> 1) * 2)


def hop(x, n, by):
    order = ring_order(n)
    pairs = []
    for i in range(n):
        for h in range(4):
            pairs.append((4 * order[i] + h, 4 * order[(i + by * (1 - 2 * (h & 1))) % n] + h))
    return lax.ppermute(x, ("frames", "heads"), pairs)


def gather_ring(streams, n):
    found = [[block] + [None] * (n - 1) for block in streams]
    for step in range(1, n // 2 + 1):
        for j, blocks in enumerate(found):
            for by in (1, -1):
                if step < n // 2 or (j % 2 == 0) == (by == 1):
                    blocks[by * step % n] = hop(blocks[by * (step - 1) % n], n, by)
    return found


def ring_distance(at_ref, owner, n):
    place, core = at_ref[0], at_ref[4]
    return (place - owner) * (1 - 2 * core) & (n - 1)


def frame_marks(at_ref, blocks, n):
    place, core = at_ref[0], at_ref[4]
    lane = lax.broadcasted_iota(jnp.int32, (TPF, HD), 1)
    marks = []
    for block in blocks:
        owner = (place - block * (1 - 2 * core)) & (n - 1)
        frame = FR_DEV * ring_distance(at_ref, owner ^ 2, n)
        for g in range(FR_DEV):
            marks.append((lane == frame + g) | (lane >= n * FR_DEV))
    return jnp.concatenate([jnp.where(mark, 1.0, 0.0) for mark in marks], axis=0).astype(jnp.bfloat16)


def key_marks(blocks, padding, n):
    lane = lax.broadcasted_iota(jnp.int32, (TPF, HD), 1)
    frames = [FR_DEV * block + g for block in blocks for g in range(FR_DEV)] + [n * FR_DEV] * (padding // TPF)
    return jnp.concatenate([jnp.where(lane == frame, -1e30, 0.0) for frame in frames], axis=0).astype(jnp.bfloat16)


def rows_of(refs, cols, padding=0):
    pieces = [ref[:, cols] for ref in refs]
    if padding:
        pieces.append(jnp.zeros((padding, HD), jnp.bfloat16))
    return jnp.concatenate(pieces, axis=0)


def scores_of(queries, keys):
    return lax.dot_general(queries, keys, (((1,), (1,)), ((), ())), preferred_element_type=jnp.float32)


def soften(scores, floor=None):
    weights, tops = [], []
    for r in range(0, scores.shape[0], TPF):
        parts = [scores[r : r + TPF, c : c + HD] for c in range(0, scores.shape[1], HD)]
        top = jnp.max(functools.reduce(jnp.maximum, parts), axis=1, keepdims=True)
        top = jnp.broadcast_to(top, (TPF, HD))
        if floor is not None:
            top = jnp.maximum(top, floor[r : r + TPF])
        weights.append(jnp.concatenate([jnp.exp2((p - top) * SCALE).astype(jnp.bfloat16) for p in parts], axis=1))
        tops.append(top)
    return jnp.concatenate(weights, axis=0), jnp.concatenate(tops, axis=0)


def mix(weights, values):
    ones = jnp.ones(values.shape, values.dtype)
    mixed = jnp.dot(weights, jnp.concatenate([values, ones], axis=1), preferred_element_type=jnp.float32)
    return mixed[:, :HD], mixed[:, HD:]


PATTERNS = ((3, 0, 2, 1), (1, 3, 1, 3), (2, 1, 3, 0), (0, 2, 0, 2))


def look_up(table, index):
    code = sum(entry << (2 * i) for i, entry in enumerate(table))
    return (jnp.int32(code - (code >> 31 << 32)) >> (2 * index)) & 3


def slot_blocks(at_ref, flip_x, flip_core, n):
    z, y, x, core = (at_ref[i] for i in range(1, 5))
    blocks = []
    for slot in range(2):
        to = look_up(sum(PATTERNS, ()), 4 * ((slot ^ y) + 2 * (x ^ flip_x)) + z)
        owner = to + (core ^ flip_core) * (n - 1 - 2 * to)
        blocks.append(ring_distance(at_ref, owner, n))
    return blocks


def ahead(scores, heads):
    columns = [slice(head * HD, (head + 1) * HD) for head in range(heads)]
    now = scores(columns[0])
    for head, cols in enumerate(columns):
        later = scores(columns[head + 1]) if head + 1 < heads else None
        yield head, cols, now
        now = later


def split_kernel(kv_ref, keys_ref, values_ref):
    keys_ref[...] = kv_ref[0]
    values_ref[...] = kv_ref[1]


def rows_kernel(n, *refs):
    for d in range(n):
        refs[n][d] = refs[d][...]


def near_kernel(heads, n, at_ref, rows_ref, *refs):
    near = [d for d in range(n) if d != n // 2]
    key_refs, value_refs, (mixed_ref, sum_ref, top_ref) = refs[: n - 1], refs[n - 1 : -3], refs[-3:]
    marks = frame_marks(at_ref, range(n), n)
    keys_marks = key_marks(near, ROWS, n)

    def scores(cols):
        queries = jnp.concatenate([rows_ref[:, :, cols].reshape(n * ROWS, HD), marks], axis=1)
        return scores_of(queries, jnp.concatenate([rows_of(key_refs, cols, ROWS), keys_marks], axis=1))

    for head, cols, now in ahead(scores, heads):
        weights, top = soften(now)
        mixed, total = mix(weights, rows_of(value_refs, cols, ROWS))
        for d in range(n):
            rows = slice(d * ROWS, (d + 1) * ROWS)
            mixed_ref[head, d], sum_ref[head, d], top_ref[head, d] = mixed[rows], total[rows], top[rows]


def finish_kernel(heads, n, flips, at_ref, rows_ref, mixed_ref, sum_ref, top_ref, keys_ref, values_ref, w_ref, *refs):
    blocks = [block for flip in flips for block in slot_blocks(at_ref, *flip, n)]
    marks = frame_marks(at_ref, blocks, n)
    keys_marks = key_marks([n // 2], TPF, n)

    def of(ref, head):
        return jnp.concatenate([ref[head, block] for block in blocks], axis=0)

    columns = [slice(head * HD, (head + 1) * HD) for head in range(heads)]
    scores, attended = [], []
    for cols in columns:
        queries = jnp.concatenate([rows_ref[block, :, cols] for block in blocks], axis=0)
        keys = jnp.concatenate([rows_of([keys_ref], cols, TPF), keys_marks], axis=1)
        scores.append(scores_of(jnp.concatenate([queries, marks], axis=1), keys))
    softened = [soften(now, of(top_ref, head)) for head, now in enumerate(scores)]
    more = [mix(weights, rows_of([values_ref], cols, TPF)) for (weights, _), cols in zip(softened, columns)]
    for head, ((_, top), (mixed, total)) in enumerate(zip(softened, more)):
        kept = jnp.exp2((of(top_ref, head) - top) * SCALE)
        mixed, total = mixed + of(mixed_ref, head) * kept, total + of(sum_ref, head) * kept
        attended.append((mixed / total).astype(jnp.bfloat16))
    rows = jnp.concatenate(attended, axis=1)
    refs[-1][...] = jnp.dot(rows, w_ref[...], preferred_element_type=jnp.float32).astype(refs[-1].dtype)


def sum_kernel(rows, kept_ref, from_core_ref, from_x_ref, total_ref):
    total = kept_ref[rows] + from_core_ref[1, rows].astype(jnp.float32) + from_x_ref[...].astype(jnp.float32)
    total_ref[...] = total.astype(total_ref.dtype)


def call(kernel, scalars, operands, outs, flops, after=()):
    vmem = pl.BlockSpec(memory_space=pltpu.VMEM)
    return pl.pallas_call(
        kernel,
        out_shape=[jax.ShapeDtypeStruct(shape, dtype) for shape, dtype in outs],
        in_specs=[pl.BlockSpec(memory_space=pltpu.SMEM)] * len(scalars)
        + [vmem] * len(operands)
        + [pl.BlockSpec(memory_space=pl.ANY)] * len(after),
        out_specs=[vmem] * len(outs),
        compiler_params=pltpu.CompilerParams(vmem_limit_bytes=20 * 1024 * 1024),
        cost_estimate=pl.CostEstimate(flops=flops, bytes_accessed=0, transcendentals=0),
    )(*scalars, *operands, *after)


def on_device_ring(queries, keys_values, out_weight):
    n = lax.axis_size("frames")
    frame, head = lax.axis_index("frames"), lax.axis_index("heads")
    z, y, x, core = frame >> 1, frame & 1, head >> 1, head & 1
    where = jnp.stack([ring_place(frame, n), z, y, x, core]).astype(jnp.int32)
    width, cols = out_weight.shape
    heads = width // HD
    f32, bf16 = jnp.float32, jnp.bfloat16
    block = (queries.shape, bf16)
    own = call(split_kernel, (), [keys_values], [block, block], 0)
    queries, keys, values = gather_ring([queries, *own], n)
    (rows,) = call(functools.partial(rows_kernel, n), (), queries, [((n, ROWS, width), bf16)], 0)
    far = n // 2
    state = call(
        functools.partial(near_kernel, heads, n),
        (where,),
        [rows, *(blocks[d] for blocks in (keys, values) for d in range(n) if d != far)],
        [((heads, n, ROWS, HD), f32)] * 3,
        4 * n * (n - 1) * ROWS**2 * width,
    )

    def finish(flips, dtype, after=()):
        (sums,) = call(
            functools.partial(finish_kernel, heads, n, flips),
            (where,),
            [rows, *state, keys[far], values[far], out_weight],
            [((len(flips) * 2 * ROWS, cols), dtype)],
            n * ROWS * width * cols,
            after,
        )
        return sums.reshape(len(flips), 2 * ROWS, cols)

    given = finish([(1, 1), (0, 1)], bf16)
    from_core = lax.ppermute(given, "heads", [(h, h ^ 1) for h in range(4)])
    sums = finish([(1, 0)], f32, (given,))[0]
    parts = [slice(slot * ROWS, (slot + 1) * ROWS) for slot in range(2)]
    given = [(sums[part] + from_core[0, part].astype(f32)).astype(bf16) for part in parts]
    from_x = [lax.ppermute(block, "heads", [(h, h ^ 2) for h in range(4)]) for block in given]
    kept = finish([(0, 0)], f32, given)[0]
    arrived = []
    for slot, part in enumerate(parts):
        pairs = []
        for f in range(n):
            for h in range(4):
                to = PATTERNS[(slot ^ (f & 1)) + 2 * (h >> 1)][f >> 1]
                pairs.append((4 * f + h, 4 * (2 * to + (h & 1)) + (f >> 1)))
        (total,) = call(
            functools.partial(sum_kernel, part), (), [kept, from_core, from_x[slot]], [((ROWS, cols), bf16)], 0
        )
        arrived.append(lax.ppermute(total, ("frames", "heads"), pairs))
    patterns = [[p[source] for p in PATTERNS].index(to) for source in range(4) for to in range(4)]
    straight = look_up(patterns, 4 * head + z) & 1 == 0
    low, high = arrived
    return jnp.concatenate([jnp.where(straight, low, high), jnp.where(straight, high, low)], axis=1)


def solution(mesh):
    in_specs = (P("frames", "heads"), P(None, "frames", "heads"), P("heads", "frames"))
    out_specs = P("frames", "heads")
    n, heads = mesh.shape["frames"], mesh.shape["heads"]
    total_frames = n * FR_DEV
    reach = min(reach_cap, (total_frames - 1) // 2)
    every = total_frames == 2 * reach + 2 and heads == 4 and n == 2 * heads
    return jax.shard_map(
        on_device_ring if every else on_device_band,
        mesh=mesh,
        in_specs=in_specs,
        out_specs=out_specs,
        check_vma=False,
    )
```

```python
import functools
import math

import jax
import jax.numpy as jnp
from jax import lax
from jax.experimental import pallas as pl
from jax.experimental.pallas import tpu as pltpu
from jax.sharding import PartitionSpec as P

HD = 128
TPF = 32
FR_DEV = 3
ROWS = FR_DEV * TPF
SCALE = HD ** (-0.5) * math.log2(math.e)


reach_cap = 32


def from_behind(x, axis, by):
    devices = lax.axis_size(axis)
    return lax.ppermute(x, axis, [(i, (i + by) % devices) for i in range(devices)])


def on_device_band(queries, keys_values, out_weight):
    total_frames = lax.axis_size("frames") * FR_DEV
    reach = min(reach_cap, (total_frames - 1) // 2)
    steps = (reach + FR_DEV - 1) // FR_DEV
    width = keys_values.shape[2]
    span = FR_DEV + 2 * reach
    stacked = keys_values.reshape(2, FR_DEV, TPF, width)
    pieces = []
    for offset in range(-steps, steps + 1):
        if offset == 0:
            pieces.append(stacked)
        else:
            pieces.append(from_behind(stacked, "frames", -offset))
    window = jnp.concatenate(pieces, axis=1)
    lower_frame = steps * FR_DEV - reach
    extended = window[:, lower_frame : lower_frame + span]
    keys_ext = extended[0].reshape(span * TPF, width)
    values_ext = extended[1].reshape(span * TPF, width)
    row_frame = jnp.arange(FR_DEV * TPF, dtype=jnp.int32) // TPF
    col_frame = jnp.arange(span * TPF, dtype=jnp.int32) // TPF
    allowed = (col_frame[None, :] >= row_frame[:, None]) & (
        col_frame[None, :] <= row_frame[:, None] + 2 * reach
    )
    results = []
    for head in range(width // HD):
        lower = head * HD
        query_cols = queries[:, lower : lower + HD]
        key_cols = keys_ext[:, lower : lower + HD]
        scores = lax.dot_general(
            query_cols, key_cols, (((1,), (1,)), ((), ())), preferred_element_type=jnp.float32
        )
        scores = scores * HD ** (-0.5)
        top = jnp.max(jnp.where(allowed, scores, -1e30), axis=1, keepdims=True)
        weights = jnp.where(allowed, jnp.exp(scores - top), 0.0)
        probs = (weights / jnp.sum(weights, axis=1, keepdims=True)).astype(jnp.bfloat16)
        results.append(
            jnp.dot(
                probs, values_ext[:, lower : lower + HD], preferred_element_type=jnp.float32
            ).astype(jnp.bfloat16)
        )
    attended = jnp.concatenate(results, axis=1)
    partial_rows = jnp.dot(
        attended,
        lax.all_gather(out_weight, "frames", axis=1, tiled=True),
        preferred_element_type=jnp.float32,
    )
    return lax.psum_scatter(
        partial_rows.astype(jnp.bfloat16), "heads", scatter_dimension=1, tiled=True
    )


def ring_order(n):
    return list(range(0, n, 2)) + list(range(n - 1, 0, -2))


def ring_place(f, n):
    return (f >> 1) + (f & 1) * (n - 1 - (f >> 1) * 2)


def hop(x, n, by):
    order = ring_order(n)
    pairs = []
    for i in range(n):
        for h in range(4):
            pairs.append((4 * order[i] + h, 4 * order[(i + by * (1 - 2 * (h & 1))) % n] + h))
    return lax.ppermute(x, ("frames", "heads"), pairs)


def gather_ring(streams, n):
    found = [[block] + [None] * (n - 1) for block in streams]
    for step in range(1, n // 2 + 1):
        for j, blocks in enumerate(found):
            for by in (1, -1):
                if step < n // 2 or (j % 2 == 0) == (by == 1):
                    blocks[by * step % n] = hop(blocks[by * (step - 1) % n], n, by)
    return found


def ring_distance(at_ref, owner, n):
    place, core = at_ref[0], at_ref[4]
    return (place - owner) * (1 - 2 * core) & (n - 1)


def frame_marks(at_ref, blocks, n):
    place, core = at_ref[0], at_ref[4]
    lane = lax.broadcasted_iota(jnp.int32, (TPF, HD), 1)
    marks = []
    for block in blocks:
        owner = (place - block * (1 - 2 * core)) & (n - 1)
        frame = FR_DEV * ring_distance(at_ref, owner ^ 2, n)
        for g in range(FR_DEV):
            marks.append((lane == frame + g) | (lane >= n * FR_DEV))
    return jnp.concatenate([jnp.where(mark, 1.0, 0.0) for mark in marks], axis=0).astype(jnp.bfloat16)


def key_marks(blocks, padding, n):
    lane = lax.broadcasted_iota(jnp.int32, (TPF, HD), 1)
    frames = [FR_DEV * block + g for block in blocks for g in range(FR_DEV)] + [n * FR_DEV] * (padding // TPF)
    return jnp.concatenate([jnp.where(lane == frame, -1e30, 0.0) for frame in frames], axis=0).astype(jnp.bfloat16)


def rows_of(refs, cols, padding=0):
    pieces = [ref[:, cols] for ref in refs]
    if padding:
        pieces.append(jnp.zeros((padding, HD), jnp.bfloat16))
    return jnp.concatenate(pieces, axis=0)


def scores_of(queries, keys):
    return lax.dot_general(queries, keys, (((1,), (1,)), ((), ())), preferred_element_type=jnp.float32)


def soften(scores, floor=None):
    weights, tops = [], []
    for r in range(0, scores.shape[0], TPF):
        parts = [scores[r : r + TPF, c : c + HD] for c in range(0, scores.shape[1], HD)]
        top = jnp.max(functools.reduce(jnp.maximum, parts), axis=1, keepdims=True)
        top = jnp.broadcast_to(top, (TPF, HD))
        if floor is not None:
            top = jnp.maximum(top, floor[r : r + TPF])
        weights.append(jnp.concatenate([jnp.exp2(((p - top) * SCALE).astype(jnp.bfloat16)) for p in parts], axis=1))
        tops.append(top)
    return jnp.concatenate(weights, axis=0), jnp.concatenate(tops, axis=0)


def mix(weights, values):
    ones = jnp.ones(values.shape, values.dtype)
    mixed = jnp.dot(weights, jnp.concatenate([values, ones], axis=1), preferred_element_type=jnp.float32)
    return mixed[:, :HD], mixed[:, HD:]


PATTERNS = ((3, 0, 2, 1), (1, 3, 1, 3), (2, 1, 3, 0), (0, 2, 0, 2))


def look_up(table, index):
    code = sum(entry << (2 * i) for i, entry in enumerate(table))
    return (jnp.int32(code - (code >> 31 << 32)) >> (2 * index)) & 3


def slot_blocks(at_ref, flip_x, flip_core, n):
    z, y, x, core = (at_ref[i] for i in range(1, 5))
    blocks = []
    for slot in range(2):
        to = look_up(sum(PATTERNS, ()), 4 * ((slot ^ y) + 2 * (x ^ flip_x)) + z)
        owner = to + (core ^ flip_core) * (n - 1 - 2 * to)
        blocks.append(ring_distance(at_ref, owner, n))
    return blocks


def ahead(scores, heads):
    columns = [slice(head * HD, (head + 1) * HD) for head in range(heads)]
    now = scores(columns[0])
    for head, cols in enumerate(columns):
        later = scores(columns[head + 1]) if head + 1 < heads else None
        yield head, cols, now
        now = later


def split_kernel(kv_ref, keys_ref, values_ref):
    keys_ref[...] = kv_ref[0]
    values_ref[...] = kv_ref[1]


def rows_kernel(n, *refs):
    for d in range(n):
        refs[n][d] = refs[d][...]


def near_kernel(heads, n, at_ref, rows_ref, *refs):
    near = [d for d in range(n) if d != n // 2]
    key_refs, value_refs, (mixed_ref, sum_ref, top_ref) = refs[: n - 1], refs[n - 1 : -3], refs[-3:]
    marks = frame_marks(at_ref, range(n), n)
    keys_marks = key_marks(near, ROWS, n)

    def scores(cols):
        queries = jnp.concatenate([rows_ref[:, :, cols].reshape(n * ROWS, HD), marks], axis=1)
        return scores_of(queries, jnp.concatenate([rows_of(key_refs, cols, ROWS), keys_marks], axis=1))

    for head, cols, now in ahead(scores, heads):
        weights, top = soften(now)
        mixed, total = mix(weights, rows_of(value_refs, cols, ROWS))
        for d in range(n):
            rows = slice(d * ROWS, (d + 1) * ROWS)
            mixed_ref[head, d], sum_ref[head, d], top_ref[head, d] = mixed[rows], total[rows], top[rows]


def finish_kernel(heads, n, flips, at_ref, rows_ref, mixed_ref, sum_ref, top_ref, keys_ref, values_ref, w_ref, *refs):
    blocks = [block for flip in flips for block in slot_blocks(at_ref, *flip, n)]
    marks = frame_marks(at_ref, blocks, n)
    keys_marks = key_marks([n // 2], TPF, n)

    def of(ref, head):
        return jnp.concatenate([ref[head, block] for block in blocks], axis=0)

    columns = [slice(head * HD, (head + 1) * HD) for head in range(heads)]
    scores, attended = [], []
    for cols in columns:
        queries = jnp.concatenate([rows_ref[block, :, cols] for block in blocks], axis=0)
        keys = jnp.concatenate([rows_of([keys_ref], cols, TPF), keys_marks], axis=1)
        scores.append(scores_of(jnp.concatenate([queries, marks], axis=1), keys))
    softened = [soften(now, of(top_ref, head)) for head, now in enumerate(scores)]
    more = [mix(weights, rows_of([values_ref], cols, TPF)) for (weights, _), cols in zip(softened, columns)]
    for head, ((_, top), (mixed, total)) in enumerate(zip(softened, more)):
        kept = jnp.exp2((of(top_ref, head) - top) * SCALE)
        mixed, total = mixed + of(mixed_ref, head) * kept, total + of(sum_ref, head) * kept
        attended.append((mixed / total).astype(jnp.bfloat16))
    rows = jnp.concatenate(attended, axis=1)
    result = jnp.dot(rows, w_ref[...], preferred_element_type=jnp.float32)
    for i, out_ref in enumerate(refs[-len(flips) :]):
        out_ref[...] = result[2 * i * ROWS : 2 * (i + 1) * ROWS].astype(out_ref.dtype)


def sum_kernel(rows, kept_ref, from_core_ref, from_x_ref, total_ref):
    total = kept_ref[rows] + from_core_ref[rows].astype(jnp.float32) + from_x_ref[...].astype(jnp.float32)
    total_ref[...] = total.astype(total_ref.dtype)


def call(kernel, scalars, operands, outs, flops, after=()):
    vmem = pl.BlockSpec(memory_space=pltpu.VMEM)
    return pl.pallas_call(
        kernel,
        out_shape=[jax.ShapeDtypeStruct(shape, dtype) for shape, dtype in outs],
        in_specs=[pl.BlockSpec(memory_space=pltpu.SMEM)] * len(scalars)
        + [vmem] * len(operands)
        + [pl.BlockSpec(memory_space=pl.ANY)] * len(after),
        out_specs=[vmem] * len(outs),
        compiler_params=pltpu.CompilerParams(vmem_limit_bytes=20 * 1024 * 1024),
        cost_estimate=pl.CostEstimate(flops=flops, bytes_accessed=0, transcendentals=0),
    )(*scalars, *operands, *after)


def on_device_ring(queries, keys_values, out_weight):
    n = lax.axis_size("frames")
    frame, head = lax.axis_index("frames"), lax.axis_index("heads")
    z, y, x, core = frame >> 1, frame & 1, head >> 1, head & 1
    where = jnp.stack([ring_place(frame, n), z, y, x, core]).astype(jnp.int32)
    width, cols = out_weight.shape
    heads = width // HD
    f32, bf16 = jnp.float32, jnp.bfloat16
    block = (queries.shape, bf16)
    own = call(split_kernel, (), [keys_values], [block, block], 0)
    queries, keys, values = gather_ring([queries, *own], n)
    (rows,) = call(functools.partial(rows_kernel, n), (), queries, [((n, ROWS, width), bf16)], 0)
    far = n // 2
    state = call(
        functools.partial(near_kernel, heads, n),
        (where,),
        [rows, *(blocks[d] for blocks in (keys, values) for d in range(n) if d != far)],
        [((heads, n, ROWS, HD), f32)] * 3,
        4 * n * (n - 1) * ROWS**2 * width,
    )

    def finish(flips, dtype, after=()):
        return call(
            functools.partial(finish_kernel, heads, n, flips),
            (where,),
            [rows, *state, keys[far], values[far], out_weight],
            [((2 * ROWS, cols), dtype)] * len(flips),
            n * ROWS * width * cols,
            after,
        )

    given = finish([(1, 1), (0, 1)], bf16)
    from_core = [lax.ppermute(block, "heads", [(h, h ^ 1) for h in range(4)]) for block in given]
    sums = finish([(1, 0)], f32, given)[0]
    parts = [slice(slot * ROWS, (slot + 1) * ROWS) for slot in range(2)]
    given = [(sums[part] + from_core[0][part].astype(f32)).astype(bf16) for part in parts]
    from_x = [lax.ppermute(block, "heads", [(h, h ^ 2) for h in range(4)]) for block in given]
    kept = finish([(0, 0)], f32, given)[0]
    arrived = []
    for slot, part in enumerate(parts):
        pairs = []
        for f in range(n):
            for h in range(4):
                to = PATTERNS[(slot ^ (f & 1)) + 2 * (h >> 1)][f >> 1]
                pairs.append((4 * f + h, 4 * (2 * to + (h & 1)) + (f >> 1)))
        (total,) = call(
            functools.partial(sum_kernel, part), (), [kept, from_core[1], from_x[slot]], [((ROWS, cols), bf16)], 0
        )
        arrived.append(lax.ppermute(total, ("frames", "heads"), pairs))
    patterns = [[p[source] for p in PATTERNS].index(to) for source in range(4) for to in range(4)]
    straight = look_up(patterns, 4 * head + z) & 1 == 0
    low, high = arrived
    return jnp.concatenate([jnp.where(straight, low, high), jnp.where(straight, high, low)], axis=1)


def solution(mesh):
    in_specs = (P("frames", "heads"), P(None, "frames", "heads"), P("heads", "frames"))
    out_specs = P("frames", "heads")
    n, heads = mesh.shape["frames"], mesh.shape["heads"]
    total_frames = n * FR_DEV
    reach = min(reach_cap, (total_frames - 1) // 2)
    every = total_frames == 2 * reach + 2 and heads == 4 and n == 2 * heads
    return jax.shard_map(
        on_device_ring if every else on_device_band,
        mesh=mesh,
        in_specs=in_specs,
        out_specs=out_specs,
        check_vma=False,
    )
```

```python
import functools
import math

import jax
import jax.numpy as jnp
from jax import lax
from jax.experimental import pallas as pl
from jax.experimental.pallas import tpu as pltpu
from jax.sharding import PartitionSpec as P

HD = 128
TPF = 32
FR_DEV = 3
ROWS = FR_DEV * TPF
SCALE = HD ** (-0.5) * math.log2(math.e)


reach_cap = 32


def from_behind(x, axis, by):
    devices = lax.axis_size(axis)
    return lax.ppermute(x, axis, [(i, (i + by) % devices) for i in range(devices)])


def on_device_band(queries, keys_values, out_weight):
    total_frames = lax.axis_size("frames") * FR_DEV
    reach = min(reach_cap, (total_frames - 1) // 2)
    steps = (reach + FR_DEV - 1) // FR_DEV
    width = keys_values.shape[2]
    span = FR_DEV + 2 * reach
    stacked = keys_values.reshape(2, FR_DEV, TPF, width)
    pieces = []
    for offset in range(-steps, steps + 1):
        if offset == 0:
            pieces.append(stacked)
        else:
            pieces.append(from_behind(stacked, "frames", -offset))
    window = jnp.concatenate(pieces, axis=1)
    lower_frame = steps * FR_DEV - reach
    extended = window[:, lower_frame : lower_frame + span]
    keys_ext = extended[0].reshape(span * TPF, width)
    values_ext = extended[1].reshape(span * TPF, width)
    row_frame = jnp.arange(FR_DEV * TPF, dtype=jnp.int32) // TPF
    col_frame = jnp.arange(span * TPF, dtype=jnp.int32) // TPF
    allowed = (col_frame[None, :] >= row_frame[:, None]) & (
        col_frame[None, :] <= row_frame[:, None] + 2 * reach
    )
    results = []
    for head in range(width // HD):
        lower = head * HD
        query_cols = queries[:, lower : lower + HD]
        key_cols = keys_ext[:, lower : lower + HD]
        scores = lax.dot_general(
            query_cols, key_cols, (((1,), (1,)), ((), ())), preferred_element_type=jnp.float32
        )
        scores = scores * HD ** (-0.5)
        top = jnp.max(jnp.where(allowed, scores, -1e30), axis=1, keepdims=True)
        weights = jnp.where(allowed, jnp.exp(scores - top), 0.0)
        probs = (weights / jnp.sum(weights, axis=1, keepdims=True)).astype(jnp.bfloat16)
        results.append(
            jnp.dot(
                probs, values_ext[:, lower : lower + HD], preferred_element_type=jnp.float32
            ).astype(jnp.bfloat16)
        )
    attended = jnp.concatenate(results, axis=1)
    partial_rows = jnp.dot(
        attended,
        lax.all_gather(out_weight, "frames", axis=1, tiled=True),
        preferred_element_type=jnp.float32,
    )
    return lax.psum_scatter(
        partial_rows.astype(jnp.bfloat16), "heads", scatter_dimension=1, tiled=True
    )


def ring_order(n):
    return list(range(0, n, 2)) + list(range(n - 1, 0, -2))


def ring_place(f, n):
    return (f >> 1) + (f & 1) * (n - 1 - (f >> 1) * 2)


def hop(x, n, by):
    order = ring_order(n)
    pairs = []
    for i in range(n):
        for h in range(4):
            pairs.append((4 * order[i] + h, 4 * order[(i + by * (1 - 2 * (h & 1))) % n] + h))
    return lax.ppermute(x, ("frames", "heads"), pairs)


def gather_ring(streams, n):
    found = [[block] + [None] * (n - 1) for block in streams]
    for step in range(1, n // 2 + 1):
        for j, blocks in enumerate(found):
            for by in (1, -1):
                if step < n // 2 or (j % 2 == 0) == (by == 1):
                    blocks[by * step % n] = hop(blocks[by * (step - 1) % n], n, by)
    return found


def ring_distance(at_ref, owner, n):
    place, core = at_ref[0], at_ref[4]
    return (place - owner) * (1 - 2 * core) & (n - 1)


def frame_marks(at_ref, blocks, n):
    place, core = at_ref[0], at_ref[4]
    lane = lax.broadcasted_iota(jnp.int32, (TPF, HD), 1)
    marks = []
    for block in blocks:
        owner = (place - block * (1 - 2 * core)) & (n - 1)
        frame = FR_DEV * ring_distance(at_ref, owner ^ 2, n)
        for g in range(FR_DEV):
            marks.append((lane == frame + g) | (lane >= n * FR_DEV))
    return jnp.concatenate([jnp.where(mark, 1.0, 0.0) for mark in marks], axis=0).astype(jnp.bfloat16)


def key_marks(blocks, padding, n):
    lane = lax.broadcasted_iota(jnp.int32, (TPF, HD), 1)
    frames = [FR_DEV * block + g for block in blocks for g in range(FR_DEV)] + [n * FR_DEV] * (padding // TPF)
    return jnp.concatenate([jnp.where(lane == frame, -1e30, 0.0) for frame in frames], axis=0).astype(jnp.bfloat16)


def rows_of(refs, cols, padding=0):
    pieces = [ref[:, cols] for ref in refs]
    if padding:
        pieces.append(jnp.zeros((padding, HD), jnp.bfloat16))
    return jnp.concatenate(pieces, axis=0)


def scores_of(queries, keys):
    return lax.dot_general(queries, keys, (((1,), (1,)), ((), ())), preferred_element_type=jnp.float32)


def soften(scores, floor=None):
    weights, tops = [], []
    for r in range(0, scores.shape[0], TPF):
        parts = [scores[r : r + TPF, c : c + HD] for c in range(0, scores.shape[1], HD)]
        top = jnp.max(functools.reduce(jnp.maximum, parts), axis=1, keepdims=True)
        top = jnp.broadcast_to(top, (TPF, HD))
        if floor is not None:
            top = jnp.maximum(top, floor[r : r + TPF])
        weights.append(jnp.concatenate([jnp.exp2((p - top) * SCALE).astype(jnp.bfloat16) for p in parts], axis=1))
        tops.append(top)
    return jnp.concatenate(weights, axis=0), jnp.concatenate(tops, axis=0)


def mix(weights, values):
    ones = jnp.ones(values.shape, values.dtype)
    mixed = jnp.dot(weights, jnp.concatenate([values, ones], axis=1), preferred_element_type=jnp.float32)
    return mixed[:, :HD], mixed[:, HD:]


PATTERNS = ((2, 0, 1, 3), (3, 1, 0, 2), (0, 2, 3, 1), (1, 3, 2, 0))


def look_up(table, index):
    code = sum(entry << (2 * i) for i, entry in enumerate(table))
    return (jnp.int32(code - (code >> 31 << 32)) >> (2 * index)) & 3


def slot_blocks(at_ref, flip_x, flip_core, n):
    z, y, x, core = (at_ref[i] for i in range(1, 5))
    blocks = []
    for slot in range(2):
        to = look_up(sum(PATTERNS, ()), 4 * ((slot ^ y) + 2 * (x ^ flip_x)) + z)
        owner = to + (core ^ flip_core) * (n - 1 - 2 * to)
        blocks.append(ring_distance(at_ref, owner, n))
    return blocks


def ahead(scores, heads):
    columns = [slice(head * HD, (head + 1) * HD) for head in range(heads)]
    now = scores(columns[0])
    for head, cols in enumerate(columns):
        later = scores(columns[head + 1]) if head + 1 < heads else None
        yield head, cols, now
        now = later


def split_kernel(kv_ref, keys_ref, values_ref):
    keys_ref[...] = kv_ref[0]
    values_ref[...] = kv_ref[1]


def rows_kernel(n, *refs):
    for d in range(n):
        refs[n][d] = refs[d][...]


def near_kernel(heads, n, at_ref, rows_ref, *refs):
    near = [d for d in range(n) if d != n // 2]
    key_refs, value_refs, (mixed_ref, sum_ref, top_ref) = refs[: n - 1], refs[n - 1 : -3], refs[-3:]
    marks = frame_marks(at_ref, range(n), n)
    keys_marks = key_marks(near, ROWS, n)

    def scores(cols):
        queries = jnp.concatenate([rows_ref[:, :, cols].reshape(n * ROWS, HD), marks], axis=1)
        return scores_of(queries, jnp.concatenate([rows_of(key_refs, cols, ROWS), keys_marks], axis=1))

    for head, cols, now in ahead(scores, heads):
        weights, top = soften(now)
        mixed, total = mix(weights, rows_of(value_refs, cols, ROWS))
        for d in range(n):
            rows = slice(d * ROWS, (d + 1) * ROWS)
            mixed_ref[head, d], sum_ref[head, d], top_ref[head, d] = mixed[rows], total[rows], top[rows]


def finish_kernel(heads, n, flips, at_ref, rows_ref, mixed_ref, sum_ref, top_ref, keys_ref, values_ref, w_ref, *refs):
    blocks = [block for flip in flips for block in slot_blocks(at_ref, *flip, n)]
    marks = frame_marks(at_ref, blocks, n)
    keys_marks = key_marks([n // 2], TPF, n)

    def of(ref, head):
        return jnp.concatenate([ref[head, block] for block in blocks], axis=0)

    columns = [slice(head * HD, (head + 1) * HD) for head in range(heads)]
    scores, attended = [], []
    for cols in columns:
        queries = jnp.concatenate([rows_ref[block, :, cols] for block in blocks], axis=0)
        keys = jnp.concatenate([rows_of([keys_ref], cols, TPF), keys_marks], axis=1)
        scores.append(scores_of(jnp.concatenate([queries, marks], axis=1), keys))
    softened = [soften(now, of(top_ref, head)) for head, now in enumerate(scores)]
    more = [mix(weights, rows_of([values_ref], cols, TPF)) for (weights, _), cols in zip(softened, columns)]
    for head, ((_, top), (mixed, total)) in enumerate(zip(softened, more)):
        kept = jnp.exp2((of(top_ref, head) - top) * SCALE)
        mixed, total = mixed + of(mixed_ref, head) * kept, total + of(sum_ref, head) * kept
        attended.append((mixed / total).astype(jnp.bfloat16))
    rows = jnp.concatenate(attended, axis=1)
    refs[-1][...] = jnp.dot(rows, w_ref[...], preferred_element_type=jnp.float32).astype(refs[-1].dtype)


def sum_kernel(rows, kept_ref, from_core_ref, from_x_ref, total_ref):
    total = kept_ref[rows] + from_core_ref[1, rows].astype(jnp.float32) + from_x_ref[...].astype(jnp.float32)
    total_ref[...] = total.astype(total_ref.dtype)


def call(kernel, scalars, operands, outs, flops, after=()):
    vmem = pl.BlockSpec(memory_space=pltpu.VMEM)
    return pl.pallas_call(
        kernel,
        out_shape=[jax.ShapeDtypeStruct(shape, dtype) for shape, dtype in outs],
        in_specs=[pl.BlockSpec(memory_space=pltpu.SMEM)] * len(scalars)
        + [vmem] * len(operands)
        + [pl.BlockSpec(memory_space=pl.ANY)] * len(after),
        out_specs=[vmem] * len(outs),
        compiler_params=pltpu.CompilerParams(vmem_limit_bytes=20 * 1024 * 1024),
        cost_estimate=pl.CostEstimate(flops=flops, bytes_accessed=0, transcendentals=0),
    )(*scalars, *operands, *after)


def on_device_ring(queries, keys_values, out_weight):
    n = lax.axis_size("frames")
    frame, head = lax.axis_index("frames"), lax.axis_index("heads")
    z, y, x, core = frame >> 1, frame & 1, head >> 1, head & 1
    where = jnp.stack([ring_place(frame, n), z, y, x, core]).astype(jnp.int32)
    width, cols = out_weight.shape
    heads = width // HD
    f32, bf16 = jnp.float32, jnp.bfloat16
    block = (queries.shape, bf16)
    own = call(split_kernel, (), [keys_values], [block, block], 0)
    queries, keys, values = gather_ring([queries, *own], n)
    (rows,) = call(functools.partial(rows_kernel, n), (), queries, [((n, ROWS, width), bf16)], 0)
    far = n // 2
    state = call(
        functools.partial(near_kernel, heads, n),
        (where,),
        [rows, *(blocks[d] for blocks in (keys, values) for d in range(n) if d != far)],
        [((heads, n, ROWS, HD), f32)] * 3,
        4 * n * (n - 1) * ROWS**2 * width,
    )

    def finish(flips, dtype, after=()):
        (sums,) = call(
            functools.partial(finish_kernel, heads, n, flips),
            (where,),
            [rows, *state, keys[far], values[far], out_weight],
            [((len(flips) * 2 * ROWS, cols), dtype)],
            n * ROWS * width * cols,
            after,
        )
        return sums.reshape(len(flips), 2 * ROWS, cols)

    given = finish([(1, 1), (0, 1)], bf16)
    from_core = lax.ppermute(given, "heads", [(h, h ^ 1) for h in range(4)])
    sums = finish([(1, 0)], f32, (given,))[0]
    parts = [slice(slot * ROWS, (slot + 1) * ROWS) for slot in range(2)]
    given = [(sums[part] + from_core[0, part].astype(f32)).astype(bf16) for part in parts]
    from_x = [lax.ppermute(block, "heads", [(h, h ^ 2) for h in range(4)]) for block in given]
    kept = finish([(0, 0)], f32, given)[0]
    arrived = []
    for slot, part in enumerate(parts):
        pairs = []
        for f in range(n):
            for h in range(4):
                to = PATTERNS[(slot ^ (f & 1)) + 2 * (h >> 1)][f >> 1]
                pairs.append((4 * f + h, 4 * (2 * to + (h & 1)) + (f >> 1)))
        (total,) = call(
            functools.partial(sum_kernel, part), (), [kept, from_core, from_x[slot]], [((ROWS, cols), bf16)], 0
        )
        arrived.append(lax.ppermute(total, ("frames", "heads"), pairs))
    patterns = [[p[source] for p in PATTERNS].index(to) for source in range(4) for to in range(4)]
    straight = look_up(patterns, 4 * head + z) & 1 == 0
    low, high = arrived
    return jnp.concatenate([jnp.where(straight, low, high), jnp.where(straight, high, low)], axis=1)


def solution(mesh):
    in_specs = (P("frames", "heads"), P(None, "frames", "heads"), P("heads", "frames"))
    out_specs = P("frames", "heads")
    n, heads = mesh.shape["frames"], mesh.shape["heads"]
    total_frames = n * FR_DEV
    reach = min(reach_cap, (total_frames - 1) // 2)
    every = total_frames == 2 * reach + 2 and heads == 4 and n == 2 * heads
    return jax.shard_map(
        on_device_ring if every else on_device_band,
        mesh=mesh,
        in_specs=in_specs,
        out_specs=out_specs,
        check_vma=False,
    )
```

```python
import functools
import math

import jax
import jax.numpy as jnp
from jax import lax
from jax.experimental import pallas as pl
from jax.experimental.pallas import tpu as pltpu
from jax.sharding import PartitionSpec as P

HD = 128
TPF = 32
FR_DEV = 3
ROWS = FR_DEV * TPF
SCALE = HD ** (-0.5) * math.log2(math.e)


reach_cap = 32


def from_behind(x, axis, by):
    devices = lax.axis_size(axis)
    return lax.ppermute(x, axis, [(i, (i + by) % devices) for i in range(devices)])


def on_device_band(queries, keys_values, out_weight):
    total_frames = lax.axis_size("frames") * FR_DEV
    reach = min(reach_cap, (total_frames - 1) // 2)
    steps = (reach + FR_DEV - 1) // FR_DEV
    width = keys_values.shape[2]
    span = FR_DEV + 2 * reach
    stacked = keys_values.reshape(2, FR_DEV, TPF, width)
    pieces = []
    for offset in range(-steps, steps + 1):
        if offset == 0:
            pieces.append(stacked)
        else:
            pieces.append(from_behind(stacked, "frames", -offset))
    window = jnp.concatenate(pieces, axis=1)
    lower_frame = steps * FR_DEV - reach
    extended = window[:, lower_frame : lower_frame + span]
    keys_ext = extended[0].reshape(span * TPF, width)
    values_ext = extended[1].reshape(span * TPF, width)
    row_frame = jnp.arange(FR_DEV * TPF, dtype=jnp.int32) // TPF
    col_frame = jnp.arange(span * TPF, dtype=jnp.int32) // TPF
    allowed = (col_frame[None, :] >= row_frame[:, None]) & (
        col_frame[None, :] <= row_frame[:, None] + 2 * reach
    )
    results = []
    for head in range(width // HD):
        lower = head * HD
        query_cols = queries[:, lower : lower + HD]
        key_cols = keys_ext[:, lower : lower + HD]
        scores = lax.dot_general(
            query_cols, key_cols, (((1,), (1,)), ((), ())), preferred_element_type=jnp.float32
        )
        scores = scores * HD ** (-0.5)
        top = jnp.max(jnp.where(allowed, scores, -1e30), axis=1, keepdims=True)
        weights = jnp.where(allowed, jnp.exp(scores - top), 0.0)
        probs = (weights / jnp.sum(weights, axis=1, keepdims=True)).astype(jnp.bfloat16)
        results.append(
            jnp.dot(
                probs, values_ext[:, lower : lower + HD], preferred_element_type=jnp.float32
            ).astype(jnp.bfloat16)
        )
    attended = jnp.concatenate(results, axis=1)
    partial_rows = jnp.dot(
        attended,
        lax.all_gather(out_weight, "frames", axis=1, tiled=True),
        preferred_element_type=jnp.float32,
    )
    return lax.psum_scatter(
        partial_rows.astype(jnp.bfloat16), "heads", scatter_dimension=1, tiled=True
    )


def ring_order(n):
    return list(range(0, n, 2)) + list(range(n - 1, 0, -2))


def ring_place(f, n):
    return (f >> 1) + (f & 1) * (n - 1 - (f >> 1) * 2)


def hop(x, n, by):
    order = ring_order(n)
    pairs = []
    for i in range(n):
        for h in range(4):
            pairs.append((4 * order[i] + h, 4 * order[(i + by * (1 - 2 * (h & 1))) % n] + h))
    return lax.ppermute(x, ("frames", "heads"), pairs)


def gather_ring(streams, n):
    found = [[block] + [None] * (n - 1) for block in streams]
    for step in range(1, n // 2 + 1):
        for j, blocks in enumerate(found):
            for by in (1, -1):
                if step < n // 2 or (j % 2 == 0) == (by == 1):
                    blocks[by * step % n] = hop(blocks[by * (step - 1) % n], n, by)
    return found


def ring_distance(at_ref, owner, n):
    place, core = at_ref[0], at_ref[4]
    return (place - owner) * (1 - 2 * core) & (n - 1)


def frame_marks(at_ref, blocks, n):
    place, core = at_ref[0], at_ref[4]
    lane = lax.broadcasted_iota(jnp.int32, (TPF, HD), 1)
    marks = []
    for block in blocks:
        owner = (place - block * (1 - 2 * core)) & (n - 1)
        frame = FR_DEV * ring_distance(at_ref, owner ^ 2, n)
        for g in range(FR_DEV):
            marks.append((lane == frame + g) | (lane >= n * FR_DEV))
    return jnp.concatenate([jnp.where(mark, 1.0, 0.0) for mark in marks], axis=0).astype(jnp.bfloat16)


def key_marks(blocks, padding, n):
    lane = lax.broadcasted_iota(jnp.int32, (TPF, HD), 1)
    frames = [FR_DEV * block + g for block in blocks for g in range(FR_DEV)] + [n * FR_DEV] * (padding // TPF)
    return jnp.concatenate([jnp.where(lane == frame, -1e30, 0.0) for frame in frames], axis=0).astype(jnp.bfloat16)


def rows_of(refs, cols, padding=0):
    pieces = [ref[:, cols] for ref in refs]
    if padding:
        pieces.append(jnp.zeros((padding, HD), jnp.bfloat16))
    return jnp.concatenate(pieces, axis=0)


def scores_of(queries, keys):
    return lax.dot_general(queries, keys, (((1,), (1,)), ((), ())), preferred_element_type=jnp.float32)


def soften(scores, floor=None):
    weights, tops = [], []
    for r in range(0, scores.shape[0], TPF):
        parts = [scores[r : r + TPF, c : c + HD] for c in range(0, scores.shape[1], HD)]
        top = jnp.max(functools.reduce(jnp.maximum, parts), axis=1, keepdims=True)
        top = jnp.broadcast_to(top, (TPF, HD))
        if floor is not None:
            top = jnp.maximum(top, floor[r : r + TPF])
        weights.append(jnp.concatenate([jnp.exp2((p - top) * SCALE).astype(jnp.bfloat16) for p in parts], axis=1))
        tops.append(top)
    return jnp.concatenate(weights, axis=0), jnp.concatenate(tops, axis=0)


def mix(weights, values):
    ones = jnp.ones(values.shape, values.dtype)
    mixed = jnp.dot(weights, jnp.concatenate([values, ones], axis=1), preferred_element_type=jnp.float32)
    return mixed[:, :HD], mixed[:, HD:]


PATTERNS = ((3, 0, 2, 1), (1, 3, 1, 3), (2, 1, 3, 0), (0, 2, 0, 2))


def look_up(table, index):
    code = sum(entry << (2 * i) for i, entry in enumerate(table))
    return (jnp.int32(code - (code >> 31 << 32)) >> (2 * index)) & 3


def slot_blocks(at_ref, flip_x, flip_core, n):
    z, y, x, core = (at_ref[i] for i in range(1, 5))
    blocks = []
    for slot in range(2):
        to = look_up(sum(PATTERNS, ()), 4 * ((slot ^ y) + 2 * (x ^ flip_x)) + z)
        owner = to + (core ^ flip_core) * (n - 1 - 2 * to)
        blocks.append(ring_distance(at_ref, owner, n))
    return blocks


def add_keys(mixed, total, before, top, more):
    kept = jnp.exp2((before - top) * SCALE)
    return more[0] + mixed * kept, more[1] + total * kept


def ahead(scores, heads):
    columns = [slice(head * HD, (head + 1) * HD) for head in range(heads)]
    now = scores(columns[0])
    for head, cols in enumerate(columns):
        later = scores(columns[head + 1]) if head + 1 < heads else None
        yield head, cols, now
        now = later


def split_kernel(queries_ref, kv_ref, copy_ref, keys_ref, values_ref):
    copy_ref[...] = queries_ref[...]
    keys_ref[...] = kv_ref[0]
    values_ref[...] = kv_ref[1]


def rows_kernel(n, *refs):
    for d in range(n):
        refs[n][d] = refs[d][...]


def near_kernel(heads, n, blocks, at_ref, rows_ref, *refs):
    count = len(blocks)
    key_refs, value_refs, state, outs = refs[:count], refs[count : 2 * count], refs[2 * count : -3], refs[-3:]
    padding = -count * ROWS % (2 * HD)
    marks = frame_marks(at_ref, range(n), n)
    keys_marks = key_marks(blocks, padding, n)

    def scores(cols):
        queries = jnp.concatenate([rows_ref[:, :, cols].reshape(n * ROWS, HD), marks], axis=1)
        return scores_of(queries, jnp.concatenate([rows_of(key_refs, cols, padding), keys_marks], axis=1))

    for head, cols, now in ahead(scores, heads):
        values = rows_of(value_refs, cols, padding)
        if state:
            mixed, total, before = (ref[head].reshape(n * ROWS, HD) for ref in state)
            weights, top = soften(now, before)
            mixed, total = add_keys(mixed, total, before, top, mix(weights, values))
        else:
            weights, top = soften(now)
            mixed, total = mix(weights, values)
        for ref, result in zip(outs, (mixed, total, top)):
            ref[head] = result.reshape(n, ROWS, HD)


def finish_kernel(heads, n, flips, at_ref, rows_ref, mixed_ref, sum_ref, top_ref, keys_ref, values_ref, w_ref, *refs):
    blocks = [block for flip in flips for block in slot_blocks(at_ref, *flip, n)]
    marks = frame_marks(at_ref, blocks, n)
    keys_marks = key_marks([n // 2], TPF, n)

    def of(ref, head):
        return jnp.concatenate([ref[head, block] for block in blocks], axis=0)

    columns = [slice(head * HD, (head + 1) * HD) for head in range(heads)]
    scores, attended = [], []
    for cols in columns:
        queries = jnp.concatenate([rows_ref[block, :, cols] for block in blocks], axis=0)
        keys = jnp.concatenate([rows_of([keys_ref], cols, TPF), keys_marks], axis=1)
        scores.append(scores_of(jnp.concatenate([queries, marks], axis=1), keys))
    softened = [soften(now, of(top_ref, head)) for head, now in enumerate(scores)]
    more = [mix(weights, rows_of([values_ref], cols, TPF)) for (weights, _), cols in zip(softened, columns)]
    for head, ((_, top), (mixed, total)) in enumerate(zip(softened, more)):
        now = mixed, total
        mixed, total = add_keys(of(mixed_ref, head), of(sum_ref, head), of(top_ref, head), top, now)
        attended.append((mixed / total).astype(jnp.bfloat16))
    rows = jnp.concatenate(attended, axis=1)
    refs[-1][...] = jnp.dot(rows, w_ref[...], preferred_element_type=jnp.float32).astype(refs[-1].dtype)


def sum_kernel(rows, kept_ref, from_core_ref, from_x_ref, total_ref):
    total = kept_ref[rows] + from_core_ref[1, rows].astype(jnp.float32) + from_x_ref[...].astype(jnp.float32)
    total_ref[...] = total.astype(total_ref.dtype)


def call(kernel, scalars, operands, outs, flops, after=()):
    vmem = pl.BlockSpec(memory_space=pltpu.VMEM)
    return pl.pallas_call(
        kernel,
        out_shape=[jax.ShapeDtypeStruct(shape, dtype) for shape, dtype in outs],
        in_specs=[pl.BlockSpec(memory_space=pltpu.SMEM)] * len(scalars)
        + [vmem] * len(operands)
        + [pl.BlockSpec(memory_space=pl.ANY)] * len(after),
        out_specs=[vmem] * len(outs),
        compiler_params=pltpu.CompilerParams(vmem_limit_bytes=20 * 1024 * 1024),
        cost_estimate=pl.CostEstimate(flops=flops, bytes_accessed=0, transcendentals=0),
    )(*scalars, *operands, *after)


def on_device_ring(queries, keys_values, out_weight):
    n = lax.axis_size("frames")
    frame, head = lax.axis_index("frames"), lax.axis_index("heads")
    z, y, x, core = frame >> 1, frame & 1, head >> 1, head & 1
    where = jnp.stack([ring_place(frame, n), z, y, x, core]).astype(jnp.int32)
    width, cols = out_weight.shape
    heads = width // HD
    f32, bf16 = jnp.float32, jnp.bfloat16
    block = (queries.shape, bf16)
    own_queries, *own = call(split_kernel, (), [queries, keys_values], [block] * 3, 0)
    queries, keys, values = gather_ring([queries, *own], n)
    (rows,) = call(functools.partial(rows_kernel, n), (), [own_queries, *queries[1:]], [((n, ROWS, width), bf16)], 0)
    far = n // 2
    state = []
    for blocks in ([0, 1, 2, n - 2, n - 1], list(range(3, far)) + list(range(far + 1, n - 2))):
        state = call(
            functools.partial(near_kernel, heads, n, blocks),
            (where,),
            [rows, *(keys[d] for d in blocks), *(values[d] for d in blocks), *state],
            [((heads, n, ROWS, HD), f32)] * 3,
            4 * n * len(blocks) * ROWS**2 * width,
        )

    def finish(flips, dtype, after=()):
        (sums,) = call(
            functools.partial(finish_kernel, heads, n, flips),
            (where,),
            [rows, *state, keys[far], values[far], out_weight],
            [((len(flips) * 2 * ROWS, cols), dtype)],
            n * ROWS * width * cols,
            after,
        )
        return sums.reshape(len(flips), 2 * ROWS, cols)

    given = finish([(1, 1), (0, 1)], bf16)
    from_core = lax.ppermute(given, "heads", [(h, h ^ 1) for h in range(4)])
    sums = finish([(1, 0)], f32, (given,))[0]
    parts = [slice(slot * ROWS, (slot + 1) * ROWS) for slot in range(2)]
    given = [(sums[part] + from_core[0, part].astype(f32)).astype(bf16) for part in parts]
    from_x = [lax.ppermute(block, "heads", [(h, h ^ 2) for h in range(4)]) for block in given]
    kept = finish([(0, 0)], f32, given)[0]
    arrived = []
    for slot, part in enumerate(parts):
        pairs = []
        for f in range(n):
            for h in range(4):
                to = PATTERNS[(slot ^ (f & 1)) + 2 * (h >> 1)][f >> 1]
                pairs.append((4 * f + h, 4 * (2 * to + (h & 1)) + (f >> 1)))
        (total,) = call(
            functools.partial(sum_kernel, part), (), [kept, from_core, from_x[slot]], [((ROWS, cols), bf16)], 0
        )
        arrived.append(lax.ppermute(total, ("frames", "heads"), pairs))
    patterns = [[p[source] for p in PATTERNS].index(to) for source in range(4) for to in range(4)]
    straight = look_up(patterns, 4 * head + z) & 1 == 0
    low, high = arrived
    return jnp.concatenate([jnp.where(straight, low, high), jnp.where(straight, high, low)], axis=1)


def solution(mesh):
    in_specs = (P("frames", "heads"), P(None, "frames", "heads"), P("heads", "frames"))
    out_specs = P("frames", "heads")
    n, heads = mesh.shape["frames"], mesh.shape["heads"]
    total_frames = n * FR_DEV
    reach = min(reach_cap, (total_frames - 1) // 2)
    every = total_frames == 2 * reach + 2 and heads == 4 and n == 2 * heads
    return jax.shard_map(
        on_device_ring if every else on_device_band,
        mesh=mesh,
        in_specs=in_specs,
        out_specs=out_specs,
        check_vma=False,
    )
```

```python
import functools
import math

import jax
import jax.numpy as jnp
from jax import lax
from jax.experimental import pallas as pl
from jax.experimental.pallas import tpu as pltpu
from jax.sharding import PartitionSpec as P

HD = 128
TPF = 32
FR_DEV = 3
ROWS = FR_DEV * TPF
SCALE = HD ** (-0.5) * math.log2(math.e)


reach_cap = 32


def from_behind(x, axis, by):
    devices = lax.axis_size(axis)
    return lax.ppermute(x, axis, [(i, (i + by) % devices) for i in range(devices)])


def on_device_band(queries, keys_values, out_weight):
    total_frames = lax.axis_size("frames") * FR_DEV
    reach = min(reach_cap, (total_frames - 1) // 2)
    steps = (reach + FR_DEV - 1) // FR_DEV
    width = keys_values.shape[2]
    span = FR_DEV + 2 * reach
    stacked = keys_values.reshape(2, FR_DEV, TPF, width)
    pieces = []
    for offset in range(-steps, steps + 1):
        if offset == 0:
            pieces.append(stacked)
        else:
            pieces.append(from_behind(stacked, "frames", -offset))
    window = jnp.concatenate(pieces, axis=1)
    lower_frame = steps * FR_DEV - reach
    extended = window[:, lower_frame : lower_frame + span]
    keys_ext = extended[0].reshape(span * TPF, width)
    values_ext = extended[1].reshape(span * TPF, width)
    row_frame = jnp.arange(FR_DEV * TPF, dtype=jnp.int32) // TPF
    col_frame = jnp.arange(span * TPF, dtype=jnp.int32) // TPF
    allowed = (col_frame[None, :] >= row_frame[:, None]) & (
        col_frame[None, :] <= row_frame[:, None] + 2 * reach
    )
    results = []
    for head in range(width // HD):
        lower = head * HD
        query_cols = queries[:, lower : lower + HD]
        key_cols = keys_ext[:, lower : lower + HD]
        scores = lax.dot_general(
            query_cols, key_cols, (((1,), (1,)), ((), ())), preferred_element_type=jnp.float32
        )
        scores = scores * HD ** (-0.5)
        top = jnp.max(jnp.where(allowed, scores, -1e30), axis=1, keepdims=True)
        weights = jnp.where(allowed, jnp.exp(scores - top), 0.0)
        probs = (weights / jnp.sum(weights, axis=1, keepdims=True)).astype(jnp.bfloat16)
        results.append(
            jnp.dot(
                probs, values_ext[:, lower : lower + HD], preferred_element_type=jnp.float32
            ).astype(jnp.bfloat16)
        )
    attended = jnp.concatenate(results, axis=1)
    partial_rows = jnp.dot(
        attended,
        lax.all_gather(out_weight, "frames", axis=1, tiled=True),
        preferred_element_type=jnp.float32,
    )
    return lax.psum_scatter(
        partial_rows.astype(jnp.bfloat16), "heads", scatter_dimension=1, tiled=True
    )


def ring_order(n):
    return list(range(0, n, 2)) + list(range(n - 1, 0, -2))


def ring_place(f, n):
    return (f >> 1) + (f & 1) * (n - 1 - (f >> 1) * 2)


def hop(x, n, by):
    order = ring_order(n)
    pairs = []
    for i in range(n):
        for h in range(4):
            pairs.append((4 * order[i] + h, 4 * order[(i + by * (1 - 2 * (h & 1))) % n] + h))
    return lax.ppermute(x, ("frames", "heads"), pairs)


def gather_ring(streams, n):
    found = [[block] + [None] * (n - 1) for block in streams]
    far, half = n // 2, ROWS // 2
    for step in range(1, far + 1):
        for j, blocks in enumerate(found):
            before = {by: blocks[by * (step - 1) % n] for by in (1, -1)}
            if step < far:
                for by in (1, -1):
                    blocks[by * step % n] = hop(before[by], n, by)
            elif j == 0:
                blocks[far] = hop(before[1][:half], n, 1), hop(before[-1][half:], n, -1)
            else:
                by = 1 if j % 2 == 0 else -1
                blocks[far] = hop(before[by], n, by)
    return found


def ring_distance(at_ref, owner, n):
    place, core = at_ref[0], at_ref[4]
    return (place - owner) * (1 - 2 * core) & (n - 1)


def frame_marks(at_ref, blocks, n):
    place, core = at_ref[0], at_ref[4]
    lane = lax.broadcasted_iota(jnp.int32, (TPF, HD), 1)
    marks = []
    for block in blocks:
        owner = (place - block * (1 - 2 * core)) & (n - 1)
        frame = FR_DEV * ring_distance(at_ref, owner ^ 2, n)
        for g in range(FR_DEV):
            marks.append((lane == frame + g) | (lane >= n * FR_DEV))
    return jnp.concatenate([jnp.where(mark, 1.0, 0.0) for mark in marks], axis=0).astype(jnp.bfloat16)


def key_marks(blocks, padding, n):
    lane = lax.broadcasted_iota(jnp.int32, (TPF, HD), 1)
    frames = [FR_DEV * block + g for block in blocks for g in range(FR_DEV)] + [n * FR_DEV] * (padding // TPF)
    return jnp.concatenate([jnp.where(lane == frame, -1e30, 0.0) for frame in frames], axis=0).astype(jnp.bfloat16)


def rows_of(refs, cols, padding=0):
    pieces = [ref[:, cols] for ref in refs]
    if padding:
        pieces.append(jnp.zeros((padding, HD), jnp.bfloat16))
    return jnp.concatenate(pieces, axis=0)


def scores_of(queries, keys):
    return lax.dot_general(queries, keys, (((1,), (1,)), ((), ())), preferred_element_type=jnp.float32)


def soften(scores, floor=None):
    weights, tops = [], []
    for r in range(0, scores.shape[0], TPF):
        parts = [scores[r : r + TPF, c : c + HD] for c in range(0, scores.shape[1], HD)]
        top = jnp.max(functools.reduce(jnp.maximum, parts), axis=1, keepdims=True)
        top = jnp.broadcast_to(top, (TPF, HD))
        if floor is not None:
            top = jnp.maximum(top, floor[r : r + TPF])
        weights.append(jnp.concatenate([jnp.exp2((p - top) * SCALE).astype(jnp.bfloat16) for p in parts], axis=1))
        tops.append(top)
    return jnp.concatenate(weights, axis=0), jnp.concatenate(tops, axis=0)


def mix(weights, values):
    ones = jnp.ones(values.shape, values.dtype)
    mixed = jnp.dot(weights, jnp.concatenate([values, ones], axis=1), preferred_element_type=jnp.float32)
    return mixed[:, :HD], mixed[:, HD:]


PATTERNS = ((3, 0, 2, 1), (1, 3, 1, 3), (2, 1, 3, 0), (0, 2, 0, 2))


def look_up(table, index):
    code = sum(entry << (2 * i) for i, entry in enumerate(table))
    return (jnp.int32(code - (code >> 31 << 32)) >> (2 * index)) & 3


def slot_blocks(at_ref, flip_x, flip_core, n):
    z, y, x, core = (at_ref[i] for i in range(1, 5))
    blocks = []
    for slot in range(2):
        to = look_up(sum(PATTERNS, ()), 4 * ((slot ^ y) + 2 * (x ^ flip_x)) + z)
        owner = to + (core ^ flip_core) * (n - 1 - 2 * to)
        blocks.append(ring_distance(at_ref, owner, n))
    return blocks


def ahead(scores, heads):
    columns = [slice(head * HD, (head + 1) * HD) for head in range(heads)]
    now = scores(columns[0])
    for head, cols in enumerate(columns):
        later = scores(columns[head + 1]) if head + 1 < heads else None
        yield head, cols, now
        now = later


def split_kernel(kv_ref, keys_ref, values_ref):
    keys_ref[...] = kv_ref[0]
    values_ref[...] = kv_ref[1]


def rows_kernel(n, *refs):
    far, half = n // 2, ROWS // 2
    *query_refs, top_ref, bottom_ref, rows_ref = refs
    for d, ref in zip([d for d in range(n) if d != far], query_refs):
        rows_ref[d] = ref[...]
    rows_ref[far, :half] = top_ref[...]
    rows_ref[far, half:] = bottom_ref[...]


def near_kernel(heads, n, at_ref, rows_ref, *refs):
    near = [d for d in range(n) if d != n // 2]
    key_refs, value_refs, (mixed_ref, sum_ref, top_ref) = refs[: n - 1], refs[n - 1 : -3], refs[-3:]
    marks = frame_marks(at_ref, range(n), n)
    keys_marks = key_marks(near, ROWS, n)

    def scores(cols):
        queries = jnp.concatenate([rows_ref[:, :, cols].reshape(n * ROWS, HD), marks], axis=1)
        return scores_of(queries, jnp.concatenate([rows_of(key_refs, cols, ROWS), keys_marks], axis=1))

    for head, cols, now in ahead(scores, heads):
        weights, top = soften(now)
        mixed, total = mix(weights, rows_of(value_refs, cols, ROWS))
        for d in range(n):
            rows = slice(d * ROWS, (d + 1) * ROWS)
            mixed_ref[head, d], sum_ref[head, d], top_ref[head, d] = mixed[rows], total[rows], top[rows]


def finish_kernel(heads, n, flips, at_ref, rows_ref, mixed_ref, sum_ref, top_ref, keys_ref, values_ref, w_ref, *refs):
    blocks = [block for flip in flips for block in slot_blocks(at_ref, *flip, n)]
    marks = frame_marks(at_ref, blocks, n)
    keys_marks = key_marks([n // 2], TPF, n)

    def of(ref, head):
        return jnp.concatenate([ref[head, block] for block in blocks], axis=0)

    columns = [slice(head * HD, (head + 1) * HD) for head in range(heads)]
    scores, attended = [], []
    for cols in columns:
        queries = jnp.concatenate([rows_ref[block, :, cols] for block in blocks], axis=0)
        keys = jnp.concatenate([rows_of([keys_ref], cols, TPF), keys_marks], axis=1)
        scores.append(scores_of(jnp.concatenate([queries, marks], axis=1), keys))
    softened = [soften(now, of(top_ref, head)) for head, now in enumerate(scores)]
    more = [mix(weights, rows_of([values_ref], cols, TPF)) for (weights, _), cols in zip(softened, columns)]
    for head, ((_, top), (mixed, total)) in enumerate(zip(softened, more)):
        kept = jnp.exp2((of(top_ref, head) - top) * SCALE)
        mixed, total = mixed + of(mixed_ref, head) * kept, total + of(sum_ref, head) * kept
        attended.append((mixed / total).astype(jnp.bfloat16))
    rows = jnp.concatenate(attended, axis=1)
    refs[-1][...] = jnp.dot(rows, w_ref[...], preferred_element_type=jnp.float32).astype(refs[-1].dtype)


def sum_kernel(rows, kept_ref, from_core_ref, from_x_ref, total_ref):
    total = kept_ref[rows] + from_core_ref[1, rows].astype(jnp.float32) + from_x_ref[...].astype(jnp.float32)
    total_ref[...] = total.astype(total_ref.dtype)


def call(kernel, scalars, operands, outs, flops, after=()):
    vmem = pl.BlockSpec(memory_space=pltpu.VMEM)
    return pl.pallas_call(
        kernel,
        out_shape=[jax.ShapeDtypeStruct(shape, dtype) for shape, dtype in outs],
        in_specs=[pl.BlockSpec(memory_space=pltpu.SMEM)] * len(scalars)
        + [vmem] * len(operands)
        + [pl.BlockSpec(memory_space=pl.ANY)] * len(after),
        out_specs=[vmem] * len(outs),
        compiler_params=pltpu.CompilerParams(vmem_limit_bytes=20 * 1024 * 1024),
        cost_estimate=pl.CostEstimate(flops=flops, bytes_accessed=0, transcendentals=0),
    )(*scalars, *operands, *after)


def on_device_ring(queries, keys_values, out_weight):
    n = lax.axis_size("frames")
    frame, head = lax.axis_index("frames"), lax.axis_index("heads")
    z, y, x, core = frame >> 1, frame & 1, head >> 1, head & 1
    where = jnp.stack([ring_place(frame, n), z, y, x, core]).astype(jnp.int32)
    width, cols = out_weight.shape
    heads = width // HD
    f32, bf16 = jnp.float32, jnp.bfloat16
    block = (queries.shape, bf16)
    own = call(split_kernel, (), [keys_values], [block, block], 0)
    queries, keys, values = gather_ring([queries, *own], n)
    far = n // 2
    queries = [*queries[:far], *queries[far + 1 :], *queries[far]]
    (rows,) = call(functools.partial(rows_kernel, n), (), queries, [((n, ROWS, width), bf16)], 0)
    state = call(
        functools.partial(near_kernel, heads, n),
        (where,),
        [rows, *(blocks[d] for blocks in (keys, values) for d in range(n) if d != far)],
        [((heads, n, ROWS, HD), f32)] * 3,
        4 * n * (n - 1) * ROWS**2 * width,
    )

    def finish(flips, dtype, after=()):
        (sums,) = call(
            functools.partial(finish_kernel, heads, n, flips),
            (where,),
            [rows, *state, keys[far], values[far], out_weight],
            [((len(flips) * 2 * ROWS, cols), dtype)],
            n * ROWS * width * cols,
            after,
        )
        return sums.reshape(len(flips), 2 * ROWS, cols)

    given = finish([(1, 1), (0, 1)], bf16)
    from_core = lax.ppermute(given, "heads", [(h, h ^ 1) for h in range(4)])
    sums = finish([(1, 0)], f32, (given,))[0]
    parts = [slice(slot * ROWS, (slot + 1) * ROWS) for slot in range(2)]
    given = [(sums[part] + from_core[0, part].astype(f32)).astype(bf16) for part in parts]
    from_x = [lax.ppermute(block, "heads", [(h, h ^ 2) for h in range(4)]) for block in given]
    kept = finish([(0, 0)], f32, given)[0]
    arrived = []
    for slot, part in enumerate(parts):
        pairs = []
        for f in range(n):
            for h in range(4):
                to = PATTERNS[(slot ^ (f & 1)) + 2 * (h >> 1)][f >> 1]
                pairs.append((4 * f + h, 4 * (2 * to + (h & 1)) + (f >> 1)))
        (total,) = call(
            functools.partial(sum_kernel, part), (), [kept, from_core, from_x[slot]], [((ROWS, cols), bf16)], 0
        )
        arrived.append(lax.ppermute(total, ("frames", "heads"), pairs))
    patterns = [[p[source] for p in PATTERNS].index(to) for source in range(4) for to in range(4)]
    straight = look_up(patterns, 4 * head + z) & 1 == 0
    low, high = arrived
    return jnp.concatenate([jnp.where(straight, low, high), jnp.where(straight, high, low)], axis=1)


def solution(mesh):
    in_specs = (P("frames", "heads"), P(None, "frames", "heads"), P("heads", "frames"))
    out_specs = P("frames", "heads")
    n, heads = mesh.shape["frames"], mesh.shape["heads"]
    total_frames = n * FR_DEV
    reach = min(reach_cap, (total_frames - 1) // 2)
    every = total_frames == 2 * reach + 2 and heads == 4 and n == 2 * heads
    return jax.shard_map(
        on_device_ring if every else on_device_band,
        mesh=mesh,
        in_specs=in_specs,
        out_specs=out_specs,
        check_vma=False,
    )
```

```python
import functools
import math

import jax
import jax.numpy as jnp
from jax import lax
from jax.experimental import pallas as pl
from jax.experimental.pallas import tpu as pltpu
from jax.sharding import PartitionSpec as P

HD = 128
TPF = 32
FR_DEV = 3
ROWS = FR_DEV * TPF
SCALE = HD ** (-0.5) * math.log2(math.e)


reach_cap = 32


def from_behind(x, axis, by):
    devices = lax.axis_size(axis)
    return lax.ppermute(x, axis, [(i, (i + by) % devices) for i in range(devices)])


def on_device_band(queries, keys_values, out_weight):
    total_frames = lax.axis_size("frames") * FR_DEV
    reach = min(reach_cap, (total_frames - 1) // 2)
    steps = (reach + FR_DEV - 1) // FR_DEV
    width = keys_values.shape[2]
    span = FR_DEV + 2 * reach
    stacked = keys_values.reshape(2, FR_DEV, TPF, width)
    pieces = []
    for offset in range(-steps, steps + 1):
        if offset == 0:
            pieces.append(stacked)
        else:
            pieces.append(from_behind(stacked, "frames", -offset))
    window = jnp.concatenate(pieces, axis=1)
    lower_frame = steps * FR_DEV - reach
    extended = window[:, lower_frame : lower_frame + span]
    keys_ext = extended[0].reshape(span * TPF, width)
    values_ext = extended[1].reshape(span * TPF, width)
    row_frame = jnp.arange(FR_DEV * TPF, dtype=jnp.int32) // TPF
    col_frame = jnp.arange(span * TPF, dtype=jnp.int32) // TPF
    allowed = (col_frame[None, :] >= row_frame[:, None]) & (
        col_frame[None, :] <= row_frame[:, None] + 2 * reach
    )
    results = []
    for head in range(width // HD):
        lower = head * HD
        query_cols = queries[:, lower : lower + HD]
        key_cols = keys_ext[:, lower : lower + HD]
        scores = lax.dot_general(
            query_cols, key_cols, (((1,), (1,)), ((), ())), preferred_element_type=jnp.float32
        )
        scores = scores * HD ** (-0.5)
        top = jnp.max(jnp.where(allowed, scores, -1e30), axis=1, keepdims=True)
        weights = jnp.where(allowed, jnp.exp(scores - top), 0.0)
        probs = (weights / jnp.sum(weights, axis=1, keepdims=True)).astype(jnp.bfloat16)
        results.append(
            jnp.dot(
                probs, values_ext[:, lower : lower + HD], preferred_element_type=jnp.float32
            ).astype(jnp.bfloat16)
        )
    attended = jnp.concatenate(results, axis=1)
    partial_rows = jnp.dot(
        attended,
        lax.all_gather(out_weight, "frames", axis=1, tiled=True),
        preferred_element_type=jnp.float32,
    )
    return lax.psum_scatter(
        partial_rows.astype(jnp.bfloat16), "heads", scatter_dimension=1, tiled=True
    )


def ring_order(n):
    return list(range(0, n, 2)) + list(range(n - 1, 0, -2))


def ring_place(f, n):
    return (f >> 1) + (f & 1) * (n - 1 - (f >> 1) * 2)


def hop(x, n, by):
    order = ring_order(n)
    pairs = []
    for i in range(n):
        for h in range(4):
            pairs.append((4 * order[i] + h, 4 * order[(i + by * (1 - 2 * (h & 1))) % n] + h))
    return lax.ppermute(x, ("frames", "heads"), pairs)


def gather_ring(streams, n):
    found = [[block] + [None] * (n - 1) for block in streams]
    for step in range(1, n // 2 + 1):
        for j, blocks in enumerate(found):
            for by in (1, -1):
                if step < n // 2 or (j % 2 == 0) == (by == 1):
                    block = blocks[by * (step - 1) % n]
                    if step == n // 2 and j > 0:
                        other = blocks[-by * (step - 1) % n]
                        (block,) = call(copy_kernel, (), [block], [(block.shape, block.dtype)], 0, (other,))
                    blocks[by * step % n] = hop(block, n, by)
    return found


def ring_distance(at_ref, owner, n):
    place, core = at_ref[0], at_ref[4]
    return (place - owner) * (1 - 2 * core) & (n - 1)


def frame_marks(at_ref, blocks, n):
    place, core = at_ref[0], at_ref[4]
    lane = lax.broadcasted_iota(jnp.int32, (TPF, HD), 1)
    marks = []
    for block in blocks:
        owner = (place - block * (1 - 2 * core)) & (n - 1)
        frame = FR_DEV * ring_distance(at_ref, owner ^ 2, n)
        for g in range(FR_DEV):
            marks.append((lane == frame + g) | (lane >= n * FR_DEV))
    return jnp.concatenate([jnp.where(mark, 1.0, 0.0) for mark in marks], axis=0).astype(jnp.bfloat16)


def key_marks(blocks, padding, n):
    lane = lax.broadcasted_iota(jnp.int32, (TPF, HD), 1)
    frames = [FR_DEV * block + g for block in blocks for g in range(FR_DEV)] + [n * FR_DEV] * (padding // TPF)
    return jnp.concatenate([jnp.where(lane == frame, -1e30, 0.0) for frame in frames], axis=0).astype(jnp.bfloat16)


def rows_of(refs, cols, padding=0):
    pieces = [ref[:, cols] for ref in refs]
    if padding:
        pieces.append(jnp.zeros((padding, HD), jnp.bfloat16))
    return jnp.concatenate(pieces, axis=0)


def scores_of(queries, keys):
    return lax.dot_general(queries, keys, (((1,), (1,)), ((), ())), preferred_element_type=jnp.float32)


def soften(scores, floor=None):
    weights, tops = [], []
    for r in range(0, scores.shape[0], TPF):
        parts = [scores[r : r + TPF, c : c + HD] for c in range(0, scores.shape[1], HD)]
        top = jnp.max(functools.reduce(jnp.maximum, parts), axis=1, keepdims=True)
        top = jnp.broadcast_to(top, (TPF, HD))
        if floor is not None:
            top = jnp.maximum(top, floor[r : r + TPF])
        weights.append(jnp.concatenate([jnp.exp2((p - top) * SCALE).astype(jnp.bfloat16) for p in parts], axis=1))
        tops.append(top)
    return jnp.concatenate(weights, axis=0), jnp.concatenate(tops, axis=0)


def mix(weights, values):
    ones = jnp.ones(values.shape, values.dtype)
    mixed = jnp.dot(weights, jnp.concatenate([values, ones], axis=1), preferred_element_type=jnp.float32)
    return mixed[:, :HD], mixed[:, HD:]


PATTERNS = ((3, 0, 2, 1), (1, 3, 1, 3), (2, 1, 3, 0), (0, 2, 0, 2))


def look_up(table, index):
    code = sum(entry << (2 * i) for i, entry in enumerate(table))
    return (jnp.int32(code - (code >> 31 << 32)) >> (2 * index)) & 3


def slot_blocks(at_ref, flip_x, flip_core, n):
    z, y, x, core = (at_ref[i] for i in range(1, 5))
    blocks = []
    for slot in range(2):
        to = look_up(sum(PATTERNS, ()), 4 * ((slot ^ y) + 2 * (x ^ flip_x)) + z)
        owner = to + (core ^ flip_core) * (n - 1 - 2 * to)
        blocks.append(ring_distance(at_ref, owner, n))
    return blocks


def ahead(scores, heads):
    columns = [slice(head * HD, (head + 1) * HD) for head in range(heads)]
    now = scores(columns[0])
    for head, cols in enumerate(columns):
        later = scores(columns[head + 1]) if head + 1 < heads else None
        yield head, cols, now
        now = later


def copy_kernel(from_ref, *refs):
    refs[-1][...] = from_ref[...]


def split_kernel(kv_ref, keys_ref, values_ref):
    keys_ref[...] = kv_ref[0]
    values_ref[...] = kv_ref[1]


def rows_kernel(n, *refs):
    for d in range(n):
        refs[n][d] = refs[d][...]


def near_kernel(heads, n, at_ref, rows_ref, *refs):
    near = [d for d in range(n) if d != n // 2]
    key_refs, value_refs, (mixed_ref, sum_ref, top_ref) = refs[: n - 1], refs[n - 1 : -3], refs[-3:]
    marks = frame_marks(at_ref, range(n), n)
    keys_marks = key_marks(near, ROWS, n)

    def scores(cols):
        queries = jnp.concatenate([rows_ref[:, :, cols].reshape(n * ROWS, HD), marks], axis=1)
        return scores_of(queries, jnp.concatenate([rows_of(key_refs, cols, ROWS), keys_marks], axis=1))

    for head, cols, now in ahead(scores, heads):
        weights, top = soften(now)
        mixed, total = mix(weights, rows_of(value_refs, cols, ROWS))
        for d in range(n):
            rows = slice(d * ROWS, (d + 1) * ROWS)
            mixed_ref[head, d], sum_ref[head, d], top_ref[head, d] = mixed[rows], total[rows], top[rows]


def finish_kernel(heads, n, flips, at_ref, rows_ref, mixed_ref, sum_ref, top_ref, keys_ref, values_ref, w_ref, *refs):
    blocks = [block for flip in flips for block in slot_blocks(at_ref, *flip, n)]
    marks = frame_marks(at_ref, blocks, n)
    keys_marks = key_marks([n // 2], TPF, n)

    def of(ref, head):
        return jnp.concatenate([ref[head, block] for block in blocks], axis=0)

    columns = [slice(head * HD, (head + 1) * HD) for head in range(heads)]
    scores, attended = [], []
    for cols in columns:
        queries = jnp.concatenate([rows_ref[block, :, cols] for block in blocks], axis=0)
        keys = jnp.concatenate([rows_of([keys_ref], cols, TPF), keys_marks], axis=1)
        scores.append(scores_of(jnp.concatenate([queries, marks], axis=1), keys))
    softened = [soften(now, of(top_ref, head)) for head, now in enumerate(scores)]
    more = [mix(weights, rows_of([values_ref], cols, TPF)) for (weights, _), cols in zip(softened, columns)]
    for head, ((_, top), (mixed, total)) in enumerate(zip(softened, more)):
        kept = jnp.exp2((of(top_ref, head) - top) * SCALE)
        mixed, total = mixed + of(mixed_ref, head) * kept, total + of(sum_ref, head) * kept
        attended.append((mixed / total).astype(jnp.bfloat16))
    rows = jnp.concatenate(attended, axis=1)
    refs[-1][...] = jnp.dot(rows, w_ref[...], preferred_element_type=jnp.float32).astype(refs[-1].dtype)


def sum_kernel(rows, kept_ref, from_core_ref, from_x_ref, total_ref):
    total = kept_ref[rows] + from_core_ref[1, rows].astype(jnp.float32) + from_x_ref[...].astype(jnp.float32)
    total_ref[...] = total.astype(total_ref.dtype)


def call(kernel, scalars, operands, outs, flops, after=()):
    vmem = pl.BlockSpec(memory_space=pltpu.VMEM)
    return pl.pallas_call(
        kernel,
        out_shape=[jax.ShapeDtypeStruct(shape, dtype) for shape, dtype in outs],
        in_specs=[pl.BlockSpec(memory_space=pltpu.SMEM)] * len(scalars)
        + [vmem] * len(operands)
        + [pl.BlockSpec(memory_space=pl.ANY)] * len(after),
        out_specs=[vmem] * len(outs),
        compiler_params=pltpu.CompilerParams(vmem_limit_bytes=20 * 1024 * 1024),
        cost_estimate=pl.CostEstimate(flops=flops, bytes_accessed=0, transcendentals=0),
    )(*scalars, *operands, *after)


def on_device_ring(queries, keys_values, out_weight):
    n = lax.axis_size("frames")
    frame, head = lax.axis_index("frames"), lax.axis_index("heads")
    z, y, x, core = frame >> 1, frame & 1, head >> 1, head & 1
    where = jnp.stack([ring_place(frame, n), z, y, x, core]).astype(jnp.int32)
    width, cols = out_weight.shape
    heads = width // HD
    f32, bf16 = jnp.float32, jnp.bfloat16
    block = (queries.shape, bf16)
    own = call(split_kernel, (), [keys_values], [block, block], 0)
    queries, keys, values = gather_ring([queries, *own], n)
    (rows,) = call(functools.partial(rows_kernel, n), (), queries, [((n, ROWS, width), bf16)], 0)
    far = n // 2
    state = call(
        functools.partial(near_kernel, heads, n),
        (where,),
        [rows, *(blocks[d] for blocks in (keys, values) for d in range(n) if d != far)],
        [((heads, n, ROWS, HD), f32)] * 3,
        4 * n * (n - 1) * ROWS**2 * width,
    )

    def finish(flips, dtype, after=()):
        (sums,) = call(
            functools.partial(finish_kernel, heads, n, flips),
            (where,),
            [rows, *state, keys[far], values[far], out_weight],
            [((len(flips) * 2 * ROWS, cols), dtype)],
            n * ROWS * width * cols,
            after,
        )
        return sums.reshape(len(flips), 2 * ROWS, cols)

    given = finish([(1, 1), (0, 1)], bf16)
    from_core = lax.ppermute(given, "heads", [(h, h ^ 1) for h in range(4)])
    sums = finish([(1, 0)], f32, (given,))[0]
    parts = [slice(slot * ROWS, (slot + 1) * ROWS) for slot in range(2)]
    given = [(sums[part] + from_core[0, part].astype(f32)).astype(bf16) for part in parts]
    from_x = [lax.ppermute(block, "heads", [(h, h ^ 2) for h in range(4)]) for block in given]
    kept = finish([(0, 0)], f32, given)[0]
    arrived = []
    for slot, part in enumerate(parts):
        pairs = []
        for f in range(n):
            for h in range(4):
                to = PATTERNS[(slot ^ (f & 1)) + 2 * (h >> 1)][f >> 1]
                pairs.append((4 * f + h, 4 * (2 * to + (h & 1)) + (f >> 1)))
        (total,) = call(
            functools.partial(sum_kernel, part), (), [kept, from_core, from_x[slot]], [((ROWS, cols), bf16)], 0
        )
        arrived.append(lax.ppermute(total, ("frames", "heads"), pairs))
    patterns = [[p[source] for p in PATTERNS].index(to) for source in range(4) for to in range(4)]
    straight = look_up(patterns, 4 * head + z) & 1 == 0
    low, high = arrived
    return jnp.concatenate([jnp.where(straight, low, high), jnp.where(straight, high, low)], axis=1)


def solution(mesh):
    in_specs = (P("frames", "heads"), P(None, "frames", "heads"), P("heads", "frames"))
    out_specs = P("frames", "heads")
    n, heads = mesh.shape["frames"], mesh.shape["heads"]
    total_frames = n * FR_DEV
    reach = min(reach_cap, (total_frames - 1) // 2)
    every = total_frames == 2 * reach + 2 and heads == 4 and n == 2 * heads
    return jax.shard_map(
        on_device_ring if every else on_device_band,
        mesh=mesh,
        in_specs=in_specs,
        out_specs=out_specs,
        check_vma=False,
    )
```

```python
import functools
import math

import jax
import jax.numpy as jnp
from jax import lax
from jax.experimental import pallas as pl
from jax.experimental.pallas import tpu as pltpu
from jax.sharding import PartitionSpec as P

HD = 128
TPF = 32
FR_DEV = 3
ROWS = FR_DEV * TPF
SCALE = HD ** (-0.5) * math.log2(math.e)


reach_cap = 32


def from_behind(x, axis, by):
    devices = lax.axis_size(axis)
    return lax.ppermute(x, axis, [(i, (i + by) % devices) for i in range(devices)])


def on_device_band(queries, keys_values, out_weight):
    total_frames = lax.axis_size("frames") * FR_DEV
    reach = min(reach_cap, (total_frames - 1) // 2)
    steps = (reach + FR_DEV - 1) // FR_DEV
    width = keys_values.shape[2]
    span = FR_DEV + 2 * reach
    stacked = keys_values.reshape(2, FR_DEV, TPF, width)
    pieces = []
    for offset in range(-steps, steps + 1):
        if offset == 0:
            pieces.append(stacked)
        else:
            pieces.append(from_behind(stacked, "frames", -offset))
    window = jnp.concatenate(pieces, axis=1)
    lower_frame = steps * FR_DEV - reach
    extended = window[:, lower_frame : lower_frame + span]
    keys_ext = extended[0].reshape(span * TPF, width)
    values_ext = extended[1].reshape(span * TPF, width)
    row_frame = jnp.arange(FR_DEV * TPF, dtype=jnp.int32) // TPF
    col_frame = jnp.arange(span * TPF, dtype=jnp.int32) // TPF
    allowed = (col_frame[None, :] >= row_frame[:, None]) & (
        col_frame[None, :] <= row_frame[:, None] + 2 * reach
    )
    results = []
    for head in range(width // HD):
        lower = head * HD
        query_cols = queries[:, lower : lower + HD]
        key_cols = keys_ext[:, lower : lower + HD]
        scores = lax.dot_general(
            query_cols, key_cols, (((1,), (1,)), ((), ())), preferred_element_type=jnp.float32
        )
        scores = scores * HD ** (-0.5)
        top = jnp.max(jnp.where(allowed, scores, -1e30), axis=1, keepdims=True)
        weights = jnp.where(allowed, jnp.exp(scores - top), 0.0)
        probs = (weights / jnp.sum(weights, axis=1, keepdims=True)).astype(jnp.bfloat16)
        results.append(
            jnp.dot(
                probs, values_ext[:, lower : lower + HD], preferred_element_type=jnp.float32
            ).astype(jnp.bfloat16)
        )
    attended = jnp.concatenate(results, axis=1)
    partial_rows = jnp.dot(
        attended,
        lax.all_gather(out_weight, "frames", axis=1, tiled=True),
        preferred_element_type=jnp.float32,
    )
    return lax.psum_scatter(
        partial_rows.astype(jnp.bfloat16), "heads", scatter_dimension=1, tiled=True
    )


def ring_order(n):
    return list(range(0, n, 2)) + list(range(n - 1, 0, -2))


def ring_place(f, n):
    return (f >> 1) + (f & 1) * (n - 1 - (f >> 1) * 2)


def hop(x, n, by):
    order = ring_order(n)
    pairs = []
    for i in range(n):
        for h in range(4):
            pairs.append((4 * order[i] + h, 4 * order[(i + by * (1 - 2 * (h & 1))) % n] + h))
    return lax.ppermute(x, ("frames", "heads"), pairs)


def gather_ring(streams, n):
    found = [[block] + [None] * (n - 1) for block in streams]
    for step in range(1, n // 2 + 1):
        for j, blocks in enumerate(found):
            for by in (1, -1):
                if step < n // 2 or (j % 2 == 0) == (by == 1):
                    blocks[by * step % n] = hop(blocks[by * (step - 1) % n], n, by)
    return found


def ring_distance(at_ref, owner, n):
    place, core = at_ref[0], at_ref[4]
    return (place - owner) * (1 - 2 * core) & (n - 1)


def frame_marks(at_ref, blocks, n):
    place, core = at_ref[0], at_ref[4]
    lane = lax.broadcasted_iota(jnp.int32, (TPF, HD), 1)
    marks = []
    for block in blocks:
        owner = (place - block * (1 - 2 * core)) & (n - 1)
        frame = FR_DEV * ring_distance(at_ref, owner ^ 2, n)
        for g in range(FR_DEV):
            marks.append((lane == frame + g) | (lane >= n * FR_DEV))
    return jnp.concatenate([jnp.where(mark, 1.0, 0.0) for mark in marks], axis=0).astype(jnp.bfloat16)


def key_marks(blocks, padding, n):
    lane = lax.broadcasted_iota(jnp.int32, (TPF, HD), 1)
    frames = [FR_DEV * block + g for block in blocks for g in range(FR_DEV)] + [n * FR_DEV] * (padding // TPF)
    return jnp.concatenate([jnp.where(lane == frame, -1e30, 0.0) for frame in frames], axis=0).astype(jnp.bfloat16)


def rows_of(refs, cols, padding=0):
    pieces = [ref[:, cols] for ref in refs]
    if padding:
        pieces.append(jnp.zeros((padding, HD), jnp.bfloat16))
    return jnp.concatenate(pieces, axis=0)


def scores_of(queries, keys):
    return lax.dot_general(queries, keys, (((1,), (1,)), ((), ())), preferred_element_type=jnp.float32)


def soften(scores, floor=None):
    weights, tops = [], []
    for r in range(0, scores.shape[0], TPF):
        parts = [scores[r : r + TPF, c : c + HD] for c in range(0, scores.shape[1], HD)]
        top = jnp.max(functools.reduce(jnp.maximum, parts), axis=1, keepdims=True)
        top = jnp.broadcast_to(top, (TPF, HD))
        if floor is not None:
            top = jnp.maximum(top, floor[r : r + TPF])
        weights.append(jnp.concatenate([jnp.exp2((p - top) * SCALE).astype(jnp.bfloat16) for p in parts], axis=1))
        tops.append(top)
    return jnp.concatenate(weights, axis=0), jnp.concatenate(tops, axis=0)


def mix(weights, values):
    ones = jnp.ones(values.shape, values.dtype)
    mixed = jnp.dot(weights, jnp.concatenate([values, ones], axis=1), preferred_element_type=jnp.float32)
    return mixed[:, :HD], mixed[:, HD:]


PATTERNS = ((3, 1, 0, 2), (0, 2, 3, 1), (1, 3, 2, 0), (2, 0, 1, 3))


def look_up(table, index):
    code = sum(entry << (2 * i) for i, entry in enumerate(table))
    return (jnp.int32(code - (code >> 31 << 32)) >> (2 * index)) & 3


def slot_blocks(at_ref, flip_x, flip_core, n):
    z, y, x, core = (at_ref[i] for i in range(1, 5))
    blocks = []
    for slot in range(2):
        to = look_up(sum(PATTERNS, ()), 4 * ((slot ^ y) + 2 * (x ^ flip_x)) + z)
        owner = to + (core ^ flip_core) * (n - 1 - 2 * to)
        blocks.append(ring_distance(at_ref, owner, n))
    return blocks


def ahead(scores, heads):
    columns = [slice(head * HD, (head + 1) * HD) for head in range(heads)]
    now = scores(columns[0])
    for head, cols in enumerate(columns):
        later = scores(columns[head + 1]) if head + 1 < heads else None
        yield head, cols, now
        now = later


def split_kernel(kv_ref, keys_ref, values_ref):
    keys_ref[...] = kv_ref[0]
    values_ref[...] = kv_ref[1]


def rows_kernel(n, *refs):
    for d in range(n):
        refs[n][d] = refs[d][...]


def near_kernel(heads, n, at_ref, rows_ref, *refs):
    near = [d for d in range(n) if d != n // 2]
    key_refs, value_refs, (mixed_ref, sum_ref, top_ref) = refs[: n - 1], refs[n - 1 : -3], refs[-3:]
    marks = frame_marks(at_ref, range(n), n)
    keys_marks = key_marks(near, ROWS, n)

    def scores(cols):
        queries = jnp.concatenate([rows_ref[:, :, cols].reshape(n * ROWS, HD), marks], axis=1)
        return scores_of(queries, jnp.concatenate([rows_of(key_refs, cols, ROWS), keys_marks], axis=1))

    for head, cols, now in ahead(scores, heads):
        weights, top = soften(now)
        mixed, total = mix(weights, rows_of(value_refs, cols, ROWS))
        for d in range(n):
            rows = slice(d * ROWS, (d + 1) * ROWS)
            mixed_ref[head, d], sum_ref[head, d], top_ref[head, d] = mixed[rows], total[rows], top[rows]


def finish_kernel(heads, n, flips, at_ref, rows_ref, mixed_ref, sum_ref, top_ref, keys_ref, values_ref, w_ref, *refs):
    blocks = [block for flip in flips for block in slot_blocks(at_ref, *flip, n)]
    marks = frame_marks(at_ref, blocks, n)
    keys_marks = key_marks([n // 2], TPF, n)

    def of(ref, head):
        return jnp.concatenate([ref[head, block] for block in blocks], axis=0)

    columns = [slice(head * HD, (head + 1) * HD) for head in range(heads)]
    scores, attended = [], []
    for cols in columns:
        queries = jnp.concatenate([rows_ref[block, :, cols] for block in blocks], axis=0)
        keys = jnp.concatenate([rows_of([keys_ref], cols, TPF), keys_marks], axis=1)
        scores.append(scores_of(jnp.concatenate([queries, marks], axis=1), keys))
    softened = [soften(now, of(top_ref, head)) for head, now in enumerate(scores)]
    more = [mix(weights, rows_of([values_ref], cols, TPF)) for (weights, _), cols in zip(softened, columns)]
    for head, ((_, top), (mixed, total)) in enumerate(zip(softened, more)):
        kept = jnp.exp2((of(top_ref, head) - top) * SCALE)
        mixed, total = mixed + of(mixed_ref, head) * kept, total + of(sum_ref, head) * kept
        attended.append((mixed / total).astype(jnp.bfloat16))
    rows = jnp.concatenate(attended, axis=1)
    refs[-1][...] = jnp.dot(rows, w_ref[...], preferred_element_type=jnp.float32).astype(refs[-1].dtype)


def sum_kernel(rows, kept_ref, from_core_ref, from_x_ref, total_ref):
    total = kept_ref[rows] + from_core_ref[1, rows].astype(jnp.float32) + from_x_ref[...].astype(jnp.float32)
    total_ref[...] = total.astype(total_ref.dtype)


def call(kernel, scalars, operands, outs, flops, after=()):
    vmem = pl.BlockSpec(memory_space=pltpu.VMEM)
    return pl.pallas_call(
        kernel,
        out_shape=[jax.ShapeDtypeStruct(shape, dtype) for shape, dtype in outs],
        in_specs=[pl.BlockSpec(memory_space=pltpu.SMEM)] * len(scalars)
        + [vmem] * len(operands)
        + [pl.BlockSpec(memory_space=pl.ANY)] * len(after),
        out_specs=[vmem] * len(outs),
        compiler_params=pltpu.CompilerParams(vmem_limit_bytes=20 * 1024 * 1024),
        cost_estimate=pl.CostEstimate(flops=flops, bytes_accessed=0, transcendentals=0),
    )(*scalars, *operands, *after)


def on_device_ring(queries, keys_values, out_weight):
    n = lax.axis_size("frames")
    frame, head = lax.axis_index("frames"), lax.axis_index("heads")
    z, y, x, core = frame >> 1, frame & 1, head >> 1, head & 1
    where = jnp.stack([ring_place(frame, n), z, y, x, core]).astype(jnp.int32)
    width, cols = out_weight.shape
    heads = width // HD
    f32, bf16 = jnp.float32, jnp.bfloat16
    block = (queries.shape, bf16)
    own = call(split_kernel, (), [keys_values], [block, block], 0)
    queries, keys, values = gather_ring([queries, *own], n)
    (rows,) = call(functools.partial(rows_kernel, n), (), queries, [((n, ROWS, width), bf16)], 0)
    far = n // 2
    state = call(
        functools.partial(near_kernel, heads, n),
        (where,),
        [rows, *(blocks[d] for blocks in (keys, values) for d in range(n) if d != far)],
        [((heads, n, ROWS, HD), f32)] * 3,
        4 * n * (n - 1) * ROWS**2 * width,
    )

    def finish(flips, dtype, after=()):
        (sums,) = call(
            functools.partial(finish_kernel, heads, n, flips),
            (where,),
            [rows, *state, keys[far], values[far], out_weight],
            [((len(flips) * 2 * ROWS, cols), dtype)],
            n * ROWS * width * cols,
            after,
        )
        return sums.reshape(len(flips), 2 * ROWS, cols)

    given = finish([(1, 1), (0, 1)], bf16)
    from_core = lax.ppermute(given, "heads", [(h, h ^ 1) for h in range(4)])
    sums = finish([(1, 0)], f32, (given,))[0]
    parts = [slice(slot * ROWS, (slot + 1) * ROWS) for slot in range(2)]
    given = [(sums[part] + from_core[0, part].astype(f32)).astype(bf16) for part in parts]
    from_x = [lax.ppermute(block, "heads", [(h, h ^ 2) for h in range(4)]) for block in given]
    kept = finish([(0, 0)], f32, given)[0]
    arrived = []
    for slot, part in enumerate(parts):
        pairs = []
        for f in range(n):
            for h in range(4):
                to = PATTERNS[(slot ^ (f & 1)) + 2 * (h >> 1)][f >> 1]
                pairs.append((4 * f + h, 4 * (2 * to + (h & 1)) + (f >> 1)))
        (total,) = call(
            functools.partial(sum_kernel, part), (), [kept, from_core, from_x[slot]], [((ROWS, cols), bf16)], 0
        )
        arrived.append(lax.ppermute(total, ("frames", "heads"), pairs))
    patterns = [[p[source] for p in PATTERNS].index(to) for source in range(4) for to in range(4)]
    straight = look_up(patterns, 4 * head + z) & 1 == 0
    low, high = arrived
    return jnp.concatenate([jnp.where(straight, low, high), jnp.where(straight, high, low)], axis=1)


def solution(mesh):
    in_specs = (P("frames", "heads"), P(None, "frames", "heads"), P("heads", "frames"))
    out_specs = P("frames", "heads")
    n, heads = mesh.shape["frames"], mesh.shape["heads"]
    total_frames = n * FR_DEV
    reach = min(reach_cap, (total_frames - 1) // 2)
    every = total_frames == 2 * reach + 2 and heads == 4 and n == 2 * heads
    return jax.shard_map(
        on_device_ring if every else on_device_band,
        mesh=mesh,
        in_specs=in_specs,
        out_specs=out_specs,
        check_vma=False,
    )
```

```python
import functools
import math

import jax
import jax.numpy as jnp
from jax import lax
from jax.experimental import pallas as pl
from jax.experimental.pallas import tpu as pltpu
from jax.sharding import PartitionSpec as P

HD = 128
TPF = 32
FR_DEV = 3
ROWS = FR_DEV * TPF
SCALE = HD ** (-0.5) * math.log2(math.e)


reach_cap = 32


def from_behind(x, axis, by):
    devices = lax.axis_size(axis)
    return lax.ppermute(x, axis, [(i, (i + by) % devices) for i in range(devices)])


def on_device_band(queries, keys_values, out_weight):
    total_frames = lax.axis_size("frames") * FR_DEV
    reach = min(reach_cap, (total_frames - 1) // 2)
    steps = (reach + FR_DEV - 1) // FR_DEV
    width = keys_values.shape[2]
    span = FR_DEV + 2 * reach
    stacked = keys_values.reshape(2, FR_DEV, TPF, width)
    pieces = []
    for offset in range(-steps, steps + 1):
        if offset == 0:
            pieces.append(stacked)
        else:
            pieces.append(from_behind(stacked, "frames", -offset))
    window = jnp.concatenate(pieces, axis=1)
    lower_frame = steps * FR_DEV - reach
    extended = window[:, lower_frame : lower_frame + span]
    keys_ext = extended[0].reshape(span * TPF, width)
    values_ext = extended[1].reshape(span * TPF, width)
    row_frame = jnp.arange(FR_DEV * TPF, dtype=jnp.int32) // TPF
    col_frame = jnp.arange(span * TPF, dtype=jnp.int32) // TPF
    allowed = (col_frame[None, :] >= row_frame[:, None]) & (
        col_frame[None, :] <= row_frame[:, None] + 2 * reach
    )
    results = []
    for head in range(width // HD):
        lower = head * HD
        query_cols = queries[:, lower : lower + HD]
        key_cols = keys_ext[:, lower : lower + HD]
        scores = lax.dot_general(
            query_cols, key_cols, (((1,), (1,)), ((), ())), preferred_element_type=jnp.float32
        )
        scores = scores * HD ** (-0.5)
        top = jnp.max(jnp.where(allowed, scores, -1e30), axis=1, keepdims=True)
        weights = jnp.where(allowed, jnp.exp(scores - top), 0.0)
        probs = (weights / jnp.sum(weights, axis=1, keepdims=True)).astype(jnp.bfloat16)
        results.append(
            jnp.dot(
                probs, values_ext[:, lower : lower + HD], preferred_element_type=jnp.float32
            ).astype(jnp.bfloat16)
        )
    attended = jnp.concatenate(results, axis=1)
    partial_rows = jnp.dot(
        attended,
        lax.all_gather(out_weight, "frames", axis=1, tiled=True),
        preferred_element_type=jnp.float32,
    )
    return lax.psum_scatter(
        partial_rows.astype(jnp.bfloat16), "heads", scatter_dimension=1, tiled=True
    )


def ring_order(n):
    return list(range(0, n, 2)) + list(range(n - 1, 0, -2))


def ring_place(f, n):
    return (f >> 1) + (f & 1) * (n - 1 - (f >> 1) * 2)


def hop(x, n, by):
    order = ring_order(n)
    pairs = []
    for i in range(n):
        for h in range(4):
            pairs.append((4 * order[i] + h, 4 * order[(i + by * (1 - 2 * (h & 1))) % n] + h))
    return lax.ppermute(x, ("frames", "heads"), pairs)


def gather_ring(streams, n):
    found = [[block] + [None] * (n - 1) for block in streams]
    for step in range(1, n // 2 + 1):
        for j, blocks in enumerate(found):
            for by in (1, -1):
                if step < n // 2 or (j % 2 == 0) == (by == 1):
                    blocks[by * step % n] = hop(blocks[by * (step - 1) % n], n, by)
    return found


def ring_distance(at_ref, owner, n):
    place, core = at_ref[0], at_ref[4]
    return (place - owner) * (1 - 2 * core) & (n - 1)


def frame_marks(at_ref, blocks, n):
    place, core = at_ref[0], at_ref[4]
    lane = lax.broadcasted_iota(jnp.int32, (TPF, HD), 1)
    marks = []
    for block in blocks:
        owner = (place - block * (1 - 2 * core)) & (n - 1)
        frame = FR_DEV * ring_distance(at_ref, owner ^ 2, n)
        for g in range(FR_DEV):
            marks.append((lane == frame + g) | (lane >= n * FR_DEV))
    return jnp.concatenate([jnp.where(mark, 1.0, 0.0) for mark in marks], axis=0).astype(jnp.bfloat16)


def key_marks(blocks, padding, n):
    lane = lax.broadcasted_iota(jnp.int32, (TPF, HD), 1)
    frames = [FR_DEV * block + g for block in blocks for g in range(FR_DEV)] + [n * FR_DEV] * (padding // TPF)
    return jnp.concatenate([jnp.where(lane == frame, -1e30, 0.0) for frame in frames], axis=0).astype(jnp.bfloat16)


def rows_of(refs, cols, padding=0):
    pieces = [ref[:, cols] for ref in refs]
    if padding:
        pieces.append(jnp.zeros((padding, HD), jnp.bfloat16))
    return jnp.concatenate(pieces, axis=0)


def scores_of(queries, keys):
    return lax.dot_general(queries, keys, (((1,), (1,)), ((), ())), preferred_element_type=jnp.float32)


def soften(scores, floor=None):
    weights, tops = [], []
    for r in range(0, scores.shape[0], TPF):
        parts = [scores[r : r + TPF, c : c + HD] for c in range(0, scores.shape[1], HD)]
        top = jnp.max(functools.reduce(jnp.maximum, parts), axis=1, keepdims=True)
        top = jnp.broadcast_to(top, (TPF, HD))
        if floor is not None:
            top = jnp.maximum(top, floor[r : r + TPF])
        weights.append(jnp.concatenate([jnp.exp2((p - top) * SCALE).astype(jnp.bfloat16) for p in parts], axis=1))
        tops.append(top)
    return jnp.concatenate(weights, axis=0), jnp.concatenate(tops, axis=0)


def mix(weights, values):
    ones = jnp.ones(values.shape, values.dtype)
    mixed = jnp.dot(weights, jnp.concatenate([values, ones], axis=1), preferred_element_type=jnp.float32)
    return mixed[:, :HD], mixed[:, HD:]


PATTERNS = ((3, 0, 1, 3), (1, 3, 2, 1), (2, 1, 0, 2), (0, 2, 3, 0))


def look_up(table, index):
    code = sum(entry << (2 * i) for i, entry in enumerate(table))
    return (jnp.int32(code - (code >> 31 << 32)) >> (2 * index)) & 3


def slot_blocks(at_ref, flip_x, flip_core, n):
    z, y, x, core = (at_ref[i] for i in range(1, 5))
    blocks = []
    for slot in range(2):
        to = look_up(sum(PATTERNS, ()), 4 * ((slot ^ y) + 2 * (x ^ flip_x)) + z)
        owner = to + (core ^ flip_core) * (n - 1 - 2 * to)
        blocks.append(ring_distance(at_ref, owner, n))
    return blocks


def ahead(scores, heads):
    columns = [slice(head * HD, (head + 1) * HD) for head in range(heads)]
    now = scores(columns[0])
    for head, cols in enumerate(columns):
        later = scores(columns[head + 1]) if head + 1 < heads else None
        yield head, cols, now
        now = later


def split_kernel(kv_ref, keys_ref, values_ref):
    keys_ref[...] = kv_ref[0]
    values_ref[...] = kv_ref[1]


def rows_kernel(n, *refs):
    for d in range(n):
        refs[n][d] = refs[d][...]


def near_kernel(heads, n, at_ref, rows_ref, *refs):
    near = [d for d in range(n) if d != n // 2]
    key_refs, value_refs, (mixed_ref, sum_ref, top_ref) = refs[: n - 1], refs[n - 1 : -3], refs[-3:]
    marks = frame_marks(at_ref, range(n), n)
    keys_marks = key_marks(near, ROWS, n)

    def scores(cols):
        queries = jnp.concatenate([rows_ref[:, :, cols].reshape(n * ROWS, HD), marks], axis=1)
        return scores_of(queries, jnp.concatenate([rows_of(key_refs, cols, ROWS), keys_marks], axis=1))

    for head, cols, now in ahead(scores, heads):
        weights, top = soften(now)
        mixed, total = mix(weights, rows_of(value_refs, cols, ROWS))
        for d in range(n):
            rows = slice(d * ROWS, (d + 1) * ROWS)
            mixed_ref[head, d], sum_ref[head, d], top_ref[head, d] = mixed[rows], total[rows], top[rows]


def finish_kernel(heads, n, flips, at_ref, rows_ref, mixed_ref, sum_ref, top_ref, keys_ref, values_ref, w_ref, *refs):
    blocks = [block for flip in flips for block in slot_blocks(at_ref, *flip, n)]
    marks = frame_marks(at_ref, blocks, n)
    keys_marks = key_marks([n // 2], TPF, n)

    def of(ref, head):
        return jnp.concatenate([ref[head, block] for block in blocks], axis=0)

    columns = [slice(head * HD, (head + 1) * HD) for head in range(heads)]
    scores, attended = [], []
    for cols in columns:
        queries = jnp.concatenate([rows_ref[block, :, cols] for block in blocks], axis=0)
        keys = jnp.concatenate([rows_of([keys_ref], cols, TPF), keys_marks], axis=1)
        scores.append(scores_of(jnp.concatenate([queries, marks], axis=1), keys))
    softened = [soften(now, of(top_ref, head)) for head, now in enumerate(scores)]
    more = [mix(weights, rows_of([values_ref], cols, TPF)) for (weights, _), cols in zip(softened, columns)]
    for head, ((_, top), (mixed, total)) in enumerate(zip(softened, more)):
        kept = jnp.exp2((of(top_ref, head) - top) * SCALE)
        mixed, total = mixed + of(mixed_ref, head) * kept, total + of(sum_ref, head) * kept
        attended.append((mixed / total).astype(jnp.bfloat16))
    rows = jnp.concatenate(attended, axis=1)
    refs[-1][...] = jnp.dot(rows, w_ref[...], preferred_element_type=jnp.float32).astype(refs[-1].dtype)


def sum_kernel(rows, kept_ref, from_core_ref, from_x_ref, total_ref):
    total = kept_ref[rows] + from_core_ref[1, rows].astype(jnp.float32) + from_x_ref[...].astype(jnp.float32)
    total_ref[...] = total.astype(total_ref.dtype)


def call(kernel, scalars, operands, outs, flops, after=()):
    vmem = pl.BlockSpec(memory_space=pltpu.VMEM)
    return pl.pallas_call(
        kernel,
        out_shape=[jax.ShapeDtypeStruct(shape, dtype) for shape, dtype in outs],
        in_specs=[pl.BlockSpec(memory_space=pltpu.SMEM)] * len(scalars)
        + [vmem] * len(operands)
        + [pl.BlockSpec(memory_space=pl.ANY)] * len(after),
        out_specs=[vmem] * len(outs),
        compiler_params=pltpu.CompilerParams(vmem_limit_bytes=20 * 1024 * 1024),
        cost_estimate=pl.CostEstimate(flops=flops, bytes_accessed=0, transcendentals=0),
    )(*scalars, *operands, *after)


def on_device_ring(queries, keys_values, out_weight):
    n = lax.axis_size("frames")
    frame, head = lax.axis_index("frames"), lax.axis_index("heads")
    z, y, x, core = frame >> 1, frame & 1, head >> 1, head & 1
    where = jnp.stack([ring_place(frame, n), z, y, x, core]).astype(jnp.int32)
    width, cols = out_weight.shape
    heads = width // HD
    f32, bf16 = jnp.float32, jnp.bfloat16
    block = (queries.shape, bf16)
    own = call(split_kernel, (), [keys_values], [block, block], 0)
    queries, keys, values = gather_ring([queries, *own], n)
    (rows,) = call(functools.partial(rows_kernel, n), (), queries, [((n, ROWS, width), bf16)], 0)
    far = n // 2
    state = call(
        functools.partial(near_kernel, heads, n),
        (where,),
        [rows, *(blocks[d] for blocks in (keys, values) for d in range(n) if d != far)],
        [((heads, n, ROWS, HD), f32)] * 3,
        4 * n * (n - 1) * ROWS**2 * width,
    )

    def finish(flips, dtype, after=()):
        (sums,) = call(
            functools.partial(finish_kernel, heads, n, flips),
            (where,),
            [rows, *state, keys[far], values[far], out_weight],
            [((len(flips) * 2 * ROWS, cols), dtype)],
            n * ROWS * width * cols,
            after,
        )
        return sums.reshape(len(flips), 2 * ROWS, cols)

    given = finish([(1, 1), (0, 1)], bf16)
    from_core = lax.ppermute(given, "heads", [(h, h ^ 1) for h in range(4)])
    sums = finish([(1, 0)], f32, (given,))[0]
    parts = [slice(slot * ROWS, (slot + 1) * ROWS) for slot in range(2)]
    given = [(sums[part] + from_core[0, part].astype(f32)).astype(bf16) for part in parts]
    from_x = [lax.ppermute(block, "heads", [(h, h ^ 2) for h in range(4)]) for block in given]
    kept = finish([(0, 0)], f32, given)[0]
    arrived = []
    for slot, part in enumerate(parts):
        pairs = []
        for f in range(n):
            for h in range(4):
                to = PATTERNS[(slot ^ (f & 1)) + 2 * (h >> 1)][f >> 1]
                pairs.append((4 * f + h, 4 * (2 * to + (h & 1)) + (f >> 1)))
        (total,) = call(
            functools.partial(sum_kernel, part), (), [kept, from_core, from_x[slot]], [((ROWS, cols), bf16)], 0
        )
        arrived.append(lax.ppermute(total, ("frames", "heads"), pairs))
    patterns = [[p[source] for p in PATTERNS].index(to) for source in range(4) for to in range(4)]
    straight = look_up(patterns, 4 * head + z) & 1 == 0
    low, high = arrived
    return jnp.concatenate([jnp.where(straight, low, high), jnp.where(straight, high, low)], axis=1)


def solution(mesh):
    in_specs = (P("frames", "heads"), P(None, "frames", "heads"), P("heads", "frames"))
    out_specs = P("frames", "heads")
    n, heads = mesh.shape["frames"], mesh.shape["heads"]
    total_frames = n * FR_DEV
    reach = min(reach_cap, (total_frames - 1) // 2)
    every = total_frames == 2 * reach + 2 and heads == 4 and n == 2 * heads
    return jax.shard_map(
        on_device_ring if every else on_device_band,
        mesh=mesh,
        in_specs=in_specs,
        out_specs=out_specs,
        check_vma=False,
    )
```

```python
import functools
import math

import jax
import jax.numpy as jnp
from jax import lax
from jax.experimental import pallas as pl
from jax.experimental.pallas import tpu as pltpu
from jax.sharding import PartitionSpec as P

HD = 128
TPF = 32
FR_DEV = 3
ROWS = FR_DEV * TPF
SCALE = HD ** (-0.5) * math.log2(math.e)


reach_cap = 32


def from_behind(x, axis, by):
    devices = lax.axis_size(axis)
    return lax.ppermute(x, axis, [(i, (i + by) % devices) for i in range(devices)])


def on_device_band(queries, keys_values, out_weight):
    total_frames = lax.axis_size("frames") * FR_DEV
    reach = min(reach_cap, (total_frames - 1) // 2)
    steps = (reach + FR_DEV - 1) // FR_DEV
    width = keys_values.shape[2]
    span = FR_DEV + 2 * reach
    stacked = keys_values.reshape(2, FR_DEV, TPF, width)
    pieces = []
    for offset in range(-steps, steps + 1):
        if offset == 0:
            pieces.append(stacked)
        else:
            pieces.append(from_behind(stacked, "frames", -offset))
    window = jnp.concatenate(pieces, axis=1)
    lower_frame = steps * FR_DEV - reach
    extended = window[:, lower_frame : lower_frame + span]
    keys_ext = extended[0].reshape(span * TPF, width)
    values_ext = extended[1].reshape(span * TPF, width)
    row_frame = jnp.arange(FR_DEV * TPF, dtype=jnp.int32) // TPF
    col_frame = jnp.arange(span * TPF, dtype=jnp.int32) // TPF
    allowed = (col_frame[None, :] >= row_frame[:, None]) & (
        col_frame[None, :] <= row_frame[:, None] + 2 * reach
    )
    results = []
    for head in range(width // HD):
        lower = head * HD
        query_cols = queries[:, lower : lower + HD]
        key_cols = keys_ext[:, lower : lower + HD]
        scores = lax.dot_general(
            query_cols, key_cols, (((1,), (1,)), ((), ())), preferred_element_type=jnp.float32
        )
        scores = scores * HD ** (-0.5)
        top = jnp.max(jnp.where(allowed, scores, -1e30), axis=1, keepdims=True)
        weights = jnp.where(allowed, jnp.exp(scores - top), 0.0)
        probs = (weights / jnp.sum(weights, axis=1, keepdims=True)).astype(jnp.bfloat16)
        results.append(
            jnp.dot(
                probs, values_ext[:, lower : lower + HD], preferred_element_type=jnp.float32
            ).astype(jnp.bfloat16)
        )
    attended = jnp.concatenate(results, axis=1)
    partial_rows = jnp.dot(
        attended,
        lax.all_gather(out_weight, "frames", axis=1, tiled=True),
        preferred_element_type=jnp.float32,
    )
    return lax.psum_scatter(
        partial_rows.astype(jnp.bfloat16), "heads", scatter_dimension=1, tiled=True
    )


def ring_order(n):
    return list(range(0, n, 2)) + list(range(n - 1, 0, -2))


def ring_place(f, n):
    return (f >> 1) + (f & 1) * (n - 1 - (f >> 1) * 2)


def hop(x, n, by):
    order = ring_order(n)
    pairs = []
    for i in range(n):
        for h in range(4):
            pairs.append((4 * order[i] + h, 4 * order[(i + by * (1 - 2 * (h & 1))) % n] + h))
    return lax.ppermute(x, ("frames", "heads"), pairs)


def gather_ring(streams, n):
    found = [[block] + [None] * (n - 1) for block in streams]
    for step in range(1, n // 2 + 1):
        for j, blocks in enumerate(found):
            for by in (1, -1):
                if step < n // 2 or (j % 2 == 0) == (by == 1):
                    blocks[by * step % n] = hop(blocks[by * (step - 1) % n], n, by)
    return found


def ring_distance(at_ref, owner, n):
    place, core = at_ref[0], at_ref[4]
    return (place - owner) * (1 - 2 * core) & (n - 1)


def frame_marks(at_ref, blocks, n):
    place, core = at_ref[0], at_ref[4]
    lane = lax.broadcasted_iota(jnp.int32, (TPF, HD), 1)
    marks = []
    for block in blocks:
        owner = (place - block * (1 - 2 * core)) & (n - 1)
        frame = FR_DEV * ring_distance(at_ref, owner ^ 2, n)
        for g in range(FR_DEV):
            marks.append((lane == frame + g) | (lane >= n * FR_DEV))
    return jnp.concatenate([jnp.where(mark, 1.0, 0.0) for mark in marks], axis=0).astype(jnp.bfloat16)


def key_marks(blocks, padding, n):
    lane = lax.broadcasted_iota(jnp.int32, (TPF, HD), 1)
    frames = [FR_DEV * block + g for block in blocks for g in range(FR_DEV)] + [n * FR_DEV] * (padding // TPF)
    return jnp.concatenate([jnp.where(lane == frame, -1e30, 0.0) for frame in frames], axis=0).astype(jnp.bfloat16)


def rows_of(refs, cols, padding=0):
    pieces = [ref[:, cols] for ref in refs]
    if padding:
        pieces.append(jnp.zeros((padding, HD), jnp.bfloat16))
    return jnp.concatenate(pieces, axis=0)


def scores_of(queries, keys):
    return lax.dot_general(queries, keys, (((1,), (1,)), ((), ())), preferred_element_type=jnp.float32)


def soften(scores, floor=None):
    weights, tops = [], []
    for r in range(0, scores.shape[0], TPF):
        parts = [scores[r : r + TPF, c : c + HD] for c in range(0, scores.shape[1], HD)]
        top = jnp.max(functools.reduce(jnp.maximum, parts), axis=1, keepdims=True)
        top = jnp.broadcast_to(top, (TPF, HD))
        if floor is not None:
            top = jnp.maximum(top, floor[r : r + TPF])
        weights.append(jnp.concatenate([jnp.exp2((p - top) * SCALE).astype(jnp.bfloat16) for p in parts], axis=1))
        tops.append(top)
    return jnp.concatenate(weights, axis=0), jnp.concatenate(tops, axis=0)


def mix(weights, values):
    ones = jnp.ones(values.shape, values.dtype)
    mixed = jnp.dot(weights, jnp.concatenate([values, ones], axis=1), preferred_element_type=jnp.float32)
    return mixed[:, :HD], mixed[:, HD:]


PATTERNS = ((3, 0, 1, 3), (1, 3, 2, 1), (2, 1, 0, 2), (0, 2, 3, 0))


def look_up(table, index):
    code = sum(entry << (2 * i) for i, entry in enumerate(table))
    return (jnp.int32(code - (code >> 31 << 32)) >> (2 * index)) & 3


def slot_blocks(at_ref, flip_x, flip_core, n):
    z, y, x, core = (at_ref[i] for i in range(1, 5))
    blocks = []
    for slot in range(2):
        to = look_up(sum(PATTERNS, ()), 4 * ((slot ^ y) + 2 * (x ^ flip_x)) + z)
        owner = to + (core ^ flip_core) * (n - 1 - 2 * to)
        blocks.append(ring_distance(at_ref, owner, n))
    return blocks


def ahead(scores, units):
    now = scores(units[0])
    for unit, following in zip(units, [*units[1:], None]):
        later = scores(following) if following else None
        yield unit, now
        now = later


def split_kernel(kv_ref, keys_ref, values_ref):
    keys_ref[...] = kv_ref[0]
    values_ref[...] = kv_ref[1]


def rows_kernel(n, *refs):
    for d in range(n):
        refs[n][d] = refs[d][...]


def near_kernel(heads, n, at_ref, rows_ref, *refs):
    near = [d for d in range(n) if d != n // 2]
    key_refs, value_refs, (mixed_ref, sum_ref, top_ref) = refs[: n - 1], refs[n - 1 : -3], refs[-3:]
    keys_marks = key_marks(near, ROWS, n)
    parts = [range(first, first + n // 2) for first in (0, n // 2)]
    marks = [frame_marks(at_ref, part, n) for part in parts]
    columns = [slice(head * HD, (head + 1) * HD) for head in range(heads)]
    units = [(head, i) for head in range(heads) for i in range(2)]

    def scores(unit):
        head, i = unit
        cols = columns[head]
        queries = jnp.concatenate([rows_ref[d, :, cols] for d in parts[i]], axis=0)
        keys = jnp.concatenate([rows_of(key_refs, cols, ROWS), keys_marks], axis=1)
        return scores_of(jnp.concatenate([queries, marks[i]], axis=1), keys)

    for (head, i), now in ahead(scores, units):
        weights, top = soften(now)
        mixed, total = mix(weights, rows_of(value_refs, columns[head], ROWS))
        for r, d in enumerate(parts[i]):
            rows = slice(r * ROWS, (r + 1) * ROWS)
            mixed_ref[head, d], sum_ref[head, d], top_ref[head, d] = mixed[rows], total[rows], top[rows]


def finish_kernel(heads, n, flips, at_ref, rows_ref, mixed_ref, sum_ref, top_ref, keys_ref, values_ref, w_ref, *refs):
    blocks = [block for flip in flips for block in slot_blocks(at_ref, *flip, n)]
    marks = frame_marks(at_ref, blocks, n)
    keys_marks = key_marks([n // 2], TPF, n)

    def of(ref, head):
        return jnp.concatenate([ref[head, block] for block in blocks], axis=0)

    columns = [slice(head * HD, (head + 1) * HD) for head in range(heads)]
    scores, attended = [], []
    for cols in columns:
        queries = jnp.concatenate([rows_ref[block, :, cols] for block in blocks], axis=0)
        keys = jnp.concatenate([rows_of([keys_ref], cols, TPF), keys_marks], axis=1)
        scores.append(scores_of(jnp.concatenate([queries, marks], axis=1), keys))
    softened = [soften(now, of(top_ref, head)) for head, now in enumerate(scores)]
    more = [mix(weights, rows_of([values_ref], cols, TPF)) for (weights, _), cols in zip(softened, columns)]
    for head, ((_, top), (mixed, total)) in enumerate(zip(softened, more)):
        kept = jnp.exp2((of(top_ref, head) - top) * SCALE)
        mixed, total = mixed + of(mixed_ref, head) * kept, total + of(sum_ref, head) * kept
        attended.append((mixed / total).astype(jnp.bfloat16))
    rows = jnp.concatenate(attended, axis=1)
    refs[-1][...] = jnp.dot(rows, w_ref[...], preferred_element_type=jnp.float32).astype(refs[-1].dtype)


def sum_kernel(rows, kept_ref, from_core_ref, from_x_ref, total_ref):
    total = kept_ref[rows] + from_core_ref[1, rows].astype(jnp.float32) + from_x_ref[...].astype(jnp.float32)
    total_ref[...] = total.astype(total_ref.dtype)


def call(kernel, scalars, operands, outs, flops, after=()):
    vmem = pl.BlockSpec(memory_space=pltpu.VMEM)
    return pl.pallas_call(
        kernel,
        out_shape=[jax.ShapeDtypeStruct(shape, dtype) for shape, dtype in outs],
        in_specs=[pl.BlockSpec(memory_space=pltpu.SMEM)] * len(scalars)
        + [vmem] * len(operands)
        + [pl.BlockSpec(memory_space=pl.ANY)] * len(after),
        out_specs=[vmem] * len(outs),
        compiler_params=pltpu.CompilerParams(vmem_limit_bytes=20 * 1024 * 1024),
        cost_estimate=pl.CostEstimate(flops=flops, bytes_accessed=0, transcendentals=0),
    )(*scalars, *operands, *after)


def on_device_ring(queries, keys_values, out_weight):
    n = lax.axis_size("frames")
    frame, head = lax.axis_index("frames"), lax.axis_index("heads")
    z, y, x, core = frame >> 1, frame & 1, head >> 1, head & 1
    where = jnp.stack([ring_place(frame, n), z, y, x, core]).astype(jnp.int32)
    width, cols = out_weight.shape
    heads = width // HD
    f32, bf16 = jnp.float32, jnp.bfloat16
    block = (queries.shape, bf16)
    own = call(split_kernel, (), [keys_values], [block, block], 0)
    queries, keys, values = gather_ring([queries, *own], n)
    (rows,) = call(functools.partial(rows_kernel, n), (), queries, [((n, ROWS, width), bf16)], 0)
    far = n // 2
    state = call(
        functools.partial(near_kernel, heads, n),
        (where,),
        [rows, *(blocks[d] for blocks in (keys, values) for d in range(n) if d != far)],
        [((heads, n, ROWS, HD), f32)] * 3,
        4 * n * (n - 1) * ROWS**2 * width,
    )

    def finish(flips, dtype, after=()):
        (sums,) = call(
            functools.partial(finish_kernel, heads, n, flips),
            (where,),
            [rows, *state, keys[far], values[far], out_weight],
            [((len(flips) * 2 * ROWS, cols), dtype)],
            n * ROWS * width * cols,
            after,
        )
        return sums.reshape(len(flips), 2 * ROWS, cols)

    given = finish([(1, 1), (0, 1)], bf16)
    from_core = lax.ppermute(given, "heads", [(h, h ^ 1) for h in range(4)])
    sums = finish([(1, 0)], f32, (given,))[0]
    parts = [slice(slot * ROWS, (slot + 1) * ROWS) for slot in range(2)]
    given = [(sums[part] + from_core[0, part].astype(f32)).astype(bf16) for part in parts]
    from_x = [lax.ppermute(block, "heads", [(h, h ^ 2) for h in range(4)]) for block in given]
    kept = finish([(0, 0)], f32, given)[0]
    arrived = []
    for slot, part in enumerate(parts):
        pairs = []
        for f in range(n):
            for h in range(4):
                to = PATTERNS[(slot ^ (f & 1)) + 2 * (h >> 1)][f >> 1]
                pairs.append((4 * f + h, 4 * (2 * to + (h & 1)) + (f >> 1)))
        (total,) = call(
            functools.partial(sum_kernel, part), (), [kept, from_core, from_x[slot]], [((ROWS, cols), bf16)], 0
        )
        arrived.append(lax.ppermute(total, ("frames", "heads"), pairs))
    patterns = [[p[source] for p in PATTERNS].index(to) for source in range(4) for to in range(4)]
    straight = look_up(patterns, 4 * head + z) & 1 == 0
    low, high = arrived
    return jnp.concatenate([jnp.where(straight, low, high), jnp.where(straight, high, low)], axis=1)


def solution(mesh):
    in_specs = (P("frames", "heads"), P(None, "frames", "heads"), P("heads", "frames"))
    out_specs = P("frames", "heads")
    n, heads = mesh.shape["frames"], mesh.shape["heads"]
    total_frames = n * FR_DEV
    reach = min(reach_cap, (total_frames - 1) // 2)
    every = total_frames == 2 * reach + 2 and heads == 4 and n == 2 * heads
    return jax.shard_map(
        on_device_ring if every else on_device_band,
        mesh=mesh,
        in_specs=in_specs,
        out_specs=out_specs,
        check_vma=False,
    )
```

```python
import functools
import math

import jax
import jax.numpy as jnp
from jax import lax
from jax.experimental import pallas as pl
from jax.experimental.pallas import tpu as pltpu
from jax.sharding import PartitionSpec as P

HD = 128
TPF = 32
FR_DEV = 3
ROWS = FR_DEV * TPF
SCALE = HD ** (-0.5) * math.log2(math.e)


reach_cap = 32


def from_behind(x, axis, by):
    devices = lax.axis_size(axis)
    return lax.ppermute(x, axis, [(i, (i + by) % devices) for i in range(devices)])


def on_device_band(queries, keys_values, out_weight):
    total_frames = lax.axis_size("frames") * FR_DEV
    reach = min(reach_cap, (total_frames - 1) // 2)
    steps = (reach + FR_DEV - 1) // FR_DEV
    width = keys_values.shape[2]
    span = FR_DEV + 2 * reach
    stacked = keys_values.reshape(2, FR_DEV, TPF, width)
    pieces = []
    for offset in range(-steps, steps + 1):
        if offset == 0:
            pieces.append(stacked)
        else:
            pieces.append(from_behind(stacked, "frames", -offset))
    window = jnp.concatenate(pieces, axis=1)
    lower_frame = steps * FR_DEV - reach
    extended = window[:, lower_frame : lower_frame + span]
    keys_ext = extended[0].reshape(span * TPF, width)
    values_ext = extended[1].reshape(span * TPF, width)
    row_frame = jnp.arange(FR_DEV * TPF, dtype=jnp.int32) // TPF
    col_frame = jnp.arange(span * TPF, dtype=jnp.int32) // TPF
    allowed = (col_frame[None, :] >= row_frame[:, None]) & (
        col_frame[None, :] <= row_frame[:, None] + 2 * reach
    )
    results = []
    for head in range(width // HD):
        lower = head * HD
        query_cols = queries[:, lower : lower + HD]
        key_cols = keys_ext[:, lower : lower + HD]
        scores = lax.dot_general(
            query_cols, key_cols, (((1,), (1,)), ((), ())), preferred_element_type=jnp.float32
        )
        scores = scores * HD ** (-0.5)
        top = jnp.max(jnp.where(allowed, scores, -1e30), axis=1, keepdims=True)
        weights = jnp.where(allowed, jnp.exp(scores - top), 0.0)
        probs = (weights / jnp.sum(weights, axis=1, keepdims=True)).astype(jnp.bfloat16)
        results.append(
            jnp.dot(
                probs, values_ext[:, lower : lower + HD], preferred_element_type=jnp.float32
            ).astype(jnp.bfloat16)
        )
    attended = jnp.concatenate(results, axis=1)
    partial_rows = jnp.dot(
        attended,
        lax.all_gather(out_weight, "frames", axis=1, tiled=True),
        preferred_element_type=jnp.float32,
    )
    return lax.psum_scatter(
        partial_rows.astype(jnp.bfloat16), "heads", scatter_dimension=1, tiled=True
    )


def ring_order(n):
    return list(range(0, n, 2)) + list(range(n - 1, 0, -2))


def ring_place(f, n):
    return (f >> 1) + (f & 1) * (n - 1 - (f >> 1) * 2)


def hop(x, n, by):
    order = ring_order(n)
    pairs = []
    for i in range(n):
        for h in range(4):
            pairs.append((4 * order[i] + h, 4 * order[(i + by * (1 - 2 * (h & 1))) % n] + h))
    return lax.ppermute(x, ("frames", "heads"), pairs)


def gather_ring(streams, n):
    found = [[block] + [None] * (n - 1) for block in streams]
    for step in range(1, n // 2 + 1):
        for j, blocks in enumerate(found):
            for by in (1, -1):
                if step < n // 2 or (j % 2 == 0) == (by == 1):
                    blocks[by * step % n] = hop(blocks[by * (step - 1) % n], n, by)
    return found


def ring_distance(at_ref, owner, n):
    place, core = at_ref[0], at_ref[4]
    return (place - owner) * (1 - 2 * core) & (n - 1)


def frame_marks(at_ref, blocks, n):
    place, core = at_ref[0], at_ref[4]
    lane = lax.broadcasted_iota(jnp.int32, (TPF, HD), 1)
    marks = []
    for block in blocks:
        owner = (place - block * (1 - 2 * core)) & (n - 1)
        frame = FR_DEV * ring_distance(at_ref, owner ^ 2, n)
        for g in range(FR_DEV):
            marks.append((lane == frame + g) | (lane >= n * FR_DEV))
    return jnp.concatenate([jnp.where(mark, 1.0, 0.0) for mark in marks], axis=0).astype(jnp.bfloat16)


def key_marks(blocks, padding, n):
    lane = lax.broadcasted_iota(jnp.int32, (TPF, HD), 1)
    frames = [FR_DEV * block + g for block in blocks for g in range(FR_DEV)] + [n * FR_DEV] * (padding // TPF)
    return jnp.concatenate([jnp.where(lane == frame, -1e30, 0.0) for frame in frames], axis=0).astype(jnp.bfloat16)


def rows_of(refs, cols, padding=0):
    pieces = [ref[:, cols] for ref in refs]
    if padding:
        pieces.append(jnp.zeros((padding, HD), jnp.bfloat16))
    return jnp.concatenate(pieces, axis=0)


def scores_of(queries, keys):
    return lax.dot_general(queries, keys, (((1,), (1,)), ((), ())), preferred_element_type=jnp.float32)


def soften(scores, floor=None):
    weights, tops = [], []
    for r in range(0, scores.shape[0], TPF):
        parts = [scores[r : r + TPF, c : c + HD] for c in range(0, scores.shape[1], HD)]
        top = jnp.max(functools.reduce(jnp.maximum, parts), axis=1, keepdims=True)
        top = jnp.broadcast_to(top, (TPF, HD))
        if floor is not None:
            top = jnp.maximum(top, floor[r : r + TPF])
        weights.append(jnp.concatenate([jnp.exp2((p - top) * SCALE).astype(jnp.bfloat16) for p in parts], axis=1))
        tops.append(top)
    return jnp.concatenate(weights, axis=0), jnp.concatenate(tops, axis=0)


def mix(weights, values):
    ones = jnp.ones(values.shape, values.dtype)
    mixed = jnp.dot(weights, jnp.concatenate([values, ones], axis=1), preferred_element_type=jnp.float32)
    return mixed[:, :HD], mixed[:, HD:]


PATTERNS = ((3, 0, 1, 3), (1, 3, 2, 1), (2, 1, 0, 2), (0, 2, 3, 0))


def look_up(table, index):
    code = sum(entry << (2 * i) for i, entry in enumerate(table))
    return (jnp.int32(code - (code >> 31 << 32)) >> (2 * index)) & 3


def slot_blocks(at_ref, flip_x, flip_core, n):
    z, y, x, core = (at_ref[i] for i in range(1, 5))
    blocks = []
    for slot in range(2):
        row_y = core ^ flip_core
        to = look_up(sum(PATTERNS, ()), 4 * ((slot ^ y ^ row_y) + 2 * (x ^ flip_x)) + z)
        owner = to + row_y * (n - 1 - 2 * to)
        blocks.append(ring_distance(at_ref, owner, n))
    return blocks


def ahead(scores, heads):
    columns = [slice(head * HD, (head + 1) * HD) for head in range(heads)]
    now = scores(columns[0])
    for head, cols in enumerate(columns):
        later = scores(columns[head + 1]) if head + 1 < heads else None
        yield head, cols, now
        now = later


def split_kernel(kv_ref, keys_ref, values_ref):
    keys_ref[...] = kv_ref[0]
    values_ref[...] = kv_ref[1]


def rows_kernel(n, *refs):
    for d in range(n):
        refs[n][d] = refs[d][...]


def near_kernel(heads, n, at_ref, rows_ref, *refs):
    near = [d for d in range(n) if d != n // 2]
    key_refs, value_refs, (mixed_ref, sum_ref, top_ref) = refs[: n - 1], refs[n - 1 : -3], refs[-3:]
    marks = frame_marks(at_ref, range(n), n)
    keys_marks = key_marks(near, ROWS, n)

    def scores(cols):
        queries = jnp.concatenate([rows_ref[:, :, cols].reshape(n * ROWS, HD), marks], axis=1)
        return scores_of(queries, jnp.concatenate([rows_of(key_refs, cols, ROWS), keys_marks], axis=1))

    for head, cols, now in ahead(scores, heads):
        weights, top = soften(now)
        mixed, total = mix(weights, rows_of(value_refs, cols, ROWS))
        for d in range(n):
            rows = slice(d * ROWS, (d + 1) * ROWS)
            mixed_ref[head, d], sum_ref[head, d], top_ref[head, d] = mixed[rows], total[rows], top[rows]


def finish_kernel(heads, n, flips, at_ref, rows_ref, mixed_ref, sum_ref, top_ref, keys_ref, values_ref, w_ref, *refs):
    blocks = [block for flip in flips for block in slot_blocks(at_ref, *flip, n)]
    marks = frame_marks(at_ref, blocks, n)
    keys_marks = key_marks([n // 2], TPF, n)

    def of(ref, head):
        return jnp.concatenate([ref[head, block] for block in blocks], axis=0)

    columns = [slice(head * HD, (head + 1) * HD) for head in range(heads)]
    scores, attended = [], []
    for cols in columns:
        queries = jnp.concatenate([rows_ref[block, :, cols] for block in blocks], axis=0)
        keys = jnp.concatenate([rows_of([keys_ref], cols, TPF), keys_marks], axis=1)
        scores.append(scores_of(jnp.concatenate([queries, marks], axis=1), keys))
    softened = [soften(now, of(top_ref, head)) for head, now in enumerate(scores)]
    more = [mix(weights, rows_of([values_ref], cols, TPF)) for (weights, _), cols in zip(softened, columns)]
    for head, ((_, top), (mixed, total)) in enumerate(zip(softened, more)):
        kept = jnp.exp2((of(top_ref, head) - top) * SCALE)
        mixed, total = mixed + of(mixed_ref, head) * kept, total + of(sum_ref, head) * kept
        attended.append((mixed / total).astype(jnp.bfloat16))
    rows = jnp.concatenate(attended, axis=1)
    refs[-1][...] = jnp.dot(rows, w_ref[...], preferred_element_type=jnp.float32).astype(refs[-1].dtype)


def sum_kernel(rows, kept_ref, from_core_ref, from_x_ref, total_ref):
    total = kept_ref[rows] + from_core_ref[1, rows].astype(jnp.float32) + from_x_ref[...].astype(jnp.float32)
    total_ref[...] = total.astype(total_ref.dtype)


def call(kernel, scalars, operands, outs, flops, after=()):
    vmem = pl.BlockSpec(memory_space=pltpu.VMEM)
    return pl.pallas_call(
        kernel,
        out_shape=[jax.ShapeDtypeStruct(shape, dtype) for shape, dtype in outs],
        in_specs=[pl.BlockSpec(memory_space=pltpu.SMEM)] * len(scalars)
        + [vmem] * len(operands)
        + [pl.BlockSpec(memory_space=pl.ANY)] * len(after),
        out_specs=[vmem] * len(outs),
        compiler_params=pltpu.CompilerParams(vmem_limit_bytes=20 * 1024 * 1024),
        cost_estimate=pl.CostEstimate(flops=flops, bytes_accessed=0, transcendentals=0),
    )(*scalars, *operands, *after)


def on_device_ring(queries, keys_values, out_weight):
    n = lax.axis_size("frames")
    frame, head = lax.axis_index("frames"), lax.axis_index("heads")
    z, y, x, core = frame >> 1, frame & 1, head >> 1, head & 1
    where = jnp.stack([ring_place(frame, n), z, y, x, core]).astype(jnp.int32)
    width, cols = out_weight.shape
    heads = width // HD
    f32, bf16 = jnp.float32, jnp.bfloat16
    block = (queries.shape, bf16)
    own = call(split_kernel, (), [keys_values], [block, block], 0)
    queries, keys, values = gather_ring([queries, *own], n)
    (rows,) = call(functools.partial(rows_kernel, n), (), queries, [((n, ROWS, width), bf16)], 0)
    far = n // 2
    state = call(
        functools.partial(near_kernel, heads, n),
        (where,),
        [rows, *(blocks[d] for blocks in (keys, values) for d in range(n) if d != far)],
        [((heads, n, ROWS, HD), f32)] * 3,
        4 * n * (n - 1) * ROWS**2 * width,
    )

    def finish(flips, dtype, after=()):
        (sums,) = call(
            functools.partial(finish_kernel, heads, n, flips),
            (where,),
            [rows, *state, keys[far], values[far], out_weight],
            [((len(flips) * 2 * ROWS, cols), dtype)],
            n * ROWS * width * cols,
            after,
        )
        return sums.reshape(len(flips), 2 * ROWS, cols)

    given = finish([(1, 1), (0, 1)], bf16)
    from_core = lax.ppermute(given, "heads", [(h, h ^ 1) for h in range(4)])
    sums = finish([(1, 0)], f32, (given,))[0]
    parts = [slice(slot * ROWS, (slot + 1) * ROWS) for slot in range(2)]
    given = [(sums[part] + from_core[0, part].astype(f32)).astype(bf16) for part in parts]
    from_x = [lax.ppermute(block, "heads", [(h, h ^ 2) for h in range(4)]) for block in given]
    kept = finish([(0, 0)], f32, given)[0]
    arrived = []
    for slot, part in enumerate(parts):
        pairs = []
        for f in range(n):
            for h in range(4):
                to = PATTERNS[(slot ^ (f & 1) ^ (h & 1)) + 2 * (h >> 1)][f >> 1]
                pairs.append((4 * f + h, 4 * (2 * to + (h & 1)) + (f >> 1)))
        (total,) = call(
            functools.partial(sum_kernel, part), (), [kept, from_core, from_x[slot]], [((ROWS, cols), bf16)], 0
        )
        arrived.append(lax.ppermute(total, ("frames", "heads"), pairs))
    patterns = [[p[source] for p in PATTERNS].index(to) for source in range(4) for to in range(4)]
    straight = (look_up(patterns, 4 * head + z) ^ y) & 1 == 0
    low, high = arrived
    return jnp.concatenate([jnp.where(straight, low, high), jnp.where(straight, high, low)], axis=1)


def solution(mesh):
    in_specs = (P("frames", "heads"), P(None, "frames", "heads"), P("heads", "frames"))
    out_specs = P("frames", "heads")
    n, heads = mesh.shape["frames"], mesh.shape["heads"]
    total_frames = n * FR_DEV
    reach = min(reach_cap, (total_frames - 1) // 2)
    every = total_frames == 2 * reach + 2 and heads == 4 and n == 2 * heads
    return jax.shard_map(
        on_device_ring if every else on_device_band,
        mesh=mesh,
        in_specs=in_specs,
        out_specs=out_specs,
        check_vma=False,
    )
```

```python
import functools
import math

import jax
import jax.numpy as jnp
from jax import lax
from jax.experimental import pallas as pl
from jax.experimental.pallas import tpu as pltpu
from jax.sharding import PartitionSpec as P

HD = 128
TPF = 32
FR_DEV = 3
ROWS = FR_DEV * TPF
SCALE = HD ** (-0.5) * math.log2(math.e)


reach_cap = 32


def from_behind(x, axis, by):
    devices = lax.axis_size(axis)
    return lax.ppermute(x, axis, [(i, (i + by) % devices) for i in range(devices)])


def on_device_band(queries, keys_values, out_weight):
    total_frames = lax.axis_size("frames") * FR_DEV
    reach = min(reach_cap, (total_frames - 1) // 2)
    steps = (reach + FR_DEV - 1) // FR_DEV
    width = keys_values.shape[2]
    span = FR_DEV + 2 * reach
    stacked = keys_values.reshape(2, FR_DEV, TPF, width)
    pieces = []
    for offset in range(-steps, steps + 1):
        if offset == 0:
            pieces.append(stacked)
        else:
            pieces.append(from_behind(stacked, "frames", -offset))
    window = jnp.concatenate(pieces, axis=1)
    lower_frame = steps * FR_DEV - reach
    extended = window[:, lower_frame : lower_frame + span]
    keys_ext = extended[0].reshape(span * TPF, width)
    values_ext = extended[1].reshape(span * TPF, width)
    row_frame = jnp.arange(FR_DEV * TPF, dtype=jnp.int32) // TPF
    col_frame = jnp.arange(span * TPF, dtype=jnp.int32) // TPF
    allowed = (col_frame[None, :] >= row_frame[:, None]) & (
        col_frame[None, :] <= row_frame[:, None] + 2 * reach
    )
    results = []
    for head in range(width // HD):
        lower = head * HD
        query_cols = queries[:, lower : lower + HD]
        key_cols = keys_ext[:, lower : lower + HD]
        scores = lax.dot_general(
            query_cols, key_cols, (((1,), (1,)), ((), ())), preferred_element_type=jnp.float32
        )
        scores = scores * HD ** (-0.5)
        top = jnp.max(jnp.where(allowed, scores, -1e30), axis=1, keepdims=True)
        weights = jnp.where(allowed, jnp.exp(scores - top), 0.0)
        probs = (weights / jnp.sum(weights, axis=1, keepdims=True)).astype(jnp.bfloat16)
        results.append(
            jnp.dot(
                probs, values_ext[:, lower : lower + HD], preferred_element_type=jnp.float32
            ).astype(jnp.bfloat16)
        )
    attended = jnp.concatenate(results, axis=1)
    partial_rows = jnp.dot(
        attended,
        lax.all_gather(out_weight, "frames", axis=1, tiled=True),
        preferred_element_type=jnp.float32,
    )
    return lax.psum_scatter(
        partial_rows.astype(jnp.bfloat16), "heads", scatter_dimension=1, tiled=True
    )


def ring_order(n):
    return list(range(0, n, 2)) + list(range(n - 1, 0, -2))


def ring_place(f, n):
    return (f >> 1) + (f & 1) * (n - 1 - (f >> 1) * 2)


def hop(x, n, by):
    order = ring_order(n)
    pairs = []
    for i in range(n):
        for h in range(4):
            pairs.append((4 * order[i] + h, 4 * order[(i + by * (1 - 2 * (h & 1))) % n] + h))
    return lax.ppermute(x, ("frames", "heads"), pairs)


def gather_ring(streams, n):
    found = [[block] + [None] * (n - 1) for block in streams]
    for step in range(1, n // 2 + 1):
        for j, blocks in enumerate(found):
            for by in (1, -1):
                if step < n // 2 or (j % 2 == 0) == (by == 1):
                    blocks[by * step % n] = hop(blocks[by * (step - 1) % n], n, by)
    return found


def ring_distance(at_ref, owner, n):
    place, core = at_ref[0], at_ref[4]
    return (place - owner) * (1 - 2 * core) & (n - 1)


def frame_marks(at_ref, blocks, n):
    place, core = at_ref[0], at_ref[4]
    lane = lax.broadcasted_iota(jnp.int32, (TPF, HD), 1)
    marks = []
    for block in blocks:
        owner = (place - block * (1 - 2 * core)) & (n - 1)
        frame = FR_DEV * ring_distance(at_ref, owner ^ 2, n)
        for g in range(FR_DEV):
            marks.append((lane == frame + g) | (lane >= n * FR_DEV))
    return jnp.concatenate([jnp.where(mark, 1.0, 0.0) for mark in marks], axis=0).astype(jnp.bfloat16)


def key_marks(blocks, padding, n):
    lane = lax.broadcasted_iota(jnp.int32, (TPF, HD), 1)
    frames = [FR_DEV * block + g for block in blocks for g in range(FR_DEV)] + [n * FR_DEV] * (padding // TPF)
    return jnp.concatenate([jnp.where(lane == frame, -1e30, 0.0) for frame in frames], axis=0).astype(jnp.bfloat16)


def rows_of(refs, cols, padding=0):
    pieces = [ref[:, cols] for ref in refs]
    if padding:
        pieces.append(jnp.zeros((padding, HD), jnp.bfloat16))
    return jnp.concatenate(pieces, axis=0)


def scores_of(queries, keys):
    return lax.dot_general(queries, keys, (((1,), (1,)), ((), ())), preferred_element_type=jnp.float32)


def soften(scores, floor=None):
    weights, tops = [], []
    for r in range(0, scores.shape[0], TPF):
        parts = [scores[r : r + TPF, c : c + HD] for c in range(0, scores.shape[1], HD)]
        top = jnp.max(functools.reduce(jnp.maximum, parts), axis=1, keepdims=True)
        top = jnp.broadcast_to(top, (TPF, HD))
        if floor is not None:
            top = jnp.maximum(top, floor[r : r + TPF])
        weights.append(jnp.concatenate([jnp.exp2((p - top) * SCALE).astype(jnp.bfloat16) for p in parts], axis=1))
        tops.append(top)
    return jnp.concatenate(weights, axis=0), jnp.concatenate(tops, axis=0)


def mix(weights, values):
    ones = jnp.ones(values.shape, values.dtype)
    mixed = jnp.dot(weights, jnp.concatenate([values, ones], axis=1), preferred_element_type=jnp.float32)
    return mixed[:, :HD], mixed[:, HD:]


PATTERNS = ((3, 0, 1, 3), (1, 3, 2, 1), (2, 1, 0, 2), (0, 2, 3, 0))


def look_up(table, index):
    code = sum(entry << (2 * i) for i, entry in enumerate(table))
    return (jnp.int32(code - (code >> 31 << 32)) >> (2 * index)) & 3


def slot_blocks(at_ref, flip_x, flip_core, n):
    z, y, x, core = (at_ref[i] for i in range(1, 5))
    blocks = []
    for slot in range(2):
        row_y = core ^ flip_core
        to = look_up(sum(PATTERNS, ()), 4 * ((slot ^ y ^ row_y) + 2 * (x ^ flip_x)) + z)
        owner = to + row_y * (n - 1 - 2 * to)
        blocks.append(ring_distance(at_ref, owner, n))
    return blocks


def ahead(scores, units):
    now = scores(units[0])
    for unit, following in zip(units, [*units[1:], None]):
        later = scores(following) if following else None
        yield unit, now
        now = later


def split_kernel(queries_ref, kv_ref, copy_ref, keys_ref, values_ref):
    copy_ref[...] = queries_ref[...]
    keys_ref[...] = kv_ref[0]
    values_ref[...] = kv_ref[1]


def rows_kernel(n, *refs):
    for d in range(n):
        refs[n][d] = refs[d][...]


def near_kernel(heads, n, at_ref, rows_ref, *refs):
    near = [d for d in range(n) if d != n // 2]
    key_refs, value_refs, (mixed_ref, sum_ref, top_ref) = refs[: n - 1], refs[n - 1 : -3], refs[-3:]
    keys_marks = key_marks(near, ROWS, n)
    parts = [range(first, first + n // 2) for first in (0, n // 2)]
    marks = [frame_marks(at_ref, part, n) for part in parts]
    columns = [slice(head * HD, (head + 1) * HD) for head in range(heads)]
    units = [(head, i) for head in range(heads) for i in range(2)]

    def scores(unit):
        head, i = unit
        cols = columns[head]
        queries = jnp.concatenate([rows_ref[d, :, cols] for d in parts[i]], axis=0)
        keys = jnp.concatenate([rows_of(key_refs, cols, ROWS), keys_marks], axis=1)
        return scores_of(jnp.concatenate([queries, marks[i]], axis=1), keys)

    for (head, i), now in ahead(scores, units):
        weights, top = soften(now)
        mixed, total = mix(weights, rows_of(value_refs, columns[head], ROWS))
        for r, d in enumerate(parts[i]):
            rows = slice(r * ROWS, (r + 1) * ROWS)
            mixed_ref[head, d], sum_ref[head, d], top_ref[head, d] = mixed[rows], total[rows], top[rows]


def finish_kernel(heads, n, flips, at_ref, rows_ref, mixed_ref, sum_ref, top_ref, keys_ref, values_ref, w_ref, *refs):
    blocks = [block for flip in flips for block in slot_blocks(at_ref, *flip, n)]
    marks = frame_marks(at_ref, blocks, n)
    keys_marks = key_marks([n // 2], TPF, n)

    def of(ref, head):
        return jnp.concatenate([ref[head, block] for block in blocks], axis=0)

    columns = [slice(head * HD, (head + 1) * HD) for head in range(heads)]
    scores, attended = [], []
    for cols in columns:
        queries = jnp.concatenate([rows_ref[block, :, cols] for block in blocks], axis=0)
        keys = jnp.concatenate([rows_of([keys_ref], cols, TPF), keys_marks], axis=1)
        scores.append(scores_of(jnp.concatenate([queries, marks], axis=1), keys))
    softened = [soften(now, of(top_ref, head)) for head, now in enumerate(scores)]
    more = [mix(weights, rows_of([values_ref], cols, TPF)) for (weights, _), cols in zip(softened, columns)]
    for head, ((_, top), (mixed, total)) in enumerate(zip(softened, more)):
        kept = jnp.exp2((of(top_ref, head) - top) * SCALE)
        mixed, total = mixed + of(mixed_ref, head) * kept, total + of(sum_ref, head) * kept
        attended.append((mixed / total).astype(jnp.bfloat16))
    rows = jnp.concatenate(attended, axis=1)
    refs[-1][...] = jnp.dot(rows, w_ref[...], preferred_element_type=jnp.float32).astype(refs[-1].dtype)


def sum_kernel(rows, kept_ref, from_core_ref, from_x_ref, total_ref):
    total = kept_ref[rows] + from_core_ref[1, rows].astype(jnp.float32) + from_x_ref[...].astype(jnp.float32)
    total_ref[...] = total.astype(total_ref.dtype)


def call(kernel, scalars, operands, outs, flops, after=()):
    vmem = pl.BlockSpec(memory_space=pltpu.VMEM)
    return pl.pallas_call(
        kernel,
        out_shape=[jax.ShapeDtypeStruct(shape, dtype) for shape, dtype in outs],
        in_specs=[pl.BlockSpec(memory_space=pltpu.SMEM)] * len(scalars)
        + [vmem] * len(operands)
        + [pl.BlockSpec(memory_space=pl.ANY)] * len(after),
        out_specs=[vmem] * len(outs),
        compiler_params=pltpu.CompilerParams(vmem_limit_bytes=20 * 1024 * 1024),
        cost_estimate=pl.CostEstimate(flops=flops, bytes_accessed=0, transcendentals=0),
    )(*scalars, *operands, *after)


def on_device_ring(queries, keys_values, out_weight):
    n = lax.axis_size("frames")
    frame, head = lax.axis_index("frames"), lax.axis_index("heads")
    z, y, x, core = frame >> 1, frame & 1, head >> 1, head & 1
    where = jnp.stack([ring_place(frame, n), z, y, x, core]).astype(jnp.int32)
    width, cols = out_weight.shape
    heads = width // HD
    f32, bf16 = jnp.float32, jnp.bfloat16
    block = (queries.shape, bf16)
    own_queries, *own = call(split_kernel, (), [queries, keys_values], [block] * 3, 0)
    queries, keys, values = gather_ring([queries, *own], n)
    queries = [own_queries, *queries[1:]]
    (rows,) = call(functools.partial(rows_kernel, n), (), queries, [((n, ROWS, width), bf16)], 0)
    far = n // 2
    state = call(
        functools.partial(near_kernel, heads, n),
        (where,),
        [rows, *(blocks[d] for blocks in (keys, values) for d in range(n) if d != far)],
        [((heads, n, ROWS, HD), f32)] * 3,
        4 * n * (n - 1) * ROWS**2 * width,
    )

    def finish(flips, dtype, after=()):
        (sums,) = call(
            functools.partial(finish_kernel, heads, n, flips),
            (where,),
            [rows, *state, keys[far], values[far], out_weight],
            [((len(flips) * 2 * ROWS, cols), dtype)],
            n * ROWS * width * cols,
            after,
        )
        return sums.reshape(len(flips), 2 * ROWS, cols)

    given = finish([(1, 1), (0, 1)], bf16)
    from_core = lax.ppermute(given, "heads", [(h, h ^ 1) for h in range(4)])
    sums = finish([(1, 0)], f32, (given,))[0]
    parts = [slice(slot * ROWS, (slot + 1) * ROWS) for slot in range(2)]
    given = [(sums[part] + from_core[0, part].astype(f32)).astype(bf16) for part in parts]
    from_x = [lax.ppermute(block, "heads", [(h, h ^ 2) for h in range(4)]) for block in given]
    kept = finish([(0, 0)], f32, given)[0]
    arrived = []
    for slot, part in enumerate(parts):
        pairs = []
        for f in range(n):
            for h in range(4):
                to = PATTERNS[(slot ^ (f & 1) ^ (h & 1)) + 2 * (h >> 1)][f >> 1]
                pairs.append((4 * f + h, 4 * (2 * to + (h & 1)) + (f >> 1)))
        (total,) = call(
            functools.partial(sum_kernel, part), (), [kept, from_core, from_x[slot]], [((ROWS, cols), bf16)], 0
        )
        arrived.append(lax.ppermute(total, ("frames", "heads"), pairs))
    patterns = [[p[source] for p in PATTERNS].index(to) for source in range(4) for to in range(4)]
    straight = (look_up(patterns, 4 * head + z) ^ y) & 1 == 0
    low, high = arrived
    return jnp.concatenate([jnp.where(straight, low, high), jnp.where(straight, high, low)], axis=1)


def solution(mesh):
    in_specs = (P("frames", "heads"), P(None, "frames", "heads"), P("heads", "frames"))
    out_specs = P("frames", "heads")
    n, heads = mesh.shape["frames"], mesh.shape["heads"]
    total_frames = n * FR_DEV
    reach = min(reach_cap, (total_frames - 1) // 2)
    every = total_frames == 2 * reach + 2 and heads == 4 and n == 2 * heads
    return jax.shard_map(
        on_device_ring if every else on_device_band,
        mesh=mesh,
        in_specs=in_specs,
        out_specs=out_specs,
        check_vma=False,
    )
```

```python
import functools
import math

import jax
import jax.numpy as jnp
from jax import lax
from jax.experimental import pallas as pl
from jax.experimental.pallas import tpu as pltpu
from jax.sharding import PartitionSpec as P

HD = 128
TPF = 32
FR_DEV = 3
ROWS = FR_DEV * TPF
SCALE = HD ** (-0.5) * math.log2(math.e)


reach_cap = 32


def from_behind(x, axis, by):
    devices = lax.axis_size(axis)
    return lax.ppermute(x, axis, [(i, (i + by) % devices) for i in range(devices)])


def on_device_band(queries, keys_values, out_weight):
    total_frames = lax.axis_size("frames") * FR_DEV
    reach = min(reach_cap, (total_frames - 1) // 2)
    steps = (reach + FR_DEV - 1) // FR_DEV
    width = keys_values.shape[2]
    span = FR_DEV + 2 * reach
    stacked = keys_values.reshape(2, FR_DEV, TPF, width)
    pieces = []
    for offset in range(-steps, steps + 1):
        if offset == 0:
            pieces.append(stacked)
        else:
            pieces.append(from_behind(stacked, "frames", -offset))
    window = jnp.concatenate(pieces, axis=1)
    lower_frame = steps * FR_DEV - reach
    extended = window[:, lower_frame : lower_frame + span]
    keys_ext = extended[0].reshape(span * TPF, width)
    values_ext = extended[1].reshape(span * TPF, width)
    row_frame = jnp.arange(FR_DEV * TPF, dtype=jnp.int32) // TPF
    col_frame = jnp.arange(span * TPF, dtype=jnp.int32) // TPF
    allowed = (col_frame[None, :] >= row_frame[:, None]) & (
        col_frame[None, :] <= row_frame[:, None] + 2 * reach
    )
    results = []
    for head in range(width // HD):
        lower = head * HD
        query_cols = queries[:, lower : lower + HD]
        key_cols = keys_ext[:, lower : lower + HD]
        scores = lax.dot_general(
            query_cols, key_cols, (((1,), (1,)), ((), ())), preferred_element_type=jnp.float32
        )
        scores = scores * HD ** (-0.5)
        top = jnp.max(jnp.where(allowed, scores, -1e30), axis=1, keepdims=True)
        weights = jnp.where(allowed, jnp.exp(scores - top), 0.0)
        probs = (weights / jnp.sum(weights, axis=1, keepdims=True)).astype(jnp.bfloat16)
        results.append(
            jnp.dot(
                probs, values_ext[:, lower : lower + HD], preferred_element_type=jnp.float32
            ).astype(jnp.bfloat16)
        )
    attended = jnp.concatenate(results, axis=1)
    partial_rows = jnp.dot(
        attended,
        lax.all_gather(out_weight, "frames", axis=1, tiled=True),
        preferred_element_type=jnp.float32,
    )
    return lax.psum_scatter(
        partial_rows.astype(jnp.bfloat16), "heads", scatter_dimension=1, tiled=True
    )


def ring_order(n):
    return list(range(0, n, 2)) + list(range(n - 1, 0, -2))


def ring_place(f, n):
    return (f >> 1) + (f & 1) * (n - 1 - (f >> 1) * 2)


def hop(x, n, by):
    order = ring_order(n)
    pairs = []
    for i in range(n):
        for h in range(4):
            pairs.append((4 * order[i] + h, 4 * order[(i + by * (1 - 2 * (h & 1))) % n] + h))
    return lax.ppermute(x, ("frames", "heads"), pairs)


def gather_ring(streams, n):
    found = [[block] + [None] * (n - 1) for block in streams]
    for step in range(1, n // 2 + 1):
        for j, blocks in enumerate(found):
            for by in (1, -1):
                if step < n // 2 or (j % 2 == 0) == (by == 1):
                    blocks[by * step % n] = hop(blocks[by * (step - 1) % n], n, by)
    return found


def ring_distance(at_ref, owner, n):
    place, core = at_ref[0], at_ref[4]
    return (place - owner) * (1 - 2 * core) & (n - 1)


def frame_marks(at_ref, blocks, n):
    place, core = at_ref[0], at_ref[4]
    lane = lax.broadcasted_iota(jnp.int32, (TPF, HD), 1)
    marks = []
    for block in blocks:
        owner = (place - block * (1 - 2 * core)) & (n - 1)
        frame = FR_DEV * ring_distance(at_ref, owner ^ 2, n)
        for g in range(FR_DEV):
            marks.append((lane == frame + g) | (lane >= n * FR_DEV))
    return jnp.concatenate([jnp.where(mark, 1.0, 0.0) for mark in marks], axis=0).astype(jnp.bfloat16)


def key_marks(blocks, padding, n):
    lane = lax.broadcasted_iota(jnp.int32, (TPF, HD), 1)
    frames = [FR_DEV * block + g for block in blocks for g in range(FR_DEV)] + [n * FR_DEV] * (padding // TPF)
    return jnp.concatenate([jnp.where(lane == frame, -1e30, 0.0) for frame in frames], axis=0).astype(jnp.bfloat16)


def rows_of(refs, cols, padding=0):
    pieces = [ref[:, cols] for ref in refs]
    if padding:
        pieces.append(jnp.zeros((padding, HD), jnp.bfloat16))
    return jnp.concatenate(pieces, axis=0)


def scores_of(queries, keys):
    return lax.dot_general(queries, keys, (((1,), (1,)), ((), ())), preferred_element_type=jnp.float32)


def soften(scores, floor=None):
    weights, tops = [], []
    for r in range(0, scores.shape[0], TPF):
        parts = [scores[r : r + TPF, c : c + HD] for c in range(0, scores.shape[1], HD)]
        top = jnp.max(functools.reduce(jnp.maximum, parts), axis=1, keepdims=True)
        top = jnp.broadcast_to(top, (TPF, HD))
        if floor is not None:
            top = jnp.maximum(top, floor[r : r + TPF])
        weights.append(jnp.concatenate([jnp.exp2((p - top) * SCALE).astype(jnp.bfloat16) for p in parts], axis=1))
        tops.append(top)
    return jnp.concatenate(weights, axis=0), jnp.concatenate(tops, axis=0)


def mix(weights, values):
    ones = jnp.ones(values.shape, values.dtype)
    mixed = jnp.dot(weights, jnp.concatenate([values, ones], axis=1), preferred_element_type=jnp.float32)
    return mixed[:, :HD], mixed[:, HD:]


PATTERNS = ((3, 0, 1, 1), (1, 3, 2, 3), (2, 2, 3, 0), (0, 1, 0, 2))


def look_up(table, index):
    code = sum(entry << (2 * i) for i, entry in enumerate(table))
    return (jnp.int32(code - (code >> 31 << 32)) >> (2 * index)) & 3


def slot_blocks(at_ref, flip_x, flip_core, n):
    z, y, x, core = (at_ref[i] for i in range(1, 5))
    blocks = []
    for slot in range(2):
        row_y = core ^ flip_core
        to = look_up(sum(PATTERNS, ()), 4 * ((slot ^ y ^ row_y) + 2 * (x ^ flip_x)) + z)
        owner = to + row_y * (n - 1 - 2 * to)
        blocks.append(ring_distance(at_ref, owner, n))
    return blocks


def ahead(scores, heads):
    columns = [slice(head * HD, (head + 1) * HD) for head in range(heads)]
    now = scores(columns[0])
    for head, cols in enumerate(columns):
        later = scores(columns[head + 1]) if head + 1 < heads else None
        yield head, cols, now
        now = later


def split_kernel(kv_ref, keys_ref, values_ref):
    keys_ref[...] = kv_ref[0]
    values_ref[...] = kv_ref[1]


def rows_kernel(n, *refs):
    for d in range(n):
        refs[n][d] = refs[d][...]


def near_kernel(heads, n, at_ref, rows_ref, *refs):
    near = [d for d in range(n) if d != n // 2]
    key_refs, value_refs, (mixed_ref, sum_ref, top_ref) = refs[: n - 1], refs[n - 1 : -3], refs[-3:]
    marks = frame_marks(at_ref, range(n), n)
    keys_marks = key_marks(near, ROWS, n)

    def scores(cols):
        queries = jnp.concatenate([rows_ref[:, :, cols].reshape(n * ROWS, HD), marks], axis=1)
        return scores_of(queries, jnp.concatenate([rows_of(key_refs, cols, ROWS), keys_marks], axis=1))

    for head, cols, now in ahead(scores, heads):
        weights, top = soften(now)
        mixed, total = mix(weights, rows_of(value_refs, cols, ROWS))
        for d in range(n):
            rows = slice(d * ROWS, (d + 1) * ROWS)
            mixed_ref[head, d], sum_ref[head, d], top_ref[head, d] = mixed[rows], total[rows], top[rows]


def finish_kernel(heads, n, flips, at_ref, rows_ref, mixed_ref, sum_ref, top_ref, keys_ref, values_ref, w_ref, *refs):
    blocks = [block for flip in flips for block in slot_blocks(at_ref, *flip, n)]
    marks = frame_marks(at_ref, blocks, n)
    keys_marks = key_marks([n // 2], TPF, n)

    def of(ref, head):
        return jnp.concatenate([ref[head, block] for block in blocks], axis=0)

    columns = [slice(head * HD, (head + 1) * HD) for head in range(heads)]
    scores, attended = [], []
    for cols in columns:
        queries = jnp.concatenate([rows_ref[block, :, cols] for block in blocks], axis=0)
        keys = jnp.concatenate([rows_of([keys_ref], cols, TPF), keys_marks], axis=1)
        scores.append(scores_of(jnp.concatenate([queries, marks], axis=1), keys))
    softened = [soften(now, of(top_ref, head)) for head, now in enumerate(scores)]
    more = [mix(weights, rows_of([values_ref], cols, TPF)) for (weights, _), cols in zip(softened, columns)]
    for head, ((_, top), (mixed, total)) in enumerate(zip(softened, more)):
        kept = jnp.exp2((of(top_ref, head) - top) * SCALE)
        mixed, total = mixed + of(mixed_ref, head) * kept, total + of(sum_ref, head) * kept
        attended.append((mixed / total).astype(jnp.bfloat16))
    rows = jnp.concatenate(attended, axis=1)
    refs[-1][...] = jnp.dot(rows, w_ref[...], preferred_element_type=jnp.float32).astype(refs[-1].dtype)


def sum_kernel(rows, kept_ref, from_core_ref, from_x_ref, total_ref):
    total = kept_ref[rows] + from_core_ref[1, rows].astype(jnp.float32) + from_x_ref[...].astype(jnp.float32)
    total_ref[...] = total.astype(total_ref.dtype)


def call(kernel, scalars, operands, outs, flops, after=()):
    vmem = pl.BlockSpec(memory_space=pltpu.VMEM)
    return pl.pallas_call(
        kernel,
        out_shape=[jax.ShapeDtypeStruct(shape, dtype) for shape, dtype in outs],
        in_specs=[pl.BlockSpec(memory_space=pltpu.SMEM)] * len(scalars)
        + [vmem] * len(operands)
        + [pl.BlockSpec(memory_space=pl.ANY)] * len(after),
        out_specs=[vmem] * len(outs),
        compiler_params=pltpu.CompilerParams(vmem_limit_bytes=20 * 1024 * 1024),
        cost_estimate=pl.CostEstimate(flops=flops, bytes_accessed=0, transcendentals=0),
    )(*scalars, *operands, *after)


def on_device_ring(queries, keys_values, out_weight):
    n = lax.axis_size("frames")
    frame, head = lax.axis_index("frames"), lax.axis_index("heads")
    z, y, x, core = frame >> 1, frame & 1, head >> 1, head & 1
    where = jnp.stack([ring_place(frame, n), z, y, x, core]).astype(jnp.int32)
    width, cols = out_weight.shape
    heads = width // HD
    f32, bf16 = jnp.float32, jnp.bfloat16
    block = (queries.shape, bf16)
    own = call(split_kernel, (), [keys_values], [block, block], 0)
    queries, keys, values = gather_ring([queries, *own], n)
    (rows,) = call(functools.partial(rows_kernel, n), (), queries, [((n, ROWS, width), bf16)], 0)
    far = n // 2
    state = call(
        functools.partial(near_kernel, heads, n),
        (where,),
        [rows, *(blocks[d] for blocks in (keys, values) for d in range(n) if d != far)],
        [((heads, n, ROWS, HD), f32)] * 3,
        4 * n * (n - 1) * ROWS**2 * width,
    )

    def finish(flips, dtype, after=()):
        (sums,) = call(
            functools.partial(finish_kernel, heads, n, flips),
            (where,),
            [rows, *state, keys[far], values[far], out_weight],
            [((len(flips) * 2 * ROWS, cols), dtype)],
            n * ROWS * width * cols,
            after,
        )
        return sums.reshape(len(flips), 2 * ROWS, cols)

    given = finish([(1, 1), (0, 1)], bf16)
    from_core = lax.ppermute(given, "heads", [(h, h ^ 1) for h in range(4)])
    sums = finish([(1, 0)], f32, (given,))[0]
    parts = [slice(slot * ROWS, (slot + 1) * ROWS) for slot in range(2)]
    given = [(sums[part] + from_core[0, part].astype(f32)).astype(bf16) for part in parts]
    from_x = [lax.ppermute(block, "heads", [(h, h ^ 2) for h in range(4)]) for block in given]
    kept = finish([(0, 0)], f32, given)[0]
    arrived = []
    for slot, part in enumerate(parts):
        pairs = []
        for f in range(n):
            for h in range(4):
                to = PATTERNS[(slot ^ (f & 1) ^ (h & 1)) + 2 * (h >> 1)][f >> 1]
                pairs.append((4 * f + h, 4 * (2 * to + (h & 1)) + (f >> 1)))
        (total,) = call(
            functools.partial(sum_kernel, part), (), [kept, from_core, from_x[slot]], [((ROWS, cols), bf16)], 0
        )
        arrived.append(lax.ppermute(total, ("frames", "heads"), pairs))
    patterns = [[p[source] for p in PATTERNS].index(to) for source in range(4) for to in range(4)]
    straight = (look_up(patterns, 4 * head + z) ^ y) & 1 == 0
    low, high = arrived
    return jnp.concatenate([jnp.where(straight, low, high), jnp.where(straight, high, low)], axis=1)


def solution(mesh):
    in_specs = (P("frames", "heads"), P(None, "frames", "heads"), P("heads", "frames"))
    out_specs = P("frames", "heads")
    n, heads = mesh.shape["frames"], mesh.shape["heads"]
    total_frames = n * FR_DEV
    reach = min(reach_cap, (total_frames - 1) // 2)
    every = total_frames == 2 * reach + 2 and heads == 4 and n == 2 * heads
    return jax.shard_map(
        on_device_ring if every else on_device_band,
        mesh=mesh,
        in_specs=in_specs,
        out_specs=out_specs,
        check_vma=False,
    )
```

```python
import functools
import math

import jax
import jax.numpy as jnp
from jax import lax
from jax.experimental import pallas as pl
from jax.experimental.pallas import tpu as pltpu
from jax.sharding import PartitionSpec as P

HD = 128
TPF = 32
FR_DEV = 3
ROWS = FR_DEV * TPF
SCALE = HD ** (-0.5) * math.log2(math.e)


reach_cap = 32


def from_behind(x, axis, by):
    devices = lax.axis_size(axis)
    return lax.ppermute(x, axis, [(i, (i + by) % devices) for i in range(devices)])


def on_device_band(queries, keys_values, out_weight):
    total_frames = lax.axis_size("frames") * FR_DEV
    reach = min(reach_cap, (total_frames - 1) // 2)
    steps = (reach + FR_DEV - 1) // FR_DEV
    width = keys_values.shape[2]
    span = FR_DEV + 2 * reach
    stacked = keys_values.reshape(2, FR_DEV, TPF, width)
    pieces = []
    for offset in range(-steps, steps + 1):
        if offset == 0:
            pieces.append(stacked)
        else:
            pieces.append(from_behind(stacked, "frames", -offset))
    window = jnp.concatenate(pieces, axis=1)
    lower_frame = steps * FR_DEV - reach
    extended = window[:, lower_frame : lower_frame + span]
    keys_ext = extended[0].reshape(span * TPF, width)
    values_ext = extended[1].reshape(span * TPF, width)
    row_frame = jnp.arange(FR_DEV * TPF, dtype=jnp.int32) // TPF
    col_frame = jnp.arange(span * TPF, dtype=jnp.int32) // TPF
    allowed = (col_frame[None, :] >= row_frame[:, None]) & (
        col_frame[None, :] <= row_frame[:, None] + 2 * reach
    )
    results = []
    for head in range(width // HD):
        lower = head * HD
        query_cols = queries[:, lower : lower + HD]
        key_cols = keys_ext[:, lower : lower + HD]
        scores = lax.dot_general(
            query_cols, key_cols, (((1,), (1,)), ((), ())), preferred_element_type=jnp.float32
        )
        scores = scores * HD ** (-0.5)
        top = jnp.max(jnp.where(allowed, scores, -1e30), axis=1, keepdims=True)
        weights = jnp.where(allowed, jnp.exp(scores - top), 0.0)
        probs = (weights / jnp.sum(weights, axis=1, keepdims=True)).astype(jnp.bfloat16)
        results.append(
            jnp.dot(
                probs, values_ext[:, lower : lower + HD], preferred_element_type=jnp.float32
            ).astype(jnp.bfloat16)
        )
    attended = jnp.concatenate(results, axis=1)
    partial_rows = jnp.dot(
        attended,
        lax.all_gather(out_weight, "frames", axis=1, tiled=True),
        preferred_element_type=jnp.float32,
    )
    return lax.psum_scatter(
        partial_rows.astype(jnp.bfloat16), "heads", scatter_dimension=1, tiled=True
    )


def ring_order(n):
    return list(range(0, n, 2)) + list(range(n - 1, 0, -2))


def ring_place(f, n):
    return (f >> 1) + (f & 1) * (n - 1 - (f >> 1) * 2)


def hop(x, n, by):
    order = ring_order(n)
    pairs = []
    for i in range(n):
        for h in range(4):
            pairs.append((4 * order[i] + h, 4 * order[(i + by * (1 - 2 * (h & 1))) % n] + h))
    return lax.ppermute(x, ("frames", "heads"), pairs)


def gather_ring(streams, n):
    found = [[block] + [None] * (n - 1) for block in streams]
    for step in range(1, n // 2 + 1):
        for j, blocks in enumerate(found):
            for by in (1, -1):
                if step < n // 2 or (j % 2 == 0) == (by == 1):
                    blocks[by * step % n] = hop(blocks[by * (step - 1) % n], n, by)
    return found


def ring_distance(at_ref, owner, n):
    place, core = at_ref[0], at_ref[4]
    return (place - owner) * (1 - 2 * core) & (n - 1)


def frame_marks(at_ref, blocks, n):
    place, core = at_ref[0], at_ref[4]
    lane = lax.broadcasted_iota(jnp.int32, (TPF, HD), 1)
    marks = []
    for block in blocks:
        owner = (place - block * (1 - 2 * core)) & (n - 1)
        frame = FR_DEV * ring_distance(at_ref, owner ^ 2, n)
        for g in range(FR_DEV):
            marks.append((lane == frame + g) | (lane >= n * FR_DEV))
    return jnp.concatenate([jnp.where(mark, 1.0, 0.0) for mark in marks], axis=0).astype(jnp.bfloat16)


def key_marks(blocks, padding, n):
    lane = lax.broadcasted_iota(jnp.int32, (TPF, HD), 1)
    frames = [FR_DEV * block + g for block in blocks for g in range(FR_DEV)] + [n * FR_DEV] * (padding // TPF)
    return jnp.concatenate([jnp.where(lane == frame, -1e30, 0.0) for frame in frames], axis=0).astype(jnp.bfloat16)


def rows_of(refs, cols, padding=0):
    pieces = [ref[:, cols] for ref in refs]
    if padding:
        pieces.append(jnp.zeros((padding, HD), jnp.bfloat16))
    return jnp.concatenate(pieces, axis=0)


def scores_of(queries, keys):
    return lax.dot_general(queries, keys, (((1,), (1,)), ((), ())), preferred_element_type=jnp.float32)


def soften(scores, floor=None):
    weights, tops = [], []
    for r in range(0, scores.shape[0], TPF):
        parts = [scores[r : r + TPF, c : c + HD] for c in range(0, scores.shape[1], HD)]
        top = jnp.max(functools.reduce(jnp.maximum, parts), axis=1, keepdims=True)
        top = jnp.broadcast_to(top, (TPF, HD))
        if floor is not None:
            top = jnp.maximum(top, floor[r : r + TPF])
        weights.append(jnp.concatenate([jnp.exp2((p - top) * SCALE).astype(jnp.bfloat16) for p in parts], axis=1))
        tops.append(top)
    return jnp.concatenate(weights, axis=0), jnp.concatenate(tops, axis=0)


def mix(weights, values):
    ones = jnp.ones(values.shape, values.dtype)
    mixed = jnp.dot(weights, jnp.concatenate([values, ones], axis=1), preferred_element_type=jnp.float32)
    return mixed[:, :HD], mixed[:, HD:]


PATTERNS = ((3, 0, 1, 3), (1, 3, 2, 1), (2, 1, 0, 2), (0, 2, 3, 0))


def look_up(table, index):
    code = sum(entry << (2 * i) for i, entry in enumerate(table))
    return (jnp.int32(code - (code >> 31 << 32)) >> (2 * index)) & 3


def slot_blocks(at_ref, flip_x, flip_core, n):
    z, y, x, core = (at_ref[i] for i in range(1, 5))
    blocks = []
    for slot in range(2):
        row_y = core ^ flip_core
        to = look_up(sum(PATTERNS, ()), 4 * ((slot ^ y ^ row_y) + 2 * (x ^ flip_x)) + z)
        owner = to + row_y * (n - 1 - 2 * to)
        blocks.append(ring_distance(at_ref, owner, n))
    return blocks


def ahead(scores, units):
    now = scores(units[0])
    for unit, following in zip(units, [*units[1:], None]):
        later = scores(following) if following else None
        yield unit, now
        now = later


def split_kernel(kv_ref, keys_ref, values_ref):
    keys_ref[...] = kv_ref[0]
    values_ref[...] = kv_ref[1]


def rows_kernel(n, *refs):
    for d in range(n):
        refs[n][d] = refs[d][...]


def near_kernel(heads, n, at_ref, rows_ref, *refs):
    near = [d for d in range(n) if d != n // 2]
    key_refs, value_refs, (mixed_ref, sum_ref, top_ref) = refs[: n - 1], refs[n - 1 : -3], refs[-3:]
    keys_marks = key_marks(near, ROWS, n)
    parts = [range(first, first + n // 2) for first in (0, n // 2)]
    marks = [frame_marks(at_ref, part, n) for part in parts]
    columns = [slice(head * HD, (head + 1) * HD) for head in range(heads)]
    units = [(head, i) for head in range(heads) for i in range(2)]

    def scores(unit):
        head, i = unit
        cols = columns[head]
        queries = jnp.concatenate([rows_ref[d, :, cols] for d in parts[i]], axis=0)
        keys = jnp.concatenate([rows_of(key_refs, cols, ROWS), keys_marks], axis=1)
        return scores_of(jnp.concatenate([queries, marks[i]], axis=1), keys)

    for (head, i), now in ahead(scores, units):
        weights, top = soften(now)
        mixed, total = mix(weights, rows_of(value_refs, columns[head], ROWS))
        for r, d in enumerate(parts[i]):
            rows = slice(r * ROWS, (r + 1) * ROWS)
            mixed_ref[head, d], sum_ref[head, d], top_ref[head, d] = mixed[rows], total[rows], top[rows]


def finish_kernel(heads, n, flips, at_ref, rows_ref, mixed_ref, sum_ref, top_ref, keys_ref, values_ref, w_ref, *refs):
    blocks = [block for flip in flips for block in slot_blocks(at_ref, *flip, n)]
    marks = frame_marks(at_ref, blocks, n)
    keys_marks = key_marks([n // 2], TPF, n)

    def of(ref, head):
        return jnp.concatenate([ref[head, block] for block in blocks], axis=0)

    columns = [slice(head * HD, (head + 1) * HD) for head in range(heads)]
    scores, attended = [], []
    for cols in columns:
        queries = jnp.concatenate([rows_ref[block, :, cols] for block in blocks], axis=0)
        keys = jnp.concatenate([rows_of([keys_ref], cols, TPF), keys_marks], axis=1)
        scores.append(scores_of(jnp.concatenate([queries, marks], axis=1), keys))
    softened = [soften(now, of(top_ref, head)) for head, now in enumerate(scores)]
    more = [mix(weights, rows_of([values_ref], cols, TPF)) for (weights, _), cols in zip(softened, columns)]
    for head, ((_, top), (mixed, total)) in enumerate(zip(softened, more)):
        kept = jnp.exp2((of(top_ref, head) - top) * SCALE)
        mixed, total = mixed + of(mixed_ref, head) * kept, total + of(sum_ref, head) * kept
        attended.append((mixed / total).astype(jnp.bfloat16))
    rows = jnp.concatenate(attended, axis=1)
    refs[-1][...] = jnp.dot(rows, w_ref[...], preferred_element_type=jnp.float32).astype(refs[-1].dtype)


def sum_kernel(rows, kept_ref, from_core_ref, from_x_ref, total_ref):
    total = kept_ref[rows] + from_core_ref[1, rows].astype(jnp.float32) + from_x_ref[...].astype(jnp.float32)
    total_ref[...] = total.astype(total_ref.dtype)


def call(kernel, scalars, operands, outs, flops, after=()):
    vmem = pl.BlockSpec(memory_space=pltpu.VMEM)
    return pl.pallas_call(
        kernel,
        out_shape=[jax.ShapeDtypeStruct(shape, dtype) for shape, dtype in outs],
        in_specs=[pl.BlockSpec(memory_space=pltpu.SMEM)] * len(scalars)
        + [vmem] * len(operands)
        + [pl.BlockSpec(memory_space=pl.ANY)] * len(after),
        out_specs=[vmem] * len(outs),
        compiler_params=pltpu.CompilerParams(vmem_limit_bytes=20 * 1024 * 1024),
        cost_estimate=pl.CostEstimate(flops=flops, bytes_accessed=0, transcendentals=0),
    )(*scalars, *operands, *after)


def on_device_ring(queries, keys_values, out_weight):
    n = lax.axis_size("frames")
    frame, head = lax.axis_index("frames"), lax.axis_index("heads")
    z, y, x, core = frame >> 1, frame & 1, head >> 1, head & 1
    where = jnp.stack([ring_place(frame, n), z, y, x, core]).astype(jnp.int32)
    width, cols = out_weight.shape
    heads = width // HD
    f32, bf16 = jnp.float32, jnp.bfloat16
    block = (queries.shape, bf16)
    own = call(split_kernel, (), [keys_values], [block, block], 0)
    queries, keys, values = gather_ring([queries, *own], n)
    (rows,) = call(functools.partial(rows_kernel, n), (), queries, [((n, ROWS, width), bf16)], 0)
    far = n // 2
    state = call(
        functools.partial(near_kernel, heads, n),
        (where,),
        [rows, *(blocks[d] for blocks in (keys, values) for d in range(n) if d != far)],
        [((heads, n, ROWS, HD), f32)] * 3,
        4 * n * (n - 1) * ROWS**2 * width,
    )

    def finish(flips, dtype, after=()):
        (sums,) = call(
            functools.partial(finish_kernel, heads, n, flips),
            (where,),
            [rows, *state, keys[far], values[far], out_weight],
            [((len(flips) * 2 * ROWS, cols), dtype)],
            n * ROWS * width * cols,
            after,
        )
        return sums.reshape(len(flips), 2 * ROWS, cols)

    given = finish([(1, 1), (0, 1)], bf16)
    from_core = lax.ppermute(given, "heads", [(h, h ^ 1) for h in range(4)])
    sums = finish([(1, 0)], f32, (given,))[0]
    parts = [slice(slot * ROWS, (slot + 1) * ROWS) for slot in range(2)]
    given = [(sums[part] + from_core[0, part].astype(f32)).astype(bf16) for part in parts]
    from_x = [lax.ppermute(block, "heads", [(h, h ^ 2) for h in range(4)]) for block in given]
    kept = finish([(0, 0)], f32, given)[0]
    arrived = []
    for slot, part in enumerate(parts):
        pairs = []
        for f in range(n):
            for h in range(4):
                to = PATTERNS[(slot ^ (f & 1) ^ (h & 1)) + 2 * (h >> 1)][f >> 1]
                pairs.append((4 * f + h, 4 * (2 * to + (h & 1)) + (f >> 1)))
        (total,) = call(
            functools.partial(sum_kernel, part), (), [kept, from_core, from_x[slot]], [((ROWS, cols), bf16)], 0
        )
        arrived.append(lax.ppermute(total, ("frames", "heads"), pairs))
    patterns = [[p[source] for p in PATTERNS].index(to) for source in range(4) for to in range(4)]
    straight = (look_up(patterns, 4 * head + z) ^ y) & 1 == 0
    low, high = arrived
    return jnp.concatenate([jnp.where(straight, low, high), jnp.where(straight, high, low)], axis=1)


def solution(mesh):
    in_specs = (P("frames", "heads"), P(None, "frames", "heads"), P("heads", "frames"))
    out_specs = P("frames", "heads")
    n, heads = mesh.shape["frames"], mesh.shape["heads"]
    total_frames = n * FR_DEV
    reach = min(reach_cap, (total_frames - 1) // 2)
    every = total_frames == 2 * reach + 2 and heads == 4 and n == 2 * heads
    return jax.shard_map(
        on_device_ring if every else on_device_band,
        mesh=mesh,
        in_specs=in_specs,
        out_specs=out_specs,
        check_vma=False,
    )
```

```python
import functools
import math

import jax
import jax.numpy as jnp
from jax import lax
from jax.experimental import pallas as pl
from jax.experimental.pallas import tpu as pltpu
from jax.sharding import PartitionSpec as P

HD = 128
TPF = 32
FR_DEV = 3
ROWS = FR_DEV * TPF
SCALE = HD ** (-0.5) * math.log2(math.e)


reach_cap = 32


def from_behind(x, axis, by):
    devices = lax.axis_size(axis)
    return lax.ppermute(x, axis, [(i, (i + by) % devices) for i in range(devices)])


def on_device_band(queries, keys_values, out_weight):
    total_frames = lax.axis_size("frames") * FR_DEV
    reach = min(reach_cap, (total_frames - 1) // 2)
    steps = (reach + FR_DEV - 1) // FR_DEV
    width = keys_values.shape[2]
    span = FR_DEV + 2 * reach
    stacked = keys_values.reshape(2, FR_DEV, TPF, width)
    pieces = []
    for offset in range(-steps, steps + 1):
        if offset == 0:
            pieces.append(stacked)
        else:
            pieces.append(from_behind(stacked, "frames", -offset))
    window = jnp.concatenate(pieces, axis=1)
    lower_frame = steps * FR_DEV - reach
    extended = window[:, lower_frame : lower_frame + span]
    keys_ext = extended[0].reshape(span * TPF, width)
    values_ext = extended[1].reshape(span * TPF, width)
    row_frame = jnp.arange(FR_DEV * TPF, dtype=jnp.int32) // TPF
    col_frame = jnp.arange(span * TPF, dtype=jnp.int32) // TPF
    allowed = (col_frame[None, :] >= row_frame[:, None]) & (
        col_frame[None, :] <= row_frame[:, None] + 2 * reach
    )
    results = []
    for head in range(width // HD):
        lower = head * HD
        query_cols = queries[:, lower : lower + HD]
        key_cols = keys_ext[:, lower : lower + HD]
        scores = lax.dot_general(
            query_cols, key_cols, (((1,), (1,)), ((), ())), preferred_element_type=jnp.float32
        )
        scores = scores * HD ** (-0.5)
        top = jnp.max(jnp.where(allowed, scores, -1e30), axis=1, keepdims=True)
        weights = jnp.where(allowed, jnp.exp(scores - top), 0.0)
        probs = (weights / jnp.sum(weights, axis=1, keepdims=True)).astype(jnp.bfloat16)
        results.append(
            jnp.dot(
                probs, values_ext[:, lower : lower + HD], preferred_element_type=jnp.float32
            ).astype(jnp.bfloat16)
        )
    attended = jnp.concatenate(results, axis=1)
    partial_rows = jnp.dot(
        attended,
        lax.all_gather(out_weight, "frames", axis=1, tiled=True),
        preferred_element_type=jnp.float32,
    )
    return lax.psum_scatter(
        partial_rows.astype(jnp.bfloat16), "heads", scatter_dimension=1, tiled=True
    )


def ring_order(n):
    return list(range(0, n, 2)) + list(range(n - 1, 0, -2))


def ring_place(f, n):
    return (f >> 1) + (f & 1) * (n - 1 - (f >> 1) * 2)


def hop(x, n, by):
    order = ring_order(n)
    pairs = []
    for i in range(n):
        for h in range(4):
            pairs.append((4 * order[i] + h, 4 * order[(i + by * (1 - 2 * (h & 1))) % n] + h))
    return lax.ppermute(x, ("frames", "heads"), pairs)


def gather_ring(streams, n):
    found = [[block] + [None] * (n - 1) for block in streams]
    for step in range(1, n // 2 + 1):
        for j, blocks in enumerate(found):
            for by in (1, -1):
                if step < n // 2 or (j % 2 == 0) == (by == 1):
                    blocks[by * step % n] = hop(blocks[by * (step - 1) % n], n, by)
    return found


def ring_distance(at_ref, owner, n):
    place, core = at_ref[0], at_ref[4]
    return (place - owner) * (1 - 2 * core) & (n - 1)


def frame_marks(at_ref, blocks, n):
    place, core = at_ref[0], at_ref[4]
    lane = lax.broadcasted_iota(jnp.int32, (TPF, HD), 1)
    marks = []
    for block in blocks:
        owner = (place - block * (1 - 2 * core)) & (n - 1)
        frame = FR_DEV * ring_distance(at_ref, owner ^ 2, n)
        for g in range(FR_DEV):
            marks.append((lane == frame + g) | (lane >= n * FR_DEV))
    return jnp.concatenate([jnp.where(mark, 1.0, 0.0) for mark in marks], axis=0).astype(jnp.bfloat16)


def key_marks(blocks, padding, n):
    lane = lax.broadcasted_iota(jnp.int32, (TPF, HD), 1)
    frames = [FR_DEV * block + g for block in blocks for g in range(FR_DEV)] + [n * FR_DEV] * (padding // TPF)
    return jnp.concatenate([jnp.where(lane == frame, -1e30, 0.0) for frame in frames], axis=0).astype(jnp.bfloat16)


def rows_of(refs, cols, padding=0):
    pieces = [ref[:, cols] for ref in refs]
    if padding:
        pieces.append(jnp.zeros((padding, HD), jnp.bfloat16))
    return jnp.concatenate(pieces, axis=0)


def scores_of(queries, keys):
    return lax.dot_general(queries, keys, (((1,), (1,)), ((), ())), preferred_element_type=jnp.float32)


def soften(scores, floor=None):
    weights, tops = [], []
    for r in range(0, scores.shape[0], TPF):
        parts = [scores[r : r + TPF, c : c + HD] for c in range(0, scores.shape[1], HD)]
        top = jnp.max(functools.reduce(jnp.maximum, parts), axis=1, keepdims=True)
        top = jnp.broadcast_to(top, (TPF, HD))
        if floor is not None:
            top = jnp.maximum(top, floor[r : r + TPF])
        weights.append(jnp.concatenate([jnp.exp2((p - top) * SCALE).astype(jnp.bfloat16) for p in parts], axis=1))
        tops.append(top)
    return jnp.concatenate(weights, axis=0), jnp.concatenate(tops, axis=0)


def mix(weights, values):
    ones = jnp.ones(values.shape, values.dtype)
    mixed = jnp.dot(weights, jnp.concatenate([values, ones], axis=1), preferred_element_type=jnp.float32)
    return mixed[:, :HD], mixed[:, HD:]


PATTERNS = ((3, 0, 1, 3), (1, 3, 2, 1), (2, 1, 0, 2), (0, 2, 3, 0))


def look_up(table, index):
    code = sum(entry << (2 * i) for i, entry in enumerate(table))
    return (jnp.int32(code - (code >> 31 << 32)) >> (2 * index)) & 3


def slot_blocks(at_ref, flip_x, flip_core, n):
    z, y, x, core = (at_ref[i] for i in range(1, 5))
    blocks = []
    for slot in range(2):
        row_y = core ^ flip_core
        to = look_up(sum(PATTERNS, ()), 4 * ((slot ^ y ^ row_y) + 2 * (x ^ flip_x)) + z)
        owner = to + row_y * (n - 1 - 2 * to)
        blocks.append(ring_distance(at_ref, owner, n))
    return blocks


def ahead(scores, heads):
    columns = [slice(head * HD, (head + 1) * HD) for head in range(heads)]
    now = scores(columns[0])
    for head, cols in enumerate(columns):
        later = scores(columns[head + 1]) if head + 1 < heads else None
        yield head, cols, now
        now = later


def split_kernel(kv_ref, keys_ref, values_ref):
    keys_ref[...] = kv_ref[0]
    values_ref[...] = kv_ref[1]


def rows_kernel(n, *refs):
    for d in range(n):
        refs[n][d] = refs[d][...]


def near_kernel(heads, n, at_ref, rows_ref, *refs):
    near = [d for d in range(n) if d != n // 2]
    key_refs, value_refs, (mixed_ref, sum_ref, top_ref) = refs[: n - 1], refs[n - 1 : -3], refs[-3:]
    marks = frame_marks(at_ref, range(n), n)
    keys_marks = key_marks(near, ROWS, n)

    def scores(cols):
        queries = jnp.concatenate([rows_ref[:, :, cols].reshape(n * ROWS, HD), marks], axis=1)
        return scores_of(queries, jnp.concatenate([rows_of(key_refs, cols, ROWS), keys_marks], axis=1))

    for head, cols, now in ahead(scores, heads):
        weights, top = soften(now)
        mixed, total = mix(weights, rows_of(value_refs, cols, ROWS))
        for d in range(n):
            rows = slice(d * ROWS, (d + 1) * ROWS)
            mixed_ref[head, d], sum_ref[head, d], top_ref[head, d] = mixed[rows], total[rows], top[rows]


def finish_kernel(heads, n, flips, at_ref, rows_ref, mixed_ref, sum_ref, top_ref, keys_ref, values_ref, w_ref, *refs):
    blocks = [block for flip in flips for block in slot_blocks(at_ref, *flip, n)]
    marks = frame_marks(at_ref, blocks, n)
    keys_marks = key_marks([n // 2], TPF, n)

    def of(ref, head):
        return jnp.concatenate([ref[head, block] for block in blocks], axis=0)

    columns = [slice(head * HD, (head + 1) * HD) for head in range(heads)]
    scores, attended = [], []
    for cols in columns:
        queries = jnp.concatenate([rows_ref[block, :, cols] for block in blocks], axis=0)
        keys = jnp.concatenate([rows_of([keys_ref], cols, TPF), keys_marks], axis=1)
        scores.append(scores_of(jnp.concatenate([queries, marks], axis=1), keys))
    softened = [soften(now, of(top_ref, head)) for head, now in enumerate(scores)]
    more = [mix(weights, rows_of([values_ref], cols, TPF)) for (weights, _), cols in zip(softened, columns)]
    for head, ((_, top), (mixed, total)) in enumerate(zip(softened, more)):
        kept = jnp.exp2((of(top_ref, head) - top) * SCALE)
        mixed, total = mixed + of(mixed_ref, head) * kept, total + of(sum_ref, head) * kept
        attended.append((mixed / total).astype(jnp.bfloat16))
    rows = jnp.concatenate(attended, axis=1)
    refs[-1][...] = jnp.dot(rows, w_ref[...], preferred_element_type=jnp.float32).astype(refs[-1].dtype)


def sum_kernel(rows, kept_ref, from_core_ref, from_x_ref, total_ref):
    total = kept_ref[rows] + from_core_ref[1, rows].astype(jnp.float32) + from_x_ref[...].astype(jnp.float32)
    total_ref[...] = total.astype(total_ref.dtype)


def place_kernel(swapped_ref, first_ref, second_ref, out_ref, sems):
    cols = first_ref.shape[1]
    swapped = swapped_ref[0] & 1
    copies = []
    for i, (ref, at) in enumerate(((first_ref, swapped), (second_ref, 1 - swapped))):
        columns = pl.ds(pl.multiple_of(at * cols, HD), cols)
        copies.append(pltpu.make_async_copy(ref, out_ref.at[:, columns], sems.at[i]))
    for copy in copies:
        copy.start()
    for copy in copies:
        copy.wait()


def call(kernel, scalars, operands, outs, flops, after=()):
    vmem = pl.BlockSpec(memory_space=pltpu.VMEM)
    return pl.pallas_call(
        kernel,
        out_shape=[jax.ShapeDtypeStruct(shape, dtype) for shape, dtype in outs],
        in_specs=[pl.BlockSpec(memory_space=pltpu.SMEM)] * len(scalars)
        + [vmem] * len(operands)
        + [pl.BlockSpec(memory_space=pl.ANY)] * len(after),
        out_specs=[vmem] * len(outs),
        compiler_params=pltpu.CompilerParams(vmem_limit_bytes=20 * 1024 * 1024),
        cost_estimate=pl.CostEstimate(flops=flops, bytes_accessed=0, transcendentals=0),
    )(*scalars, *operands, *after)


def on_device_ring(queries, keys_values, out_weight):
    n = lax.axis_size("frames")
    frame, head = lax.axis_index("frames"), lax.axis_index("heads")
    z, y, x, core = frame >> 1, frame & 1, head >> 1, head & 1
    where = jnp.stack([ring_place(frame, n), z, y, x, core]).astype(jnp.int32)
    width, cols = out_weight.shape
    heads = width // HD
    f32, bf16 = jnp.float32, jnp.bfloat16
    block = (queries.shape, bf16)
    own = call(split_kernel, (), [keys_values], [block, block], 0)
    queries, keys, values = gather_ring([queries, *own], n)
    (rows,) = call(functools.partial(rows_kernel, n), (), queries, [((n, ROWS, width), bf16)], 0)
    far = n // 2
    state = call(
        functools.partial(near_kernel, heads, n),
        (where,),
        [rows, *(blocks[d] for blocks in (keys, values) for d in range(n) if d != far)],
        [((heads, n, ROWS, HD), f32)] * 3,
        4 * n * (n - 1) * ROWS**2 * width,
    )

    def finish(flips, dtype, after=()):
        (sums,) = call(
            functools.partial(finish_kernel, heads, n, flips),
            (where,),
            [rows, *state, keys[far], values[far], out_weight],
            [((len(flips) * 2 * ROWS, cols), dtype)],
            n * ROWS * width * cols,
            after,
        )
        return sums.reshape(len(flips), 2 * ROWS, cols)

    given = finish([(1, 1), (0, 1)], bf16)
    from_core = lax.ppermute(given, "heads", [(h, h ^ 1) for h in range(4)])
    sums = finish([(1, 0)], f32, (given,))[0]
    parts = [slice(slot * ROWS, (slot + 1) * ROWS) for slot in range(2)]
    given = [(sums[part] + from_core[0, part].astype(f32)).astype(bf16) for part in parts]
    from_x = [lax.ppermute(block, "heads", [(h, h ^ 2) for h in range(4)]) for block in given]
    kept = finish([(0, 0)], f32, given)[0]
    arrived = []
    for slot, part in enumerate(parts):
        pairs = []
        for f in range(n):
            for h in range(4):
                to = PATTERNS[(slot ^ (f & 1) ^ (h & 1)) + 2 * (h >> 1)][f >> 1]
                pairs.append((4 * f + h, 4 * (2 * to + (h & 1)) + (f >> 1)))
        (total,) = call(
            functools.partial(sum_kernel, part), (), [kept, from_core, from_x[slot]], [((ROWS, cols), bf16)], 0
        )
        arrived.append(lax.ppermute(total, ("frames", "heads"), pairs))
    patterns = [[p[source] for p in PATTERNS].index(to) for source in range(4) for to in range(4)]
    swapped = (look_up(patterns, 4 * head + z) ^ y) & 1
    vmem = pl.BlockSpec(memory_space=pltpu.VMEM)
    return pl.pallas_call(
        place_kernel,
        out_shape=jax.ShapeDtypeStruct((ROWS, 2 * cols), bf16),
        in_specs=[pl.BlockSpec(memory_space=pltpu.SMEM), vmem, vmem],
        out_specs=pl.BlockSpec(memory_space=pltpu.HBM),
        scratch_shapes=[pltpu.SemaphoreType.DMA((2,))],
    )(swapped.reshape(1).astype(jnp.int32), *arrived)


def solution(mesh):
    in_specs = (P("frames", "heads"), P(None, "frames", "heads"), P("heads", "frames"))
    out_specs = P("frames", "heads")
    n, heads = mesh.shape["frames"], mesh.shape["heads"]
    total_frames = n * FR_DEV
    reach = min(reach_cap, (total_frames - 1) // 2)
    every = total_frames == 2 * reach + 2 and heads == 4 and n == 2 * heads
    return jax.shard_map(
        on_device_ring if every else on_device_band,
        mesh=mesh,
        in_specs=in_specs,
        out_specs=out_specs,
        check_vma=False,
    )
```

```python
import functools
import math

import jax
import jax.numpy as jnp
from jax import lax
from jax.experimental import pallas as pl
from jax.experimental.pallas import tpu as pltpu
from jax.sharding import PartitionSpec as P

HD = 128
TPF = 32
FR_DEV = 3
ROWS = FR_DEV * TPF
SCALE = HD ** (-0.5) * math.log2(math.e)


reach_cap = 32


def from_behind(x, axis, by):
    devices = lax.axis_size(axis)
    return lax.ppermute(x, axis, [(i, (i + by) % devices) for i in range(devices)])


def on_device_band(queries, keys_values, out_weight):
    total_frames = lax.axis_size("frames") * FR_DEV
    reach = min(reach_cap, (total_frames - 1) // 2)
    steps = (reach + FR_DEV - 1) // FR_DEV
    width = keys_values.shape[2]
    span = FR_DEV + 2 * reach
    stacked = keys_values.reshape(2, FR_DEV, TPF, width)
    pieces = []
    for offset in range(-steps, steps + 1):
        if offset == 0:
            pieces.append(stacked)
        else:
            pieces.append(from_behind(stacked, "frames", -offset))
    window = jnp.concatenate(pieces, axis=1)
    lower_frame = steps * FR_DEV - reach
    extended = window[:, lower_frame : lower_frame + span]
    keys_ext = extended[0].reshape(span * TPF, width)
    values_ext = extended[1].reshape(span * TPF, width)
    row_frame = jnp.arange(FR_DEV * TPF, dtype=jnp.int32) // TPF
    col_frame = jnp.arange(span * TPF, dtype=jnp.int32) // TPF
    allowed = (col_frame[None, :] >= row_frame[:, None]) & (
        col_frame[None, :] <= row_frame[:, None] + 2 * reach
    )
    results = []
    for head in range(width // HD):
        lower = head * HD
        query_cols = queries[:, lower : lower + HD]
        key_cols = keys_ext[:, lower : lower + HD]
        scores = lax.dot_general(
            query_cols, key_cols, (((1,), (1,)), ((), ())), preferred_element_type=jnp.float32
        )
        scores = scores * HD ** (-0.5)
        top = jnp.max(jnp.where(allowed, scores, -1e30), axis=1, keepdims=True)
        weights = jnp.where(allowed, jnp.exp(scores - top), 0.0)
        probs = (weights / jnp.sum(weights, axis=1, keepdims=True)).astype(jnp.bfloat16)
        results.append(
            jnp.dot(
                probs, values_ext[:, lower : lower + HD], preferred_element_type=jnp.float32
            ).astype(jnp.bfloat16)
        )
    attended = jnp.concatenate(results, axis=1)
    partial_rows = jnp.dot(
        attended,
        lax.all_gather(out_weight, "frames", axis=1, tiled=True),
        preferred_element_type=jnp.float32,
    )
    return lax.psum_scatter(
        partial_rows.astype(jnp.bfloat16), "heads", scatter_dimension=1, tiled=True
    )


def ring_order(n):
    return list(range(0, n, 2)) + list(range(n - 1, 0, -2))


def ring_place(f, n):
    return (f >> 1) + (f & 1) * (n - 1 - (f >> 1) * 2)


def hop(x, n, by):
    order = ring_order(n)
    pairs = []
    for i in range(n):
        for h in range(4):
            pairs.append((4 * order[i] + h, 4 * order[(i + by * (2 * (h & 1) - 1)) % n] + h))
    return lax.ppermute(x, ("frames", "heads"), pairs)


def gather_ring(streams, n):
    found = [[block] + [None] * (n - 1) for block in streams]
    for step in range(1, n // 2 + 1):
        for j, blocks in enumerate(found):
            for by in (1, -1):
                if step < n // 2 or (j % 2 == 0) == (by == 1):
                    blocks[by * step % n] = hop(blocks[by * (step - 1) % n], n, by)
    return found


def ring_distance(at_ref, owner, n):
    place, core = at_ref[0], at_ref[4]
    return (place - owner) * (2 * core - 1) & (n - 1)


def frame_marks(at_ref, blocks, n):
    place, core = at_ref[0], at_ref[4]
    lane = lax.broadcasted_iota(jnp.int32, (TPF, HD), 1)
    marks = []
    for block in blocks:
        owner = (place - block * (2 * core - 1)) & (n - 1)
        frame = FR_DEV * ring_distance(at_ref, owner ^ 2, n)
        for g in range(FR_DEV):
            marks.append((lane == frame + g) | (lane >= n * FR_DEV))
    return jnp.concatenate([jnp.where(mark, 1.0, 0.0) for mark in marks], axis=0).astype(jnp.bfloat16)


def key_marks(blocks, padding, n):
    lane = lax.broadcasted_iota(jnp.int32, (TPF, HD), 1)
    frames = [FR_DEV * block + g for block in blocks for g in range(FR_DEV)] + [n * FR_DEV] * (padding // TPF)
    return jnp.concatenate([jnp.where(lane == frame, -1e30, 0.0) for frame in frames], axis=0).astype(jnp.bfloat16)


def rows_of(refs, cols, padding=0):
    pieces = [ref[:, cols] for ref in refs]
    if padding:
        pieces.append(jnp.zeros((padding, HD), jnp.bfloat16))
    return jnp.concatenate(pieces, axis=0)


def scores_of(queries, keys):
    return lax.dot_general(queries, keys, (((1,), (1,)), ((), ())), preferred_element_type=jnp.float32)


def soften(scores, floor=None):
    weights, tops = [], []
    for r in range(0, scores.shape[0], TPF):
        parts = [scores[r : r + TPF, c : c + HD] for c in range(0, scores.shape[1], HD)]
        top = jnp.max(functools.reduce(jnp.maximum, parts), axis=1, keepdims=True)
        top = jnp.broadcast_to(top, (TPF, HD))
        if floor is not None:
            top = jnp.maximum(top, floor[r : r + TPF])
        weights.append(jnp.concatenate([jnp.exp2((p - top) * SCALE).astype(jnp.bfloat16) for p in parts], axis=1))
        tops.append(top)
    return jnp.concatenate(weights, axis=0), jnp.concatenate(tops, axis=0)


def mix(weights, values):
    ones = jnp.ones(values.shape, values.dtype)
    mixed = jnp.dot(weights, jnp.concatenate([values, ones], axis=1), preferred_element_type=jnp.float32)
    return mixed[:, :HD], mixed[:, HD:]


PATTERNS = ((3, 0, 1, 3), (1, 3, 2, 1), (2, 1, 0, 2), (0, 2, 3, 0))


def look_up(table, index):
    code = sum(entry << (2 * i) for i, entry in enumerate(table))
    return (jnp.int32(code - (code >> 31 << 32)) >> (2 * index)) & 3


def slot_blocks(at_ref, flip_x, flip_core, n):
    z, y, x, core = (at_ref[i] for i in range(1, 5))
    blocks = []
    for slot in range(2):
        row_y = core ^ flip_core
        to = look_up(sum(PATTERNS, ()), 4 * ((slot ^ y ^ row_y) + 2 * (x ^ flip_x)) + z)
        owner = to + row_y * (n - 1 - 2 * to)
        blocks.append(ring_distance(at_ref, owner, n))
    return blocks


def ahead(scores, heads):
    columns = [slice(head * HD, (head + 1) * HD) for head in range(heads)]
    now = scores(columns[0])
    for head, cols in enumerate(columns):
        later = scores(columns[head + 1]) if head + 1 < heads else None
        yield head, cols, now
        now = later


def split_kernel(kv_ref, keys_ref, values_ref):
    keys_ref[...] = kv_ref[0]
    values_ref[...] = kv_ref[1]


def rows_kernel(n, *refs):
    for d in range(n):
        refs[n][d] = refs[d][...]


def near_kernel(heads, n, at_ref, rows_ref, *refs):
    near = [d for d in range(n) if d != n // 2]
    key_refs, value_refs, (mixed_ref, sum_ref, top_ref) = refs[: n - 1], refs[n - 1 : -3], refs[-3:]
    marks = frame_marks(at_ref, range(n), n)
    keys_marks = key_marks(near, ROWS, n)

    def scores(cols):
        queries = jnp.concatenate([rows_ref[:, :, cols].reshape(n * ROWS, HD), marks], axis=1)
        return scores_of(queries, jnp.concatenate([rows_of(key_refs, cols, ROWS), keys_marks], axis=1))

    for head, cols, now in ahead(scores, heads):
        weights, top = soften(now)
        mixed, total = mix(weights, rows_of(value_refs, cols, ROWS))
        for d in range(n):
            rows = slice(d * ROWS, (d + 1) * ROWS)
            mixed_ref[head, d], sum_ref[head, d], top_ref[head, d] = mixed[rows], total[rows], top[rows]


def finish_kernel(heads, n, flips, at_ref, rows_ref, mixed_ref, sum_ref, top_ref, keys_ref, values_ref, w_ref, *refs):
    blocks = [block for flip in flips for block in slot_blocks(at_ref, *flip, n)]
    marks = frame_marks(at_ref, blocks, n)
    keys_marks = key_marks([n // 2], TPF, n)

    def of(ref, head):
        return jnp.concatenate([ref[head, block] for block in blocks], axis=0)

    columns = [slice(head * HD, (head + 1) * HD) for head in range(heads)]
    scores, attended = [], []
    for cols in columns:
        queries = jnp.concatenate([rows_ref[block, :, cols] for block in blocks], axis=0)
        keys = jnp.concatenate([rows_of([keys_ref], cols, TPF), keys_marks], axis=1)
        scores.append(scores_of(jnp.concatenate([queries, marks], axis=1), keys))
    softened = [soften(now, of(top_ref, head)) for head, now in enumerate(scores)]
    more = [mix(weights, rows_of([values_ref], cols, TPF)) for (weights, _), cols in zip(softened, columns)]
    for head, ((_, top), (mixed, total)) in enumerate(zip(softened, more)):
        kept = jnp.exp2((of(top_ref, head) - top) * SCALE)
        mixed, total = mixed + of(mixed_ref, head) * kept, total + of(sum_ref, head) * kept
        attended.append((mixed / total).astype(jnp.bfloat16))
    rows = jnp.concatenate(attended, axis=1)
    refs[-1][...] = jnp.dot(rows, w_ref[...], preferred_element_type=jnp.float32).astype(refs[-1].dtype)


def sum_kernel(rows, kept_ref, from_core_ref, from_x_ref, total_ref):
    total = kept_ref[rows] + from_core_ref[1, rows].astype(jnp.float32) + from_x_ref[...].astype(jnp.float32)
    total_ref[...] = total.astype(total_ref.dtype)


def call(kernel, scalars, operands, outs, flops, after=()):
    vmem = pl.BlockSpec(memory_space=pltpu.VMEM)
    return pl.pallas_call(
        kernel,
        out_shape=[jax.ShapeDtypeStruct(shape, dtype) for shape, dtype in outs],
        in_specs=[pl.BlockSpec(memory_space=pltpu.SMEM)] * len(scalars)
        + [vmem] * len(operands)
        + [pl.BlockSpec(memory_space=pl.ANY)] * len(after),
        out_specs=[vmem] * len(outs),
        compiler_params=pltpu.CompilerParams(vmem_limit_bytes=20 * 1024 * 1024),
        cost_estimate=pl.CostEstimate(flops=flops, bytes_accessed=0, transcendentals=0),
    )(*scalars, *operands, *after)


def on_device_ring(queries, keys_values, out_weight):
    n = lax.axis_size("frames")
    frame, head = lax.axis_index("frames"), lax.axis_index("heads")
    z, y, x, core = frame >> 1, frame & 1, head >> 1, head & 1
    where = jnp.stack([ring_place(frame, n), z, y, x, core]).astype(jnp.int32)
    width, cols = out_weight.shape
    heads = width // HD
    f32, bf16 = jnp.float32, jnp.bfloat16
    block = (queries.shape, bf16)
    own = call(split_kernel, (), [keys_values], [block, block], 0)
    queries, keys, values = gather_ring([queries, *own], n)
    (rows,) = call(functools.partial(rows_kernel, n), (), queries, [((n, ROWS, width), bf16)], 0)
    far = n // 2
    state = call(
        functools.partial(near_kernel, heads, n),
        (where,),
        [rows, *(blocks[d] for blocks in (keys, values) for d in range(n) if d != far)],
        [((heads, n, ROWS, HD), f32)] * 3,
        4 * n * (n - 1) * ROWS**2 * width,
    )

    def finish(flips, dtype, after=()):
        (sums,) = call(
            functools.partial(finish_kernel, heads, n, flips),
            (where,),
            [rows, *state, keys[far], values[far], out_weight],
            [((len(flips) * 2 * ROWS, cols), dtype)],
            n * ROWS * width * cols,
            after,
        )
        return sums.reshape(len(flips), 2 * ROWS, cols)

    given = finish([(1, 1), (0, 1)], bf16)
    from_core = lax.ppermute(given, "heads", [(h, h ^ 1) for h in range(4)])
    sums = finish([(1, 0)], f32, (given,))[0]
    parts = [slice(slot * ROWS, (slot + 1) * ROWS) for slot in range(2)]
    given = [(sums[part] + from_core[0, part].astype(f32)).astype(bf16) for part in parts]
    from_x = [lax.ppermute(block, "heads", [(h, h ^ 2) for h in range(4)]) for block in given]
    kept = finish([(0, 0)], f32, given)[0]
    arrived = []
    for slot, part in enumerate(parts):
        pairs = []
        for f in range(n):
            for h in range(4):
                to = PATTERNS[(slot ^ (f & 1) ^ (h & 1)) + 2 * (h >> 1)][f >> 1]
                pairs.append((4 * f + h, 4 * (2 * to + (h & 1)) + (f >> 1)))
        (total,) = call(
            functools.partial(sum_kernel, part), (), [kept, from_core, from_x[slot]], [((ROWS, cols), bf16)], 0
        )
        arrived.append(lax.ppermute(total, ("frames", "heads"), pairs))
    patterns = [[p[source] for p in PATTERNS].index(to) for source in range(4) for to in range(4)]
    straight = (look_up(patterns, 4 * head + z) ^ y) & 1 == 0
    low, high = arrived
    return jnp.concatenate([jnp.where(straight, low, high), jnp.where(straight, high, low)], axis=1)


def solution(mesh):
    in_specs = (P("frames", "heads"), P(None, "frames", "heads"), P("heads", "frames"))
    out_specs = P("frames", "heads")
    n, heads = mesh.shape["frames"], mesh.shape["heads"]
    total_frames = n * FR_DEV
    reach = min(reach_cap, (total_frames - 1) // 2)
    every = total_frames == 2 * reach + 2 and heads == 4 and n == 2 * heads
    return jax.shard_map(
        on_device_ring if every else on_device_band,
        mesh=mesh,
        in_specs=in_specs,
        out_specs=out_specs,
        check_vma=False,
    )
```

```python
import functools
import math

import jax
import jax.numpy as jnp
from jax import lax
from jax.experimental import pallas as pl
from jax.experimental.pallas import tpu as pltpu
from jax.sharding import PartitionSpec as P

HD = 128
TPF = 32
FR_DEV = 3
ROWS = FR_DEV * TPF
SCALE = HD ** (-0.5) * math.log2(math.e)


reach_cap = 32


def from_behind(x, axis, by):
    devices = lax.axis_size(axis)
    return lax.ppermute(x, axis, [(i, (i + by) % devices) for i in range(devices)])


def on_device_band(queries, keys_values, out_weight):
    total_frames = lax.axis_size("frames") * FR_DEV
    reach = min(reach_cap, (total_frames - 1) // 2)
    steps = (reach + FR_DEV - 1) // FR_DEV
    width = keys_values.shape[2]
    span = FR_DEV + 2 * reach
    stacked = keys_values.reshape(2, FR_DEV, TPF, width)
    pieces = []
    for offset in range(-steps, steps + 1):
        if offset == 0:
            pieces.append(stacked)
        else:
            pieces.append(from_behind(stacked, "frames", -offset))
    window = jnp.concatenate(pieces, axis=1)
    lower_frame = steps * FR_DEV - reach
    extended = window[:, lower_frame : lower_frame + span]
    keys_ext = extended[0].reshape(span * TPF, width)
    values_ext = extended[1].reshape(span * TPF, width)
    row_frame = jnp.arange(FR_DEV * TPF, dtype=jnp.int32) // TPF
    col_frame = jnp.arange(span * TPF, dtype=jnp.int32) // TPF
    allowed = (col_frame[None, :] >= row_frame[:, None]) & (
        col_frame[None, :] <= row_frame[:, None] + 2 * reach
    )
    results = []
    for head in range(width // HD):
        lower = head * HD
        query_cols = queries[:, lower : lower + HD]
        key_cols = keys_ext[:, lower : lower + HD]
        scores = lax.dot_general(
            query_cols, key_cols, (((1,), (1,)), ((), ())), preferred_element_type=jnp.float32
        )
        scores = scores * HD ** (-0.5)
        top = jnp.max(jnp.where(allowed, scores, -1e30), axis=1, keepdims=True)
        weights = jnp.where(allowed, jnp.exp(scores - top), 0.0)
        probs = (weights / jnp.sum(weights, axis=1, keepdims=True)).astype(jnp.bfloat16)
        results.append(
            jnp.dot(
                probs, values_ext[:, lower : lower + HD], preferred_element_type=jnp.float32
            ).astype(jnp.bfloat16)
        )
    attended = jnp.concatenate(results, axis=1)
    partial_rows = jnp.dot(
        attended,
        lax.all_gather(out_weight, "frames", axis=1, tiled=True),
        preferred_element_type=jnp.float32,
    )
    return lax.psum_scatter(
        partial_rows.astype(jnp.bfloat16), "heads", scatter_dimension=1, tiled=True
    )


def ring_order(n):
    return list(range(0, n, 2)) + list(range(n - 1, 0, -2))


def ring_place(f, n):
    return (f >> 1) + (f & 1) * (n - 1 - (f >> 1) * 2)


def hop(x, n, by):
    order = ring_order(n)
    pairs = []
    for i in range(n):
        for h in range(4):
            pairs.append((4 * order[i] + h, 4 * order[(i + by * (1 - 2 * (h & 1))) % n] + h))
    return lax.ppermute(x, ("frames", "heads"), pairs)


def gather_ring(streams, n):
    found = [[block] + [None] * (n - 1) for block in streams]
    for step in range(1, n // 2 + 1):
        for j, blocks in enumerate(found):
            for by in (1, -1):
                if step < n // 2 or (j % 2 == 0) == (by == 1):
                    blocks[by * step % n] = hop(blocks[by * (step - 1) % n], n, by)
    return found


def ring_distance(at_ref, owner, n):
    place, core = at_ref[0], at_ref[4]
    return (place - owner) * (1 - 2 * core) & (n - 1)


def frame_marks(at_ref, blocks, n):
    place, core = at_ref[0], at_ref[4]
    lane = lax.broadcasted_iota(jnp.int32, (TPF, HD), 1)
    marks = []
    for block in blocks:
        owner = (place - block * (1 - 2 * core)) & (n - 1)
        frame = FR_DEV * ring_distance(at_ref, owner ^ 2, n)
        for g in range(FR_DEV):
            marks.append((lane == frame + g) | (lane >= n * FR_DEV))
    return jnp.concatenate([jnp.where(mark, 1.0, 0.0) for mark in marks], axis=0).astype(jnp.bfloat16)


def key_marks(blocks, padding, n):
    lane = lax.broadcasted_iota(jnp.int32, (TPF, HD), 1)
    frames = [FR_DEV * block + g for block in blocks for g in range(FR_DEV)] + [n * FR_DEV] * (padding // TPF)
    return jnp.concatenate([jnp.where(lane == frame, -1e30, 0.0) for frame in frames], axis=0).astype(jnp.bfloat16)


def rows_of(refs, cols, padding=0):
    pieces = [ref[:, cols] for ref in refs]
    if padding:
        pieces.append(jnp.zeros((padding, HD), jnp.bfloat16))
    return jnp.concatenate(pieces, axis=0)


def scores_of(queries, keys):
    return lax.dot_general(queries, keys, (((1,), (1,)), ((), ())), preferred_element_type=jnp.float32)


def soften(scores, floor=None):
    weights, tops = [], []
    for r in range(0, scores.shape[0], TPF):
        parts = [scores[r : r + TPF, c : c + HD] for c in range(0, scores.shape[1], HD)]
        top = jnp.max(functools.reduce(jnp.maximum, parts), axis=1, keepdims=True)
        top = jnp.broadcast_to(top, (TPF, HD))
        if floor is not None:
            top = jnp.maximum(top, floor[r : r + TPF])
        weights.append(jnp.concatenate([jnp.exp2((p - top) * SCALE).astype(jnp.bfloat16) for p in parts], axis=1))
        tops.append(top)
    return jnp.concatenate(weights, axis=0), jnp.concatenate(tops, axis=0)


def mix(weights, values):
    ones = jnp.ones(values.shape, values.dtype)
    mixed = jnp.dot(weights, jnp.concatenate([values, ones], axis=1), preferred_element_type=jnp.float32)
    return mixed[:, :HD], mixed[:, HD:]


PATTERNS = ((3, 0, 1, 3), (1, 3, 2, 1), (2, 1, 0, 2), (0, 2, 3, 0))


def look_up(table, index):
    code = sum(entry << (2 * i) for i, entry in enumerate(table))
    return (jnp.int32(code - (code >> 31 << 32)) >> (2 * index)) & 3


def slot_blocks(at_ref, flip_x, flip_core, n):
    z, y, x, core = (at_ref[i] for i in range(1, 5))
    blocks = []
    for slot in range(2):
        row_y = core ^ flip_core
        to = look_up(sum(PATTERNS, ()), 4 * ((slot ^ y ^ row_y ^ x ^ flip_x) + 2 * (x ^ flip_x)) + z)
        owner = to + row_y * (n - 1 - 2 * to)
        blocks.append(ring_distance(at_ref, owner, n))
    return blocks


def ahead(scores, heads):
    columns = [slice(head * HD, (head + 1) * HD) for head in range(heads)]
    now = scores(columns[0])
    for head, cols in enumerate(columns):
        later = scores(columns[head + 1]) if head + 1 < heads else None
        yield head, cols, now
        now = later


def split_kernel(kv_ref, keys_ref, values_ref):
    keys_ref[...] = kv_ref[0]
    values_ref[...] = kv_ref[1]


def rows_kernel(n, *refs):
    for d in range(n):
        refs[n][d] = refs[d][...]


def near_kernel(heads, n, at_ref, rows_ref, *refs):
    near = [d for d in range(n) if d != n // 2]
    key_refs, value_refs, (mixed_ref, sum_ref, top_ref) = refs[: n - 1], refs[n - 1 : -3], refs[-3:]
    marks = frame_marks(at_ref, range(n), n)
    keys_marks = key_marks(near, ROWS, n)

    def scores(cols):
        queries = jnp.concatenate([rows_ref[:, :, cols].reshape(n * ROWS, HD), marks], axis=1)
        return scores_of(queries, jnp.concatenate([rows_of(key_refs, cols, ROWS), keys_marks], axis=1))

    for head, cols, now in ahead(scores, heads):
        weights, top = soften(now)
        mixed, total = mix(weights, rows_of(value_refs, cols, ROWS))
        for d in range(n):
            rows = slice(d * ROWS, (d + 1) * ROWS)
            mixed_ref[head, d], sum_ref[head, d], top_ref[head, d] = mixed[rows], total[rows], top[rows]


def finish_kernel(heads, n, flips, at_ref, rows_ref, mixed_ref, sum_ref, top_ref, keys_ref, values_ref, w_ref, *refs):
    blocks = [block for flip in flips for block in slot_blocks(at_ref, *flip, n)]
    marks = frame_marks(at_ref, blocks, n)
    keys_marks = key_marks([n // 2], TPF, n)

    def of(ref, head):
        return jnp.concatenate([ref[head, block] for block in blocks], axis=0)

    columns = [slice(head * HD, (head + 1) * HD) for head in range(heads)]
    scores, attended = [], []
    for cols in columns:
        queries = jnp.concatenate([rows_ref[block, :, cols] for block in blocks], axis=0)
        keys = jnp.concatenate([rows_of([keys_ref], cols, TPF), keys_marks], axis=1)
        scores.append(scores_of(jnp.concatenate([queries, marks], axis=1), keys))
    softened = [soften(now, of(top_ref, head)) for head, now in enumerate(scores)]
    more = [mix(weights, rows_of([values_ref], cols, TPF)) for (weights, _), cols in zip(softened, columns)]
    for head, ((_, top), (mixed, total)) in enumerate(zip(softened, more)):
        kept = jnp.exp2((of(top_ref, head) - top) * SCALE)
        mixed, total = mixed + of(mixed_ref, head) * kept, total + of(sum_ref, head) * kept
        attended.append((mixed / total).astype(jnp.bfloat16))
    rows = jnp.concatenate(attended, axis=1)
    refs[-1][...] = jnp.dot(rows, w_ref[...], preferred_element_type=jnp.float32).astype(refs[-1].dtype)


def sum_kernel(rows, kept_ref, from_core_ref, from_x_ref, total_ref):
    total = kept_ref[rows] + from_core_ref[1, rows].astype(jnp.float32) + from_x_ref[...].astype(jnp.float32)
    total_ref[...] = total.astype(total_ref.dtype)


def call(kernel, scalars, operands, outs, flops, after=()):
    vmem = pl.BlockSpec(memory_space=pltpu.VMEM)
    return pl.pallas_call(
        kernel,
        out_shape=[jax.ShapeDtypeStruct(shape, dtype) for shape, dtype in outs],
        in_specs=[pl.BlockSpec(memory_space=pltpu.SMEM)] * len(scalars)
        + [vmem] * len(operands)
        + [pl.BlockSpec(memory_space=pl.ANY)] * len(after),
        out_specs=[vmem] * len(outs),
        compiler_params=pltpu.CompilerParams(vmem_limit_bytes=20 * 1024 * 1024),
        cost_estimate=pl.CostEstimate(flops=flops, bytes_accessed=0, transcendentals=0),
    )(*scalars, *operands, *after)


def on_device_ring(queries, keys_values, out_weight):
    n = lax.axis_size("frames")
    frame, head = lax.axis_index("frames"), lax.axis_index("heads")
    z, y, x, core = frame >> 1, frame & 1, head >> 1, head & 1
    where = jnp.stack([ring_place(frame, n), z, y, x, core]).astype(jnp.int32)
    width, cols = out_weight.shape
    heads = width // HD
    f32, bf16 = jnp.float32, jnp.bfloat16
    block = (queries.shape, bf16)
    own = call(split_kernel, (), [keys_values], [block, block], 0)
    queries, keys, values = gather_ring([queries, *own], n)
    (rows,) = call(functools.partial(rows_kernel, n), (), queries, [((n, ROWS, width), bf16)], 0)
    far = n // 2
    state = call(
        functools.partial(near_kernel, heads, n),
        (where,),
        [rows, *(blocks[d] for blocks in (keys, values) for d in range(n) if d != far)],
        [((heads, n, ROWS, HD), f32)] * 3,
        4 * n * (n - 1) * ROWS**2 * width,
    )

    def finish(flips, dtype, after=()):
        (sums,) = call(
            functools.partial(finish_kernel, heads, n, flips),
            (where,),
            [rows, *state, keys[far], values[far], out_weight],
            [((len(flips) * 2 * ROWS, cols), dtype)],
            n * ROWS * width * cols,
            after,
        )
        return sums.reshape(len(flips), 2 * ROWS, cols)

    given = finish([(1, 1), (0, 1)], bf16)
    from_core = lax.ppermute(given, "heads", [(h, h ^ 1) for h in range(4)])
    sums = finish([(1, 0)], f32, (given,))[0]
    parts = [slice(slot * ROWS, (slot + 1) * ROWS) for slot in range(2)]
    given = [(sums[part] + from_core[0, part].astype(f32)).astype(bf16) for part in parts]
    from_x = [lax.ppermute(block, "heads", [(h, h ^ 2) for h in range(4)]) for block in given]
    kept = finish([(0, 0)], f32, given)[0]
    arrived = []
    for slot, part in enumerate(parts):
        pairs = []
        for f in range(n):
            for h in range(4):
                to = PATTERNS[(slot ^ (f & 1) ^ (h & 1) ^ (h >> 1)) + 2 * (h >> 1)][f >> 1]
                pairs.append((4 * f + h, 4 * (2 * to + (h & 1)) + (f >> 1)))
        (total,) = call(
            functools.partial(sum_kernel, part), (), [kept, from_core, from_x[slot]], [((ROWS, cols), bf16)], 0
        )
        arrived.append(lax.ppermute(total, ("frames", "heads"), pairs))
    patterns = [[p[source] for p in PATTERNS].index(to) for source in range(4) for to in range(4)]
    pattern = look_up(patterns, 4 * head + z)
    straight = (pattern ^ (pattern >> 1) ^ y) & 1 == 0
    low, high = arrived
    return jnp.concatenate([jnp.where(straight, low, high), jnp.where(straight, high, low)], axis=1)


def solution(mesh):
    in_specs = (P("frames", "heads"), P(None, "frames", "heads"), P("heads", "frames"))
    out_specs = P("frames", "heads")
    n, heads = mesh.shape["frames"], mesh.shape["heads"]
    total_frames = n * FR_DEV
    reach = min(reach_cap, (total_frames - 1) // 2)
    every = total_frames == 2 * reach + 2 and heads == 4 and n == 2 * heads
    return jax.shard_map(
        on_device_ring if every else on_device_band,
        mesh=mesh,
        in_specs=in_specs,
        out_specs=out_specs,
        check_vma=False,
    )
```
